32 devices in a mesh: dp: 2 (over core), zero: 16 (over z, y, x).
Axes of the slice: x: 2, y: 2, z: 4, core: 2. Of those that a mesh axis runs over, the one named last changes fastest.
Arguments:
- tokens: bfloat16 [32768, 768], P(('dp', 'zero')), may hold values from -6 to 6
- segments: int32 [32768], P(('dp', 'zero')), may hold values from 0 to 127, never falling along the last dimension, each value on 1 to 1024 neighbouring positions
- cotangent: bfloat16 [32768, 768], P(('dp', 'zero')), may hold values from -6.05 to 6.05
- master: float32 [9440256], P('zero'), may hold values from -1.8 to 1.8
- moment_one: float32 [9440256], P('zero'), may hold values from -4 to 4
- moment_two: float32 [9440256], P('zero'), may hold values from 0.003 to 0.3
Outputs:
- output: bfloat16 [32768, 768], P(('dp', 'zero'))
- input_grad: float32 [32768, 768], P(('dp', 'zero'))
- grad_shard: float32 [9440256], P('zero')
- moment_one_new: float32 [9440256], P('zero')
- moment_two_new: float32 [9440256], P('zero')
- master_new: float32 [9440256], P('zero')
- weight_new: bfloat16 [9440256], P('zero')
The draws below stay inside these ranges and needn't reach their ends.
Inputs may be any that keep to these rules, and one draw needn't show every extreme that they name: `segments`: ids never fall along the tokens; each id covers 1 to 1024 consecutive tokens and some id covers exactly 1024.
All inputs are finite; a program needn't handle non-finite values.
Results may differ from the reference program's by a relative error of at most 0.012.
The reference program's roundings to bfloat16 on the way count: a program that leaves them out, or rounds other values in their place, can miss the bound.
Values may be sent and summed in bfloat16 or wider, within the bound.
A program may use at most 256 MiB of HBM per device.

```python
import math
import jax
import jax.numpy as jnp
import numpy as np
from jax import lax

D = 768
HEADS = 12
HEAD = 64
FF = 3072
LEN = 1024
SEQS = 32
TOKENS = 32768
PARAMS = 9440256


def draw_master(key, part):
    key = jax.random.fold_in(key, 7)
    position = jnp.arange(PARAMS)
    square_size = D * D
    wide_size = D * FF
    base = jnp.clip(jax.random.normal(key, (PARAMS,), jnp.float32), -6.0, 6.0)
    heads_end = 3 * square_size
    out_end = 4 * square_size
    gate_end = out_end + 2 * wide_size
    down_end = gate_end + wide_size
    factor_map = jnp.where(position < heads_end, D ** (-0.5), (D // 8) ** (-0.5))
    factor_map = jnp.where(position >= out_end, D ** (-0.5), factor_map)
    factor_map = jnp.where(position >= gate_end, FF ** (-0.5), factor_map)
    weight_part = base * factor_map
    stat_index = (position - down_end) // D
    stat_part = jnp.where(stat_index % 2 == 0, 1.0 + 0.1 * base, 0.3 * base)
    return jnp.where(position < down_end, weight_part, stat_part).astype(jnp.float32)


def draw_cotangent(key, part):
    key = jax.random.fold_in(key, 11)
    noise_key, common_key = jax.random.split(key)
    noise = jnp.clip(jax.random.normal(noise_key, (TOKENS, D), jnp.float32), -6.0, 6.0)
    common = 0.01 * jnp.clip(jax.random.normal(common_key, (D,), jnp.float32), -3.0, 3.0)
    return (noise + common[None, :]).astype(jnp.bfloat16)


def steps_of(rng, shape, shards, low, largest):
    def one(dim, shards_of):
        steps = jax.random.uniform(jax.random.fold_in(jax.random.fold_in(rng, 6), dim), (shards_of,), jnp.float32, low / len(shards), largest / len(shards))
        return jnp.repeat(jnp.exp(steps), shape[dim] // shards_of).reshape((-1,) + (1,) * (len(shape) - dim - 1))

    level = one(*shards[0])
    for cut in shards[1:]:
        level = level * one(*cut)
    return level


def length_profile(count, total, bound, slope):
    loads = [(1 << 20) // math.isqrt(standing ** slope) + 1 for standing in range(2, count + 1)]
    surplus, given = total - bound - (count - 1), [1] * (count - 1)
    while surplus > 0:
        movable = [i for i in range(count - 1) if given[i] < bound]
        mass, left = sum([loads[i] for i in movable]), surplus
        for i in movable:
            extra = min(bound - given[i], max(1, left * loads[i] // mass), surplus)
            given[i] = given[i] + extra
            surplus = surplus - extra
    return np.array([bound] + given)


def uneven(own_key, amount, total, limit, skew):
    if amount == 2:
        one = jax.random.randint(own_key, (), max(1, total - limit), min(limit, total - 1) + 1)
        return jnp.stack([one, total - one])
    sizes = jnp.asarray(length_profile(amount, total, limit, skew), jnp.int32)
    pairs = (amount - 1) // 2
    donor, taker = sizes[1:1 + 2 * pairs:2], sizes[2:2 + 2 * pairs:2]
    room = jnp.minimum(donor - 1, limit - taker)
    moved = jax.random.randint(jax.random.fold_in(own_key, 1), (pairs,), 0, 1 << 20) % (room + 1)
    sizes = sizes.at[1:1 + 2 * pairs:2].set(donor - moved).at[2:2 + 2 * pairs:2].set(taker + moved)
    return sizes[jax.random.permutation(jax.random.fold_in(own_key, 2), amount)]


def centred(stream_key, dims, spread, limit, cuts=(), dtype=jnp.bfloat16):
    loudness = steps_of(stream_key, dims, cuts, -0.22, 0.18) if cuts else 1.0
    values = jax.random.normal(stream_key, dims, jnp.float32) * spread * loudness
    return jnp.minimum(jnp.maximum(values, -limit), limit).astype(dtype)


def setup_inputs(seed: int = 0) -> dict:
    key_of = jax.random.split(jax.random.key(seed), 7)
    return {
        "tokens": centred(key_of[0], (TOKENS, D), 1.0, 6.0, ((0, 32),)),
        "segments": jnp.searchsorted(jnp.cumsum(uneven(key_of[1], TOKENS // (LEN // 4), TOKENS, LEN, 2)), jnp.arange(TOKENS), side="right").astype(jnp.int32),
        "cotangent": draw_cotangent(jax.random.fold_in(key_of[6], 71), 0),
        "master": draw_master(jax.random.fold_in(key_of[6], 71), 0),
        "moment_one": centred(key_of[4], (PARAMS,), 0.3, 4.0, ((0, 16),), jnp.float32),
        "moment_two": jnp.clip(jnp.exp(math.log(0.3) - 4.6051702 * jax.random.uniform(key_of[5], (PARAMS,), jnp.float32) ** steps_of(key_of[5], (PARAMS,), ((0, 16),), -0.2, 0.2)), 0.003, 0.3),
    }


@jax.custom_vjp
def low(v):
    return lax.optimization_barrier(v.astype(jnp.bfloat16)).astype(jnp.float32)

@jax.custom_vjp
def low_back(v):
    return v

def low_keep(v):
    return (low(v), None)

def low_pass(kept, grad):
    return (grad,)

def back_keep(v):
    return (v, None)

def back_low(kept, grad):
    return (low(grad),)
low.defvjp(low_keep, low_pass)
low_back.defvjp(back_keep, back_low)
learn_rate = 0.02
beta_one = 0.9
beta_two = 0.999
adam_eps = 1e-08
weight_decay = 0.01
correct_one = 1.0 - 0.9 ** 10
correct_two = 1.0 - 0.999 ** 10
norm_eps = 1e-06
highest = lax.Precision.HIGHEST

def matmul(left, right):
    return jnp.dot(left, right, precision=highest)

def split_flat(flat):
    dims_list = ((D, D), (D, D), (D, D), (D, D), (D, FF), (D, FF), (FF, D))
    pieces = []
    offset = 0
    for dims_pair in dims_list:
        length = dims_pair[0] * dims_pair[1]
        pieces.append(flat[offset:offset + length].reshape(dims_pair))
        offset = offset + length
    for number in range(4):
        pieces.append(flat[offset:offset + D])
        offset = offset + D
    return pieces

def head_slopes():
    return jnp.exp2(-8.0 * (jnp.arange(HEADS).astype(jnp.float32) + 1.0) / HEADS)

def layer_norm(value, gain, shift):
    centre = value - lax.optimization_barrier(jnp.mean(value, -1, keepdims=True))
    inverse = lax.rsqrt(lax.optimization_barrier(jnp.mean(centre * centre, -1, keepdims=True)) + norm_eps)
    return centre * inverse * gain + shift

def attend(piece):
    queries, keys_seq, values_seq, seg_ids = piece
    places = jnp.arange(LEN).astype(jnp.float32)
    distance = jnp.abs(places[:, None] - places[None, :])
    scores = jnp.einsum('qhd,khd->hqk', queries, keys_seq, precision=highest) * HEAD ** (-0.5)
    scores = scores - head_slopes()[:, None, None] * distance[None]
    same_doc = seg_ids[:, None] == seg_ids[None, :]
    scores = jnp.where(same_doc[None], scores, -1e+30)
    scores = low_back(scores)
    top = lax.optimization_barrier(jnp.max(scores, -1, keepdims=True))
    expo = jnp.exp(scores - top)
    probs = low(expo / lax.optimization_barrier(jnp.sum(expo, -1, keepdims=True)))
    return jnp.einsum('hqk,khd->qhd', probs, values_seq, precision=highest)

def forward(inputs, seg_ids, w_query, w_key, w_value, w_out, w_gate, w_up, w_down, gain_one, shift_one, gain_two, shift_two):
    count = inputs.shape[0] // LEN
    queries = low_back(low(matmul(inputs, w_query))).reshape(count, LEN, HEADS, HEAD)
    keys_all = low_back(low(matmul(inputs, w_key))).reshape(count, LEN, HEADS, HEAD)
    values_all = low_back(low(matmul(inputs, w_value))).reshape(count, LEN, HEADS, HEAD)
    attended = lax.map(jax.checkpoint(attend), (queries, keys_all, values_all, seg_ids.reshape(count, LEN)))
    mixed = low_back(low(attended.reshape(count * LEN, D)))
    branch = low_back(matmul(mixed, w_out))
    layer_one = layer_norm(inputs + branch, gain_one, shift_one)
    inner = low(layer_one)
    gate = low_back(matmul(inner, w_gate))
    up_part = low_back(matmul(inner, w_up))
    hidden = low(jax.nn.gelu(gate, approximate=False) * up_part)
    ffn = low_back(matmul(hidden, w_down))
    return layer_norm(layer_one + ffn, gain_two, shift_two)

def reference(tokens, segments, cotangent, master, moment_one, moment_two):
    weights = split_flat(master.astype(jnp.bfloat16).astype(jnp.float32))
    group = 4 if SEQS % 4 == 0 else 1
    turns = SEQS // group
    height = group * LEN
    inputs_all = tokens.astype(jnp.float32).reshape(turns, height, D)
    seg_all = segments.reshape(turns, height)
    cot_all = cotangent.astype(jnp.float32).reshape(turns, height, D)

    def accumulate(total, piece):
        inputs, seg_ids, cot = piece

        def apply(inputs_in, *params):
            return forward(inputs_in, seg_ids, *params)
        result, pull = jax.vjp(apply, inputs, *weights)
        grads = pull(cot)
        flat = jnp.concatenate([grad_part.reshape(-1) for grad_part in grads[1:]])
        return (total + flat, (result, grads[0]))
    total, (results, input_grads) = lax.scan(accumulate, jnp.zeros((PARAMS,), jnp.float32), (inputs_all, seg_all, cot_all))
    gradient = total / SEQS
    first = beta_one * moment_one + (1.0 - beta_one) * gradient
    second = beta_two * moment_two + (1.0 - beta_two) * gradient * gradient
    update = first / correct_one / (jnp.sqrt(second / correct_two) + adam_eps)
    master_new = master - learn_rate * (update + weight_decay * master)
    return (results.reshape(TOKENS, D).astype(jnp.bfloat16), input_grads.reshape(TOKENS, D), gradient, first, second, master_new, master_new.astype(jnp.bfloat16))
```

```python
import functools

import jax
import jax.numpy as jnp
from jax import lax
from jax.sharding import PartitionSpec as P
import jax.experimental.pallas as pl
import jax.experimental.pallas.tpu as pltpu

D = 768
HEADS = 12
HEAD = 64
FF = 3072
LEN = 1024


learn_rate = 0.02
beta_one = 0.9
beta_two = 0.999
adam_eps = 1e-08
weight_decay = 0.01
correct_one = 1.0 - 0.9**10
correct_two = 1.0 - 0.999**10
norm_eps = 1e-06
inv_root_two = 0.7071067811865476
inv_root_tau = 0.3989422804014327


def head_slopes():
    return jnp.exp2(-8.0 * (jnp.arange(HEADS).astype(jnp.float32) + 1.0) / HEADS)


def layer_stats(value):
    centre = value - jnp.mean(value, -1, keepdims=True)
    inverse = lax.rsqrt(jnp.mean(centre * centre, -1, keepdims=True) + norm_eps)
    return (centre * inverse, inverse)


def norm_back(grad_normed, normed, inverse):
    centred = grad_normed - jnp.mean(grad_normed, -1, keepdims=True)
    return inverse * (centred - normed * jnp.mean(grad_normed * normed, -1, keepdims=True))


def project(left, right):
    return jnp.dot(left, right, preferred_element_type=jnp.float32)


def left_trans(left, right):
    return jnp.einsum("rd,re->de", left, right, preferred_element_type=jnp.float32)


def right_trans(left, right):
    return jnp.einsum("re,de->rd", left, right, preferred_element_type=jnp.float32)


def block_scores(q_block, keys_seq, seg_block, seg_seq, begin):
    width = q_block.shape[0]
    raw = jnp.einsum(
        "qhd,khd->hqk", q_block, keys_seq, preferred_element_type=jnp.float32
    ) * HEAD ** (-0.5)
    q_places = (begin + jnp.arange(width)).astype(jnp.float32)
    k_places = jnp.arange(keys_seq.shape[0]).astype(jnp.float32)
    distance = jnp.abs(q_places[:, None] - k_places[None, :])
    raw = raw - head_slopes()[:, None, None] * distance[None]
    same_doc = seg_block[:, None] == seg_seq[None, :]
    return jnp.where(same_doc[None], raw, -1e30)


def attend_forward(piece):
    queries, keys_seq, values_seq, seg_seq = piece
    span = min(512, LEN)
    outputs = []
    log_sums = []
    for begin in range(0, LEN, span):
        scores = block_scores(
            queries[begin : begin + span], keys_seq, seg_seq[begin : begin + span], seg_seq, begin
        )
        top = jnp.max(scores, -1, keepdims=True)
        expo = jnp.exp(scores - top)
        total = jnp.sum(expo, -1, keepdims=True)
        probs = (expo / total).astype(jnp.bfloat16)
        outputs.append(
            jnp.einsum("hqk,khd->qhd", probs, values_seq, preferred_element_type=jnp.float32)
        )
        log_sums.append(top[..., 0] + jnp.log(total[..., 0]))
    return (jnp.concatenate(outputs, 0), jnp.concatenate(log_sums, 1))


def attend_backward(piece):
    queries, keys_seq, values_seq, seg_seq, grad_out, log_sum = piece
    span = min(512, LEN)
    scale_factor = HEAD ** (-0.5)
    key_grad = jnp.zeros(keys_seq.shape, jnp.float32)
    value_grad = jnp.zeros(values_seq.shape, jnp.float32)
    query_grads = []
    for begin in range(0, LEN, span):
        q_block = queries[begin : begin + span]
        g_block = grad_out[begin : begin + span]
        scores = block_scores(q_block, keys_seq, seg_seq[begin : begin + span], seg_seq, begin)
        probs = jnp.exp(scores - log_sum[:, begin : begin + span, None])
        grad_probs = jnp.einsum(
            "qhd,khd->hqk", g_block, values_seq, preferred_element_type=jnp.float32
        )
        delta = jnp.sum(probs * grad_probs, -1, keepdims=True)
        grad_scores = (probs * (grad_probs - delta)).astype(jnp.bfloat16)
        query_grads.append(
            jnp.einsum("hqk,khd->qhd", grad_scores, keys_seq, preferred_element_type=jnp.float32)
            * scale_factor
        )
        key_grad = (
            key_grad
            + jnp.einsum("hqk,qhd->khd", grad_scores, q_block, preferred_element_type=jnp.float32)
            * scale_factor
        )
        value_grad = value_grad + jnp.einsum(
            "hqk,qhd->khd", probs.astype(jnp.bfloat16), g_block, preferred_element_type=jnp.float32
        )
    query_grad = jnp.concatenate(query_grads, 0)
    return (
        query_grad.astype(jnp.bfloat16),
        key_grad.astype(jnp.bfloat16),
        value_grad.astype(jnp.bfloat16),
    )


MESH=pl.DeviceIdType.MESH
RA,RB,RC=48,128,208
OFFS=(0,RA,RA+RB)
LENS=(RA,RB,RC)
HALF=384

def place():
    i=lax.axis_index("zero"); c=lax.axis_index("dp")
    z=i//4; y=(i//2)%2; x=i%2
    return i,c,z,y,x

def enter_barrier(i,c,z):
    bar=pltpu.get_barrier_semaphore()
    for dev in ((c,i+1-2*(i%2)),(c,i+2-4*((i//2)%2)),(1-c,i)):
        pl.semaphore_signal(bar,inc=1,device_id=dev,device_id_type=MESH)
    @pl.when(z>0)
    def _(): pl.semaphore_signal(bar,inc=1,device_id=(c,i-4),device_id_type=MESH)
    @pl.when(z<3)
    def _(): pl.semaphore_signal(bar,inc=1,device_id=(c,i+4),device_id_type=MESH)
    pl.semaphore_wait(bar,3+jnp.minimum(z,1)+jnp.minimum(3-z,1))

def ag_kernel(blk,result,out,own_sem,out_sem,rx,ry,rz,sx,sy,szr,szl,rs,ss):
    i,c,z,y,x=place()
    xp=(c,i+1-2*x); yp=(c,i+2-4*y); sib=(1-c,i); zr=(c,i+4); zl=(c,i-4)
    enter_barrier(i,c,z)
    own=pltpu.make_async_copy(blk,out.at[z,y,x],own_sem)
    own.start(); own.wait()
    rows=[pl.ds(pl.multiple_of(c*HALF+OFFS[k],16),LENS[k]) for k in range(3)]
    orow=[pl.ds(pl.multiple_of((1-c)*HALF+OFFS[k],16),LENS[k]) for k in range(3)]
    def cp(sl,dev,s,r):
        return pltpu.make_async_remote_copy(src_ref=out.at[sl],dst_ref=out.at[sl],send_sem=s,recv_sem=r,device_id=dev,device_id_type=MESH)
    al=slice(None)
    pend=[]
    def A1(xx,R=rows): return (z,y,xx,R[0])
    def A2(yy,R=rows): return (z,yy,al,R[0])
    def A3(zs,R=rows): return (zs,al,al,R[0])
    def B1(yy,R=rows): return (z,yy,x,R[1])
    def B2(zs,xx,R=rows): return (zs,al,xx,R[1])
    def C1(zs,R=rows): return (zs,y,x,R[2])
    def C2(zs,xx,R=rows): return (zs,y,xx,R[2])
    def C3(zs,yy,R=rows): return (zs,yy,al,R[2])
    def sibsend(sl,k):
        cp(sl,sib,ss.at[k],rs.at[k]).start()
    def sibwait(sl,k):
        d=cp(sl,sib,ss.at[k],rs.at[k]); d.wait_send(); d.wait_recv()
    def zsend(sl,zs,base):
        @pl.when(jnp.logical_and(zs<=z,z<3))
        def _(): cp(sl,zr,szr.at[base+zs],rz.at[base+zs]).start()
        @pl.when(jnp.logical_and(zs>=z,z>0))
        def _(): cp(sl,zl,szl.at[base+zs],rz.at[base+zs]).start()
    def zsent(sl,zs,base):
        @pl.when(jnp.logical_and(zs<=z,z<3))
        def _(): cp(sl,zr,szr.at[base+zs],rz.at[base+zs]).wait_send()
        @pl.when(jnp.logical_and(zs>=z,z>0))
        def _(): cp(sl,zl,szl.at[base+zs],rz.at[base+zs]).wait_send()
    def zwait(sl,zs,base):
        cp(sl,zr,szr.at[base+zs],rz.at[base+zs]).wait_recv()
    A,B,C=0,4,8
    def xs(sl,k): cp(sl,xp,sx.at[k],rx.at[k]).start()
    def xw(sl,k): cp(sl,xp,sx.at[k],rx.at[k]).wait_recv()
    def xd(sl,k): cp(sl,xp,sx.at[k],rx.at[k]).wait_send()
    def ys(sl,k): cp(sl,yp,sy.at[k],ry.at[k]).start()
    def yw(sl,k): cp(sl,yp,sy.at[k],ry.at[k]).wait_recv()
    def yd(sl,k): cp(sl,yp,sy.at[k],ry.at[k]).wait_send()
    xs(A1(x),0); ys(B1(y),1); zsend(C1(z),z,C); xs(C2(z,x),5+z)
    xw(A1(1-x),0); ys(A2(y),0); sibsend(A1(1-x),0)
    yw(B1(1-y),1); zsend(B2(z,x),z,B); xs(B2(z,x),1+z); sibsend(B1(1-y),6)
    xw(C2(z,1-x),5+z); ys(C3(z,y),2+z); sibsend(C2(z,1-x),19+z)
    def late(zs):
        xw(C2(zs,1-x),5+zs); ys(C3(zs,y),2+zs); sibsend(C2(zs,1-x),19+zs)
    def early(zs):
        zwait(C1(zs),zs,C); zsend(C1(zs),zs,C); xs(C2(zs,x),5+zs); sibsend(C1(zs),15+zs)
        zwait(B2(zs,x),zs,B); zsend(B2(zs,x),zs,B); xs(B2(zs,x),1+zs); sibsend(B2(zs,x),7+zs)
    def both(s,f):
        @pl.when(z-s>=0)
        def _(): f(z-s)
        @pl.when(z+s<=3)
        def _(): f(z+s)
    both(1,early)
    yw(A2(1-y),0); zsend(A3(z),z,A); sibsend(A2(1-y),1)
    both(1,late)
    both(2,early)
    def a3(zs):
        zwait(A3(zs),zs,A); zsend(A3(zs),zs,A); sibsend(A3(zs),2+zs)
    both(1,a3)
    both(2,late)
    both(3,early)
    both(2,a3)
    both(3,late)
    both(3,a3)
    for s in range(4):
        def fin(zs):
            xw(B2(zs,1-x),1+zs); sibsend(B2(zs,1-x),11+zs)
            yw(C3(zs,1-y),2+zs); sibsend(C3(zs,1-y),23+zs)
        if s==0: fin(z)
        else: both(s,fin)
    xd(A1(x),0); yd(A2(y),0); yd(B1(y),1)
    sibwait(A1(1-x,orow),0) ; sibwait(A2(1-y,orow),1); sibwait(B1(1-y,orow),6)
    for zs in range(4):
        xd(B2(zs,x),1+zs); xd(C2(zs,x),5+zs); yd(C3(zs,y),2+zs)
        zsent(A3(zs),zs,A); zsent(B2(zs,x),zs,B); zsent(C1(zs),zs,C)
        sibwait(B2(zs,1-x,orow),11+zs); sibwait(C2(zs,1-x,orow),19+zs); sibwait(C3(zs,1-y,orow),23+zs)
        @pl.when(zs!=z)
        def _():
            sibwait(A3(zs,orow),2+zs); sibwait(B2(zs,x,orow),7+zs); sibwait(C1(zs,orow),15+zs)
    leave=[pltpu.make_async_copy(out.at[zs],result.at[zs],out_sem.at[zs]) for zs in range(4)]
    for move in leave: move.start()
    for move in leave: move.wait()

def gather_blocks(blk):
    D=pltpu.SemaphoreType.DMA
    return pl.pallas_call(ag_kernel,out_shape=jax.ShapeDtypeStruct((4,2,2,768,768),jnp.bfloat16),
        in_specs=[pl.BlockSpec(memory_space=pl.ANY)],out_specs=pl.BlockSpec(memory_space=pl.ANY),
        scratch_shapes=[pltpu.VMEM((4,2,2,768,768),jnp.bfloat16),D,D((4,)),D((9,)),D((6,)),D((12,)),D((9,)),D((6,)),D((12,)),D((12,)),D((27,)),D((27,))],
        compiler_params=pltpu.CompilerParams(collective_id=1,has_side_effects=True,vmem_limit_bytes=40<<20),name="gather_blocks")(blk)


ALL = slice(None)

def rs_kernel(g,out,own,sl,la1,la2,lafr,lafl,lb1,lb2r,lb2l,lb3,lc1r,lc1l,lc2,lc3,res,
              own_sem,ss,rs,rx,ry,rzr,rzl,sx,sy,szr,szl,fs,fr,osem):
    i,c,z,y,x=place()
    xp=(c,i+1-2*x); yp=(c,i+2-4*y); sib=(1-c,i); zr=(c,i+4); zl=(c,i-4)
    mine=pl.ds(pl.multiple_of(c*HALF,16),HALF); other=pl.ds(pl.multiple_of((1-c)*HALF,16),HALF)
    locs=[pltpu.make_async_copy(g.at[zt,:,:,mine],own.at[zt],own_sem.at[zt]) for zt in range(4)]
    for d in locs: d.start()
    enter_barrier(i,c,z)
    sibs=[pltpu.make_async_remote_copy(src_ref=g.at[zt,:,:,other],dst_ref=sl.at[zt],send_sem=ss.at[zt],recv_sem=rs.at[zt],device_id=sib,device_id_type=MESH) for zt in range(4)]
    for d in sibs: d.start()
    r=[pl.ds(OFFS[k],LENS[k]) for k in range(3)]
    def rc(src,dst,dev,s,q):
        return pltpu.make_async_remote_copy(src_ref=src,dst_ref=dst,send_sem=s,recv_sem=q,device_id=dev,device_id_type=MESH)
    def add(dst,src,n,rows,step):
        @pl.loop(0,rows//step)
        def _(k):
            q=pl.ds(pl.multiple_of(k*step,16),step)
            dst(q)[...]=(dst(q)[...].astype(jnp.float32)+src(q)[...].astype(jnp.float32)).astype(jnp.bfloat16)
    def sub(k,q): return pl.ds(pl.multiple_of(OFFS[k]+q.start,16),q.size)
    def add2(ownidx,k,land):
        add(lambda q: own.at[tuple(ownidx)+(sub(k,q),)], lambda q: land.at[tuple([ALL]*(len(land.shape)-2))+(q,)],0,LENS[k],16)
    def C3(zt): return rc(own.at[zt,1-y,:,r[2]],lc3.at[zt],yp,sy.at[zt],ry.at[zt])
    def B3(zt): return rc(own.at[zt,:,1-x,r[1]],lb3.at[zt],xp,sx.at[zt],rx.at[zt])
    def C2(zt): return rc(own.at[zt,y,1-x,r[2]],lc2.at[zt],xp,sx.at[4+zt],rx.at[4+zt])
    A2=rc(own.at[z,1-y,:,r[0]],la2,yp,sy.at[4],ry.at[4])
    A1=rc(own.at[z,y,1-x,r[0]],la1,xp,sx.at[8],rx.at[8])
    B1=rc(own.at[z,1-y,x,r[1]],lb1,yp,sy.at[5],ry.at[5])
    def zline(src,landr,landl,base):
        def R(zt): return rc(src(zt),landr.at[zt],zr,szr.at[base+zt],rzr.at[base+zt])
        def L(zt): return rc(src(zt),landl.at[zt],zl,szl.at[base+zt],rzl.at[base+zt])
        return R,L
    AR,AL=zline(lambda zt: own.at[zt,:,:,r[0]],lafr,lafl,0)
    BR,BL=zline(lambda zt: own.at[zt,:,x,r[1]],lb2r,lb2l,4)
    CR,CL=zline(lambda zt: own.at[zt,y,x,r[2]],lc1r,lc1l,8)
    def zgo(zt,idx,k,R,L,landr,landl):
        @pl.when(zt>z)
        def _():
            @pl.when(z>0)
            def _():
                R(zt).wait_recv(); add2(idx,k,landr.at[zt])
            R(zt).start()
        @pl.when(zt<z)
        def _():
            @pl.when(z<3)
            def _():
                L(zt).wait_recv(); add2(idx,k,landl.at[zt])
            L(zt).start()
    def zfin(idx,k,R,L,landr,landl):
        @pl.when(z>0)
        def _(): R(z).wait_recv(); add2(idx,k,landr.at[z])
        @pl.when(z<3)
        def _(): L(z).wait_recv(); add2(idx,k,landl.at[z])
    def far(s):
        return s
    def sumsib(zt):
        locs[zt].wait(); sibs[zt].wait_recv()
        @pl.loop(0,HALF//16)
        def _(k):
            q=pl.ds(pl.multiple_of(k*16,16),16)
            own[zt,:,:,q]=(own[zt,:,:,q].astype(jnp.float32)+sl[zt,:,:,q].astype(jnp.float32)).astype(jnp.bfloat16)
    order=[3,0,2,1]
    for zt in order:
        sumsib(zt)
        C3(zt).start(); B3(zt).start()
        zgo(zt,(zt,ALL,ALL),0,AR,AL,lafr,lafl)
    def c3done(zt):
        C3(zt).wait_recv(); add2((zt,y,ALL),2,lc3.at[zt]); C2(zt).start()
    def b3done(zt):
        B3(zt).wait_recv(); add2((zt,ALL,x),1,lb3.at[zt])
        zgo(zt,(zt,ALL,x),1,BR,BL,lb2r,lb2l)
    def c2done(zt):
        C2(zt).wait_recv(); add2((zt,y,x),2,lc2.at[zt])
        zgo(zt,(zt,y,x),2,CR,CL,lc1r,lc1l)
    c3done(3); b3done(3); c3done(0); b3done(0); c2done(3); c3done(2); b3done(2); c2done(0); c3done(1); b3done(1); c2done(2); c2done(1)
    zfin((z,ALL,ALL),0,AR,AL,lafr,lafl)
    A2.start()
    zfin((z,ALL,x),1,BR,BL,lb2r,lb2l)
    B1.start()
    A2.wait_recv(); add2((z,y,ALL),0,la2)
    A1.start()
    zfin((z,y,x),2,CR,CL,lc1r,lc1l)
    def final(k,land):
        @pl.loop(0,LENS[k]//16)
        def _(t):
            q=pl.ds(pl.multiple_of(t*16,16),16)
            o=pl.ds(pl.multiple_of(OFFS[k]+t*16,16),16)
            v=own[z,y,x,o].astype(jnp.float32)
            if land is not None: v=v+land[q].astype(jnp.float32)
            res[o]=v
    final(2,None)
    B1.wait_recv(); final(1,lb1)
    A1.wait_recv(); final(0,la1)
    fin=rc(res,out.at[mine],sib,fs,fr)
    fin.start()
    loc=pltpu.make_async_copy(res,out.at[mine],osem)
    loc.start()
    for zt in range(4):
        sibs[zt].wait_send(); C3(zt).wait_send(); B3(zt).wait_send(); C2(zt).wait_send()
        for R,L in ((AR,AL),(BR,BL),(CR,CL)):
            @pl.when(zt>z)
            def _(): R(zt).wait_send()
            @pl.when(zt<z)
            def _(): L(zt).wait_send()
    A2.wait_send(); A1.wait_send(); B1.wait_send()
    loc.wait(); fin.wait_send()
    rc(res,out.at[other],sib,fs,fr).wait_recv()

def reduce_blocks(g):
    D=pltpu.SemaphoreType.DMA
    bf=jnp.bfloat16
    V=lambda *s: pltpu.VMEM(s,bf)
    return pl.pallas_call(rs_kernel,out_shape=jax.ShapeDtypeStruct((768,768),jnp.float32),
        in_specs=[pl.BlockSpec(memory_space=pl.ANY)],out_specs=pl.BlockSpec(memory_space=pl.ANY),
        scratch_shapes=[V(4,2,2,HALF,768),V(4,2,2,HALF,768),V(RA,768),V(2,RA,768),V(4,2,2,RA,768),V(4,2,2,RA,768),
            V(RB,768),V(4,2,RB,768),V(4,2,RB,768),V(4,2,RB,768),V(4,RC,768),V(4,RC,768),V(4,RC,768),V(4,2,RC,768),pltpu.VMEM((HALF,768),jnp.float32),
            D((4,)),D((4,)),D((4,)),D((9,)),D((6,)),D((12,)),D((12,)),D((9,)),D((6,)),D((12,)),D((12,)),D,D,D],
        compiler_params=pltpu.CompilerParams(collective_id=2,has_side_effects=True,vmem_limit_bytes=58<<20),name="reduce_blocks")(g)

SQUARE = D * D
TAIL = 4 * D


def from_wide(blocks):
    return blocks.reshape(4, 4, D // 4, D).transpose(0, 2, 1, 3).reshape(D, FF)


def to_wide(value):
    return value.reshape(4, D // 4, 4, D).transpose(0, 2, 1, 3).reshape(2, 2, D, D)


def swap_wide(block, index, inverse):
    dims = (4, D // 4, D) if inverse else (D // 4, 4, D)
    swapped = block.reshape(dims).transpose(1, 0, 2).reshape(D, D)
    wide = jnp.logical_and(index >= 4, index < 12)
    return jnp.where(wide, swapped, block)


def gather_weights(master):
    count = lax.axis_size("zero")
    index = lax.axis_index("zero")
    size = 16 * SQUARE // count
    weights = master.astype(jnp.bfloat16)
    last = weights[-TAIL:]
    before = lax.ppermute(last, "zero", [(k, k + 1) for k in range(count - 1)])
    joined = jnp.concatenate([before, weights])
    block = lax.dynamic_slice(joined, (TAIL - TAIL // count * index,), (size,))
    norms = lax.psum(jnp.where(index == count - 1, last.astype(jnp.float32), 0.0), "zero")
    if count == 16:
        blocks = gather_blocks(swap_wide(block.reshape(D, D), index, False))
    else:
        natural = lax.all_gather(block.reshape(-1, D), "zero", axis=0, tiled=True)
        parts = natural.reshape(4, 4 * D, D)
        wide = [to_wide(parts[k].reshape(D, FF)) for k in (1, 2)]
        blocks = jnp.stack([parts[0].reshape(2, 2, D, D), *wide, parts[3].reshape(2, 2, D, D)])
    return blocks, norms.reshape(4, D)


def scatter_grads(grads, norm_grads):
    count = lax.axis_size("zero")
    index = lax.axis_index("zero")
    if count == 16:
        block = swap_wide(reduce_blocks(grads), index, True)
    else:
        wide = [from_wide(grads[k]).reshape(4 * D, D) for k in (1, 2)]
        natural = jnp.concatenate(
            [grads[0].reshape(4 * D, D), *wide, grads[3].reshape(4 * D, D)]
        )
        block = lax.psum_scatter(natural, "zero", scatter_dimension=0, tiled=True)
        block = lax.psum(block.astype(jnp.float32), "dp")
    tail = lax.psum(norm_grads.reshape(-1), ("dp", "zero"))
    flat = block.reshape(-1)
    after = lax.ppermute(flat[:TAIL], "zero", [(k + 1, k) for k in range(count - 1)])
    joined = jnp.concatenate([flat, jnp.where(index == count - 1, tail, after)])
    shard = flat.shape[0] + TAIL // count
    return lax.dynamic_slice(joined, (TAIL // count * index,), (shard,))


def local(tokens, segments, cotangent, master, moment_one, moment_two):
    blocks, norms = gather_weights(master)
    w_query, w_key, w_value, w_out = blocks[0].reshape(4, D, D)
    w_gate = from_wide(blocks[1])
    w_up = from_wide(blocks[2])
    w_down = blocks[3].reshape(FF, D)
    gain_one, shift_one, gain_two, shift_two = norms
    height = tokens.shape[0]
    count = height // LEN

    def head_view(value):
        return value.reshape(count, LEN, HEADS, HEAD)

    queries = project(tokens, w_query).astype(jnp.bfloat16)
    keys_all = project(tokens, w_key).astype(jnp.bfloat16)
    values_all = project(tokens, w_value).astype(jnp.bfloat16)
    seg_view = segments.reshape(count, LEN)
    attended, log_sum = lax.map(
        attend_forward, (head_view(queries), head_view(keys_all), head_view(values_all), seg_view)
    )
    mixed = attended.reshape(height, D).astype(jnp.bfloat16)
    branch = project(mixed, w_out)
    normed_one, inverse_one = layer_stats(tokens.astype(jnp.float32) + branch)
    layer_one = normed_one * gain_one + shift_one
    inner = layer_one.astype(jnp.bfloat16)
    gate = project(inner, w_gate)
    up_part = project(inner, w_up)
    cumulative = 0.5 * (1.0 + lax.erf(gate * inv_root_two))
    gelu_gate = gate * cumulative
    hidden = (gelu_gate * up_part).astype(jnp.bfloat16)
    ffn = project(hidden, w_down)
    normed_two, inverse_two = layer_stats(layer_one + ffn)
    output = normed_two * gain_two + shift_two
    grad_output = cotangent.astype(jnp.float32)
    grad_gain_two = jnp.sum(grad_output * normed_two, 0)
    grad_shift_two = jnp.sum(grad_output, 0)
    grad_mid = norm_back(grad_output * gain_two, normed_two, inverse_two)
    grad_ffn = grad_mid.astype(jnp.bfloat16)
    grad_w_down = left_trans(hidden, grad_ffn)
    grad_hidden = right_trans(grad_ffn, w_down)
    density = jnp.exp(-0.5 * gate * gate) * inv_root_tau
    grad_gate = (grad_hidden * up_part * (cumulative + gate * density)).astype(jnp.bfloat16)
    grad_up = (grad_hidden * gelu_gate).astype(jnp.bfloat16)
    grad_w_gate = left_trans(inner, grad_gate)
    grad_w_up = left_trans(inner, grad_up)
    grad_layer_one = grad_mid + right_trans(grad_gate, w_gate) + right_trans(grad_up, w_up)
    grad_gain_one = jnp.sum(grad_layer_one * normed_one, 0)
    grad_shift_one = jnp.sum(grad_layer_one, 0)
    grad_first = norm_back(grad_layer_one * gain_one, normed_one, inverse_one)
    grad_branch = grad_first.astype(jnp.bfloat16)
    grad_w_out = left_trans(mixed, grad_branch)
    grad_mixed = right_trans(grad_branch, w_out).astype(jnp.bfloat16)
    grad_query, grad_key, grad_value = lax.map(
        attend_backward,
        (
            head_view(queries),
            head_view(keys_all),
            head_view(values_all),
            seg_view,
            head_view(grad_mixed),
            log_sum,
        ),
    )
    grad_query = grad_query.reshape(height, D)
    grad_key = grad_key.reshape(height, D)
    grad_value = grad_value.reshape(height, D)
    grad_w_query = left_trans(tokens, grad_query)
    grad_w_key = left_trans(tokens, grad_key)
    grad_w_value = left_trans(tokens, grad_value)
    input_grad = (
        grad_first
        + right_trans(grad_query, w_query)
        + right_trans(grad_key, w_key)
        + right_trans(grad_value, w_value)
    )
    low = lambda value: value.astype(jnp.bfloat16)
    grads = jnp.stack(
        [
            low(jnp.stack([grad_w_query, grad_w_key, grad_w_value, grad_w_out])).reshape(2, 2, D, D),
            to_wide(low(grad_w_gate)),
            to_wide(low(grad_w_up)),
            low(grad_w_down).reshape(2, 2, D, D),
        ]
    )
    norm_grads = jnp.stack([grad_gain_one, grad_shift_one, grad_gain_two, grad_shift_two])
    groups = lax.axis_size("zero")
    replicas = lax.axis_size("dp")
    grad_shard = scatter_grads(grads, norm_grads) / (count * groups * replicas)
    first = beta_one * moment_one + (1.0 - beta_one) * grad_shard
    second = beta_two * moment_two + (1.0 - beta_two) * grad_shard * grad_shard
    update = first / correct_one / (jnp.sqrt(second / correct_two) + adam_eps)
    master_new = master - learn_rate * (update + weight_decay * master)
    return (
        output.astype(jnp.bfloat16),
        input_grad,
        grad_shard,
        first,
        second,
        master_new,
        master_new.astype(jnp.bfloat16),
    )


def solution(mesh):
    return jax.shard_map(
        local,
        mesh=mesh,
        in_specs=(
            P(("dp", "zero"), None),
            P(("dp", "zero")),
            P(("dp", "zero"), None),
            P("zero"),
            P("zero"),
            P("zero"),
        ),
        out_specs=(
            P(("dp", "zero"), None),
            P(("dp", "zero"), None),
            P("zero"),
            P("zero"),
            P("zero"),
            P("zero"),
            P("zero"),
        ),
        check_vma=False,
    )
```

```python
import functools

import jax
import jax.numpy as jnp
from jax import lax
from jax.sharding import PartitionSpec as P
import jax.experimental.pallas as pl
import jax.experimental.pallas.tpu as pltpu

D = 768
HEADS = 12
HEAD = 64
FF = 3072
LEN = 1024


learn_rate = 0.02
beta_one = 0.9
beta_two = 0.999
adam_eps = 1e-08
weight_decay = 0.01
correct_one = 1.0 - 0.9**10
correct_two = 1.0 - 0.999**10
norm_eps = 1e-06
inv_root_two = 0.7071067811865476
inv_root_tau = 0.3989422804014327


MESH=pl.DeviceIdType.MESH
RA,RB,RC=48,128,208
OFFS=(0,RA,RA+RB)
LENS=(RA,RB,RC)
HALF=384

def place():
    i=lax.axis_index("zero"); c=lax.axis_index("dp")
    z=i//4; y=(i//2)%2; x=i%2
    return i,c,z,y,x

def enter_barrier(i,c,z):
    bar=pltpu.get_barrier_semaphore()
    for dev in ((c,i+1-2*(i%2)),(c,i+2-4*((i//2)%2)),(1-c,i)):
        pl.semaphore_signal(bar,inc=1,device_id=dev,device_id_type=MESH)
    @pl.when(z>0)
    def _(): pl.semaphore_signal(bar,inc=1,device_id=(c,i-4),device_id_type=MESH)
    @pl.when(z<3)
    def _(): pl.semaphore_signal(bar,inc=1,device_id=(c,i+4),device_id_type=MESH)
    pl.semaphore_wait(bar,3+jnp.minimum(z,1)+jnp.minimum(3-z,1))

def ag_kernel(blk,last,result,tail,out,own_sem,out_sem,tr,tz,ty,tx,rx,ry,rz,sx,sy,szr,szl,rs,ss):
    i,c,z,y,x=place()
    xp=(c,i+1-2*x); yp=(c,i+2-4*y); sib=(1-c,i); zr=(c,i+4); zl=(c,i-4)
    enter_barrier(i,c,z)
    own=pltpu.make_async_copy(blk,out.at[z,y,x],own_sem)
    own.start()
    source=jnp.logical_and(z==3,jnp.logical_and(y==1,x==1))
    line=jnp.logical_and(y==1,x==1)
    @pl.when(source)
    def _(): tail[...]=last[...]
    def tcp(dev,s): return pltpu.make_async_remote_copy(src_ref=tail,dst_ref=tail,send_sem=s,recv_sem=tr,device_id=dev,device_id_type=MESH)
    def tail_along_z(first):
        @pl.when(jnp.logical_and(line,source if first else jnp.logical_not(source)))
        def _():
            if not first: tcp(zl,tz).wait_recv()
            @pl.when(z>0)
            def _(): tcp(zl,tz).start()
            tcp(yp,ty).start()
    def tail_along_x():
        @pl.when(x==1)
        def _():
            @pl.when(y==0)
            def _(): tcp(yp,ty).wait_recv()
            tcp(xp,tx).start()
    def tail_end():
        @pl.when(x==0)
        def _(): tcp(xp,tx).wait_recv()
        @pl.when(x==1)
        def _(): tcp(xp,tx).wait_send()
        @pl.when(line)
        def _():
            tcp(yp,ty).wait_send()
            @pl.when(z>0)
            def _(): tcp(zl,tz).wait_send()
    tail_along_z(True)
    own.wait()
    rows=[pl.ds(pl.multiple_of(c*HALF+OFFS[k],16),LENS[k]) for k in range(3)]
    orow=[pl.ds(pl.multiple_of((1-c)*HALF+OFFS[k],16),LENS[k]) for k in range(3)]
    def cp(sl,dev,s,r):
        return pltpu.make_async_remote_copy(src_ref=out.at[sl],dst_ref=out.at[sl],send_sem=s,recv_sem=r,device_id=dev,device_id_type=MESH)
    al=slice(None)
    pend=[]
    def A1(xx,R=rows): return (z,y,xx,R[0])
    def A2(yy,R=rows): return (z,yy,al,R[0])
    def A3(zs,R=rows): return (zs,al,al,R[0])
    def B1(yy,R=rows): return (z,yy,x,R[1])
    def B2(zs,xx,R=rows): return (zs,al,xx,R[1])
    def C1(zs,R=rows): return (zs,y,x,R[2])
    def C2(zs,xx,R=rows): return (zs,y,xx,R[2])
    def C3(zs,yy,R=rows): return (zs,yy,al,R[2])
    def sibsend(sl,k):
        cp(sl,sib,ss.at[k],rs.at[k]).start()
    def sibwait(sl,k):
        d=cp(sl,sib,ss.at[k],rs.at[k]); d.wait_send(); d.wait_recv()
    def zsend(sl,zs,base):
        @pl.when(jnp.logical_and(zs<=z,z<3))
        def _(): cp(sl,zr,szr.at[base+zs],rz.at[base+zs]).start()
        @pl.when(jnp.logical_and(zs>=z,z>0))
        def _(): cp(sl,zl,szl.at[base+zs],rz.at[base+zs]).start()
    def zsent(sl,zs,base):
        @pl.when(jnp.logical_and(zs<=z,z<3))
        def _(): cp(sl,zr,szr.at[base+zs],rz.at[base+zs]).wait_send()
        @pl.when(jnp.logical_and(zs>=z,z>0))
        def _(): cp(sl,zl,szl.at[base+zs],rz.at[base+zs]).wait_send()
    def zwait(sl,zs,base):
        cp(sl,zr,szr.at[base+zs],rz.at[base+zs]).wait_recv()
    A,B,C=0,4,8
    def xs(sl,k): cp(sl,xp,sx.at[k],rx.at[k]).start()
    def xw(sl,k): cp(sl,xp,sx.at[k],rx.at[k]).wait_recv()
    def xd(sl,k): cp(sl,xp,sx.at[k],rx.at[k]).wait_send()
    def ys(sl,k): cp(sl,yp,sy.at[k],ry.at[k]).start()
    def yw(sl,k): cp(sl,yp,sy.at[k],ry.at[k]).wait_recv()
    def yd(sl,k): cp(sl,yp,sy.at[k],ry.at[k]).wait_send()
    xs(A1(x),0); ys(B1(y),1); zsend(C1(z),z,C); xs(C2(z,x),5+z)
    xw(A1(1-x),0); ys(A2(y),0); sibsend(A1(1-x),0)
    yw(B1(1-y),1); zsend(B2(z,x),z,B); xs(B2(z,x),1+z); sibsend(B1(1-y),6)
    xw(C2(z,1-x),5+z); ys(C3(z,y),2+z); sibsend(C2(z,1-x),19+z)
    def late(zs):
        xw(C2(zs,1-x),5+zs); ys(C3(zs,y),2+zs); sibsend(C2(zs,1-x),19+zs)
    def early(zs):
        zwait(C1(zs),zs,C); zsend(C1(zs),zs,C); xs(C2(zs,x),5+zs); sibsend(C1(zs),15+zs)
        zwait(B2(zs,x),zs,B); zsend(B2(zs,x),zs,B); xs(B2(zs,x),1+zs); sibsend(B2(zs,x),7+zs)
    def both(s,f):
        @pl.when(z-s>=0)
        def _(): f(z-s)
        @pl.when(z+s<=3)
        def _(): f(z+s)
    both(1,early)
    yw(A2(1-y),0); zsend(A3(z),z,A); sibsend(A2(1-y),1)
    both(1,late)
    tail_along_z(False)
    both(2,early)
    def a3(zs):
        zwait(A3(zs),zs,A); zsend(A3(zs),zs,A); sibsend(A3(zs),2+zs)
    both(1,a3)
    both(2,late)
    tail_along_x()
    both(3,early)
    both(2,a3)
    both(3,late)
    both(3,a3)
    for s in range(4):
        def fin(zs):
            xw(B2(zs,1-x),1+zs); sibsend(B2(zs,1-x),11+zs)
            yw(C3(zs,1-y),2+zs); sibsend(C3(zs,1-y),23+zs)
        if s==0: fin(z)
        else: both(s,fin)
    xd(A1(x),0); yd(A2(y),0); yd(B1(y),1)
    sibwait(A1(1-x,orow),0) ; sibwait(A2(1-y,orow),1); sibwait(B1(1-y,orow),6)
    for zs in range(4):
        xd(B2(zs,x),1+zs); xd(C2(zs,x),5+zs); yd(C3(zs,y),2+zs)
        zsent(A3(zs),zs,A); zsent(B2(zs,x),zs,B); zsent(C1(zs),zs,C)
        sibwait(B2(zs,1-x,orow),11+zs); sibwait(C2(zs,1-x,orow),19+zs); sibwait(C3(zs,1-y,orow),23+zs)
        @pl.when(zs!=z)
        def _():
            sibwait(A3(zs,orow),2+zs); sibwait(B2(zs,x,orow),7+zs); sibwait(C1(zs,orow),15+zs)
    tail_end()
    leave=[pltpu.make_async_copy(out.at[zs],result.at[zs],out_sem.at[zs]) for zs in range(4)]
    for move in leave: move.start()
    for move in leave: move.wait()

def gather_blocks(blk,last):
    D=pltpu.SemaphoreType.DMA
    return pl.pallas_call(ag_kernel,out_shape=[jax.ShapeDtypeStruct((4,2,2,768,768),jnp.bfloat16),jax.ShapeDtypeStruct((16,768),jnp.bfloat16)],
        in_specs=[pl.BlockSpec(memory_space=pl.ANY),pl.BlockSpec(memory_space=pltpu.VMEM)],out_specs=[pl.BlockSpec(memory_space=pl.ANY),pl.BlockSpec(memory_space=pltpu.VMEM)],
        scratch_shapes=[pltpu.VMEM((4,2,2,768,768),jnp.bfloat16),D,D((4,)),D,D,D,D,D((9,)),D((6,)),D((12,)),D((9,)),D((6,)),D((12,)),D((12,)),D((27,)),D((27,))],
        compiler_params=pltpu.CompilerParams(collective_id=1,has_side_effects=True,vmem_limit_bytes=40<<20),name="gather_blocks")(blk,last)


ALL = slice(None)

def rs_kernel(g0,gwide,gdown,norm_in,out,norm_out,nx,ny,nz,nc,nacc,nrx,nry,nrz,nrc,nsx,nsy,nsz,nsc,own,sl,la1,la2,lafr,lafl,lb1,lb2r,lb2l,lb3,lc1r,lc1l,lc2,lc3,res,
              own_sem,ss,rs,rx,ry,rzr,rzl,sx,sy,szr,szl,fs,fr,osem):
    i,c,z,y,x=place()
    xp=(c,i+1-2*x); yp=(c,i+2-4*y); sib=(1-c,i); zr=(c,i+4); zl=(c,i-4)
    mine=pl.ds(pl.multiple_of(c*HALF,16),HALF); other=pl.ds(pl.multiple_of((1-c)*HALF,16),HALF)
    planes=[g0,gwide.at[0],gwide.at[1],gdown]
    locs=[pltpu.make_async_copy(planes[zt].at[:,:,mine],own.at[zt],own_sem.at[zt]) for zt in range(4)]
    for d in locs: d.start()
    enter_barrier(i,c,z)
    sibs=[pltpu.make_async_remote_copy(src_ref=planes[zt].at[:,:,other],dst_ref=sl.at[zt],send_sem=ss.at[zt],recv_sem=rs.at[zt],device_id=sib,device_id_type=MESH) for zt in range(4)]
    for d in sibs: d.start()
    r=[pl.ds(OFFS[k],LENS[k]) for k in range(3)]
    def rc(src,dst,dev,s,q):
        return pltpu.make_async_remote_copy(src_ref=src,dst_ref=dst,send_sem=s,recv_sem=q,device_id=dev,device_id_type=MESH)
    def add(dst,src,n,rows,step):
        @pl.loop(0,rows//step)
        def _(k):
            q=pl.ds(pl.multiple_of(k*step,16),step)
            dst(q)[...]=(dst(q)[...].astype(jnp.float32)+src(q)[...].astype(jnp.float32)).astype(jnp.bfloat16)
    def sub(k,q): return pl.ds(pl.multiple_of(OFFS[k]+q.start,16),q.size)
    def add2(ownidx,k,land):
        add(lambda q: own.at[tuple(ownidx)+(sub(k,q),)], lambda q: land.at[tuple([ALL]*(len(land.shape)-2))+(q,)],0,LENS[k],16)
    def C3(zt): return rc(own.at[zt,1-y,:,r[2]],lc3.at[zt],yp,sy.at[zt],ry.at[zt])
    def B3(zt): return rc(own.at[zt,:,1-x,r[1]],lb3.at[zt],xp,sx.at[zt],rx.at[zt])
    def C2(zt): return rc(own.at[zt,y,1-x,r[2]],lc2.at[zt],xp,sx.at[4+zt],rx.at[4+zt])
    A2=rc(own.at[z,1-y,:,r[0]],la2,yp,sy.at[4],ry.at[4])
    A1=rc(own.at[z,y,1-x,r[0]],la1,xp,sx.at[8],rx.at[8])
    B1=rc(own.at[z,1-y,x,r[1]],lb1,yp,sy.at[5],ry.at[5])
    def zline(src,landr,landl,base):
        def R(zt): return rc(src(zt),landr.at[zt],zr,szr.at[base+zt],rzr.at[base+zt])
        def L(zt): return rc(src(zt),landl.at[zt],zl,szl.at[base+zt],rzl.at[base+zt])
        return R,L
    AR,AL=zline(lambda zt: own.at[zt,:,:,r[0]],lafr,lafl,0)
    BR,BL=zline(lambda zt: own.at[zt,:,x,r[1]],lb2r,lb2l,4)
    CR,CL=zline(lambda zt: own.at[zt,y,x,r[2]],lc1r,lc1l,8)
    def zgo(zt,idx,k,R,L,landr,landl):
        @pl.when(zt>z)
        def _():
            @pl.when(z>0)
            def _():
                R(zt).wait_recv(); add2(idx,k,landr.at[zt])
            R(zt).start()
        @pl.when(zt<z)
        def _():
            @pl.when(z<3)
            def _():
                L(zt).wait_recv(); add2(idx,k,landl.at[zt])
            L(zt).start()
    def zfin(idx,k,R,L,landr,landl):
        @pl.when(z>0)
        def _(): R(z).wait_recv(); add2(idx,k,landr.at[z])
        @pl.when(z<3)
        def _(): L(z).wait_recv(); add2(idx,k,landl.at[z])
    def far(s):
        return s
    def sumsib(zt):
        locs[zt].wait(); sibs[zt].wait_recv()
        @pl.loop(0,HALF//16)
        def _(k):
            q=pl.ds(pl.multiple_of(k*16,16),16)
            own[zt,:,:,q]=(own[zt,:,:,q].astype(jnp.float32)+sl[zt,:,:,q].astype(jnp.float32)).astype(jnp.bfloat16)
    order=[3,0,2,1]
    nacc[...]=norm_in[...]
    NX=rc(nacc,nx,xp,nsx,nrx); NY=rc(nacc,ny,yp,nsy,nry); NZ=rc(nacc,nz,zr,nsz,nrz); NC=rc(nacc,nc,sib,nsc,nrc)
    line=jnp.logical_and(x==1,y==1)
    end=jnp.logical_and(line,z==3)
    @pl.when(x==0)
    def _(): NX.start()
    def norm_y():
        @pl.when(x==1)
        def _():
            NX.wait_recv(); nacc[...]+=nx[...]
            @pl.when(y==0)
            def _(): NY.start()
    def norm_z(k):
        @pl.when(jnp.logical_and(line,z==k))
        def _():
            NY.wait_recv(); nacc[...]+=ny[...]
            if k>0:
                NZ.wait_recv(); nacc[...]+=nz[...]
            if k<3: NZ.start()
            else: NC.start()
    def norm_end():
        @pl.when(x==0)
        def _(): NX.wait_send()
        @pl.when(jnp.logical_and(x==1,y==0))
        def _(): NY.wait_send()
        @pl.when(jnp.logical_and(line,z<3))
        def _(): NZ.wait_send()
        @pl.when(end)
        def _():
            NC.wait_recv(); NC.wait_send()
            nacc[...]+=nc[...]
        norm_out[...]=nacc[...]
    for zt in order:
        sumsib(zt)
        C3(zt).start(); B3(zt).start()
        zgo(zt,(zt,ALL,ALL),0,AR,AL,lafr,lafl)
    def c3done(zt):
        C3(zt).wait_recv(); add2((zt,y,ALL),2,lc3.at[zt]); C2(zt).start()
    def b3done(zt):
        B3(zt).wait_recv(); add2((zt,ALL,x),1,lb3.at[zt])
        zgo(zt,(zt,ALL,x),1,BR,BL,lb2r,lb2l)
    def c2done(zt):
        C2(zt).wait_recv(); add2((zt,y,x),2,lc2.at[zt])
        zgo(zt,(zt,y,x),2,CR,CL,lc1r,lc1l)
    c3done(3); b3done(3); norm_y(); c3done(0); b3done(0); norm_z(0); c2done(3); c3done(2); b3done(2); norm_z(1); c2done(0); c3done(1); b3done(1); norm_z(2); c2done(2); c2done(1); norm_z(3)
    zfin((z,ALL,ALL),0,AR,AL,lafr,lafl)
    A2.start()
    zfin((z,ALL,x),1,BR,BL,lb2r,lb2l)
    B1.start()
    A2.wait_recv(); add2((z,y,ALL),0,la2)
    A1.start()
    zfin((z,y,x),2,CR,CL,lc1r,lc1l)
    def final(k,land):
        @pl.loop(0,LENS[k]//16)
        def _(t):
            q=pl.ds(pl.multiple_of(t*16,16),16)
            o=pl.ds(pl.multiple_of(OFFS[k]+t*16,16),16)
            v=own[z,y,x,o].astype(jnp.float32)
            if land is not None: v=v+land[q].astype(jnp.float32)
            res[o]=v
    final(2,None)
    B1.wait_recv(); final(1,lb1)
    A1.wait_recv(); final(0,la1)
    fin=rc(res,out.at[mine],sib,fs,fr)
    fin.start()
    loc=pltpu.make_async_copy(res,out.at[mine],osem)
    loc.start()
    for zt in range(4):
        sibs[zt].wait_send(); C3(zt).wait_send(); B3(zt).wait_send(); C2(zt).wait_send()
        for R,L in ((AR,AL),(BR,BL),(CR,CL)):
            @pl.when(zt>z)
            def _(): R(zt).wait_send()
            @pl.when(zt<z)
            def _(): L(zt).wait_send()
    A2.wait_send(); A1.wait_send(); B1.wait_send()
    norm_end()
    loc.wait(); fin.wait_send()
    rc(res,out.at[other],sib,fs,fr).wait_recv()

def reduce_blocks(g0,gwide,gdown,norms):
    D=pltpu.SemaphoreType.DMA
    bf=jnp.bfloat16
    V=lambda *s: pltpu.VMEM(s,bf)
    return pl.pallas_call(rs_kernel,out_shape=[jax.ShapeDtypeStruct((768,768),jnp.float32),jax.ShapeDtypeStruct((4,768),jnp.float32)],
        in_specs=[pl.BlockSpec(memory_space=pl.ANY)]*3+[pl.BlockSpec(memory_space=pltpu.VMEM)],out_specs=[pl.BlockSpec(memory_space=pl.ANY),pl.BlockSpec(memory_space=pltpu.VMEM)],
        scratch_shapes=[*[pltpu.VMEM((4,768),jnp.float32)]*5,*[D]*8,V(4,2,2,HALF,768),V(4,2,2,HALF,768),V(RA,768),V(2,RA,768),V(4,2,2,RA,768),V(4,2,2,RA,768),
            V(RB,768),V(4,2,RB,768),V(4,2,RB,768),V(4,2,RB,768),V(4,RC,768),V(4,RC,768),V(4,RC,768),V(4,2,RC,768),pltpu.VMEM((HALF,768),jnp.float32),
            D((4,)),D((4,)),D((4,)),D((9,)),D((6,)),D((12,)),D((12,)),D((9,)),D((6,)),D((12,)),D((12,)),D,D,D],
        compiler_params=pltpu.CompilerParams(collective_id=2,has_side_effects=True,vmem_limit_bytes=58<<20),name="reduce_blocks")(g0,gwide,gdown,norms)

bf16=jnp.bfloat16; f32=jnp.float32
FAR=1e33
VM=pl.BlockSpec(memory_space=pltpu.VMEM)

def dot(a,b): return lax.dot_general(a,b,(((1,),(0,)),((),())),preferred_element_type=f32)
def dot_tn(a,b): return lax.dot_general(a,b,(((0,),(0,)),((),())),preferred_element_type=f32)
def dot_nt(a,b): return lax.dot_general(a,b,(((1,),(1,)),((),())),preferred_element_type=f32)

def slope(h):
    return jnp.exp2(-8.0/HEADS*(jnp.full((1,1),h,jnp.int32).astype(f32)+1.0))

def fill_distance(dist,seg_col,seg_row):
    @pl.loop(0,LEN//128)
    def _(k):
        r=pl.ds(pl.multiple_of(k*128,128),128)
        kk=(lax.broadcasted_iota(jnp.int32,(128,LEN),0)+k*128)
        qq=lax.broadcasted_iota(jnp.int32,(128,LEN),1)
        d=jnp.abs(kk-qq).astype(f32)
        dist[r]=jnp.where(seg_col[r]==seg_row[...],d,FAR)

QB=256
def attend_kernel(tokens,w,seg_col,seg_row,tokT,qT,kT,vT,mixT,lse,dist,kn):
    tokT[...]=tokens[...].astype(f32).T.astype(bf16)
    fill_distance(dist,seg_col,seg_row)
    for n,(o,s) in enumerate(((qT,0.125),(kT,1.0),(vT,1.0))):
        @pl.loop(0,3)
        def _(t):
            c=pl.ds(pl.multiple_of(t*256,256),256)
            r=dot_tn(w[0,n//2,n%2,:,c],tokT[...])
            o[c]=r.astype(bf16)
    @pl.loop(0,HEADS)
    def _(h):
        rows=pl.ds(pl.multiple_of(h*HEAD,HEAD),HEAD)
        kn[...]=kT[rows].astype(f32).T.astype(bf16)
        m=slope(h)
        for b in range(LEN//QB):
            cols=pl.ds(b*QB,QB)
            q=(qT[rows,cols]*bf16(0.125))
            s=dot(kn[...],q)-m*dist[:,cols]
            top=jnp.max(s,0,keepdims=True)
            e=jnp.exp(s-top)
            total=jnp.sum(e,0,keepdims=True)
            o=dot(vT[rows],e.astype(bf16))/total
            mixT[rows,cols]=o
            lse[h,:,cols]=top+jnp.log(total)

def attend(tokens,w,seg):
    T=jax.ShapeDtypeStruct((D,LEN),bf16)
    tokT,qT,kT,vT,mixT,lse=pl.pallas_call(attend_kernel,grid=(1,),
        in_specs=[VM,pl.BlockSpec((1,2,2,D,D),lambda i:(0,0,0,0,0)),VM,VM],out_specs=[VM]*6,
        out_shape=[T,T,T,T,jax.ShapeDtypeStruct((D,LEN),f32),jax.ShapeDtypeStruct((HEADS,1,LEN),f32)],
        scratch_shapes=[pltpu.VMEM((LEN,LEN),f32),pltpu.VMEM((LEN,HEAD),bf16)],
        compiler_params=pltpu.CompilerParams(vmem_limit_bytes=58<<20),name="attend")(tokens,w,seg.reshape(LEN,1),seg.reshape(1,LEN))
    return (tokT,qT,kT,vT),mixT,lse

def attend_back_kernel(w,seg_col,seg_row,tokT,qT,kT,vT,mixT,lse,dO,first,gout,g0,grad_in,dist,kn,vn,p_all,ds_all,dqT,dkT,dvT):
    fill_distance(dist,seg_col,seg_row)
    @pl.loop(0,HEADS)
    def _(h):
        rows=pl.ds(pl.multiple_of(h*HEAD,HEAD),HEAD)
        kn[...]=kT[rows].astype(f32).T.astype(bf16)
        vn[...]=vT[rows].astype(f32).T.astype(bf16)
        m=slope(h)
        for b in range(LEN//QB):
            cols=pl.ds(b*QB,QB)
            q=(qT[rows,cols]*bf16(0.125))
            s=dot(kn[...],q)-m*dist[:,cols]
            p=jnp.exp(s-lse[h,:,cols])
            do=dO[rows,cols]
            delta=jnp.sum(do.astype(f32)*mixT[rows,cols],0,keepdims=True)
            dp=dot(vn[...],do)
            p_all[:,cols]=p.astype(bf16)
            ds=(p*(dp-delta)).astype(bf16)
            ds_all[:,cols]=ds
            dqT[rows,cols]=(dot(kT[rows],ds)*0.125).astype(bf16)
        dvT[rows]=dot_nt(dO[rows],p_all[...]).astype(bf16)
        dkT[rows]=(dot_nt(qT[rows],ds_all[...])*0.125).astype(bf16)
    g0[1,1]=gout[...]
    for n,g in enumerate((dqT,dkT,dvT)):
        g0[n//2,n%2]=dot_nt(tokT[...],g[...]).astype(bf16)
    @pl.loop(0,4)
    def _(t):
        c=pl.ds(pl.multiple_of(t*256,256),256)
        acc=dot(w[0,0,0],dqT[:,c])+dot(w[0,0,1],dkT[:,c])+dot(w[0,1,0],dvT[:,c])
        grad_in[c]=first[c]+acc.T

def attend_back(w,seg,tokT,qT,kT,vT,mixT,lse,dO,first,gout):
    B=lambda: pltpu.VMEM((D,LEN),bf16)
    return pl.pallas_call(attend_back_kernel,grid=(1,),
        in_specs=[pl.BlockSpec((1,2,2,D,D),lambda i:(0,0,0,0,0))]+[VM]*11,out_specs=[VM]*2,
        out_shape=[jax.ShapeDtypeStruct((2,2,D,D),bf16),jax.ShapeDtypeStruct((LEN,D),f32)],
        scratch_shapes=[pltpu.VMEM((LEN,LEN),f32),pltpu.VMEM((LEN,HEAD),bf16),pltpu.VMEM((LEN,HEAD),bf16),pltpu.VMEM((LEN,LEN),bf16),pltpu.VMEM((LEN,LEN),bf16),B(),B(),B()],
        compiler_params=pltpu.CompilerParams(vmem_limit_bytes=60<<20),name="attend_back")(w,seg.reshape(LEN,1),seg.reshape(1,LEN),tokT,qT,kT,vT,mixT,lse,dO,first,gout)

TB=256
def feed_kernel(tokens,cot,mixT,wo,w1,w2,w3,norms,output,first,dO,ng,gout,gdown,gwide,inner,hidden,gg,gu,gffn,gbranch,fa,fb,mixb):
    step=pl.program_id(0)
    gain1=norms[0:1]; shift1=norms[1:2]; gain2=norms[2:3]; shift2=norms[3:4]
    def stats(v):
        c=v-jnp.mean(v,-1,keepdims=True)
        r=lax.rsqrt(jnp.mean(c*c,-1,keepdims=True)+norm_eps)
        return c*r,r
    def back(e,n,r):
        return r*(e-jnp.mean(e,-1,keepdims=True)-n*jnp.mean(e*n,-1,keepdims=True))
    W=lambda p,j: (w1,w2)[p-1][0,:,j].reshape(D,D)
    WD=lambda j: w3[0,j].reshape(D,D)
    WO=lambda: wo[0,0].reshape(D,D)
    @pl.when(step==0)
    def _(): ng[...]=jnp.zeros_like(ng)
    @pl.when(step<LEN//TB)
    def _():
        rows=pl.ds(pl.multiple_of(step*TB,TB),TB)
        mb=mixT[...].astype(bf16)
        mixb[:,rows]=mb
        branch=dot_tn(mb,WO())
        n1,r1=stats(tokens[...].astype(f32)+branch)
        l1=n1*gain1+shift1
        inn=l1.astype(bf16)
        inner[rows]=inn
        ffn=None
        for j in range(4):
            cols=pl.ds(j*D,D)
            ga=dot(inn,W(1,j)); up=dot(inn,W(2,j))
            cum=0.5*(1.0+lax.erf(ga*inv_root_two))
            gel=ga*cum
            fb[j]=gel
            fa[j]=up*(cum+ga*(jnp.exp(-0.5*ga*ga)*inv_root_tau))
            hid=(gel*up).astype(bf16)
            hidden[rows,cols]=hid
            t=dot(hid,WD(j))
            ffn=t if ffn is None else ffn+t
        n2,r2=stats(l1+ffn)
        output[...]=(n2*gain2+shift2).astype(bf16)
        c=cot[...].astype(f32)
        ng[2:3]+=jnp.sum(c*n2,0,keepdims=True)
        ng[3:4]+=jnp.sum(c,0,keepdims=True)
        mid=back(c*gain2,n2,r2)
        gf=mid.astype(bf16)
        gffn[rows]=gf
        gl=mid
        for j in range(4):
            cols=pl.ds(j*D,D)
            gh=dot_nt(gf,WD(j))
            a=(gh*fa[j]).astype(bf16); b=(gh*fb[j]).astype(bf16)
            gg[rows,cols]=a; gu[rows,cols]=b
            gl=gl+dot_nt(a,W(1,j))+dot_nt(b,W(2,j))
        ng[0:1]+=jnp.sum(gl*n1,0,keepdims=True)
        ng[1:2]+=jnp.sum(gl,0,keepdims=True)
        gfirst=back(gl*gain1,n1,r1)
        first[...]=gfirst
        gb=gfirst.astype(bf16)
        gbranch[rows]=gb
        dO[...]=dot_nt(WO(),gb).astype(bf16)
    def put(g,v):
        g[...]=v.astype(bf16).reshape(g.shape)
    base=LEN//TB
    for j in range(4):
        cols=pl.ds(j*D,D)
        @pl.when(step==base+j)
        def _(): put(gdown,dot_tn(hidden[:,cols],gffn[...]))
        @pl.when(step==base+4+j)
        def _(): put(gwide,dot_tn(inner[...],gg[:,cols]))
        @pl.when(step==base+8+j)
        def _(): put(gwide,dot_tn(inner[...],gu[:,cols]))
    @pl.when(step==base+12)
    def _(): put(gout,dot(mixb[...],gbranch[...]))

def feed(tokens,cot,mixT,w,norms):
    n=LEN//TB
    last=n-1
    row=lambda i:(jnp.minimum(i,last),0)
    col=lambda i:(0,jnp.minimum(i,last))
    one=pl.Buffered(1)
    S=jax.ShapeDtypeStruct
    V=lambda s,d=bf16: pltpu.VMEM(s,d)
    clip=lambda v,a,b: jnp.minimum(jnp.maximum(v,a),b)
    return pl.pallas_call(feed_kernel,grid=(n+13,),
        in_specs=[pl.BlockSpec((TB,D),row),pl.BlockSpec((TB,D),row),pl.BlockSpec((D,TB),col),
            pl.BlockSpec((1,1,4,D//4,D),lambda i:(0,3,0,0,0),pipeline_mode=one),*[pl.BlockSpec((1,4,4,D//4,D),lambda i,p=p:(p,0,0,0,0),pipeline_mode=one) for p in (1,2,3)],pl.BlockSpec((4,D),lambda i:(0,0))],
        out_specs=[pl.BlockSpec((TB,D),row),pl.BlockSpec((TB,D),row),pl.BlockSpec((D,TB),col),
            pl.BlockSpec((4,D),lambda i:(0,0)),
            pl.BlockSpec((D,D),lambda i:(0,0)),
            pl.BlockSpec((1,D,D),lambda i:(clip(i-n,0,3),0,0)),
            pl.BlockSpec((1,4,1,D//4,D),lambda i:(clip((i-n-4)//4,0,1),0,clip(i-n-4,0,7)%4,0,0))],
        out_shape=[S((LEN,D),bf16),S((LEN,D),f32),S((D,LEN),bf16),S((4,D),f32),S((D,D),bf16),S((4,D,D),bf16),S((2,4,4,D//4,D),bf16)],
        scratch_shapes=[V((LEN,D)),V((LEN,FF)),V((LEN,FF)),V((LEN,FF)),V((LEN,D)),V((LEN,D)),V((4,TB,D),f32),V((4,TB,D),f32),V((D,LEN))],
        compiler_params=pltpu.CompilerParams(vmem_limit_bytes=62<<20),name="feed")(tokens,cot,mixT,*[w.reshape(4,4,4,D//4,D)]*4,norms)

SQUARE = D * D
TAIL = 4 * D


def from_wide(blocks):
    return blocks.reshape(4, 4, D // 4, D).transpose(0, 2, 1, 3).reshape(D, FF)


def to_wide(value):
    return value.reshape(4, D // 4, 4, D).transpose(0, 2, 1, 3).reshape(2, 2, D, D)


def swap_wide(block, index, inverse):
    dims = (4, D // 4, D) if inverse else (D // 4, 4, D)
    swapped = block.reshape(dims).transpose(1, 0, 2).reshape(D, D)
    wide = jnp.logical_and(index >= 4, index < 12)
    return jnp.where(wide, swapped, block)


def gather_weights(master):
    count = lax.axis_size("zero")
    index = lax.axis_index("zero")
    size = 16 * SQUARE // count
    weights = master.astype(bf16)
    last = weights[-TAIL:]
    before = lax.ppermute(last, "zero", [(k, k + 1) for k in range(count - 1)])
    joined = jnp.concatenate([before, weights])
    block = lax.dynamic_slice(joined, (TAIL - TAIL // count * index,), (size,))
    if count == 16:
        padded = jnp.pad(last.reshape(4, D), ((0, 12), (0, 0)))
        blocks, tail = gather_blocks(swap_wide(block.reshape(D, D), index, False), padded)
        norms = tail[:4].astype(f32)
    else:
        natural = lax.all_gather(block.reshape(-1, D), "zero", axis=0, tiled=True)
        parts = natural.reshape(4, 4 * D, D)
        wide = [to_wide(parts[k].reshape(D, FF)) for k in (1, 2)]
        blocks = jnp.stack([parts[0].reshape(2, 2, D, D), *wide, parts[3].reshape(2, 2, D, D)])
        norms = lax.psum(jnp.where(index == count - 1, last.astype(f32), 0.0), "zero").reshape(4, D)
    return blocks, norms


def scatter_grads(square, wide, down, norm_grads):
    count = lax.axis_size("zero")
    index = lax.axis_index("zero")
    if count == 16:
        block, tail = reduce_blocks(square, wide, down, norm_grads)
        block = swap_wide(block, index, True)
    else:
        natural = [from_wide(wide[k]).reshape(4 * D, D) for k in (0, 1)]
        natural = jnp.concatenate([square.reshape(4 * D, D), *natural, down.reshape(4 * D, D)])
        block = lax.psum_scatter(natural, "zero", scatter_dimension=0, tiled=True)
        block = lax.psum(block.astype(f32), "dp")
        tail = lax.psum(norm_grads, ("dp", "zero"))
    flat = block.reshape(-1)
    after = lax.ppermute(flat[:TAIL], "zero", [(k + 1, k) for k in range(count - 1)])
    joined = jnp.concatenate([flat, jnp.where(index == count - 1, tail.reshape(-1), after)])
    shard = flat.shape[0] + TAIL // count
    return lax.dynamic_slice(joined, (TAIL // count * index,), (shard,))


def local(tokens, segments, cotangent, master, moment_one, moment_two):
    blocks, norms = gather_weights(master)
    kept, mixed, log_sum = attend(tokens, blocks, segments)
    output, first_grad, grad_mixed, norm_grads, out_grad, down_grad, wide_grad = feed(
        tokens, cotangent, mixed, blocks, norms
    )
    square_grad, input_grad = attend_back(
        blocks, segments, *kept, mixed, log_sum, grad_mixed, first_grad, out_grad
    )
    grad_shard = scatter_grads(
        square_grad, wide_grad.reshape(2, 2, 2, D, D), down_grad.reshape(2, 2, D, D), norm_grads
    )
    grad_shard = grad_shard / (lax.axis_size("zero") * lax.axis_size("dp"))
    first = beta_one * moment_one + (1.0 - beta_one) * grad_shard
    second = beta_two * moment_two + (1.0 - beta_two) * grad_shard * grad_shard
    update = first / correct_one / (jnp.sqrt(second / correct_two) + adam_eps)
    master_new = master - learn_rate * (update + weight_decay * master)
    return (
        output,
        input_grad,
        grad_shard,
        first,
        second,
        master_new,
        master_new.astype(jnp.bfloat16),
    )


def solution(mesh):
    return jax.shard_map(
        local,
        mesh=mesh,
        in_specs=(
            P(("dp", "zero"), None),
            P(("dp", "zero")),
            P(("dp", "zero"), None),
            P("zero"),
            P("zero"),
            P("zero"),
        ),
        out_specs=(
            P(("dp", "zero"), None),
            P(("dp", "zero"), None),
            P("zero"),
            P("zero"),
            P("zero"),
            P("zero"),
            P("zero"),
        ),
        check_vma=False,
    )
```

```python
import functools

import jax
import jax.numpy as jnp
from jax import lax
from jax.sharding import PartitionSpec as P
import jax.experimental.pallas as pl
import jax.experimental.pallas.tpu as pltpu

D = 768
HEADS = 12
HEAD = 64
FF = 3072
LEN = 1024


learn_rate = 0.02
beta_one = 0.9
beta_two = 0.999
adam_eps = 1e-08
weight_decay = 0.01
correct_one = 1.0 - 0.9**10
correct_two = 1.0 - 0.999**10
norm_eps = 1e-06
inv_root_two = 0.7071067811865476
inv_root_tau = 0.3989422804014327


MESH=pl.DeviceIdType.MESH
RA,RB,RC=48,128,208
OFFS=(0,RA,RA+RB)
LENS=(RA,RB,RC)
HALF=384

def place():
    i=lax.axis_index("zero"); c=lax.axis_index("dp")
    z=i//4; y=(i//2)%2; x=i%2
    return i,c,z,y,x

def enter_barrier(i,c,z):
    bar=pltpu.get_barrier_semaphore()
    for dev in ((c,i+1-2*(i%2)),(c,i+2-4*((i//2)%2)),(1-c,i)):
        pl.semaphore_signal(bar,inc=1,device_id=dev,device_id_type=MESH)
    @pl.when(z>0)
    def _(): pl.semaphore_signal(bar,inc=1,device_id=(c,i-4),device_id_type=MESH)
    @pl.when(z<3)
    def _(): pl.semaphore_signal(bar,inc=1,device_id=(c,i+4),device_id_type=MESH)
    pl.semaphore_wait(bar,3+jnp.minimum(z,1)+jnp.minimum(3-z,1))

def ag_kernel(blk,last,result,tail,out,own_sem,out_sem,tr,tz,ty,tx,rx,ry,rz,sx,sy,szr,szl,rs,ss):
    i,c,z,y,x=place()
    xp=(c,i+1-2*x); yp=(c,i+2-4*y); sib=(1-c,i); zr=(c,i+4); zl=(c,i-4)
    enter_barrier(i,c,z)
    own=pltpu.make_async_copy(blk,out.at[z,y,x],own_sem)
    own.start()
    source=jnp.logical_and(z==3,jnp.logical_and(y==1,x==1))
    line=jnp.logical_and(y==1,x==1)
    @pl.when(source)
    def _(): tail[...]=last[...]
    def tcp(dev,s): return pltpu.make_async_remote_copy(src_ref=tail,dst_ref=tail,send_sem=s,recv_sem=tr,device_id=dev,device_id_type=MESH)
    def tail_along_z(first):
        @pl.when(jnp.logical_and(line,source if first else jnp.logical_not(source)))
        def _():
            if not first: tcp(zl,tz).wait_recv()
            @pl.when(z>0)
            def _(): tcp(zl,tz).start()
            tcp(yp,ty).start()
    def tail_along_x():
        @pl.when(x==1)
        def _():
            @pl.when(y==0)
            def _(): tcp(yp,ty).wait_recv()
            tcp(xp,tx).start()
    def tail_end():
        @pl.when(x==0)
        def _(): tcp(xp,tx).wait_recv()
        @pl.when(x==1)
        def _(): tcp(xp,tx).wait_send()
        @pl.when(line)
        def _():
            tcp(yp,ty).wait_send()
            @pl.when(z>0)
            def _(): tcp(zl,tz).wait_send()
    tail_along_z(True)
    own.wait()
    rows=[pl.ds(pl.multiple_of(c*HALF+OFFS[k],16),LENS[k]) for k in range(3)]
    orow=[pl.ds(pl.multiple_of((1-c)*HALF+OFFS[k],16),LENS[k]) for k in range(3)]
    def cp(sl,dev,s,r):
        return pltpu.make_async_remote_copy(src_ref=out.at[sl],dst_ref=out.at[sl],send_sem=s,recv_sem=r,device_id=dev,device_id_type=MESH)
    al=slice(None)
    pend=[]
    def A1(xx,R=rows): return (z,y,xx,R[0])
    def A2(yy,R=rows): return (z,yy,al,R[0])
    def A3(zs,R=rows): return (zs,al,al,R[0])
    def B1(yy,R=rows): return (z,yy,x,R[1])
    def B2(zs,xx,R=rows): return (zs,al,xx,R[1])
    def C1(zs,R=rows): return (zs,y,x,R[2])
    def C2(zs,xx,R=rows): return (zs,y,xx,R[2])
    def C3(zs,yy,R=rows): return (zs,yy,al,R[2])
    def sibsend(sl,k):
        cp(sl,sib,ss.at[k],rs.at[k]).start()
    def sibwait(sl,k):
        d=cp(sl,sib,ss.at[k],rs.at[k]); d.wait_send(); d.wait_recv()
    def zsend(sl,zs,base):
        @pl.when(jnp.logical_and(zs<=z,z<3))
        def _(): cp(sl,zr,szr.at[base+zs],rz.at[base+zs]).start()
        @pl.when(jnp.logical_and(zs>=z,z>0))
        def _(): cp(sl,zl,szl.at[base+zs],rz.at[base+zs]).start()
    def zsent(sl,zs,base):
        @pl.when(jnp.logical_and(zs<=z,z<3))
        def _(): cp(sl,zr,szr.at[base+zs],rz.at[base+zs]).wait_send()
        @pl.when(jnp.logical_and(zs>=z,z>0))
        def _(): cp(sl,zl,szl.at[base+zs],rz.at[base+zs]).wait_send()
    def zwait(sl,zs,base):
        cp(sl,zr,szr.at[base+zs],rz.at[base+zs]).wait_recv()
    A,B,C=0,4,8
    def xs(sl,k): cp(sl,xp,sx.at[k],rx.at[k]).start()
    def xw(sl,k): cp(sl,xp,sx.at[k],rx.at[k]).wait_recv()
    def xd(sl,k): cp(sl,xp,sx.at[k],rx.at[k]).wait_send()
    def ys(sl,k): cp(sl,yp,sy.at[k],ry.at[k]).start()
    def yw(sl,k): cp(sl,yp,sy.at[k],ry.at[k]).wait_recv()
    def yd(sl,k): cp(sl,yp,sy.at[k],ry.at[k]).wait_send()
    xs(A1(x),0); ys(B1(y),1); zsend(C1(z),z,C); xs(C2(z,x),5+z)
    xw(A1(1-x),0); ys(A2(y),0); sibsend(A1(1-x),0)
    yw(B1(1-y),1); zsend(B2(z,x),z,B); xs(B2(z,x),1+z); sibsend(B1(1-y),6)
    xw(C2(z,1-x),5+z); ys(C3(z,y),2+z); sibsend(C2(z,1-x),19+z)
    def late(zs):
        xw(C2(zs,1-x),5+zs); ys(C3(zs,y),2+zs); sibsend(C2(zs,1-x),19+zs)
    def early(zs):
        zwait(C1(zs),zs,C); zsend(C1(zs),zs,C); xs(C2(zs,x),5+zs); sibsend(C1(zs),15+zs)
        zwait(B2(zs,x),zs,B); zsend(B2(zs,x),zs,B); xs(B2(zs,x),1+zs); sibsend(B2(zs,x),7+zs)
    def both(s,f):
        @pl.when(z-s>=0)
        def _(): f(z-s)
        @pl.when(z+s<=3)
        def _(): f(z+s)
    both(1,early)
    yw(A2(1-y),0); zsend(A3(z),z,A); sibsend(A2(1-y),1)
    both(1,late)
    tail_along_z(False)
    both(2,early)
    def a3(zs):
        zwait(A3(zs),zs,A); zsend(A3(zs),zs,A); sibsend(A3(zs),2+zs)
    both(1,a3)
    both(2,late)
    tail_along_x()
    both(3,early)
    both(2,a3)
    both(3,late)
    both(3,a3)
    for s in range(4):
        def fin(zs):
            xw(B2(zs,1-x),1+zs); sibsend(B2(zs,1-x),11+zs)
            yw(C3(zs,1-y),2+zs); sibsend(C3(zs,1-y),23+zs)
        if s==0: fin(z)
        else: both(s,fin)
    xd(A1(x),0); yd(A2(y),0); yd(B1(y),1)
    sibwait(A1(1-x,orow),0) ; sibwait(A2(1-y,orow),1); sibwait(B1(1-y,orow),6)
    for zs in range(4):
        xd(B2(zs,x),1+zs); xd(C2(zs,x),5+zs); yd(C3(zs,y),2+zs)
        zsent(A3(zs),zs,A); zsent(B2(zs,x),zs,B); zsent(C1(zs),zs,C)
        sibwait(B2(zs,1-x,orow),11+zs); sibwait(C2(zs,1-x,orow),19+zs); sibwait(C3(zs,1-y,orow),23+zs)
        @pl.when(zs!=z)
        def _():
            sibwait(A3(zs,orow),2+zs); sibwait(B2(zs,x,orow),7+zs); sibwait(C1(zs,orow),15+zs)
    tail_end()
    leave=[pltpu.make_async_copy(out.at[zs],result.at[zs],out_sem.at[zs]) for zs in range(4)]
    for move in leave: move.start()
    for move in leave: move.wait()

def gather_blocks(blk,last):
    D=pltpu.SemaphoreType.DMA
    return pl.pallas_call(ag_kernel,out_shape=[jax.ShapeDtypeStruct((4,2,2,768,768),jnp.bfloat16),jax.ShapeDtypeStruct((16,768),jnp.bfloat16)],
        in_specs=[pl.BlockSpec(memory_space=pl.ANY),pl.BlockSpec(memory_space=pltpu.VMEM)],out_specs=[pl.BlockSpec(memory_space=pl.ANY),pl.BlockSpec(memory_space=pltpu.VMEM)],
        scratch_shapes=[pltpu.VMEM((4,2,2,768,768),jnp.bfloat16),D,D((4,)),D,D,D,D,D((9,)),D((6,)),D((12,)),D((9,)),D((6,)),D((12,)),D((12,)),D((27,)),D((27,))],
        compiler_params=pltpu.CompilerParams(collective_id=1,has_side_effects=True,vmem_limit_bytes=40<<20),name="gather_blocks")(blk,last)


ALL = slice(None)

def rs_kernel(g0,gwide,gdown,norm_in,out,norm_out,nx,ny,nz,nc,nacc,nrx,nry,nrz,nrc,nsx,nsy,nsz,nsc,own,sl,la1,la2,lafr,lafl,lb1,lb2r,lb2l,lb3,lc1r,lc1l,lc2,lc3,res,
              own_sem,ss,rs,rx,ry,rzr,rzl,sx,sy,szr,szl,fs,fr,osem):
    i,c,z,y,x=place()
    xp=(c,i+1-2*x); yp=(c,i+2-4*y); sib=(1-c,i); zr=(c,i+4); zl=(c,i-4)
    mine=pl.ds(pl.multiple_of(c*HALF,16),HALF); other=pl.ds(pl.multiple_of((1-c)*HALF,16),HALF)
    planes=[g0,gwide.at[0],gwide.at[1],gdown]
    locs=[pltpu.make_async_copy(planes[zt].at[:,:,mine],own.at[zt],own_sem.at[zt]) for zt in range(4)]
    for d in locs: d.start()
    enter_barrier(i,c,z)
    sibs=[pltpu.make_async_remote_copy(src_ref=planes[zt].at[:,:,other],dst_ref=sl.at[zt],send_sem=ss.at[zt],recv_sem=rs.at[zt],device_id=sib,device_id_type=MESH) for zt in range(4)]
    for d in sibs: d.start()
    r=[pl.ds(OFFS[k],LENS[k]) for k in range(3)]
    def rc(src,dst,dev,s,q):
        return pltpu.make_async_remote_copy(src_ref=src,dst_ref=dst,send_sem=s,recv_sem=q,device_id=dev,device_id_type=MESH)
    def add(dst,src,n,rows,step):
        @pl.loop(0,rows//step)
        def _(k):
            q=pl.ds(pl.multiple_of(k*step,16),step)
            dst(q)[...]=(dst(q)[...].astype(jnp.float32)+src(q)[...].astype(jnp.float32)).astype(jnp.bfloat16)
    def sub(k,q): return pl.ds(pl.multiple_of(OFFS[k]+q.start,16),q.size)
    def add2(ownidx,k,land):
        add(lambda q: own.at[tuple(ownidx)+(sub(k,q),)], lambda q: land.at[tuple([ALL]*(len(land.shape)-2))+(q,)],0,LENS[k],16)
    def C3(zt): return rc(own.at[zt,1-y,:,r[2]],lc3.at[zt],yp,sy.at[zt],ry.at[zt])
    def B3(zt): return rc(own.at[zt,:,1-x,r[1]],lb3.at[zt],xp,sx.at[zt],rx.at[zt])
    def C2(zt): return rc(own.at[zt,y,1-x,r[2]],lc2.at[zt],xp,sx.at[4+zt],rx.at[4+zt])
    A2=rc(own.at[z,1-y,:,r[0]],la2,yp,sy.at[4],ry.at[4])
    A1=rc(own.at[z,y,1-x,r[0]],la1,xp,sx.at[8],rx.at[8])
    B1=rc(own.at[z,1-y,x,r[1]],lb1,yp,sy.at[5],ry.at[5])
    def zline(src,landr,landl,base):
        def R(zt): return rc(src(zt),landr.at[zt],zr,szr.at[base+zt],rzr.at[base+zt])
        def L(zt): return rc(src(zt),landl.at[zt],zl,szl.at[base+zt],rzl.at[base+zt])
        return R,L
    AR,AL=zline(lambda zt: own.at[zt,:,:,r[0]],lafr,lafl,0)
    BR,BL=zline(lambda zt: own.at[zt,:,x,r[1]],lb2r,lb2l,4)
    CR,CL=zline(lambda zt: own.at[zt,y,x,r[2]],lc1r,lc1l,8)
    def zgo(zt,idx,k,R,L,landr,landl):
        @pl.when(zt>z)
        def _():
            @pl.when(z>0)
            def _():
                R(zt).wait_recv(); add2(idx,k,landr.at[zt])
            R(zt).start()
        @pl.when(zt<z)
        def _():
            @pl.when(z<3)
            def _():
                L(zt).wait_recv(); add2(idx,k,landl.at[zt])
            L(zt).start()
    def zfin(idx,k,R,L,landr,landl):
        @pl.when(z>0)
        def _(): R(z).wait_recv(); add2(idx,k,landr.at[z])
        @pl.when(z<3)
        def _(): L(z).wait_recv(); add2(idx,k,landl.at[z])
    def far(s):
        return s
    def sumsib(zt):
        locs[zt].wait(); sibs[zt].wait_recv()
        @pl.loop(0,HALF//16)
        def _(k):
            q=pl.ds(pl.multiple_of(k*16,16),16)
            own[zt,:,:,q]=(own[zt,:,:,q].astype(jnp.float32)+sl[zt,:,:,q].astype(jnp.float32)).astype(jnp.bfloat16)
    order=[3,0,2,1]
    nacc[...]=norm_in[...]
    NX=rc(nacc,nx,xp,nsx,nrx); NY=rc(nacc,ny,yp,nsy,nry); NZ=rc(nacc,nz,zr,nsz,nrz); NC=rc(nacc,nc,sib,nsc,nrc)
    line=jnp.logical_and(x==1,y==1)
    end=jnp.logical_and(line,z==3)
    @pl.when(x==0)
    def _(): NX.start()
    def norm_y():
        @pl.when(x==1)
        def _():
            NX.wait_recv(); nacc[...]+=nx[...]
            @pl.when(y==0)
            def _(): NY.start()
    def norm_z(k):
        @pl.when(jnp.logical_and(line,z==k))
        def _():
            NY.wait_recv(); nacc[...]+=ny[...]
            if k>0:
                NZ.wait_recv(); nacc[...]+=nz[...]
            if k<3: NZ.start()
            else: NC.start()
    def norm_end():
        @pl.when(x==0)
        def _(): NX.wait_send()
        @pl.when(jnp.logical_and(x==1,y==0))
        def _(): NY.wait_send()
        @pl.when(jnp.logical_and(line,z<3))
        def _(): NZ.wait_send()
        @pl.when(end)
        def _():
            NC.wait_recv(); NC.wait_send()
            nacc[...]+=nc[...]
        norm_out[...]=nacc[...]
    for zt in order:
        sumsib(zt)
        C3(zt).start(); B3(zt).start()
        zgo(zt,(zt,ALL,ALL),0,AR,AL,lafr,lafl)
    def c3done(zt):
        C3(zt).wait_recv(); add2((zt,y,ALL),2,lc3.at[zt]); C2(zt).start()
    def b3done(zt):
        B3(zt).wait_recv(); add2((zt,ALL,x),1,lb3.at[zt])
        zgo(zt,(zt,ALL,x),1,BR,BL,lb2r,lb2l)
    def c2done(zt):
        C2(zt).wait_recv(); add2((zt,y,x),2,lc2.at[zt])
        zgo(zt,(zt,y,x),2,CR,CL,lc1r,lc1l)
    c3done(3); b3done(3); norm_y(); c3done(0); b3done(0); norm_z(0); c2done(3); c3done(2); b3done(2); norm_z(1); c2done(0); c3done(1); b3done(1); norm_z(2); c2done(2); c2done(1); norm_z(3)
    zfin((z,ALL,ALL),0,AR,AL,lafr,lafl)
    A2.start()
    zfin((z,ALL,x),1,BR,BL,lb2r,lb2l)
    B1.start()
    A2.wait_recv(); add2((z,y,ALL),0,la2)
    A1.start()
    zfin((z,y,x),2,CR,CL,lc1r,lc1l)
    def final(k,land):
        @pl.loop(0,LENS[k]//16)
        def _(t):
            q=pl.ds(pl.multiple_of(t*16,16),16)
            o=pl.ds(pl.multiple_of(OFFS[k]+t*16,16),16)
            v=own[z,y,x,o].astype(jnp.float32)
            if land is not None: v=v+land[q].astype(jnp.float32)
            res[o]=v
    final(2,None)
    B1.wait_recv(); final(1,lb1)
    A1.wait_recv(); final(0,la1)
    fin=rc(res,out.at[mine],sib,fs,fr)
    fin.start()
    loc=pltpu.make_async_copy(res,out.at[mine],osem)
    loc.start()
    for zt in range(4):
        sibs[zt].wait_send(); C3(zt).wait_send(); B3(zt).wait_send(); C2(zt).wait_send()
        for R,L in ((AR,AL),(BR,BL),(CR,CL)):
            @pl.when(zt>z)
            def _(): R(zt).wait_send()
            @pl.when(zt<z)
            def _(): L(zt).wait_send()
    A2.wait_send(); A1.wait_send(); B1.wait_send()
    norm_end()
    loc.wait(); fin.wait_send()
    rc(res,out.at[other],sib,fs,fr).wait_recv()

def reduce_blocks(g0,gwide,gdown,norms):
    D=pltpu.SemaphoreType.DMA
    bf=jnp.bfloat16
    V=lambda *s: pltpu.VMEM(s,bf)
    return pl.pallas_call(rs_kernel,out_shape=[jax.ShapeDtypeStruct((768,768),jnp.float32),jax.ShapeDtypeStruct((4,768),jnp.float32)],
        in_specs=[pl.BlockSpec(memory_space=pl.ANY)]*3+[pl.BlockSpec(memory_space=pltpu.VMEM)],out_specs=[pl.BlockSpec(memory_space=pl.ANY),pl.BlockSpec(memory_space=pltpu.VMEM)],
        scratch_shapes=[*[pltpu.VMEM((4,768),jnp.float32)]*5,*[D]*8,V(4,2,2,HALF,768),V(4,2,2,HALF,768),V(RA,768),V(2,RA,768),V(4,2,2,RA,768),V(4,2,2,RA,768),
            V(RB,768),V(4,2,RB,768),V(4,2,RB,768),V(4,2,RB,768),V(4,RC,768),V(4,RC,768),V(4,RC,768),V(4,2,RC,768),pltpu.VMEM((HALF,768),jnp.float32),
            D((4,)),D((4,)),D((4,)),D((9,)),D((6,)),D((12,)),D((12,)),D((9,)),D((6,)),D((12,)),D((12,)),D,D,D],
        compiler_params=pltpu.CompilerParams(collective_id=2,has_side_effects=True,vmem_limit_bytes=58<<20),name="reduce_blocks")(g0,gwide,gdown,norms)

bf16=jnp.bfloat16; f32=jnp.float32
FAR=1e33
VM=pl.BlockSpec(memory_space=pltpu.VMEM)

def dot(a,b): return lax.dot_general(a,b,(((1,),(0,)),((),())),preferred_element_type=f32)
def dot_tn(a,b): return lax.dot_general(a,b,(((0,),(0,)),((),())),preferred_element_type=f32)
def dot_nt(a,b): return lax.dot_general(a,b,(((1,),(1,)),((),())),preferred_element_type=f32)

def slope(h):
    return jnp.exp2(-8.0/HEADS*(jnp.full((1,1),h,jnp.int32).astype(f32)+1.0))

def fill_distance(dist,seg_col,seg_row):
    @pl.loop(0,LEN//128)
    def _(k):
        r=pl.ds(pl.multiple_of(k*128,128),128)
        kk=(lax.broadcasted_iota(jnp.int32,(128,LEN),0)+k*128)
        qq=lax.broadcasted_iota(jnp.int32,(128,LEN),1)
        d=jnp.abs(kk-qq).astype(f32)
        dist[r]=jnp.where(seg_col[r]==seg_row[...],d,FAR)

QB=256
def attend_kernel(tokens,w,seg_col,seg_row,tokT,qT,kT,vT,mixT,mixb,lse,dist,kn):
    tokT[...]=tokens[...].astype(f32).T.astype(bf16)
    fill_distance(dist,seg_col,seg_row)
    for n,(o,s) in enumerate(((qT,0.125),(kT,1.0),(vT,1.0))):
        @pl.loop(0,3)
        def _(t):
            c=pl.ds(pl.multiple_of(t*256,256),256)
            r=dot_tn(w[0,n//2,n%2,:,c],tokT[...])
            o[c]=r.astype(bf16)
    @pl.loop(0,HEADS)
    def _(h):
        rows=pl.ds(pl.multiple_of(h*HEAD,HEAD),HEAD)
        kn[...]=kT[rows].astype(f32).T.astype(bf16)
        m=slope(h)
        for b in range(LEN//QB):
            cols=pl.ds(b*QB,QB)
            q=(qT[rows,cols]*bf16(0.125))
            s=dot(kn[...],q)-m*dist[:,cols]
            top=jnp.max(s,0,keepdims=True)
            e=jnp.exp(s-top)
            total=jnp.sum(e,0,keepdims=True)
            o=dot(vT[rows],e.astype(bf16))/total
            mixT[rows,cols]=o
            mixb[rows,cols]=o.astype(bf16)
            lse[h,:,cols]=top+jnp.log(total)

def attend(tokens,w,seg):
    T=jax.ShapeDtypeStruct((D,LEN),bf16)
    tokT,qT,kT,vT,mixT,mixb,lse=pl.pallas_call(attend_kernel,grid=(1,),
        in_specs=[VM,pl.BlockSpec((1,2,2,D,D),lambda i:(0,0,0,0,0)),VM,VM],out_specs=[VM]*7,
        out_shape=[T,T,T,T,jax.ShapeDtypeStruct((D,LEN),f32),T,jax.ShapeDtypeStruct((HEADS,1,LEN),f32)],
        scratch_shapes=[pltpu.VMEM((LEN,LEN),f32),pltpu.VMEM((LEN,HEAD),bf16)],
        compiler_params=pltpu.CompilerParams(vmem_limit_bytes=58<<20),name="attend")(tokens,w,seg.reshape(LEN,1),seg.reshape(1,LEN))
    return (tokT,qT,kT,vT,mixT),mixb,lse

def attend_back_kernel(w,seg_col,seg_row,tokT,qT,kT,vT,mixT,lse,dO,first,gbranch,g0,grad_in,dist,kn,vn,p_all,ds_all,dqT,dkT,dvT):
    fill_distance(dist,seg_col,seg_row)
    @pl.loop(0,HEADS)
    def _(h):
        rows=pl.ds(pl.multiple_of(h*HEAD,HEAD),HEAD)
        kn[...]=kT[rows].astype(f32).T.astype(bf16)
        vn[...]=vT[rows].astype(f32).T.astype(bf16)
        m=slope(h)
        for b in range(LEN//QB):
            cols=pl.ds(b*QB,QB)
            q=(qT[rows,cols]*bf16(0.125))
            s=dot(kn[...],q)-m*dist[:,cols]
            p=jnp.exp(s-lse[h,:,cols])
            do=dO[rows,cols]
            delta=jnp.sum(do.astype(f32)*mixT[rows,cols],0,keepdims=True)
            dp=dot(vn[...],do)
            p_all[:,cols]=p.astype(bf16)
            ds=(p*(dp-delta)).astype(bf16)
            ds_all[:,cols]=ds
            dqT[rows,cols]=(dot(kT[rows],ds)*0.125).astype(bf16)
        dvT[rows]=dot_nt(dO[rows],p_all[...]).astype(bf16)
        dkT[rows]=(dot_nt(qT[rows],ds_all[...])*0.125).astype(bf16)
    g0[1,1]=dot(mixT[...].astype(bf16),gbranch[...]).astype(bf16)
    for n,g in enumerate((dqT,dkT,dvT)):
        g0[n//2,n%2]=dot_nt(tokT[...],g[...]).astype(bf16)
    @pl.loop(0,4)
    def _(t):
        c=pl.ds(pl.multiple_of(t*256,256),256)
        acc=dot(w[0,0,0],dqT[:,c])+dot(w[0,0,1],dkT[:,c])+dot(w[0,1,0],dvT[:,c])
        grad_in[c]=first[c]+acc.T

def attend_back(w,seg,tokT,qT,kT,vT,mixT,lse,dO,first,gbranch):
    B=lambda: pltpu.VMEM((D,LEN),bf16)
    return pl.pallas_call(attend_back_kernel,grid=(1,),
        in_specs=[pl.BlockSpec((1,2,2,D,D),lambda i:(0,0,0,0,0))]+[VM]*11,out_specs=[VM]*2,
        out_shape=[jax.ShapeDtypeStruct((2,2,D,D),bf16),jax.ShapeDtypeStruct((LEN,D),f32)],
        scratch_shapes=[pltpu.VMEM((LEN,LEN),f32),pltpu.VMEM((LEN,HEAD),bf16),pltpu.VMEM((LEN,HEAD),bf16),pltpu.VMEM((LEN,LEN),bf16),pltpu.VMEM((LEN,LEN),bf16),B(),B(),B()],
        compiler_params=pltpu.CompilerParams(vmem_limit_bytes=60<<20),name="attend_back")(w,seg.reshape(LEN,1),seg.reshape(1,LEN),tokT,qT,kT,vT,mixT,lse,dO,first,gbranch)

TB=256
def feed_kernel(tokens,cot,mixb,wo,w1,w2,w3,norms,output,first,dO,gbranch,ng,gdown,gwide,inner,wide,gffn,fa,fb,acc,hid):
    step=pl.program_id(0)
    gain1=norms[0:1]; shift1=norms[1:2]; gain2=norms[2:3]; shift2=norms[3:4]
    def stats(v):
        c=v-jnp.mean(v,-1,keepdims=True)
        r=lax.rsqrt(jnp.mean(c*c,-1,keepdims=True)+norm_eps)
        return c*r,r
    def back(e,n,r):
        return r*(e-jnp.mean(e,-1,keepdims=True)-n*jnp.mean(e*n,-1,keepdims=True))
    W=lambda p,j: (w1,w2)[p-1][0,:,j].reshape(D,D)
    WD=lambda j: w3[0,j].reshape(D,D)
    WO=lambda: wo[0,0].reshape(D,D)
    @pl.when(step==0)
    def _(): ng[...]=jnp.zeros_like(ng)
    @pl.when(step<LEN//TB)
    def _():
        rows=pl.ds(pl.multiple_of(step*TB,TB),TB)
        branch=dot_tn(mixb[...],WO())
        n1,r1=stats(tokens[...].astype(f32)+branch)
        l1=n1*gain1+shift1
        inner[rows]=l1.astype(bf16)
        acc[...]=l1
        @pl.loop(0,4,unroll=2)
        def _(j):
            inn=inner[rows]
            ga=dot(inn,W(1,j)); up=dot(inn,W(2,j))
            cum=0.5*(1.0+lax.erf(ga*inv_root_two))
            gel=ga*cum
            fb[j]=gel
            fa[j]=up*(cum+ga*(jnp.exp(-0.5*ga*ga)*inv_root_tau))
            h=(gel*up).astype(bf16)
            hid[j,rows]=h
            acc[...]+=dot(h,WD(j))
        n2,r2=stats(acc[...])
        output[...]=(n2*gain2+shift2).astype(bf16)
        c=cot[...].astype(f32)
        ng[2:3]+=jnp.sum(c*n2,0,keepdims=True)
        ng[3:4]+=jnp.sum(c,0,keepdims=True)
        mid=back(c*gain2,n2,r2)
        gffn[rows]=mid.astype(bf16)
        acc[...]=mid
        @pl.loop(0,4,unroll=2)
        def _(j):
            gh=dot_nt(gffn[rows],WD(j))
            a=(gh*fa[j]).astype(bf16); b=(gh*fb[j]).astype(bf16)
            wide[j,rows]=a; wide[4+j,rows]=b
            acc[...]+=dot_nt(a,W(1,j))+dot_nt(b,W(2,j))
        gl=acc[...]
        ng[0:1]+=jnp.sum(gl*n1,0,keepdims=True)
        ng[1:2]+=jnp.sum(gl,0,keepdims=True)
        gfirst=back(gl*gain1,n1,r1)
        first[...]=gfirst
        gb=gfirst.astype(bf16)
        gbranch[...]=gb
        dO[...]=dot_nt(WO(),gb).astype(bf16)
    def put(g,v):
        g[...]=v.astype(bf16).reshape(g.shape)
    base=LEN//TB
    @pl.when(jnp.logical_and(step>=base,step<base+4))
    def _(): put(gdown,dot_tn(hid[step-base],gffn[...]))
    @pl.when(jnp.logical_and(step>=base+4,step<base+12))
    def _(): put(gwide,dot_tn(inner[...],wide[step-base-4]))

def feed(tokens,cot,mixb,w,norms):
    n=LEN//TB
    last=n-1
    row=lambda i:(jnp.minimum(i,last),0)
    col=lambda i:(0,jnp.minimum(i,last))
    one=pl.Buffered(1)
    S=jax.ShapeDtypeStruct
    V=lambda s,d=bf16: pltpu.VMEM(s,d)
    clip=lambda v,a,b: jnp.minimum(jnp.maximum(v,a),b)
    return pl.pallas_call(feed_kernel,grid=(n+12,),
        in_specs=[pl.BlockSpec((TB,D),row),pl.BlockSpec((TB,D),row),pl.BlockSpec((D,TB),col),
            pl.BlockSpec((1,1,4,D//4,D),lambda i:(0,3,0,0,0),pipeline_mode=one),*[pl.BlockSpec((1,4,4,D//4,D),lambda i,p=p:(p,0,0,0,0),pipeline_mode=one) for p in (1,2,3)],pl.BlockSpec((4,D),lambda i:(0,0))],
        out_specs=[pl.BlockSpec((TB,D),row),pl.BlockSpec((TB,D),row),pl.BlockSpec((D,TB),col),pl.BlockSpec((TB,D),row),
            pl.BlockSpec((4,D),lambda i:(0,0)),
            pl.BlockSpec((1,D,D),lambda i:(clip(i-n,0,3),0,0)),
            pl.BlockSpec((1,4,1,D//4,D),lambda i:(clip((i-n-4)//4,0,1),0,clip(i-n-4,0,7)%4,0,0))],
        out_shape=[S((LEN,D),bf16),S((LEN,D),f32),S((D,LEN),bf16),S((LEN,D),bf16),S((4,D),f32),S((4,D,D),bf16),S((2,4,4,D//4,D),bf16)],
        scratch_shapes=[V((LEN,D)),V((8,LEN,D)),V((LEN,D)),V((4,TB,D),f32),V((4,TB,D),f32),V((TB,D),f32),V((4,LEN,D))],
        compiler_params=pltpu.CompilerParams(vmem_limit_bytes=62<<20),name="feed")(tokens,cot,mixb,*[w.reshape(4,4,4,D//4,D)]*4,norms)

SQUARE = D * D
TAIL = 4 * D


def from_wide(blocks):
    return blocks.reshape(4, 4, D // 4, D).transpose(0, 2, 1, 3).reshape(D, FF)


def to_wide(value):
    return value.reshape(4, D // 4, 4, D).transpose(0, 2, 1, 3).reshape(2, 2, D, D)


def swap_wide(block, index, inverse):
    dims = (4, D // 4, D) if inverse else (D // 4, 4, D)
    swapped = block.reshape(dims).transpose(1, 0, 2).reshape(D, D)
    wide = jnp.logical_and(index >= 4, index < 12)
    return jnp.where(wide, swapped, block)


def gather_weights(master):
    count = lax.axis_size("zero")
    index = lax.axis_index("zero")
    size = 16 * SQUARE // count
    weights = master.astype(bf16)
    last = weights[-TAIL:]
    before = lax.ppermute(last, "zero", [(k, k + 1) for k in range(count - 1)])
    joined = jnp.concatenate([before, weights])
    block = lax.dynamic_slice(joined, (TAIL - TAIL // count * index,), (size,))
    if count == 16:
        padded = jnp.pad(last.reshape(4, D), ((0, 12), (0, 0)))
        blocks, tail = gather_blocks(swap_wide(block.reshape(D, D), index, False), padded)
        norms = tail[:4].astype(f32)
    else:
        natural = lax.all_gather(block.reshape(-1, D), "zero", axis=0, tiled=True)
        parts = natural.reshape(4, 4 * D, D)
        wide = [to_wide(parts[k].reshape(D, FF)) for k in (1, 2)]
        blocks = jnp.stack([parts[0].reshape(2, 2, D, D), *wide, parts[3].reshape(2, 2, D, D)])
        norms = lax.psum(jnp.where(index == count - 1, last.astype(f32), 0.0), "zero").reshape(4, D)
    return blocks, norms


def scatter_grads(square, wide, down, norm_grads):
    count = lax.axis_size("zero")
    index = lax.axis_index("zero")
    if count == 16:
        block, tail = reduce_blocks(square, wide, down, norm_grads)
        block = swap_wide(block, index, True)
    else:
        natural = [from_wide(wide[k]).reshape(4 * D, D) for k in (0, 1)]
        natural = jnp.concatenate([square.reshape(4 * D, D), *natural, down.reshape(4 * D, D)])
        block = lax.psum_scatter(natural, "zero", scatter_dimension=0, tiled=True)
        block = lax.psum(block.astype(f32), "dp")
        tail = lax.psum(norm_grads, ("dp", "zero"))
    flat = block.reshape(-1)
    after = lax.ppermute(flat[:TAIL], "zero", [(k + 1, k) for k in range(count - 1)])
    joined = jnp.concatenate([flat, jnp.where(index == count - 1, tail.reshape(-1), after)])
    shard = flat.shape[0] + TAIL // count
    return lax.dynamic_slice(joined, (TAIL // count * index,), (shard,))


def local(tokens, segments, cotangent, master, moment_one, moment_two):
    blocks, norms = gather_weights(master)
    kept, mixed, log_sum = attend(tokens, blocks, segments)
    output, first_grad, grad_mixed, branch_grad, norm_grads, down_grad, wide_grad = feed(
        tokens, cotangent, mixed, blocks, norms
    )
    square_grad, input_grad = attend_back(
        blocks, segments, *kept, log_sum, grad_mixed, first_grad, branch_grad
    )
    grad_shard = scatter_grads(
        square_grad, wide_grad.reshape(2, 2, 2, D, D), down_grad.reshape(2, 2, D, D), norm_grads
    )
    grad_shard = grad_shard / (lax.axis_size("zero") * lax.axis_size("dp"))
    first = beta_one * moment_one + (1.0 - beta_one) * grad_shard
    second = beta_two * moment_two + (1.0 - beta_two) * grad_shard * grad_shard
    update = first / correct_one / (jnp.sqrt(second / correct_two) + adam_eps)
    master_new = master - learn_rate * (update + weight_decay * master)
    return (
        output,
        input_grad,
        grad_shard,
        first,
        second,
        master_new,
        master_new.astype(jnp.bfloat16),
    )


def solution(mesh):
    return jax.shard_map(
        local,
        mesh=mesh,
        in_specs=(
            P(("dp", "zero"), None),
            P(("dp", "zero")),
            P(("dp", "zero"), None),
            P("zero"),
            P("zero"),
            P("zero"),
        ),
        out_specs=(
            P(("dp", "zero"), None),
            P(("dp", "zero"), None),
            P("zero"),
            P("zero"),
            P("zero"),
            P("zero"),
            P("zero"),
        ),
        check_vma=False,
    )
```

```python
import functools

import jax
import jax.numpy as jnp
from jax import lax
from jax.sharding import PartitionSpec as P
import jax.experimental.pallas as pl
import jax.experimental.pallas.tpu as pltpu

D = 768
HEADS = 12
HEAD = 64
FF = 3072
LEN = 1024


learn_rate = 0.02
beta_one = 0.9
beta_two = 0.999
adam_eps = 1e-08
weight_decay = 0.01
correct_one = 1.0 - 0.9**10
correct_two = 1.0 - 0.999**10
norm_eps = 1e-06
inv_root_two = 0.7071067811865476
inv_root_tau = 0.3989422804014327


RA,RB,RC=48,128,208
OFFS=(0,RA,RA+RB)
LENS=(RA,RB,RC)

def enter_barrier(i,c,z):
    bar=pltpu.get_barrier_semaphore()
    for dev in ((c,i+1-2*(i%2)),(c,i+2-4*((i//2)%2)),(1-c,i)):
        pl.semaphore_signal(bar,inc=1,device_id=dev,device_id_type=MESH)
    @pl.when(z>0)
    def _(): pl.semaphore_signal(bar,inc=1,device_id=(c,i-4),device_id_type=MESH)
    @pl.when(z<3)
    def _(): pl.semaphore_signal(bar,inc=1,device_id=(c,i+4),device_id_type=MESH)
    pl.semaphore_wait(bar,3+jnp.minimum(z,1)+jnp.minimum(3-z,1))

def rs_kernel(g0,gwide,gdown,norm_in,out,norm_out,nx,ny,nz,nc,nacc,nrx,nry,nrz,nrc,nsx,nsy,nsz,nsc,own,sl,la1,la2,lafr,lafl,lb1,lb2r,lb2l,lb3,lc1r,lc1l,lc2,lc3,res,
              own_sem,ss,rs,rx,ry,rzr,rzl,sx,sy,szr,szl,fs,fr,osem):
    i,c,z,y,x=place()
    xp=(c,i+1-2*x); yp=(c,i+2-4*y); sib=(1-c,i); zr=(c,i+4); zl=(c,i-4)
    mine=pl.ds(pl.multiple_of(c*HALF,16),HALF); other=pl.ds(pl.multiple_of((1-c)*HALF,16),HALF)
    planes=[g0,gwide.at[0],gwide.at[1],gdown]
    locs=[pltpu.make_async_copy(planes[zt].at[:,:,mine],own.at[zt],own_sem.at[zt]) for zt in range(4)]
    for d in locs: d.start()
    enter_barrier(i,c,z)
    sibs=[pltpu.make_async_remote_copy(src_ref=planes[zt].at[:,:,other],dst_ref=sl.at[zt],send_sem=ss.at[zt],recv_sem=rs.at[zt],device_id=sib,device_id_type=MESH) for zt in range(4)]
    for d in sibs: d.start()
    r=[pl.ds(OFFS[k],LENS[k]) for k in range(3)]
    def rc(src,dst,dev,s,q):
        return pltpu.make_async_remote_copy(src_ref=src,dst_ref=dst,send_sem=s,recv_sem=q,device_id=dev,device_id_type=MESH)
    def add(dst,src,n,rows,step):
        @pl.loop(0,rows//step)
        def _(k):
            q=pl.ds(pl.multiple_of(k*step,16),step)
            dst(q)[...]=(dst(q)[...].astype(jnp.float32)+src(q)[...].astype(jnp.float32)).astype(jnp.bfloat16)
    def sub(k,q): return pl.ds(pl.multiple_of(OFFS[k]+q.start,16),q.size)
    def add2(ownidx,k,land):
        add(lambda q: own.at[tuple(ownidx)+(sub(k,q),)], lambda q: land.at[tuple([ALL]*(len(land.shape)-2))+(q,)],0,LENS[k],16)
    def C3(zt): return rc(own.at[zt,1-y,:,r[2]],lc3.at[zt],yp,sy.at[zt],ry.at[zt])
    def B3(zt): return rc(own.at[zt,:,1-x,r[1]],lb3.at[zt],xp,sx.at[zt],rx.at[zt])
    def C2(zt): return rc(own.at[zt,y,1-x,r[2]],lc2.at[zt],xp,sx.at[4+zt],rx.at[4+zt])
    A2=rc(own.at[z,1-y,:,r[0]],la2,yp,sy.at[4],ry.at[4])
    A1=rc(own.at[z,y,1-x,r[0]],la1,xp,sx.at[8],rx.at[8])
    B1=rc(own.at[z,1-y,x,r[1]],lb1,yp,sy.at[5],ry.at[5])
    def zline(src,landr,landl,base):
        def R(zt): return rc(src(zt),landr.at[zt],zr,szr.at[base+zt],rzr.at[base+zt])
        def L(zt): return rc(src(zt),landl.at[zt],zl,szl.at[base+zt],rzl.at[base+zt])
        return R,L
    AR,AL=zline(lambda zt: own.at[zt,:,:,r[0]],lafr,lafl,0)
    BR,BL=zline(lambda zt: own.at[zt,:,x,r[1]],lb2r,lb2l,4)
    CR,CL=zline(lambda zt: own.at[zt,y,x,r[2]],lc1r,lc1l,8)
    def zgo(zt,idx,k,R,L,landr,landl):
        @pl.when(zt>z)
        def _():
            @pl.when(z>0)
            def _():
                R(zt).wait_recv(); add2(idx,k,landr.at[zt])
            R(zt).start()
        @pl.when(zt<z)
        def _():
            @pl.when(z<3)
            def _():
                L(zt).wait_recv(); add2(idx,k,landl.at[zt])
            L(zt).start()
    def zfin(idx,k,R,L,landr,landl):
        @pl.when(z>0)
        def _(): R(z).wait_recv(); add2(idx,k,landr.at[z])
        @pl.when(z<3)
        def _(): L(z).wait_recv(); add2(idx,k,landl.at[z])
    def far(s):
        return s
    def sumsib(zt):
        locs[zt].wait(); sibs[zt].wait_recv()
        @pl.loop(0,HALF//16)
        def _(k):
            q=pl.ds(pl.multiple_of(k*16,16),16)
            own[zt,:,:,q]=(own[zt,:,:,q].astype(jnp.float32)+sl[zt,:,:,q].astype(jnp.float32)).astype(jnp.bfloat16)
    order=[3,0,2,1]
    nacc[...]=norm_in[...]
    NX=rc(nacc,nx,xp,nsx,nrx); NY=rc(nacc,ny,yp,nsy,nry); NZ=rc(nacc,nz,zr,nsz,nrz); NC=rc(nacc,nc,sib,nsc,nrc)
    line=jnp.logical_and(x==1,y==1)
    end=jnp.logical_and(line,z==3)
    @pl.when(x==0)
    def _(): NX.start()
    def norm_y():
        @pl.when(x==1)
        def _():
            NX.wait_recv(); nacc[...]+=nx[...]
            @pl.when(y==0)
            def _(): NY.start()
    def norm_z(k):
        @pl.when(jnp.logical_and(line,z==k))
        def _():
            NY.wait_recv(); nacc[...]+=ny[...]
            if k>0:
                NZ.wait_recv(); nacc[...]+=nz[...]
            if k<3: NZ.start()
            else: NC.start()
    def norm_end():
        @pl.when(x==0)
        def _(): NX.wait_send()
        @pl.when(jnp.logical_and(x==1,y==0))
        def _(): NY.wait_send()
        @pl.when(jnp.logical_and(line,z<3))
        def _(): NZ.wait_send()
        @pl.when(end)
        def _():
            NC.wait_recv(); NC.wait_send()
            nacc[...]+=nc[...]
        norm_out[...]=nacc[...]
    for zt in order:
        sumsib(zt)
        C3(zt).start(); B3(zt).start()
        zgo(zt,(zt,ALL,ALL),0,AR,AL,lafr,lafl)
    def c3done(zt):
        C3(zt).wait_recv(); add2((zt,y,ALL),2,lc3.at[zt]); C2(zt).start()
    def b3done(zt):
        B3(zt).wait_recv(); add2((zt,ALL,x),1,lb3.at[zt])
        zgo(zt,(zt,ALL,x),1,BR,BL,lb2r,lb2l)
    def c2done(zt):
        C2(zt).wait_recv(); add2((zt,y,x),2,lc2.at[zt])
        zgo(zt,(zt,y,x),2,CR,CL,lc1r,lc1l)
    c3done(3); b3done(3); norm_y(); c3done(0); b3done(0); norm_z(0); c2done(3); c3done(2); b3done(2); norm_z(1); c2done(0); c3done(1); b3done(1); norm_z(2); c2done(2); c2done(1); norm_z(3)
    zfin((z,ALL,ALL),0,AR,AL,lafr,lafl)
    A2.start()
    zfin((z,ALL,x),1,BR,BL,lb2r,lb2l)
    B1.start()
    A2.wait_recv(); add2((z,y,ALL),0,la2)
    A1.start()
    zfin((z,y,x),2,CR,CL,lc1r,lc1l)
    def final(k,land):
        @pl.loop(0,LENS[k]//16)
        def _(t):
            q=pl.ds(pl.multiple_of(t*16,16),16)
            o=pl.ds(pl.multiple_of(OFFS[k]+t*16,16),16)
            v=own[z,y,x,o].astype(jnp.float32)
            if land is not None: v=v+land[q].astype(jnp.float32)
            res[o]=v
    final(2,None)
    B1.wait_recv(); final(1,lb1)
    A1.wait_recv(); final(0,la1)
    fin=rc(res,out.at[mine],sib,fs,fr)
    fin.start()
    loc=pltpu.make_async_copy(res,out.at[mine],osem)
    loc.start()
    for zt in range(4):
        sibs[zt].wait_send(); C3(zt).wait_send(); B3(zt).wait_send(); C2(zt).wait_send()
        for R,L in ((AR,AL),(BR,BL),(CR,CL)):
            @pl.when(zt>z)
            def _(): R(zt).wait_send()
            @pl.when(zt<z)
            def _(): L(zt).wait_send()
    A2.wait_send(); A1.wait_send(); B1.wait_send()
    norm_end()
    loc.wait(); fin.wait_send()
    rc(res,out.at[other],sib,fs,fr).wait_recv()

def reduce_blocks(g0,gwide,gdown,norms):
    D=pltpu.SemaphoreType.DMA
    bf=jnp.bfloat16
    V=lambda *s: pltpu.VMEM(s,bf)
    return pl.pallas_call(rs_kernel,out_shape=[jax.ShapeDtypeStruct((768,768),jnp.float32),jax.ShapeDtypeStruct((4,768),jnp.float32)],
        in_specs=[pl.BlockSpec(memory_space=pl.ANY)]*3+[pl.BlockSpec(memory_space=pltpu.VMEM)],out_specs=[pl.BlockSpec(memory_space=pl.ANY),pl.BlockSpec(memory_space=pltpu.VMEM)],
        scratch_shapes=[*[pltpu.VMEM((4,768),jnp.float32)]*5,*[D]*8,V(4,2,2,HALF,768),V(4,2,2,HALF,768),V(RA,768),V(2,RA,768),V(4,2,2,RA,768),V(4,2,2,RA,768),
            V(RB,768),V(4,2,RB,768),V(4,2,RB,768),V(4,2,RB,768),V(4,RC,768),V(4,RC,768),V(4,RC,768),V(4,2,RC,768),pltpu.VMEM((HALF,768),jnp.float32),
            D((4,)),D((4,)),D((4,)),D((9,)),D((6,)),D((12,)),D((12,)),D((9,)),D((6,)),D((12,)),D((12,)),D,D,D],
        compiler_params=pltpu.CompilerParams(collective_id=2,has_side_effects=True,vmem_limit_bytes=58<<20),name="reduce_blocks")(g0,gwide,gdown,norms)

bf16=jnp.bfloat16; f32=jnp.float32
FAR=1e33
VM=pl.BlockSpec(memory_space=pltpu.VMEM)

def dot(a,b): return lax.dot_general(a,b,(((1,),(0,)),((),())),preferred_element_type=f32)
def dot_tn(a,b): return lax.dot_general(a,b,(((0,),(0,)),((),())),preferred_element_type=f32)
def dot_nt(a,b): return lax.dot_general(a,b,(((1,),(1,)),((),())),preferred_element_type=f32)

def slope(h):
    return jnp.exp2(-8.0/HEADS*(jnp.full((1,1),h,jnp.int32).astype(f32)+1.0))

def fill_distance(dist,seg_col,seg_row):
    @pl.loop(0,LEN//128)
    def _(k):
        r=pl.ds(pl.multiple_of(k*128,128),128)
        kk=(lax.broadcasted_iota(jnp.int32,(128,LEN),0)+k*128)
        qq=lax.broadcasted_iota(jnp.int32,(128,LEN),1)
        d=jnp.abs(kk-qq).astype(f32)
        dist[r]=jnp.where(seg_col[r]==seg_row[...],d,FAR)

QB=256
def project_all(w,tokT,qT,kT,vT):
    for n,o in enumerate((qT,kT,vT)):
        @pl.loop(0,3)
        def _(t):
            c=pl.ds(pl.multiple_of(t*256,256),256)
            o[c]=dot_tn(w[0,n//2,n%2,:,c],tokT[...]).astype(bf16)

def attend_head(h,dist,kn,qT,kT,vT,mixT,mixb,lse):
    rows=pl.ds(pl.multiple_of(h*HEAD,HEAD),HEAD)
    kn[...]=kT[rows].astype(f32).T.astype(bf16)
    m=slope(h)
    for b in range(LEN//QB):
        cols=pl.ds(b*QB,QB)
        q=(qT[rows,cols]*bf16(0.125))
        s=dot(kn[...],q)-m*dist[:,cols]
        top=jnp.max(s,0,keepdims=True)
        e=jnp.exp(s-top)
        total=jnp.sum(e,0,keepdims=True)
        o=dot(vT[rows],e.astype(bf16))/total
        mixT[rows,cols]=o
        mixb[rows,cols]=o.astype(bf16)
        lse[h,:,cols]=top+jnp.log(total)

def attend_kernel(tokens,w,seg_col,seg_row,tokT,qT,kT,vT,mixT,mixb,lse,dist,kn):
    tokT[...]=tokens[...].astype(f32).T.astype(bf16)
    fill_distance(dist,seg_col,seg_row)
    project_all(w,tokT,qT,kT,vT)
    @pl.loop(0,HEADS)
    def _(h):
        attend_head(h,dist,kn,qT,kT,vT,mixT,mixb,lse)

def attend(tokens,w,seg):
    T=jax.ShapeDtypeStruct((D,LEN),bf16)
    tokT,qT,kT,vT,mixT,mixb,lse=pl.pallas_call(attend_kernel,grid=(1,),
        in_specs=[VM,pl.BlockSpec((1,2,2,D,D),lambda i:(0,0,0,0,0)),VM,VM],out_specs=[VM]*7,
        out_shape=[T,T,T,T,jax.ShapeDtypeStruct((D,LEN),f32),T,jax.ShapeDtypeStruct((HEADS,1,LEN),f32)],
        scratch_shapes=[pltpu.VMEM((LEN,LEN),f32),pltpu.VMEM((LEN,HEAD),bf16)],
        compiler_params=pltpu.CompilerParams(vmem_limit_bytes=58<<20),name="attend")(tokens,w,seg.reshape(LEN,1),seg.reshape(1,LEN))
    return (tokT,qT,kT,vT,mixT),mixb,lse

def attend_back_kernel(w,seg_col,seg_row,tokT,qT,kT,vT,mixT,lse,dO,first,gbranch,g0,grad_in,dist,kn,vn,p_all,ds_all,dqT,dkT,dvT):
    fill_distance(dist,seg_col,seg_row)
    @pl.loop(0,HEADS)
    def _(h):
        rows=pl.ds(pl.multiple_of(h*HEAD,HEAD),HEAD)
        kn[...]=kT[rows].astype(f32).T.astype(bf16)
        vn[...]=vT[rows].astype(f32).T.astype(bf16)
        m=slope(h)
        for b in range(LEN//QB):
            cols=pl.ds(b*QB,QB)
            q=(qT[rows,cols]*bf16(0.125))
            s=dot(kn[...],q)-m*dist[:,cols]
            p=jnp.exp(s-lse[h,:,cols])
            do=dO[rows,cols]
            delta=jnp.sum(do.astype(f32)*mixT[rows,cols],0,keepdims=True)
            dp=dot(vn[...],do)
            p_all[:,cols]=p.astype(bf16)
            ds=(p*(dp-delta)).astype(bf16)
            ds_all[:,cols]=ds
            dqT[rows,cols]=(dot(kT[rows],ds)*0.125).astype(bf16)
        dvT[rows]=dot_nt(dO[rows],p_all[...]).astype(bf16)
        dkT[rows]=(dot_nt(qT[rows],ds_all[...])*0.125).astype(bf16)
    g0[1,1]=dot(mixT[...].astype(bf16),gbranch[...]).astype(bf16)
    for n,g in enumerate((dqT,dkT,dvT)):
        g0[n//2,n%2]=dot_nt(tokT[...],g[...]).astype(bf16)
    @pl.loop(0,4)
    def _(t):
        c=pl.ds(pl.multiple_of(t*256,256),256)
        acc=dot(w[0,0,0],dqT[:,c])+dot(w[0,0,1],dkT[:,c])+dot(w[0,1,0],dvT[:,c])
        grad_in[c]=first[c]+acc.T

def attend_back(w,seg,tokT,qT,kT,vT,mixT,lse,dO,first,gbranch):
    B=lambda: pltpu.VMEM((D,LEN),bf16)
    return pl.pallas_call(attend_back_kernel,grid=(1,),
        in_specs=[pl.BlockSpec((1,2,2,D,D),lambda i:(0,0,0,0,0))]+[VM]*11,out_specs=[VM]*2,
        out_shape=[jax.ShapeDtypeStruct((2,2,D,D),bf16),jax.ShapeDtypeStruct((LEN,D),f32)],
        scratch_shapes=[pltpu.VMEM((LEN,LEN),f32),pltpu.VMEM((LEN,HEAD),bf16),pltpu.VMEM((LEN,HEAD),bf16),pltpu.VMEM((LEN,LEN),bf16),pltpu.VMEM((LEN,LEN),bf16),B(),B(),B()],
        compiler_params=pltpu.CompilerParams(vmem_limit_bytes=60<<20),name="attend_back")(w,seg.reshape(LEN,1),seg.reshape(1,LEN),tokT,qT,kT,vT,mixT,lse,dO,first,gbranch)

TB=256
def feed_kernel(tokens,cot,mixb,wo,w1,w2,w3,norms,output,first,dO,gbranch,ng,gdown,gwide,inner,wide,gffn,fa,fb,acc,hid):
    step=pl.program_id(0)
    gain1=norms[0:1]; shift1=norms[1:2]; gain2=norms[2:3]; shift2=norms[3:4]
    def stats(v):
        c=v-jnp.mean(v,-1,keepdims=True)
        r=lax.rsqrt(jnp.mean(c*c,-1,keepdims=True)+norm_eps)
        return c*r,r
    def back(e,n,r):
        return r*(e-jnp.mean(e,-1,keepdims=True)-n*jnp.mean(e*n,-1,keepdims=True))
    W=lambda p,j: (w1,w2)[p-1][0,:,j].reshape(D,D)
    WD=lambda j: w3[0,j].reshape(D,D)
    WO=lambda: wo[0,0].reshape(D,D)
    @pl.when(step==0)
    def _(): ng[...]=jnp.zeros_like(ng)
    @pl.when(step<LEN//TB)
    def _():
        rows=pl.ds(pl.multiple_of(step*TB,TB),TB)
        branch=dot_tn(mixb[...],WO())
        n1,r1=stats(tokens[...].astype(f32)+branch)
        l1=n1*gain1+shift1
        inner[rows]=l1.astype(bf16)
        acc[...]=l1
        @pl.loop(0,4,unroll=2)
        def _(j):
            inn=inner[rows]
            ga=dot(inn,W(1,j)); up=dot(inn,W(2,j))
            cum=0.5*(1.0+lax.erf(ga*inv_root_two))
            gel=ga*cum
            fb[j]=gel
            fa[j]=up*(cum+ga*(jnp.exp(-0.5*ga*ga)*inv_root_tau))
            h=(gel*up).astype(bf16)
            hid[j,rows]=h
            acc[...]+=dot(h,WD(j))
        n2,r2=stats(acc[...])
        output[...]=(n2*gain2+shift2).astype(bf16)
        c=cot[...].astype(f32)
        ng[2:3]+=jnp.sum(c*n2,0,keepdims=True)
        ng[3:4]+=jnp.sum(c,0,keepdims=True)
        mid=back(c*gain2,n2,r2)
        gffn[rows]=mid.astype(bf16)
        acc[...]=mid
        @pl.loop(0,4,unroll=2)
        def _(j):
            gh=dot_nt(gffn[rows],WD(j))
            a=(gh*fa[j]).astype(bf16); b=(gh*fb[j]).astype(bf16)
            wide[j,rows]=a; wide[4+j,rows]=b
            acc[...]+=dot_nt(a,W(1,j))+dot_nt(b,W(2,j))
        gl=acc[...]
        ng[0:1]+=jnp.sum(gl*n1,0,keepdims=True)
        ng[1:2]+=jnp.sum(gl,0,keepdims=True)
        gfirst=back(gl*gain1,n1,r1)
        first[...]=gfirst
        gb=gfirst.astype(bf16)
        gbranch[...]=gb
        dO[...]=dot_nt(WO(),gb).astype(bf16)
    def put(g,v):
        g[...]=v.astype(bf16).reshape(g.shape)
    base=LEN//TB
    @pl.when(jnp.logical_and(step>=base,step<base+4))
    def _(): put(gdown,dot_tn(hid[step-base],gffn[...]))
    @pl.when(jnp.logical_and(step>=base+4,step<base+12))
    def _(): put(gwide,dot_tn(inner[...],wide[step-base-4]))

def feed(tokens,cot,mixb,w,norms):
    n=LEN//TB
    last=n-1
    row=lambda i:(jnp.minimum(i,last),0)
    col=lambda i:(0,jnp.minimum(i,last))
    one=pl.Buffered(1)
    S=jax.ShapeDtypeStruct
    V=lambda s,d=bf16: pltpu.VMEM(s,d)
    clip=lambda v,a,b: jnp.minimum(jnp.maximum(v,a),b)
    return pl.pallas_call(feed_kernel,grid=(n+12,),
        in_specs=[pl.BlockSpec((TB,D),row),pl.BlockSpec((TB,D),row),pl.BlockSpec((D,TB),col),
            pl.BlockSpec((1,1,4,D//4,D),lambda i:(0,3,0,0,0),pipeline_mode=one),*[pl.BlockSpec((1,4,4,D//4,D),lambda i,p=p:(p,0,0,0,0),pipeline_mode=one) for p in (1,2,3)],pl.BlockSpec((4,D),lambda i:(0,0))],
        out_specs=[pl.BlockSpec((TB,D),row),pl.BlockSpec((TB,D),row),pl.BlockSpec((D,TB),col),pl.BlockSpec((TB,D),row),
            pl.BlockSpec((4,D),lambda i:(0,0)),
            pl.BlockSpec((1,D,D),lambda i:(clip(i-n,0,3),0,0)),
            pl.BlockSpec((1,4,1,D//4,D),lambda i:(clip((i-n-4)//4,0,1),0,clip(i-n-4,0,7)%4,0,0))],
        out_shape=[S((LEN,D),bf16),S((LEN,D),f32),S((D,LEN),bf16),S((LEN,D),bf16),S((4,D),f32),S((4,D,D),bf16),S((2,4,4,D//4,D),bf16)],
        scratch_shapes=[V((LEN,D)),V((8,LEN,D)),V((LEN,D)),V((4,TB,D),f32),V((4,TB,D),f32),V((TB,D),f32),V((4,LEN,D))],
        compiler_params=pltpu.CompilerParams(vmem_limit_bytes=62<<20),name="feed")(tokens,cot,mixb,*[w.reshape(4,4,4,D//4,D)]*4,norms)
MESH = pl.DeviceIdType.MESH
ALL = slice(None)
HALF = D // 2
B_ROWS, C_ROWS = 144, 240
CHUNK = 96


def place():
    i = lax.axis_index("zero")
    c = lax.axis_index("dp")
    return i, c, i // 4, (i // 2) % 2, i % 2


def partners(i, c, z, y, x):
    return (c, i + 1 - 2 * x), (c, i + 2 - 4 * y), (1 - c, i), (c, i + 4), (c, i - 4)


def enter(i, c, z, y, x):
    barrier = pltpu.get_barrier_semaphore()
    xp, yp, sib, up, down = partners(i, c, z, y, x)
    for peer in (xp, yp, sib):
        pl.semaphore_signal(barrier, inc=1, device_id=peer, device_id_type=MESH)

    @pl.when(z > 0)
    def _():
        pl.semaphore_signal(barrier, inc=1, device_id=down, device_id_type=MESH)

    @pl.when(z < 3)
    def _():
        pl.semaphore_signal(barrier, inc=1, device_id=up, device_id_type=MESH)

    pl.semaphore_wait(barrier, 3 + jnp.minimum(z, 1) + jnp.minimum(3 - z, 1))


class Lane:
    def __init__(self, peer, sends, recvs):
        self.peer, self.sends, self.recvs = peer, sends, recvs

    def copy(self, ref, n):
        return pltpu.make_async_remote_copy(
            src_ref=ref, dst_ref=ref, send_sem=self.sends.at[n], recv_sem=self.recvs.at[n],
            device_id=self.peer, device_id_type=MESH,
        )

    def go(self, ref, n):
        self.copy(ref, n).start()

    def got(self, ref, n):
        self.copy(ref, n).wait_recv()

    def gone(self, ref, n):
        self.copy(ref, n).wait_send()


def when(cond, fn):
    @pl.when(cond)
    def _():
        fn()


def gather_steps(out, tail, result, last, own_sem, out_sem, blk, sems):
    i, c, z, y, x = place()
    xp, yp, sib, up, down = partners(i, c, z, y, x)
    (sp0z, rp0z, sp0f, rp0f, sp0g, rp0g, ssib0, rsib0, sx, rx, sy, ry, sup, sdown, rz, ssib, rsib,
     st, rt) = sems
    lane0z = Lane(up, sp0z, rp0z)
    half = c * HALF
    other = (1 - c) * HALF

    def rows(base, start, size):
        return pl.ds(pl.multiple_of(base + start, 16), size)

    def p0(k, kind, base, mine):
        r = rows(base, k * CHUNK, CHUNK)
        if kind == "z":
            return out.at[0, y, x, r]
        if k % 2 == 0:
            if kind == "f":
                return out.at[0, y, x if mine else 1 - x, r]
            return out.at[0, y if mine else 1 - y, ALL, r]
        if kind == "f":
            return out.at[0, y if mine else 1 - y, x, r]
        return out.at[0, ALL, x if mine else 1 - x, r]

    def first(k):
        return Lane(xp if k % 2 == 0 else yp, sp0f, rp0f)

    def second(k):
        return Lane(yp if k % 2 == 0 else xp, sp0g, rp0g)

    lane0s = Lane(sib, ssib0, rsib0)
    lx, ly, ls = Lane(xp, sx, rx), Lane(yp, sy, ry), Lane(sib, ssib, rsib)
    lup, ldown = Lane(up, sup, rz), Lane(down, sdown, rz)

    def b1(yy, base=half):
        return out.at[z, yy, x, rows(base, 0, B_ROWS)]

    def b2(zs, xx, base=half):
        return out.at[zs, ALL, xx, rows(base, 0, B_ROWS)]

    def c1(zs, base=half):
        return out.at[zs, y, x, rows(base, B_ROWS, C_ROWS)]

    def c2(zs, xx, base=half):
        return out.at[zs, y, xx, rows(base, B_ROWS, C_ROWS)]

    def c3(zs, yy, base=half):
        return out.at[zs, yy, ALL, rows(base, B_ROWS, C_ROWS)]

    B, C = 0, 4
    SB1, SB2, SB3, SC1, SC2, SC3 = 0, 1, 5, 9, 13, 17

    def z_up(ref, n):
        when(z < 3, lambda: lup.go(ref, n))

    def z_down(ref, n):
        when(z > 0, lambda: ldown.go(ref, n))

    def z_on(ref, zs, base):
        when(jnp.logical_and(zs < z, z < 3), lambda: lup.go(ref, base + zs))
        when(jnp.logical_and(zs > z, z > 0), lambda: ldown.go(ref, base + zs))

    def own(fn):
        when(z > 0, fn)

    def both(s, fn):
        when(z - s >= 1, lambda: fn(z - s))
        when(z + s <= 3, lambda: fn(z + s))

    line = jnp.logical_and(y == 1, x == 1)
    source = jnp.logical_and(line, z == 3)
    tz, ty, tx = Lane(down, st, rt), Lane(yp, st, rt), Lane(xp, st, rt)

    def tail_z(at_source):
        def send():
            if not at_source:
                tz.copy(tail, 0).wait_recv()
            when(z > 0, lambda: tail_copy(down, 0).start())
            tail_copy(yp, 1).start()

        when(jnp.logical_and(line, source if at_source else jnp.logical_not(source)), send)

    def tail_copy(peer, n):
        return pltpu.make_async_remote_copy(
            src_ref=tail, dst_ref=tail, send_sem=st.at[n], recv_sem=rt.at[0],
            device_id=peer, device_id_type=MESH,
        )

    def tail_x():
        def send():
            when(y == 0, lambda: tail_copy(yp, 1).wait_recv())
            tail_copy(xp, 2).start()

        when(x == 1, send)

    def tail_end():
        when(x == 0, lambda: tail_copy(xp, 2).wait_recv())
        when(x == 1, lambda: tail_copy(xp, 2).wait_send())

        def sent():
            tail_copy(yp, 1).wait_send()
            when(z > 0, lambda: tail_copy(down, 0).wait_send())

        when(line, sent)

    def begin():
        local = pltpu.make_async_copy(blk, out.at[z, y, x], own_sem)
        local.start()
        when(source, lambda: tail.__setitem__(Ellipsis, last[...]))
        local.wait()
        tail_z(True)

        def at_zero():
            for k in range(4):
                lane0z.go(p0(k, "z", half, True), k)
            for k in range(4):
                first(k).go(p0(k, "f", half, True), k)

        when(z == 0, at_zero)

        def others():
            ly.go(b1(y), 4)
            lx.go(c2(z, x), C + z)
            ldown.go(c1(z), C + z)

        own(others)

        def pass_on(k):
            def there():
                lane0z.got(p0(k, "z", half, True), k)
                when(z < 3, lambda: lane0z.go(p0(k, "z", half, True), k))
                lane0s.go(p0(k, "z", half, True), k)
                first(k).go(p0(k, "f", half, True), k)

            own(there)

        def turn(k):
            first(k).got(p0(k, "f", half, False), k)
            second(k).go(p0(k, "g", half, True), k)
            lane0s.go(p0(k, "f", half, False), 4 + k)

        pass_on(0)
        pass_on(1)
        turn(0)
        pass_on(2)
        turn(1)
        pass_on(3)
        turn(2)

        def own_b():
            ly.got(b1(1 - y), 4)
            ls.go(b1(1 - y), SB1)
            z_up(c1(z), C + z)
            z_down(b2(z, x), B + z)
            z_up(b2(z, x), B + z)
            lx.go(b2(z, x), B + z)

        turn(3)
        own(own_b)
        for k in range(4):
            second(k).got(p0(k, "g", half, False), k)
            lane0s.go(p0(k, "g", half, False), 8 + k)
        for k in range(4):
            own(lambda k=k: lane0s.got(p0(k, "z", other, True), k))
            lane0s.got(p0(k, "f", other, False), 4 + k)
            lane0s.got(p0(k, "g", other, False), 8 + k)

    def early_c(zs):
        lup.got(c1(zs), C + zs)
        z_on(c1(zs), zs, C)
        lx.go(c2(zs, x), C + zs)
        ls.go(c1(zs), SC1 + zs)

    def early_b(zs):
        lup.got(b2(zs, x), B + zs)
        z_on(b2(zs, x), zs, B)
        lx.go(b2(zs, x), B + zs)
        ls.go(b2(zs, x), SB2 + zs)

    def late(zs):
        lx.got(c2(zs, 1 - x), C + zs)
        ly.go(c3(zs, y), zs)
        ls.go(c2(zs, 1 - x), SC2 + zs)

    def fin(zs):
        lx.got(b2(zs, 1 - x), B + zs)
        ls.go(b2(zs, 1 - x), SB3 + zs)
        ly.got(c3(zs, 1 - y), zs)
        ls.go(c3(zs, 1 - y), SC3 + zs)

    steps = [
        lambda: (own(lambda: late(z)), both(1, early_c)),
        lambda: (both(1, early_b), tail_z(False)),
        lambda: (both(1, late), both(2, early_c)),
        lambda: (both(2, early_b), tail_x()),
        lambda: both(2, late),
        lambda: (own(lambda: fin(z)), both(3, early_c)),
        lambda: both(3, early_b),
        lambda: (both(3, late), both(1, fin)),
        lambda: both(2, fin),
        lambda: both(3, fin),
    ]

    def leave(zs):
        return pltpu.make_async_copy(out.at[zs], result.at[zs], out_sem.at[zs])

    def sib_got(zs):
        def own_items():
            ls.got(b1(1 - y, other), SB1)

        def their_items():
            ls.got(c1(zs, other), SC1 + zs)
            ls.got(b2(zs, x, other), SB2 + zs)

        when(zs == z, own_items)
        when(zs != z, their_items)
        ls.got(c2(zs, 1 - x, other), SC2 + zs)
        ls.got(b2(zs, 1 - x, other), SB3 + zs)
        ls.got(c3(zs, 1 - y, other), SC3 + zs)

    def end():
        leave(0).start()
        for zs in range(1, 4):
            sib_got(zs)
            leave(zs).start()
        tail_end()
        for k in range(4):
            when(z < 3, lambda: lane0z.gone(p0(k, "z", half, True), k))
            first(k).gone(p0(k, "f", half, True), k)
            second(k).gone(p0(k, "g", half, True), k)
            own(lambda: lane0s.gone(p0(k, "z", half, True), k))
            lane0s.gone(p0(k, "f", half, False), 4 + k)
            lane0s.gone(p0(k, "g", half, False), 8 + k)

        def own_sent():
            ly.gone(b1(y), 4)
            ls.gone(b1(1 - y), SB1)

        own(own_sent)
        for zs in range(1, 4):
            lx.gone(c2(zs, x), C + zs)
            lx.gone(b2(zs, x), B + zs)
            ly.gone(c3(zs, y), zs)
            for ref, base in ((c1(zs), C), (b2(zs, x), B)):
                when(jnp.logical_and(zs <= z, z < 3), lambda: lup.gone(ref, base + zs))
                when(jnp.logical_and(zs >= z, z > 0), lambda: ldown.gone(ref, base + zs))

            def theirs():
                ls.gone(c1(zs), SC1 + zs)
                ls.gone(b2(zs, x), SB2 + zs)

            when(zs != z, theirs)
            ls.gone(c2(zs, 1 - x), SC2 + zs)
            ls.gone(b2(zs, 1 - x), SB3 + zs)
            ls.gone(c3(zs, 1 - y), SC3 + zs)
        for zs in range(4):
            leave(zs).wait()

    return begin, steps, end


def gather_attend_kernel(blk, last, tokens, seg_col, seg_row, result, tail, tokT, qT, kT, vT, mixT, mixb,
                         lse, held, dist, kn, own_sem, out_sem, *sems):
    i, c, z, y, x = place()
    with jax.named_scope("enter"):
        enter(i, c, z, y, x)
    begin, steps, end = gather_steps(held, tail, result, last, own_sem, out_sem, blk, sems)
    with jax.named_scope("distance"):
        tokT[...] = tokens[...].astype(f32).T.astype(bf16)
        fill_distance(dist, seg_col, seg_row)
    with jax.named_scope("begin"):
        begin()
    with jax.named_scope("project"):
        project_all(held, tokT, qT, kT, vT)

    @pl.loop(0, HEADS)
    def _(h):
        if True:
            for n, step in enumerate(steps):
                when(h == n + 1, step)
        with jax.named_scope("head"):
            attend_head(h, dist, kn, qT, kT, vT, mixT, mixb, lse)

    with jax.named_scope("end"):
        end()


def gather_attend(blk, last, tokens, seg):
    T = jax.ShapeDtypeStruct((D, LEN), bf16)
    Q = pltpu.SemaphoreType.DMA
    any_space = pl.BlockSpec(memory_space=pl.ANY)
    counts = [4] * 6 + [12, 12, 8, 8, 5, 5, 8, 8, 8, 21, 21, 3, 1]
    outs = pl.pallas_call(
        gather_attend_kernel,
        in_specs=[any_space, VM, VM, VM, VM],
        out_specs=[any_space] + [VM] * 8,
        out_shape=[
            jax.ShapeDtypeStruct((4, 2, 2, D, D), bf16), jax.ShapeDtypeStruct((16, D), bf16), T, T, T, T,
            jax.ShapeDtypeStruct((D, LEN), f32), T, jax.ShapeDtypeStruct((HEADS, 1, LEN), f32),
        ],
        scratch_shapes=[
            pltpu.VMEM((4, 2, 2, D, D), bf16), pltpu.VMEM((LEN, LEN), f32), pltpu.VMEM((LEN, HEAD), bf16),
            Q, Q((4,)), *[Q((n,)) for n in counts],
        ],
        compiler_params=pltpu.CompilerParams(
            collective_id=1, has_side_effects=True, vmem_limit_bytes=58 << 20
        ),
        name="gather_attend",
    )(blk, last, tokens, seg.reshape(LEN, 1), seg.reshape(1, LEN))
    blocks, tail, tokT, qT, kT, vT, mixT, mixb, lse = outs
    return blocks, tail, (tokT, qT, kT, vT, mixT), mixb, lse


SQUARE = D * D
TAIL = 4 * D


def from_wide(blocks):
    return blocks.reshape(4, 4, D // 4, D).transpose(0, 2, 1, 3).reshape(D, FF)


def to_wide(value):
    return value.reshape(4, D // 4, 4, D).transpose(0, 2, 1, 3).reshape(2, 2, D, D)


def swap_wide(block, index, inverse):
    dims = (4, D // 4, D) if inverse else (D // 4, 4, D)
    swapped = block.reshape(dims).transpose(1, 0, 2).reshape(D, D)
    wide = jnp.logical_and(index >= 4, index < 12)
    return jnp.where(wide, swapped, block)


def gather_and_attend(master, tokens, segments):
    count = lax.axis_size("zero")
    index = lax.axis_index("zero")
    size = 16 * SQUARE // count
    weights = master.astype(bf16)
    last = weights[-TAIL:]
    before = lax.ppermute(last, "zero", [(k, k + 1) for k in range(count - 1)])
    joined = jnp.concatenate([before, weights])
    block = lax.dynamic_slice(joined, (TAIL - TAIL // count * index,), (size,))
    if count == 16:
        padded = jnp.pad(last.reshape(4, D), ((0, 12), (0, 0)))
        block = swap_wide(block.reshape(D, D), index, False)
        blocks, tail, *attended = gather_attend(block, padded, tokens, segments)
        norms = tail[:4].astype(f32)
    else:
        natural = lax.all_gather(block.reshape(-1, D), "zero", axis=0, tiled=True)
        parts = natural.reshape(4, 4 * D, D)
        wide = [to_wide(parts[k].reshape(D, FF)) for k in (1, 2)]
        blocks = jnp.stack([parts[0].reshape(2, 2, D, D), *wide, parts[3].reshape(2, 2, D, D)])
        norms = lax.psum(jnp.where(index == count - 1, last.astype(f32), 0.0), "zero").reshape(4, D)
        attended = attend(tokens, blocks, segments)
    return blocks, norms, *attended


def scatter_grads(square, wide, down, norm_grads):
    count = lax.axis_size("zero")
    index = lax.axis_index("zero")
    if count == 16:
        block, tail = reduce_blocks(square, wide, down, norm_grads)
        block = swap_wide(block, index, True)
    else:
        natural = [from_wide(wide[k]).reshape(4 * D, D) for k in (0, 1)]
        natural = jnp.concatenate([square.reshape(4 * D, D), *natural, down.reshape(4 * D, D)])
        block = lax.psum_scatter(natural, "zero", scatter_dimension=0, tiled=True)
        block = lax.psum(block.astype(f32), "dp")
        tail = lax.psum(norm_grads, ("dp", "zero"))
    flat = block.reshape(-1)
    after = lax.ppermute(flat[:TAIL], "zero", [(k + 1, k) for k in range(count - 1)])
    joined = jnp.concatenate([flat, jnp.where(index == count - 1, tail.reshape(-1), after)])
    shard = flat.shape[0] + TAIL // count
    return lax.dynamic_slice(joined, (TAIL // count * index,), (shard,))


def local(tokens, segments, cotangent, master, moment_one, moment_two):
    blocks, norms, kept, mixed, log_sum = gather_and_attend(master, tokens, segments)
    output, first_grad, grad_mixed, branch_grad, norm_grads, down_grad, wide_grad = feed(
        tokens, cotangent, mixed, blocks, norms
    )
    square_grad, input_grad = attend_back(
        blocks, segments, *kept, log_sum, grad_mixed, first_grad, branch_grad
    )
    grad_shard = scatter_grads(
        square_grad, wide_grad.reshape(2, 2, 2, D, D), down_grad.reshape(2, 2, D, D), norm_grads
    )
    grad_shard = grad_shard / (lax.axis_size("zero") * lax.axis_size("dp"))
    first = beta_one * moment_one + (1.0 - beta_one) * grad_shard
    second = beta_two * moment_two + (1.0 - beta_two) * grad_shard * grad_shard
    update = first / correct_one / (jnp.sqrt(second / correct_two) + adam_eps)
    master_new = master - learn_rate * (update + weight_decay * master)
    return (
        output,
        input_grad,
        grad_shard,
        first,
        second,
        master_new,
        master_new.astype(jnp.bfloat16),
    )


def solution(mesh):
    return jax.shard_map(
        local,
        mesh=mesh,
        in_specs=(
            P(("dp", "zero"), None),
            P(("dp", "zero")),
            P(("dp", "zero"), None),
            P("zero"),
            P("zero"),
            P("zero"),
        ),
        out_specs=(
            P(("dp", "zero"), None),
            P(("dp", "zero"), None),
            P("zero"),
            P("zero"),
            P("zero"),
            P("zero"),
            P("zero"),
        ),
        check_vma=False,
    )
```

```python
import functools

import jax
import jax.numpy as jnp
from jax import lax
from jax.sharding import PartitionSpec as P
import jax.experimental.pallas as pl
import jax.experimental.pallas.tpu as pltpu

D = 768
HEADS = 12
HEAD = 64
FF = 3072
LEN = 1024


learn_rate = 0.02
beta_one = 0.9
beta_two = 0.999
adam_eps = 1e-08
weight_decay = 0.01
correct_one = 1.0 - 0.9**10
correct_two = 1.0 - 0.999**10
norm_eps = 1e-06
inv_root_two = 0.7071067811865476
inv_root_tau = 0.3989422804014327


bf16=jnp.bfloat16; f32=jnp.float32
FAR=1e33
VM=pl.BlockSpec(memory_space=pltpu.VMEM)

def dot(a,b): return lax.dot_general(a,b,(((1,),(0,)),((),())),preferred_element_type=f32)
def dot_tn(a,b): return lax.dot_general(a,b,(((0,),(0,)),((),())),preferred_element_type=f32)
def dot_nt(a,b): return lax.dot_general(a,b,(((1,),(1,)),((),())),preferred_element_type=f32)

def slope(h):
    return jnp.exp2(-8.0/HEADS*(jnp.full((1,1),h,jnp.int32).astype(f32)+1.0))

def fill_distance(dist,seg_col,seg_row):
    @pl.loop(0,LEN//128)
    def _(k):
        r=pl.ds(pl.multiple_of(k*128,128),128)
        kk=(lax.broadcasted_iota(jnp.int32,(128,LEN),0)+k*128)
        qq=lax.broadcasted_iota(jnp.int32,(128,LEN),1)
        d=jnp.abs(kk-qq).astype(f32)
        dist[r]=jnp.where(seg_col[r]==seg_row[...],d,FAR)

QB=256
def project_all(w,tokT,qkv):
    @pl.loop(0,3)
    def _(n):
        @pl.loop(0,3)
        def _(t):
            c=pl.ds(pl.multiple_of(t*256,256),256)
            qkv[n,c]=dot_tn(w[0,n//2,n%2,:,c],tokT[...]).astype(bf16)

def attend_head(h,dist,kn,qkv,mixb,lse):
    rows=pl.ds(pl.multiple_of(h*HEAD,HEAD),HEAD)
    kn[...]=qkv[1,rows].astype(f32).T.astype(bf16)
    m=slope(h)
    for b in range(LEN//QB):
        cols=pl.ds(b*QB,QB)
        q=qkv[0,rows,cols]*bf16(0.125)
        s=dot(kn[...],q)-m*dist[:,cols]
        top=jnp.max(s,0,keepdims=True)
        e=jnp.exp(s-top)
        total=jnp.sum(e,0,keepdims=True)
        o=dot(qkv[2,rows],e.astype(bf16))/total
        mixb[rows,cols]=o.astype(bf16)
        lse[h,:,cols]=top+jnp.log(total)

def attend_kernel(tokens,w,seg_col,seg_row,tokT,qkv,mixb,lse,dist,kn):
    tokT[...]=tokens[...].astype(f32).T.astype(bf16)
    fill_distance(dist,seg_col,seg_row)
    project_all(w,tokT,qkv)
    @pl.loop(0,HEADS)
    def _(h):
        attend_head(h,dist,kn,qkv,mixb,lse)

def attend_shapes():
    S=jax.ShapeDtypeStruct
    return [S((D,LEN),bf16),S((3,D,LEN),bf16),S((D,LEN),bf16),S((HEADS,1,LEN),f32)]

def attend(tokens,w,seg):
    return pl.pallas_call(attend_kernel,grid=(1,),
        in_specs=[VM,pl.BlockSpec((1,2,2,D,D),lambda i:(0,0,0,0,0)),VM,VM],out_specs=[VM]*4,
        out_shape=attend_shapes(),
        scratch_shapes=[pltpu.VMEM((LEN,LEN),f32),pltpu.VMEM((LEN,HEAD),bf16)],
        compiler_params=pltpu.CompilerParams(vmem_limit_bytes=58<<20),name="attend")(tokens,w,seg.reshape(LEN,1),seg.reshape(1,LEN))

def attend_back_kernel(w,seg_col,seg_row,tokT,qkv,mixb,lse,dO,first,gbranch,g0,grad_in,dist,kn,vn,p_all,ds_all,dqT,dkT,dvT):
    fill_distance(dist,seg_col,seg_row)
    @pl.loop(0,HEADS)
    def _(h):
        rows=pl.ds(pl.multiple_of(h*HEAD,HEAD),HEAD)
        kn[...]=qkv[1,rows].astype(f32).T.astype(bf16)
        vn[...]=qkv[2,rows].astype(f32).T.astype(bf16)
        m=slope(h)
        for b in range(LEN//QB):
            cols=pl.ds(b*QB,QB)
            q=qkv[0,rows,cols]*bf16(0.125)
            s=dot(kn[...],q)-m*dist[:,cols]
            p=jnp.exp(s-lse[h,:,cols])
            do=dO[rows,cols]
            delta=jnp.sum(do.astype(f32)*mixb[rows,cols].astype(f32),0,keepdims=True)
            dp=dot(vn[...],do)
            p_all[:,cols]=p.astype(bf16)
            ds=(p*(dp-delta)).astype(bf16)
            ds_all[:,cols]=ds
            dqT[rows,cols]=(dot(qkv[1,rows],ds)*0.125).astype(bf16)
        dvT[rows]=dot_nt(dO[rows],p_all[...]).astype(bf16)
        dkT[rows]=(dot_nt(qkv[0,rows],ds_all[...])*0.125).astype(bf16)
    g0[1,1]=dot(mixb[...],gbranch[...]).astype(bf16)
    for n,g in enumerate((dqT,dkT,dvT)):
        g0[n//2,n%2]=dot_nt(tokT[...],g[...]).astype(bf16)
    @pl.loop(0,4)
    def _(t):
        c=pl.ds(pl.multiple_of(t*256,256),256)
        acc=dot(w[0,0,0],dqT[:,c])+dot(w[0,0,1],dkT[:,c])+dot(w[0,1,0],dvT[:,c])
        grad_in[c]=first[c]+acc.T

def attend_back(w,seg,tokT,qkv,mixb,lse,dO,first,gbranch):
    B=lambda: pltpu.VMEM((D,LEN),bf16)
    return pl.pallas_call(attend_back_kernel,grid=(1,),
        in_specs=[pl.BlockSpec((1,2,2,D,D),lambda i:(0,0,0,0,0))]+[VM]*9,out_specs=[VM]*2,
        out_shape=[jax.ShapeDtypeStruct((2,2,D,D),bf16),jax.ShapeDtypeStruct((LEN,D),f32)],
        scratch_shapes=[pltpu.VMEM((LEN,LEN),f32),pltpu.VMEM((LEN,HEAD),bf16),pltpu.VMEM((LEN,HEAD),bf16),pltpu.VMEM((LEN,LEN),bf16),pltpu.VMEM((LEN,LEN),bf16),B(),B(),B()],
        compiler_params=pltpu.CompilerParams(vmem_limit_bytes=60<<20),name="attend_back")(w,seg.reshape(LEN,1),seg.reshape(1,LEN),tokT,qkv,mixb,lse,dO,first,gbranch)

TB=256
def feed_kernel(tokens,cot,mixb,wo,w1,w2,w3,norms,output,first,dO,gbranch,ng,gdown,gwide,inner,wide,gffn,fa,fb,acc,hid):
    step=pl.program_id(0)
    gain1=norms[0:1]; shift1=norms[1:2]; gain2=norms[2:3]; shift2=norms[3:4]
    def stats(v):
        c=v-jnp.mean(v,-1,keepdims=True)
        r=lax.rsqrt(jnp.mean(c*c,-1,keepdims=True)+norm_eps)
        return c*r,r
    def back(e,n,r):
        return r*(e-jnp.mean(e,-1,keepdims=True)-n*jnp.mean(e*n,-1,keepdims=True))
    W=lambda p,j: (w1,w2)[p-1][0,:,j].reshape(D,D)
    WD=lambda j: w3[0,j].reshape(D,D)
    WO=lambda: wo[0,0].reshape(D,D)
    @pl.when(step==0)
    def _(): ng[...]=jnp.zeros_like(ng)
    @pl.when(step<LEN//TB)
    def _():
        rows=pl.ds(pl.multiple_of(step*TB,TB),TB)
        branch=dot_tn(mixb[...],WO())
        n1,r1=stats(tokens[...].astype(f32)+branch)
        l1=n1*gain1+shift1
        inner[rows]=l1.astype(bf16)
        acc[...]=l1
        @pl.loop(0,4,unroll=2)
        def _(j):
            inn=inner[rows]
            ga=dot(inn,W(1,j)); up=dot(inn,W(2,j))
            cum=0.5*(1.0+lax.erf(ga*inv_root_two))
            gel=ga*cum
            fb[j]=gel
            fa[j]=up*(cum+ga*(jnp.exp(-0.5*ga*ga)*inv_root_tau))
            h=(gel*up).astype(bf16)
            hid[j,rows]=h
            acc[...]+=dot(h,WD(j))
        n2,r2=stats(acc[...])
        output[...]=(n2*gain2+shift2).astype(bf16)
        c=cot[...].astype(f32)
        ng[2:3]+=jnp.sum(c*n2,0,keepdims=True)
        ng[3:4]+=jnp.sum(c,0,keepdims=True)
        mid=back(c*gain2,n2,r2)
        gffn[rows]=mid.astype(bf16)
        acc[...]=mid
        @pl.loop(0,4,unroll=2)
        def _(j):
            gh=dot_nt(gffn[rows],WD(j))
            a=(gh*fa[j]).astype(bf16); b=(gh*fb[j]).astype(bf16)
            wide[j,rows]=a; wide[4+j,rows]=b
            acc[...]+=dot_nt(a,W(1,j))+dot_nt(b,W(2,j))
        gl=acc[...]
        ng[0:1]+=jnp.sum(gl*n1,0,keepdims=True)
        ng[1:2]+=jnp.sum(gl,0,keepdims=True)
        gfirst=back(gl*gain1,n1,r1)
        first[...]=gfirst
        gb=gfirst.astype(bf16)
        gbranch[...]=gb
        dO[...]=dot_nt(WO(),gb).astype(bf16)
    def put(g,v):
        g[...]=v.astype(bf16).reshape(g.shape)
    base=LEN//TB
    @pl.when(jnp.logical_and(step>=base,step<base+4))
    def _(): put(gdown,dot_tn(hid[step-base],gffn[...]))
    @pl.when(jnp.logical_and(step>=base+4,step<base+12))
    def _(): put(gwide,dot_tn(inner[...],wide[step-base-4]))

def feed(tokens,cot,mixb,w,norms):
    n=LEN//TB
    last=n-1
    row=lambda i:(jnp.minimum(i,last),0)
    col=lambda i:(0,jnp.minimum(i,last))
    one=pl.Buffered(1)
    S=jax.ShapeDtypeStruct
    V=lambda s,d=bf16: pltpu.VMEM(s,d)
    clip=lambda v,a,b: jnp.minimum(jnp.maximum(v,a),b)
    return pl.pallas_call(feed_kernel,grid=(n+12,),
        in_specs=[pl.BlockSpec((TB,D),row),pl.BlockSpec((TB,D),row),pl.BlockSpec((D,TB),col),
            pl.BlockSpec((1,1,4,D//4,D),lambda i:(0,3,0,0,0),pipeline_mode=one),*[pl.BlockSpec((1,4,4,D//4,D),lambda i,p=p:(p,0,0,0,0),pipeline_mode=one) for p in (1,2,3)],pl.BlockSpec((4,D),lambda i:(0,0))],
        out_specs=[pl.BlockSpec((TB,D),row),pl.BlockSpec((TB,D),row),pl.BlockSpec((D,TB),col),pl.BlockSpec((TB,D),row),
            pl.BlockSpec((4,D),lambda i:(0,0)),
            pl.BlockSpec((1,D,D),lambda i:(clip(i-n,0,3),0,0)),
            pl.BlockSpec((1,4,1,D//4,D),lambda i:(clip((i-n-4)//4,0,1),0,clip(i-n-4,0,7)%4,0,0))],
        out_shape=[S((LEN,D),bf16),S((LEN,D),f32),S((D,LEN),bf16),S((LEN,D),bf16),S((4,D),f32),S((4,D,D),bf16),S((2,4,4,D//4,D),bf16)],
        scratch_shapes=[V((LEN,D)),V((8,LEN,D)),V((LEN,D)),V((4,TB,D),f32),V((4,TB,D),f32),V((TB,D),f32),V((4,LEN,D))],
        compiler_params=pltpu.CompilerParams(vmem_limit_bytes=62<<20),name="feed")(tokens,cot,mixb,*[w.reshape(4,4,4,D//4,D)]*4,norms)

MESH = pl.DeviceIdType.MESH
ALL = slice(None)
HALF = D // 2
B_ROWS, C_ROWS = 144, 240
CHUNK = 96


def place():
    i = lax.axis_index("zero")
    c = lax.axis_index("dp")
    return i, c, i // 4, (i // 2) % 2, i % 2


def partners(i, c, z, y, x):
    return (c, i + 1 - 2 * x), (c, i + 2 - 4 * y), (1 - c, i), (c, i + 4), (c, i - 4)


def enter(i, c, z, y, x):
    barrier = pltpu.get_barrier_semaphore()
    xp, yp, sib, up, down = partners(i, c, z, y, x)
    for peer in (xp, yp, sib):
        pl.semaphore_signal(barrier, inc=1, device_id=peer, device_id_type=MESH)

    @pl.when(z > 0)
    def _():
        pl.semaphore_signal(barrier, inc=1, device_id=down, device_id_type=MESH)

    @pl.when(z < 3)
    def _():
        pl.semaphore_signal(barrier, inc=1, device_id=up, device_id_type=MESH)

    pl.semaphore_wait(barrier, 3 + jnp.minimum(z, 1) + jnp.minimum(3 - z, 1))


class Lane:
    def __init__(self, peer, sends, recvs):
        self.peer, self.sends, self.recvs = peer, sends, recvs

    def copy(self, ref, n):
        return pltpu.make_async_remote_copy(
            src_ref=ref, dst_ref=ref, send_sem=self.sends.at[n], recv_sem=self.recvs.at[n],
            device_id=self.peer, device_id_type=MESH,
        )

    def go(self, ref, n):
        self.copy(ref, n).start()

    def got(self, ref, n):
        self.copy(ref, n).wait_recv()

    def gone(self, ref, n):
        self.copy(ref, n).wait_send()


def when(cond, fn):
    @pl.when(cond)
    def _():
        fn()


def gather_steps(out, tail, result, last, own_sem, out_sem, blk, sems):
    i, c, z, y, x = place()
    xp, yp, sib, up, down = partners(i, c, z, y, x)
    (sp0z, rp0z, sp0f, rp0f, sp0g, rp0g, ssib0, rsib0, sx, rx, sy, ry, sup, sdown, rz, ssib, rsib,
     st, rt) = sems
    lane0z = Lane(up, sp0z, rp0z)
    half = c * HALF
    other = (1 - c) * HALF

    def rows(base, start, size):
        return pl.ds(pl.multiple_of(base + start, 16), size)

    def p0(k, kind, base, mine):
        r = rows(base, k * CHUNK, CHUNK)
        if kind == "z":
            return out.at[0, y, x, r]
        if k % 2 == 0:
            if kind == "f":
                return out.at[0, y, x if mine else 1 - x, r]
            return out.at[0, y if mine else 1 - y, ALL, r]
        if kind == "f":
            return out.at[0, y if mine else 1 - y, x, r]
        return out.at[0, ALL, x if mine else 1 - x, r]

    def first(k):
        return Lane(xp if k % 2 == 0 else yp, sp0f, rp0f)

    def second(k):
        return Lane(yp if k % 2 == 0 else xp, sp0g, rp0g)

    lane0s = Lane(sib, ssib0, rsib0)
    lx, ly, ls = Lane(xp, sx, rx), Lane(yp, sy, ry), Lane(sib, ssib, rsib)
    lup, ldown = Lane(up, sup, rz), Lane(down, sdown, rz)

    def b1(yy, base=half):
        return out.at[z, yy, x, rows(base, 0, B_ROWS)]

    def b2(zs, xx, base=half):
        return out.at[zs, ALL, xx, rows(base, 0, B_ROWS)]

    def c1(zs, base=half):
        return out.at[zs, y, x, rows(base, B_ROWS, C_ROWS)]

    def c2(zs, xx, base=half):
        return out.at[zs, y, xx, rows(base, B_ROWS, C_ROWS)]

    def c3(zs, yy, base=half):
        return out.at[zs, yy, ALL, rows(base, B_ROWS, C_ROWS)]

    B, C = 0, 4
    SB1, SB2, SB3, SC1, SC2, SC3 = 0, 1, 5, 9, 13, 17

    def z_up(ref, n):
        when(z < 3, lambda: lup.go(ref, n))

    def z_down(ref, n):
        when(z > 0, lambda: ldown.go(ref, n))

    def z_on(ref, zs, base):
        when(jnp.logical_and(zs < z, z < 3), lambda: lup.go(ref, base + zs))
        when(jnp.logical_and(zs > z, z > 0), lambda: ldown.go(ref, base + zs))

    def own(fn):
        when(z > 0, fn)

    def both(s, fn):
        when(z - s >= 1, lambda: fn(z - s))
        when(z + s <= 3, lambda: fn(z + s))

    line = jnp.logical_and(y == 1, x == 1)
    source = jnp.logical_and(line, z == 3)
    tz, ty, tx = Lane(down, st, rt), Lane(yp, st, rt), Lane(xp, st, rt)

    def tail_z(at_source):
        def send():
            if not at_source:
                tz.copy(tail, 0).wait_recv()
            when(z > 0, lambda: tail_copy(down, 0).start())
            tail_copy(yp, 1).start()

        when(jnp.logical_and(line, source if at_source else jnp.logical_not(source)), send)

    def tail_copy(peer, n):
        return pltpu.make_async_remote_copy(
            src_ref=tail, dst_ref=tail, send_sem=st.at[n], recv_sem=rt.at[0],
            device_id=peer, device_id_type=MESH,
        )

    def tail_x():
        def send():
            when(y == 0, lambda: tail_copy(yp, 1).wait_recv())
            tail_copy(xp, 2).start()

        when(x == 1, send)

    def tail_end():
        when(x == 0, lambda: tail_copy(xp, 2).wait_recv())
        when(x == 1, lambda: tail_copy(xp, 2).wait_send())

        def sent():
            tail_copy(yp, 1).wait_send()
            when(z > 0, lambda: tail_copy(down, 0).wait_send())

        when(line, sent)

    def begin():
        local = pltpu.make_async_copy(blk, out.at[z, y, x], own_sem)
        local.start()
        when(source, lambda: tail.__setitem__(Ellipsis, last[...]))
        local.wait()
        tail_z(True)

        def at_zero():
            for k in range(4):
                lane0z.go(p0(k, "z", half, True), k)
            for k in range(4):
                first(k).go(p0(k, "f", half, True), k)

        when(z == 0, at_zero)

        def others():
            ly.go(b1(y), 4)
            lx.go(c2(z, x), C + z)
            ldown.go(c1(z), C + z)

        own(others)

        def pass_on(k):
            def there():
                lane0z.got(p0(k, "z", half, True), k)
                when(z < 3, lambda: lane0z.go(p0(k, "z", half, True), k))
                lane0s.go(p0(k, "z", half, True), k)
                first(k).go(p0(k, "f", half, True), k)

            own(there)

        def turn(k):
            first(k).got(p0(k, "f", half, False), k)
            second(k).go(p0(k, "g", half, True), k)
            lane0s.go(p0(k, "f", half, False), 4 + k)

        pass_on(0)
        pass_on(1)
        turn(0)
        pass_on(2)
        turn(1)
        pass_on(3)
        turn(2)

        def own_b():
            ly.got(b1(1 - y), 4)
            ls.go(b1(1 - y), SB1)
            z_up(c1(z), C + z)
            z_down(b2(z, x), B + z)
            z_up(b2(z, x), B + z)
            lx.go(b2(z, x), B + z)

        turn(3)
        own(own_b)
        for k in range(4):
            second(k).got(p0(k, "g", half, False), k)
            lane0s.go(p0(k, "g", half, False), 8 + k)
        for k in range(4):
            own(lambda k=k: lane0s.got(p0(k, "z", other, True), k))
            lane0s.got(p0(k, "f", other, False), 4 + k)
            lane0s.got(p0(k, "g", other, False), 8 + k)

    def early_c(zs):
        lup.got(c1(zs), C + zs)
        z_on(c1(zs), zs, C)
        lx.go(c2(zs, x), C + zs)
        ls.go(c1(zs), SC1 + zs)

    def early_b(zs):
        lup.got(b2(zs, x), B + zs)
        z_on(b2(zs, x), zs, B)
        lx.go(b2(zs, x), B + zs)
        ls.go(b2(zs, x), SB2 + zs)

    def late(zs):
        lx.got(c2(zs, 1 - x), C + zs)
        ly.go(c3(zs, y), zs)
        ls.go(c2(zs, 1 - x), SC2 + zs)

    def fin(zs):
        lx.got(b2(zs, 1 - x), B + zs)
        ls.go(b2(zs, 1 - x), SB3 + zs)
        ly.got(c3(zs, 1 - y), zs)
        ls.go(c3(zs, 1 - y), SC3 + zs)

    steps = [
        lambda: (own(lambda: late(z)), both(1, early_c)),
        lambda: (both(1, early_b), tail_z(False)),
        lambda: (both(1, late), both(2, early_c)),
        lambda: (both(2, early_b), tail_x()),
        lambda: both(2, late),
        lambda: (own(lambda: fin(z)), both(3, early_c)),
        lambda: both(3, early_b),
        lambda: (both(3, late), both(1, fin)),
        lambda: both(2, fin),
        lambda: both(3, fin),
    ]

    def leave(zs):
        return pltpu.make_async_copy(out.at[zs], result.at[zs], out_sem.at[zs])

    def sib_got(zs):
        def own_items():
            ls.got(b1(1 - y, other), SB1)

        def their_items():
            ls.got(c1(zs, other), SC1 + zs)
            ls.got(b2(zs, x, other), SB2 + zs)

        when(zs == z, own_items)
        when(zs != z, their_items)
        ls.got(c2(zs, 1 - x, other), SC2 + zs)
        ls.got(b2(zs, 1 - x, other), SB3 + zs)
        ls.got(c3(zs, 1 - y, other), SC3 + zs)

    def end():
        leave(0).start()
        for zs in range(1, 4):
            sib_got(zs)
            leave(zs).start()
        tail_end()
        for k in range(4):
            when(z < 3, lambda: lane0z.gone(p0(k, "z", half, True), k))
            first(k).gone(p0(k, "f", half, True), k)
            second(k).gone(p0(k, "g", half, True), k)
            own(lambda: lane0s.gone(p0(k, "z", half, True), k))
            lane0s.gone(p0(k, "f", half, False), 4 + k)
            lane0s.gone(p0(k, "g", half, False), 8 + k)

        def own_sent():
            ly.gone(b1(y), 4)
            ls.gone(b1(1 - y), SB1)

        own(own_sent)
        for zs in range(1, 4):
            lx.gone(c2(zs, x), C + zs)
            lx.gone(b2(zs, x), B + zs)
            ly.gone(c3(zs, y), zs)
            for ref, base in ((c1(zs), C), (b2(zs, x), B)):
                when(jnp.logical_and(zs <= z, z < 3), lambda: lup.gone(ref, base + zs))
                when(jnp.logical_and(zs >= z, z > 0), lambda: ldown.gone(ref, base + zs))

            def theirs():
                ls.gone(c1(zs), SC1 + zs)
                ls.gone(b2(zs, x), SB2 + zs)

            when(zs != z, theirs)
            ls.gone(c2(zs, 1 - x), SC2 + zs)
            ls.gone(b2(zs, 1 - x), SB3 + zs)
            ls.gone(c3(zs, 1 - y), SC3 + zs)
        for zs in range(4):
            leave(zs).wait()

    return begin, steps, end


def gather_attend_kernel(blk, last, tokens, seg_col, seg_row, result, tail, tokT, qkv, mixb, lse,
                          held, dist, kn, own_sem, out_sem, *sems):
    i, c, z, y, x = place()
    if True:
        enter(i, c, z, y, x)
    begin, steps, end = gather_steps(held, tail, result, last, own_sem, out_sem, blk, sems)
    if True:
        tokT[...] = tokens[...].astype(f32).T.astype(bf16)
        fill_distance(dist, seg_col, seg_row)
    if True:
        begin()
    if True:
        project_all(held, tokT, qkv)

    @pl.loop(0, HEADS)
    def _(h):
        if True:
            for n, step in enumerate(steps):
                when(h == n + 1, step)
        if True:
            attend_head(h, dist, kn, qkv, mixb, lse)

    if True:
        end()


def gather_attend(blk, last, tokens, seg):
    Q = pltpu.SemaphoreType.DMA
    any_space = pl.BlockSpec(memory_space=pl.ANY)
    counts = [4] * 6 + [12, 12, 8, 8, 5, 5, 8, 8, 8, 21, 21, 3, 1]
    return pl.pallas_call(
        gather_attend_kernel,
        in_specs=[any_space, VM, VM, VM, VM],
        out_specs=[any_space] + [VM] * 5,
        out_shape=[
            jax.ShapeDtypeStruct((4, 2, 2, D, D), bf16), jax.ShapeDtypeStruct((16, D), bf16),
            *attend_shapes(),
        ],
        scratch_shapes=[
            pltpu.VMEM((4, 2, 2, D, D), bf16), pltpu.VMEM((LEN, LEN), f32), pltpu.VMEM((LEN, HEAD), bf16),
            Q, Q((4,)), *[Q((n,)) for n in counts],
        ],
        compiler_params=pltpu.CompilerParams(
            collective_id=1, has_side_effects=True, vmem_limit_bytes=58 << 20
        ),
        name="gather_attend",
    )(blk, last, tokens, seg.reshape(LEN, 1), seg.reshape(1, LEN))


PLANE_ORDER = (1, 3, 2)
BACK_PLAN = (
    (
        14709104, 65761, 422402, 475168, 2192136, 200769, 4334084, 7606533, 7685670, 2639655,
        8589896, 5255296, 8552726, 4399990, 9454628, 9671313, 3241751, 4531537, 3307544, 3543890,
        10582358, 10713620, 10517269, 3692343, 8905304, 10638131, 11634052, 8803380, 3526835, 11587925,
        9745106, 9934485, 10855635, 10987200, 11843009, 12761014, 12895683, 15779782, 15790320,
    ),
    (
        14709104, 65761, 422402, 526112, 1057139, 328707, 4224034, 7672102, 8589863, 2639425,
        3151488, 4358785, 4748871, 9446435, 9671313, 5273367, 3228453, 4487192, 7934770, 4535969,
        5339668, 5667747, 6378080, 14825527, 6457109, 8750131, 5736096, 10670132, 13719605, 9744816,
        9934485, 11776722, 5559123, 12625316, 10928469, 11842983, 12039874, 12895683, 15779782,
    ),
    (
        14709104, 65761, 422402, 526112, 1057139, 262976, 7603490, 1123905, 2572917, 8595474,
        3151488, 7766657, 2311760, 9539620, 1545106, 4749127, 3217445, 1258104, 5325689, 1324705,
        4477562, 4553635, 3684256, 8852962, 3383940, 6510213, 13644934, 6599088, 3519441, 5747410,
        9802853, 12621718, 5816787, 5481892, 12801218, 11904934, 11949492, 12895671, 15779782,
    ),
    (
        14709104, 65761, 422402, 475168, 2192136, 200769, 4334084, 7606533, 2585894, 8595474,
        3151488, 8552784, 4399990, 9454628, 9671313, 4618007, 3228965, 7870545, 5386823, 4732435,
        1352057, 8102778, 3684256, 8852962, 3383940, 6718803, 5518470, 11587687, 13723840, 5685681,
        9721141, 11703957, 12825538, 13882007, 5744036, 10987096, 11847093, 13022916, 15779767,
    ),
)


B_PART, C_PART, PARTS = 48, 80, 3
Q_PART = 96
COLS = D // 2


def pick(z, values):
    out = jnp.int32(values[3])
    for k in (2, 1, 0):
        out = jnp.where(z == k, jnp.int32(values[k]), out)
    return out


def run_plan(z, words, ops):
    count = len(words[0])
    held = [pick(z, [words[k][n] for k in range(4)]) for n in range(count)]

    @pl.loop(0, count)
    def _(n):
        word = held[0]
        for k in range(1, count):
            word = jnp.where(n == k, held[k], word)

        @pl.loop(0, 3)
        def _(m):
            code = jnp.where(m == 0, word, jnp.where(m == 1, word // 256, word // 65536)) % 256
            kind, e = code // 16, code % 16
            for k, op in enumerate(ops):
                when(kind == k, lambda op=op: op(e))


def reduce_back_kernel(wide, down, w, qkv_in, dO, mixb, lse, tokT, gbranch, first, norm_in, seg_col, seg_row,
                       grad_in, flat_out, own, sl, lc3, lc2, lcz, lczx, lb3, lbz, lbzx, lb1, lf, lg, lz, stage,
                       dist, p_all, ds_all, wv, kn, vn, qkv, fchunk, flat, nacc, nx, ny, nz, nc,
                       own_sem, qkv_sem, w_sem, f_sem, g_sem, o_sem, sib_s, sib_r, st_s, st_r,
                       c3s, c3r, b3s, b3r, c2s, c2r, bus, bur, bds, bdr, cus, cur, cds, cdr, b1s, b1r,
                       fs, fr, gs, gr, zs_, zr_, ns, nr, share_s, share_r, aft_s, aft_r):
    i, c, z, y, x = place()
    xp, yp, sib, up, down_peer = partners(i, c, z, y, x)
    base = c * HALF
    mine = pl.ds(pl.multiple_of(base, 16), HALF)
    other = pl.ds(pl.multiple_of((1 - c) * HALF, 16), HALF)
    planes = [wide.at[0], wide.at[1], down]

    def remote(src, dst, peer, s, r):
        return pltpu.make_async_remote_copy(
            src_ref=src, dst_ref=dst, send_sem=s, recv_sem=r, device_id=peer, device_id_type=MESH
        )

    def local_in(t):
        return pltpu.make_async_copy(planes[t - 1].at[:, :, mine], own.at[t], own_sem.at[t])

    def sib_in(t):
        return remote(planes[t - 1].at[:, :, other], sl.at[t], sib, sib_s.at[t], sib_r.at[t])

    for t in PLANE_ORDER:
        local_in(t).start()
    qkv_copy = pltpu.make_async_copy(qkv_in, qkv, qkv_sem)
    qkv_copy.start()
    enter_more(i, c, z, y, x)
    for t in PLANE_ORDER:
        sib_in(t).start()
    nacc[...] = norm_in[...]
    NX = remote(nacc, nx, xp, ns.at[0], nr.at[0])
    NY = remote(nacc, ny, yp, ns.at[1], nr.at[1])
    NZ = remote(nacc, nz, up, ns.at[2], nr.at[2])
    NC = remote(nacc, nc, sib, ns.at[3], nr.at[3])
    line = jnp.logical_and(x == 1, y == 1)
    last_line = jnp.logical_and(line, z == 3)
    when(x == 0, lambda: NX.start())
    fill_distance(dist, seg_col, seg_row)
    qkv_copy.wait()

    def rb(s, k=0, size=B_PART):
        return pl.ds(pl.multiple_of(s * B_PART + k, 16), size)

    def rc(s, k=0, size=C_PART):
        return pl.ds(pl.multiple_of(3 * B_PART + s * C_PART + k, 16), size)

    def add_rows(dst, src, rows):
        @pl.loop(0, rows // 16)
        def _(n):
            k = pl.multiple_of(n * 16, 16)
            a = dst(k)
            a[...] = (a[...].astype(f32) + src(k)[...].astype(f32)).astype(bf16)

    r16 = lambda k: pl.ds(k, 16)
    split = lambda e: (e // 3 + 1, e % 3)

    def C3(t, s, e):
        return remote(own.at[t, 1 - y, :, rc(s)], lc3.at[e], yp, c3s.at[e], c3r.at[e])

    def B3(t, s, e):
        return remote(own.at[t, :, 1 - x, rb(s)], lb3.at[e], xp, b3s.at[e], b3r.at[e])

    def C2(t, s, e):
        return remote(own.at[t, y, 1 - x, rc(s)], lc2.at[e], xp, c2s.at[e], c2r.at[e])

    def BU(t, s, e):
        return remote(own.at[t, :, x, rb(s)], lbz.at[e], up, bus.at[e], bur.at[e])

    def BD(t, s, e, extra=False):
        return remote(own.at[t, :, x, rb(s)], lbzx.at[s] if extra else lbz.at[e], down_peer, bds.at[e], bdr.at[e])

    def CU(t, s, e):
        return remote(own.at[t, y, x, rc(s)], lcz.at[e], up, cus.at[e], cur.at[e])

    def CD(t, s, e, extra=False):
        return remote(own.at[t, y, x, rc(s)], lczx.at[s] if extra else lcz.at[e], down_peer, cds.at[e], cdr.at[e])

    def B1(s):
        return remote(own.at[z, 1 - y, x, rb(s)], lb1.at[s], yp, b1s.at[s], b1r.at[s])

    def op_sum(e):
        t, s = split(e)

        def arrive():
            for k in (1, 2, 3):
                def both(k=k):
                    local_in(k).wait()
                    sib_in(k).wait_recv()

                when(t == k, both)

        when(s == 0, arrive)
        add_rows(lambda k: own.at[t, :, :, rb(s, k, 16)], lambda k: sl.at[t, :, :, rb(s, k, 16)], B_PART)
        add_rows(lambda k: own.at[t, :, :, rc(s, k, 16)], lambda k: sl.at[t, :, :, rc(s, k, 16)], C_PART)
        C3(t, s, e).start()
        B3(t, s, e).start()

    def op_c3(e):
        t, s = split(e)
        C3(t, s, e).wait_recv()
        add_rows(lambda k: own.at[t, y, :, rc(s, k, 16)], lambda k: lc3.at[e, :, r16(k)], C_PART)
        C2(t, s, e).start()

    def op_b3(e):
        t, s = split(e)
        B3(t, s, e).wait_recv()
        add_rows(lambda k: own.at[t, :, x, rb(s, k, 16)], lambda k: lb3.at[e, :, r16(k)], B_PART)

    def op_c2(e):
        t, s = split(e)
        C2(t, s, e).wait_recv()
        add_rows(lambda k: own.at[t, y, x, rc(s, k, 16)], lambda k: lc2.at[e, r16(k)], C_PART)

    def op_bz(e):
        t, s = split(e)
        dst = lambda k: own.at[t, :, x, rb(s, k, 16)]

        def from_below():
            BU(t, s, e).wait_recv()
            add_rows(dst, lambda k: lbz.at[e, :, r16(k)], B_PART)

        when(jnp.logical_and(t >= z, z > 0), from_below)

        def from_above():
            BD(t, s, e).wait_recv()
            add_rows(dst, lambda k: lbz.at[e, :, r16(k)], B_PART)

        when(t < z, lambda: when(z < 3, from_above))

        def from_above_last():
            BD(t, s, e).wait_recv()
            add_rows(dst, lambda k: lbzx.at[s, :, r16(k)], B_PART)

        when(jnp.logical_and(t == z, z < 3), from_above_last)
        when(t > z, lambda: BU(t, s, e).start())
        when(t == z - 1, lambda: BD(t, s, e, True).start())
        when(t < z - 1, lambda: BD(t, s, e).start())
        when(t == z, lambda: B1(s).start())

    def res(rows):
        return dist.at[rows, pl.ds(0, D)]

    def op_cz(e):
        t, s = split(e)
        dst = lambda k: own.at[t, y, x, rc(s, k, 16)]

        def from_below():
            CU(t, s, e).wait_recv()
            add_rows(dst, lambda k: lcz.at[e, r16(k)], C_PART)

        when(jnp.logical_and(t >= z, z > 0), from_below)

        def from_above():
            CD(t, s, e).wait_recv()
            add_rows(dst, lambda k: lcz.at[e, r16(k)], C_PART)

        when(t < z, lambda: when(z < 3, from_above))

        def from_above_last():
            CD(t, s, e).wait_recv()
            add_rows(dst, lambda k: lczx.at[s, r16(k)], C_PART)

        when(jnp.logical_and(t == z, z < 3), from_above_last)
        when(t > z, lambda: CU(t, s, e).start())
        when(t == z - 1, lambda: CD(t, s, e, True).start())
        when(t < z - 1, lambda: CD(t, s, e).start())

    def op_b1(e):
        t, s = split(e)
        B1(s).wait_recv()
        add_rows(lambda k: own.at[z, y, x, rb(s, k, 16)], lambda k: lb1.at[s, r16(k)], B_PART)

    def op_head(h):
        rows = pl.ds(pl.multiple_of(h * HEAD, HEAD), HEAD)
        kn[...] = qkv[1, rows].astype(f32).T.astype(bf16)
        vn[...] = qkv[2, rows].astype(f32).T.astype(bf16)
        m = slope(h)
        for b in range(LEN // QB):
            cols = pl.ds(b * QB, QB)
            q = qkv[0, rows, cols] * bf16(0.125)
            s = dot(kn[...], q) - m * dist[:, cols]
            p = jnp.exp(s - lse[h, :, cols])
            do = dO[rows, cols]
            delta = jnp.sum(do.astype(f32) * mixb[rows, cols].astype(f32), 0, keepdims=True)
            dp = dot(vn[...], do)
            p_all[:, cols] = p.astype(bf16)
            ds_all[:, cols] = (p * (dp - delta)).astype(bf16)
        grad_q = (dot(qkv[1, rows], ds_all[...]) * 0.125).astype(bf16)
        grad_k = (dot_nt(qkv[0, rows], ds_all[...]) * 0.125).astype(bf16)
        grad_v = dot_nt(dO[rows], p_all[...]).astype(bf16)
        qkv[0, rows] = grad_q
        qkv[1, rows] = grad_k
        qkv[2, rows] = grad_v

    def columns(g):
        return pl.ds(pl.multiple_of(g * COLS, 128), COLS)

    def stage_copy(e):
        g, n = e // 4, e % 4
        return remote(
            stage.at[e], sl.at[0, n // 2, n % 2, :, columns(g)], sib, st_s.at[e], st_r.at[e]
        )

    def op_dw(e):
        g, n = e // 4, e % 4
        cols = columns(g)

        def put(half, value):
            if half == 0:
                own[0, n // 2, n % 2, :, cols] = value.astype(bf16)
            else:
                stage[e] = value.astype(bf16)

        def inputs():
            right = qkv[n, pl.ds(pl.multiple_of(g * COLS, 128), COLS)]
            for half, rows in ((0, mine), (1, other)):
                put(half, dot_nt(tokT[rows], right))

        def output():
            right = gbranch[:, cols]
            for half, rows in ((0, mine), (1, other)):
                put(half, dot(mixb[rows], right))

        when(n < 3, inputs)
        when(n == 3, output)
        stage_copy(e).start()

    def rq(k, n=0, size=Q_PART):
        return pl.ds(pl.multiple_of(k * Q_PART + n, 16), size)

    def F0(e, g, k, odd):
        src = own.at[0, :, 1 - x, rq(k), columns(g)] if odd else own.at[0, 1 - y, :, rq(k), columns(g)]
        return remote(src, lf.at[e], xp if odd else yp, fs.at[e], fr.at[e])

    def G0(e, g, k, odd):
        if odd:
            return remote(own.at[0, 1 - y, x, rq(k), columns(g)], lg.at[e], yp, gs.at[e], gr.at[e])
        return remote(own.at[0, y, 1 - x, rq(k), columns(g)], lg.at[e], xp, gs.at[e], gr.at[e])

    def Z0(e, g, k):
        return remote(own.at[0, y, x, rq(k), columns(g)], lz.at[e], down_peer, zs_.at[e], zr_.at[e])

    def by_parity(k, fn):
        when(k % 2 == 0, lambda: fn(False))
        when(k % 2 == 1, lambda: fn(True))

    def op_sum0(e):
        g, k = e // 4, e % 4

        def arrive():
            @pl.loop(0, 4)
            def _(n):
                stage_copy(g * 4 + n).wait_recv()

        when(k == 0, arrive)
        add_rows(
            lambda n: own.at[0, :, :, rq(k, n, 16), columns(g)],
            lambda n: sl.at[0, :, :, rq(k, n, 16), columns(g)], Q_PART,
        )
        by_parity(k, lambda odd: F0(e, g, k, odd).start())

    def op_f0(e):
        g, k = e // 4, e % 4

        def turn(odd):
            F0(e, g, k, odd).wait_recv()
            if odd:
                dst = lambda n: own.at[0, :, x, rq(k, n, 16), columns(g)]
            else:
                dst = lambda n: own.at[0, y, :, rq(k, n, 16), columns(g)]
            add_rows(dst, lambda n: lf.at[e, :, r16(n)], Q_PART)
            G0(e, g, k, odd).start()

        by_parity(k, turn)

    def op_g0(e):
        g, k = e // 4, e % 4
        by_parity(k, lambda odd: G0(e, g, k, odd).wait_recv())
        add_rows(lambda n: own.at[0, y, x, rq(k, n, 16), columns(g)], lambda n: lg.at[e, r16(n)], Q_PART)

    def op_z0(e):
        g, k = e // 4, e % 4

        def arrive():
            Z0(e, g, k).wait_recv()
            add_rows(lambda n: own.at[0, y, x, rq(k, n, 16), columns(g)], lambda n: lz.at[e, r16(n)], Q_PART)

        when(z < 3, arrive)
        when(z > 0, lambda: Z0(e, g, k).start())

    def first_in(q):
        return pltpu.make_async_copy(first.at[pl.ds(pl.multiple_of(q * 256, 256), 256)], fchunk, f_sem)

    def grad_out(q):
        return pltpu.make_async_copy(fchunk, grad_in.at[pl.ds(pl.multiple_of(q * 256, 256), 256)], g_sem)

    def weight_in(n):
        target = (p_all.at[pl.ds(0, D), pl.ds(0, D)], ds_all.at[pl.ds(0, D), pl.ds(0, D)], wv)[n]
        return pltpu.make_async_copy(w.at[0, n // 2, n % 2], target, w_sem.at[n])

    def op_gin(q):
        def weights():
            for n in range(3):
                weight_in(n).wait()

        when(q == 0, weights)
        when(q > 0, lambda: grad_out(q - 1).wait())
        first_in(q).start()
        cols = pl.ds(pl.multiple_of(q * 256, 256), 256)
        d = pl.ds(0, D)
        acc = dot(p_all[d, d], qkv[0, :, cols]) + dot(ds_all[d, d], qkv[1, :, cols])
        acc = (acc + dot(wv[...], qkv[2, :, cols])).T
        first_in(q).wait()
        fchunk[...] += acc
        grad_out(q).start()

    def op_other(e):
        def norm_y():
            def go():
                NX.wait_recv()
                nacc[...] += nx[...]
                when(y == 0, lambda: NY.start())

            when(x == 1, go)

        def norm_z():
            def go():
                NY.wait_recv()
                nacc[...] += ny[...]

                def more():
                    NZ.wait_recv()
                    nacc[...] += nz[...]

                when(z > 0, more)
                when(z < 3, lambda: NZ.start())
                when(z == 3, lambda: NC.start())

            when(line, go)

        def load():
            for n in range(3):
                weight_in(n).start()

        when(e == 0, norm_y)
        when(e == 1, norm_z)
        when(e == 2, load)

    run_plan(z, BACK_PLAN, [op_sum, op_c3, op_b3, op_c2, op_bz, op_cz, op_b1, op_head, op_dw, op_sum0, op_f0,
                            op_g0, op_z0, op_gin, op_other])

    half = pl.ds(pl.multiple_of(base, 16), HALF)
    res(half)[...] = own[z, y, x].astype(f32)
    share = remote(res(half), res(half), sib, share_s, share_r)
    share.start()

    @pl.loop(0, 9)
    def _(e):
        t, s = split(e)
        C3(t, s, e).wait_send()
        B3(t, s, e).wait_send()
        C2(t, s, e).wait_send()

        def went_up():
            BU(t, s, e).wait_send()
            CU(t, s, e).wait_send()

        def went_down():
            BD(t, s, e).wait_send()
            CD(t, s, e).wait_send()

        when(t > z, went_up)
        when(t < z, went_down)
        when(t == z, lambda: B1(s).wait_send())

    @pl.loop(0, 8)
    def _(e):
        g, k = e // 4, e % 4
        stage_copy(e).wait_send()

        def gone(odd):
            F0(e, g, k, odd).wait_send()
            G0(e, g, k, odd).wait_send()

        by_parity(k, gone)
        when(z > 0, lambda: Z0(e, g, k).wait_send())

    for t in (1, 2, 3):
        sib_in(t).wait_send()
    when(x == 0, lambda: NX.wait_send())
    when(jnp.logical_and(x == 1, y == 0), lambda: NY.wait_send())
    when(jnp.logical_and(line, z < 3), lambda: NZ.wait_send())

    def norm_last():
        NC.wait_recv()
        NC.wait_send()
        nacc[...] += nc[...]

    when(last_line, norm_last)
    grad_out(3).wait()
    share.wait_send()
    oth = pl.ds(pl.multiple_of((1 - c) * HALF, 16), HALF)
    remote(res(oth), res(oth), sib, share_s, share_r).wait_recv()

    spread = jnp.logical_or(z == 1, z == 2)
    for n in range(6):
        cols = pl.ds(n * 128, 128)

        def plain():
            flat[pl.ds(n, D, stride=6)] = dist[pl.ds(0, D), cols]

        def swapped():
            for j in range(4):
                flat[pl.ds(j * 6 + n, D // 4, stride=24)] = dist[pl.ds(j * (D // 4), D // 4), cols]

        when(jnp.logical_not(spread), plain)
        when(spread, swapped)
        when(i == 15, lambda: flat.__setitem__((pl.ds(6 * D + n, 4, stride=6), slice(None)), nacc[:, cols]))

    head_rows, after = pl.ds(0, 24), pl.ds(6 * D, 24)
    give = remote(flat.at[head_rows], flat.at[after], (c, i - 1), aft_s, aft_r)
    when(i > 0, lambda: give.start())
    when(i < 15, lambda: give.wait_recv())
    leave = pltpu.make_async_copy(flat, flat_out, o_sem)
    leave.start()
    when(i > 0, lambda: give.wait_send())
    leave.wait()


def enter_more(i, c, z, y, x):
    barrier = pltpu.get_barrier_semaphore()
    xp, yp, sib, up, down = partners(i, c, z, y, x)

    def signal(peer):
        pl.semaphore_signal(barrier, inc=1, device_id=peer, device_id_type=MESH)

    for peer in (xp, yp, sib):
        signal(peer)
    when(z > 0, lambda: signal(down))
    when(z < 3, lambda: signal(up))
    when(jnp.logical_and(x == 0, i > 0), lambda: signal((c, i - 1)))
    when(jnp.logical_and(x == 1, i < 15), lambda: signal((c, i + 1)))
    more = 1 - jnp.where(i == 0, 1, 0) - jnp.where(i == 15, 1, 0)
    pl.semaphore_wait(barrier, 3 + jnp.minimum(z, 1) + jnp.minimum(3 - z, 1) + more)


def reduce_back(wide, down, w, qkv, dO, mixb, lse, tokT, gbranch, first, norms, seg):
    Q = pltpu.SemaphoreType.DMA
    V = lambda *s: pltpu.VMEM(s, bf16)
    F = lambda *s: pltpu.VMEM(s, f32)
    A = pl.BlockSpec(memory_space=pl.ANY)
    return pl.pallas_call(
        reduce_back_kernel,
        in_specs=[A, A, A, A, VM, VM, VM, VM, VM, A, VM, VM, VM],
        out_specs=[A, A],
        out_shape=[jax.ShapeDtypeStruct((LEN, D), f32), jax.ShapeDtypeStruct((6 * D + 24, 128), f32)],
        scratch_shapes=[
            V(4, 2, 2, HALF, D), V(4, 2, 2, HALF, D), V(9, 2, C_PART, D), V(9, C_PART, D), V(9, C_PART, D),
            V(3, C_PART, D), V(9, 2, B_PART, D), V(9, 2, B_PART, D), V(3, 2, B_PART, D), V(3, B_PART, D),
            V(8, 2, Q_PART, COLS), V(8, Q_PART, COLS), V(8, Q_PART, COLS), V(8, HALF, COLS),
            F(LEN, LEN), V(LEN, LEN), V(LEN, LEN), V(D, D), V(LEN, HEAD), V(LEN, HEAD), V(3, D, LEN),
            F(256, D), F(6 * D + 24, 128), F(4, D), F(4, D), F(4, D), F(4, D), F(4, D),
            Q((4,)), Q, Q((3,)), Q, Q, Q, Q((4,)), Q((4,)), Q((8,)), Q((8,)),
            *[Q((9,))] * 14, Q((3,)), Q((3,)), *[Q((8,))] * 6, Q((4,)), Q((4,)), Q, Q, Q, Q,
        ],
        compiler_params=pltpu.CompilerParams(
            collective_id=2, has_side_effects=True, vmem_limit_bytes=62 << 20
        ),
        name="reduce_back",
    )(wide, down, w, qkv, dO, mixb, lse, tokT, gbranch, first, norms, seg.reshape(LEN, 1), seg.reshape(1, LEN))

SQUARE = D * D
TAIL = 4 * D


def from_wide(blocks):
    return blocks.reshape(4, 4, D // 4, D).transpose(0, 2, 1, 3).reshape(D, FF)


def to_wide(value):
    return value.reshape(4, D // 4, 4, D).transpose(0, 2, 1, 3).reshape(2, 2, D, D)


def swap_wide(block, index):
    swapped = block.reshape(D // 4, 4, D).transpose(1, 0, 2).reshape(D, D)
    wide = jnp.logical_and(index >= 4, index < 12)
    return jnp.where(wide, swapped, block)


def gather_and_attend(master, tokens, segments):
    count = lax.axis_size("zero")
    index = lax.axis_index("zero")
    size = 16 * SQUARE // count
    weights = master.astype(bf16)
    last = weights[-TAIL:]
    before = lax.ppermute(last, "zero", [(k, k + 1) for k in range(count - 1)])
    joined = jnp.concatenate([before, weights])
    block = lax.dynamic_slice(joined, (TAIL - TAIL // count * index,), (size,))
    if count == 16:
        padded = jnp.pad(last.reshape(4, D), ((0, 12), (0, 0)))
        block = swap_wide(block.reshape(D, D), index)
        blocks, tail, *attended = gather_attend(block, padded, tokens, segments)
        norms = tail[:4].astype(f32)
    else:
        natural = lax.all_gather(block.reshape(-1, D), "zero", axis=0, tiled=True)
        parts = natural.reshape(4, 4 * D, D)
        wide = [to_wide(parts[k].reshape(D, FF)) for k in (1, 2)]
        blocks = jnp.stack([parts[0].reshape(2, 2, D, D), *wide, parts[3].reshape(2, 2, D, D)])
        norms = lax.psum(jnp.where(index == count - 1, last.astype(f32), 0.0), "zero").reshape(4, D)
        attended = attend(tokens, blocks, segments)
    return blocks, norms, *attended


def back_and_scatter(blocks, segments, tokT, qkv, mixed, log_sum, grad_mixed, first_grad, branch_grad, norm_grads,
                     down_grad, wide_grad):
    count = lax.axis_size("zero")
    index = lax.axis_index("zero")
    if count == 16:
        input_grad, joined = reduce_back(
            wide_grad, down_grad, blocks, qkv, grad_mixed, mixed, log_sum, tokT, branch_grad, first_grad,
            norm_grads, segments,
        )
        joined = joined.reshape(-1)
    else:
        square, input_grad = attend_back(
            blocks, segments, tokT, qkv, mixed, log_sum, grad_mixed, first_grad, branch_grad
        )
        natural = [from_wide(wide_grad[k]).reshape(4 * D, D) for k in (0, 1)]
        natural = jnp.concatenate([square.reshape(4 * D, D), *natural, down_grad.reshape(4 * D, D)])
        block = lax.psum_scatter(natural, "zero", scatter_dimension=0, tiled=True)
        block = lax.psum(block.astype(f32), "dp")
        tail = lax.psum(norm_grads, ("dp", "zero"))
        flat = block.reshape(-1)
        after = lax.ppermute(flat[:TAIL], "zero", [(k + 1, k) for k in range(count - 1)])
        joined = jnp.concatenate([flat, jnp.where(index == count - 1, tail.reshape(-1), after)])
    shard = 16 * SQUARE // count + TAIL // count
    return input_grad, lax.dynamic_slice(joined, (TAIL // count * index,), (shard,))


def local(tokens, segments, cotangent, master, moment_one, moment_two):
    blocks, norms, tokT, qkv, mixed, log_sum = gather_and_attend(master, tokens, segments)
    output, first_grad, grad_mixed, branch_grad, norm_grads, down_grad, wide_grad = feed(
        tokens, cotangent, mixed, blocks, norms
    )
    input_grad, grad_shard = back_and_scatter(
        blocks, segments, tokT, qkv, mixed, log_sum, grad_mixed, first_grad, branch_grad, norm_grads,
        down_grad.reshape(2, 2, D, D), wide_grad.reshape(2, 2, 2, D, D),
    )
    grad_shard = grad_shard / (lax.axis_size("zero") * lax.axis_size("dp"))
    first = beta_one * moment_one + (1.0 - beta_one) * grad_shard
    second = beta_two * moment_two + (1.0 - beta_two) * grad_shard * grad_shard
    update = first / correct_one / (jnp.sqrt(second / correct_two) + adam_eps)
    master_new = master - learn_rate * (update + weight_decay * master)
    return (
        output,
        input_grad,
        grad_shard,
        first,
        second,
        master_new,
        master_new.astype(jnp.bfloat16),
    )


def solution(mesh):
    return jax.shard_map(
        local,
        mesh=mesh,
        in_specs=(
            P(("dp", "zero"), None),
            P(("dp", "zero")),
            P(("dp", "zero"), None),
            P("zero"),
            P("zero"),
            P("zero"),
        ),
        out_specs=(
            P(("dp", "zero"), None),
            P(("dp", "zero"), None),
            P("zero"),
            P("zero"),
            P("zero"),
            P("zero"),
            P("zero"),
        ),
        check_vma=False,
    )
```

```python
import functools

import jax
import jax.numpy as jnp
from jax import lax
from jax.sharding import PartitionSpec as P
import jax.experimental.pallas as pl
import jax.experimental.pallas.tpu as pltpu

D = 768
HEADS = 12
HEAD = 64
FF = 3072
LEN = 1024


learn_rate = 0.02
beta_one = 0.9
beta_two = 0.999
adam_eps = 1e-08
weight_decay = 0.01
correct_one = 1.0 - 0.9**10
correct_two = 1.0 - 0.999**10
norm_eps = 1e-06
inv_root_two = 0.7071067811865476
inv_root_tau = 0.3989422804014327


bf16=jnp.bfloat16; f32=jnp.float32
FAR=1e33
VM=pl.BlockSpec(memory_space=pltpu.VMEM)

def dot(a,b): return lax.dot_general(a,b,(((1,),(0,)),((),())),preferred_element_type=f32)
def dot_tn(a,b): return lax.dot_general(a,b,(((0,),(0,)),((),())),preferred_element_type=f32)
def dot_nt(a,b): return lax.dot_general(a,b,(((1,),(1,)),((),())),preferred_element_type=f32)

def slope(h):
    return jnp.exp2(-8.0/HEADS*(jnp.full((1,1),h,jnp.int32).astype(f32)+1.0))

def fill_distance(dist,seg_col,seg_row):
    @pl.loop(0,LEN//128)
    def _(k):
        r=pl.ds(pl.multiple_of(k*128,128),128)
        kk=(lax.broadcasted_iota(jnp.int32,(128,LEN),0)+k*128)
        qq=lax.broadcasted_iota(jnp.int32,(128,LEN),1)
        d=jnp.abs(kk-qq).astype(f32)
        dist[r]=jnp.where(seg_col[r]==seg_row[...],d,FAR)

QB=256
def project_all(w,tokT,qkv):
    @pl.loop(0,3)
    def _(n):
        @pl.loop(0,3)
        def _(t):
            c=pl.ds(pl.multiple_of(t*256,256),256)
            qkv[n,c]=dot_tn(w[0,n//2,n%2,:,c],tokT[...]).astype(bf16)

def attend_head(h,dist,kn,qkv,mixb,lse):
    rows=pl.ds(pl.multiple_of(h*HEAD,HEAD),HEAD)
    kn[...]=qkv[1,rows].astype(f32).T.astype(bf16)
    m=slope(h)
    for b in range(LEN//QB):
        cols=pl.ds(b*QB,QB)
        q=qkv[0,rows,cols]*bf16(0.125)
        s=dot(kn[...],q)-m*dist[:,cols]
        top=jnp.max(s,0,keepdims=True)
        e=jnp.exp(s-top)
        total=jnp.sum(e,0,keepdims=True)
        o=dot(qkv[2,rows],e.astype(bf16))/total
        mixb[rows,cols]=o.astype(bf16)
        lse[h,:,cols]=top+jnp.log(total)

def attend_kernel(tokens,w,seg_col,seg_row,tokT,qkv,mixb,lse,dist,kn):
    tokT[...]=tokens[...].astype(f32).T.astype(bf16)
    fill_distance(dist,seg_col,seg_row)
    project_all(w,tokT,qkv)
    @pl.loop(0,HEADS)
    def _(h):
        attend_head(h,dist,kn,qkv,mixb,lse)

def attend_shapes():
    S=jax.ShapeDtypeStruct
    return [S((D,LEN),bf16),S((3,D,LEN),bf16),S((D,LEN),bf16),S((HEADS,1,LEN),f32)]

def attend(tokens,w,seg):
    return pl.pallas_call(attend_kernel,grid=(1,),
        in_specs=[VM,pl.BlockSpec((1,2,2,D,D),lambda i:(0,0,0,0,0)),VM,VM],out_specs=[VM]*4,
        out_shape=attend_shapes(),
        scratch_shapes=[pltpu.VMEM((LEN,LEN),f32),pltpu.VMEM((LEN,HEAD),bf16)],
        compiler_params=pltpu.CompilerParams(vmem_limit_bytes=58<<20),name="attend")(tokens,w,seg.reshape(LEN,1),seg.reshape(1,LEN))

def attend_back_kernel(w,seg_col,seg_row,tokT,qkv,mixb,lse,dO,first,gbranch,g0,grad_in,dist,kn,vn,p_all,ds_all,dqT,dkT,dvT):
    fill_distance(dist,seg_col,seg_row)
    @pl.loop(0,HEADS)
    def _(h):
        rows=pl.ds(pl.multiple_of(h*HEAD,HEAD),HEAD)
        kn[...]=qkv[1,rows].astype(f32).T.astype(bf16)
        vn[...]=qkv[2,rows].astype(f32).T.astype(bf16)
        m=slope(h)
        for b in range(LEN//QB):
            cols=pl.ds(b*QB,QB)
            q=qkv[0,rows,cols]*bf16(0.125)
            s=dot(kn[...],q)-m*dist[:,cols]
            p=jnp.exp(s-lse[h,:,cols])
            do=dO[rows,cols]
            delta=jnp.sum(do.astype(f32)*mixb[rows,cols].astype(f32),0,keepdims=True)
            dp=dot(vn[...],do)
            p_all[:,cols]=p.astype(bf16)
            ds=(p*(dp-delta)).astype(bf16)
            ds_all[:,cols]=ds
            dqT[rows,cols]=(dot(qkv[1,rows],ds)*0.125).astype(bf16)
        dvT[rows]=dot_nt(dO[rows],p_all[...]).astype(bf16)
        dkT[rows]=(dot_nt(qkv[0,rows],ds_all[...])*0.125).astype(bf16)
    g0[1,1]=dot(mixb[...],gbranch[...]).astype(bf16)
    for n,g in enumerate((dqT,dkT,dvT)):
        g0[n//2,n%2]=dot_nt(tokT[...],g[...]).astype(bf16)
    @pl.loop(0,4)
    def _(t):
        c=pl.ds(pl.multiple_of(t*256,256),256)
        acc=dot(w[0,0,0],dqT[:,c])+dot(w[0,0,1],dkT[:,c])+dot(w[0,1,0],dvT[:,c])
        grad_in[c]=first[c]+acc.T

def attend_back(w,seg,tokT,qkv,mixb,lse,dO,first,gbranch):
    B=lambda: pltpu.VMEM((D,LEN),bf16)
    return pl.pallas_call(attend_back_kernel,grid=(1,),
        in_specs=[pl.BlockSpec((1,2,2,D,D),lambda i:(0,0,0,0,0))]+[VM]*9,out_specs=[VM]*2,
        out_shape=[jax.ShapeDtypeStruct((2,2,D,D),bf16),jax.ShapeDtypeStruct((LEN,D),f32)],
        scratch_shapes=[pltpu.VMEM((LEN,LEN),f32),pltpu.VMEM((LEN,HEAD),bf16),pltpu.VMEM((LEN,HEAD),bf16),pltpu.VMEM((LEN,LEN),bf16),pltpu.VMEM((LEN,LEN),bf16),B(),B(),B()],
        compiler_params=pltpu.CompilerParams(vmem_limit_bytes=60<<20),name="attend_back")(w,seg.reshape(LEN,1),seg.reshape(1,LEN),tokT,qkv,mixb,lse,dO,first,gbranch)

TB=256
def feed_kernel(tokens,cot,mixb,wo,w1,w2,w3,norms,output,first,dO,gbranch,ng,gdown,gwide,inner,wide,gffn,fa,fb,acc,hid):
    step=pl.program_id(0)
    gain1=norms[0:1]; shift1=norms[1:2]; gain2=norms[2:3]; shift2=norms[3:4]
    def stats(v):
        c=v-jnp.mean(v,-1,keepdims=True)
        r=lax.rsqrt(jnp.mean(c*c,-1,keepdims=True)+norm_eps)
        return c*r,r
    def back(e,n,r):
        return r*(e-jnp.mean(e,-1,keepdims=True)-n*jnp.mean(e*n,-1,keepdims=True))
    W=lambda p,j: (w1,w2)[p-1][0,:,j].reshape(D,D)
    WD=lambda j: w3[0,j].reshape(D,D)
    WO=lambda: wo[0,0].reshape(D,D)
    @pl.when(step==0)
    def _(): ng[...]=jnp.zeros_like(ng)
    @pl.when(step<LEN//TB)
    def _():
        rows=pl.ds(pl.multiple_of(step*TB,TB),TB)
        branch=dot_tn(mixb[...],WO())
        n1,r1=stats(tokens[...].astype(f32)+branch)
        l1=n1*gain1+shift1
        inner[rows]=l1.astype(bf16)
        acc[...]=l1
        @pl.loop(0,4,unroll=2)
        def _(j):
            inn=inner[rows]
            ga=dot(inn,W(1,j)); up=dot(inn,W(2,j))
            cum=0.5*(1.0+lax.erf(ga*inv_root_two))
            gel=ga*cum
            fb[j]=gel
            fa[j]=up*(cum+ga*(jnp.exp(-0.5*ga*ga)*inv_root_tau))
            h=(gel*up).astype(bf16)
            hid[j,rows]=h
            acc[...]+=dot(h,WD(j))
        n2,r2=stats(acc[...])
        output[...]=(n2*gain2+shift2).astype(bf16)
        c=cot[...].astype(f32)
        ng[2:3]+=jnp.sum(c*n2,0,keepdims=True)
        ng[3:4]+=jnp.sum(c,0,keepdims=True)
        mid=back(c*gain2,n2,r2)
        gffn[rows]=mid.astype(bf16)
        acc[...]=mid
        @pl.loop(0,4,unroll=2)
        def _(j):
            gh=dot_nt(gffn[rows],WD(j))
            a=(gh*fa[j]).astype(bf16); b=(gh*fb[j]).astype(bf16)
            wide[j,rows]=a; wide[4+j,rows]=b
            acc[...]+=dot_nt(a,W(1,j))+dot_nt(b,W(2,j))
        gl=acc[...]
        ng[0:1]+=jnp.sum(gl*n1,0,keepdims=True)
        ng[1:2]+=jnp.sum(gl,0,keepdims=True)
        gfirst=back(gl*gain1,n1,r1)
        first[...]=gfirst
        gb=gfirst.astype(bf16)
        gbranch[...]=gb
        dO[...]=dot_nt(WO(),gb).astype(bf16)
    def put(g,v):
        g[...]=v.astype(bf16).reshape(g.shape)
    base=LEN//TB
    @pl.when(jnp.logical_and(step>=base,step<base+4))
    def _(): put(gdown,dot_tn(hid[step-base],gffn[...]))
    @pl.when(jnp.logical_and(step>=base+4,step<base+12))
    def _(): put(gwide,dot_tn(inner[...],wide[step-base-4]))

def feed(tokens,cot,mixb,w,norms):
    n=LEN//TB
    last=n-1
    row=lambda i:(jnp.minimum(i,last),0)
    col=lambda i:(0,jnp.minimum(i,last))
    one=pl.Buffered(1)
    S=jax.ShapeDtypeStruct
    V=lambda s,d=bf16: pltpu.VMEM(s,d)
    clip=lambda v,a,b: jnp.minimum(jnp.maximum(v,a),b)
    return pl.pallas_call(feed_kernel,grid=(n+12,),
        in_specs=[pl.BlockSpec((TB,D),row),pl.BlockSpec((TB,D),row),pl.BlockSpec((D,TB),col),
            pl.BlockSpec((1,1,4,D//4,D),lambda i:(0,3,0,0,0),pipeline_mode=one),*[pl.BlockSpec((1,4,4,D//4,D),lambda i,p=p:(p,0,0,0,0),pipeline_mode=one) for p in (1,2,3)],pl.BlockSpec((4,D),lambda i:(0,0))],
        out_specs=[pl.BlockSpec((TB,D),row),pl.BlockSpec((TB,D),row),pl.BlockSpec((D,TB),col),pl.BlockSpec((TB,D),row),
            pl.BlockSpec((4,D),lambda i:(0,0)),
            pl.BlockSpec((1,D,D),lambda i:(clip(i-n,0,3),0,0)),
            pl.BlockSpec((1,4,1,D//4,D),lambda i:(clip((i-n-4)//4,0,1),0,clip(i-n-4,0,7)%4,0,0))],
        out_shape=[S((LEN,D),bf16),S((LEN,D),f32),S((D,LEN),bf16),S((LEN,D),bf16),S((4,D),f32),S((4,D,D),bf16),S((2,4,4,D//4,D),bf16)],
        scratch_shapes=[V((LEN,D)),V((8,LEN,D)),V((LEN,D)),V((4,TB,D),f32),V((4,TB,D),f32),V((TB,D),f32),V((4,LEN,D))],
        compiler_params=pltpu.CompilerParams(vmem_limit_bytes=62<<20),name="feed")(tokens,cot,mixb,*[w.reshape(4,4,4,D//4,D)]*4,norms)

MESH = pl.DeviceIdType.MESH
ALL = slice(None)
HALF = D // 2
B_PART, C_PART = 48, 80
P_PART = 48


def place():
    i = lax.axis_index("zero")
    c = lax.axis_index("dp")
    return i, c, i // 4, (i // 2) % 2, i % 2


def partners(i, c, z, y, x):
    return (c, i + 1 - 2 * x), (c, i + 2 - 4 * y), (1 - c, i), (c, i + 4), (c, i - 4)


def when(cond, fn):
    @pl.when(cond)
    def _():
        fn()


def enter(i, c, z, y, x):
    barrier = pltpu.get_barrier_semaphore()
    xp, yp, sib, up, down = partners(i, c, z, y, x)

    def signal(peer):
        pl.semaphore_signal(barrier, inc=1, device_id=peer, device_id_type=MESH)

    for peer in (xp, yp, sib):
        signal(peer)
    when(z > 0, lambda: signal(down))
    when(z < 3, lambda: signal(up))
    pl.semaphore_wait(barrier, 3 + jnp.minimum(z, 1) + jnp.minimum(3 - z, 1))


def pick(z, values):
    out = jnp.int32(values[3])
    for k in (2, 1, 0):
        out = jnp.where(z == k, jnp.int32(values[k]), out)
    return out


def run_plan(z, words, ops):
    count = len(words[0])
    held = [pick(z, [words[k][n] for k in range(4)]) for n in range(count)]

    @pl.loop(0, count)
    def _(n):
        word = held[0]
        for k in range(1, count):
            word = jnp.where(n == k, held[k], word)

        @pl.loop(0, 3)
        def _(m):
            code = jnp.where(m == 0, word, jnp.where(m == 1, word // 256, word // 65536)) % 256
            kind, e = code // 16, code % 16
            for k, op in enumerate(ops):
                when(kind == k, lambda op=op: op(e))


def gather_attend_kernel(blk, last, tokens, seg_col, seg_row, result, tail, tokT, qkv, mixb, lse,
                         held, dist, kn, own_sem, out_sem, pzs, pzr, pfs, pfr, pgs, pgr, p_s, p_r,
                         b1s, b1r, c1u, c1d, c1r, b2u, b2d, b2r, c2s, c2r, b3s, b3r, c3s, c3r, ss, sr, ts, tr):
    i, c, z, y, x = place()
    xp, yp, sib, up, down = partners(i, c, z, y, x)
    half = c * HALF
    other = (1 - c) * HALF
    local = pltpu.make_async_copy(blk, held.at[z, y, x], own_sem)
    local.start()
    enter(i, c, z, y, x)

    def remote(ref, peer, s, r):
        return pltpu.make_async_remote_copy(
            src_ref=ref, dst_ref=ref, send_sem=s, recv_sem=r, device_id=peer, device_id_type=MESH
        )

    def by_parity(k, fn):
        when(k % 2 == 0, lambda: fn(False))
        when(k % 2 == 1, lambda: fn(True))

    def rp(k, base):
        return pl.ds(pl.multiple_of(base + k * P_PART, 16), P_PART)

    def z_ref(k, base=half):
        return held.at[0, y, x, rp(k, base)]

    def f_ref(k, odd, base=half):
        if odd:
            return held.at[0, 1 - y, x, rp(k, base)]
        return held.at[0, y, 1 - x, rp(k, base)]

    def g_ref(k, odd, mine, base=half):
        if odd:
            return held.at[0, ALL, x if mine else 1 - x, rp(k, base)]
        return held.at[0, y if mine else 1 - y, ALL, rp(k, base)]

    def PZ(k):
        return remote(z_ref(k), up, pzs.at[k], pzr.at[k])

    def PF(k, odd):
        return remote(z_ref(k), yp if odd else xp, pfs.at[k], pfr.at[k])

    def PG(k, odd):
        return remote(g_ref(k, odd, True), xp if odd else yp, pgs.at[k], pgr.at[k])

    def PS(ref, n):
        return remote(ref, sib, p_s.at[n], p_r.at[n])

    def op_p0z(k):
        def arrive():
            PZ(k).wait_recv()
            PS(z_ref(k), k).start()

        when(z > 0, arrive)
        when(z < 3, lambda: PZ(k).start())
        by_parity(k, lambda odd: PF(k, odd).start())

    def op_p0f(k):
        def turn(odd):
            PF(k, odd).wait_recv()
            PG(k, odd).start()
            PS(f_ref(k, odd), 8 + k).start()

        by_parity(k, turn)

    def op_p0g(k):
        def turn(odd):
            PG(k, odd).wait_recv()
            PS(g_ref(k, odd, False), 16 + k).start()

        by_parity(k, turn)

    split = lambda e: (e // 3 + 1, e % 3)

    def rb(s, base):
        return pl.ds(pl.multiple_of(base + s * B_PART, 16), B_PART)

    def rc(s, base):
        return pl.ds(pl.multiple_of(base + 3 * B_PART + s * C_PART, 16), C_PART)

    def b1_ref(s, yy, base=half):
        return held.at[z, yy, x, rb(s, base)]

    def b2_ref(t, s, xx, base=half):
        return held.at[t, ALL, xx, rb(s, base)]

    def c1_ref(t, s, base=half):
        return held.at[t, y, x, rc(s, base)]

    def c2_ref(t, s, xx, base=half):
        return held.at[t, y, xx, rc(s, base)]

    def c3_ref(t, s, yy, base=half):
        return held.at[t, yy, ALL, rc(s, base)]

    B1 = lambda s: remote(b1_ref(s, y), yp, b1s.at[s], b1r.at[s])
    C1U = lambda t, s, e: remote(c1_ref(t, s), up, c1u.at[e], c1r.at[e])
    C1D = lambda t, s, e: remote(c1_ref(t, s), down, c1d.at[e], c1r.at[e])
    B2U = lambda t, s, e: remote(b2_ref(t, s, x), up, b2u.at[e], b2r.at[e])
    B2D = lambda t, s, e: remote(b2_ref(t, s, x), down, b2d.at[e], b2r.at[e])
    C2 = lambda t, s, e: remote(c2_ref(t, s, x), xp, c2s.at[e], c2r.at[e])
    B3 = lambda t, s, e: remote(b2_ref(t, s, x), xp, b3s.at[e], b3r.at[e])
    C3 = lambda t, s, e: remote(c3_ref(t, s, y), yp, c3s.at[e], c3r.at[e])
    S = lambda ref, n: remote(ref, sib, ss.at[n], sr.at[n])

    def op_own(e):
        t, s = split(e)
        B1(s).start()
        C1D(t, s, e).start()

    def op_ownup(e):
        t, s = split(e)

        def go():
            C1U(t, s, e).start()
            B2U(t, s, e).start()

        when(z < 3, go)

    def op_b1(e):
        t, s = split(e)
        B1(s).wait_recv()
        B2D(t, s, e).start()
        S(b1_ref(s, 1 - y), 45 + s).start()

    def op_cx(e):
        t, s = split(e)
        C2(t, s, e).start()

    def op_bx(e):
        t, s = split(e)
        B3(t, s, e).start()

    def op_c1(e):
        t, s = split(e)
        C1U(t, s, e).wait_recv()
        when(jnp.logical_and(t < z, z < 3), lambda: C1U(t, s, e).start())
        when(jnp.logical_and(t > z, z > 0), lambda: C1D(t, s, e).start())
        S(c1_ref(t, s), e).start()

    def op_b2(e):
        t, s = split(e)
        B2U(t, s, e).wait_recv()
        when(jnp.logical_and(t < z, z < 3), lambda: B2U(t, s, e).start())
        when(jnp.logical_and(t > z, z > 0), lambda: B2D(t, s, e).start())
        S(b2_ref(t, s, x), 9 + e).start()

    def op_c2(e):
        t, s = split(e)
        C2(t, s, e).wait_recv()
        C3(t, s, e).start()
        S(c2_ref(t, s, 1 - x), 18 + e).start()

    def op_b3(e):
        t, s = split(e)
        B3(t, s, e).wait_recv()
        S(b2_ref(t, s, 1 - x), 27 + e).start()

    def op_c3(e):
        t, s = split(e)
        C3(t, s, e).wait_recv()
        S(c3_ref(t, s, 1 - y), 36 + e).start()

    def op_proj(n):
        def arrive():
            @pl.loop(0, 8)
            def _(k):
                def got(odd):
                    PS(f_ref(k, odd, other), 8 + k).wait_recv()
                    PS(g_ref(k, odd, False, other), 16 + k).wait_recv()

                by_parity(k, got)
                when(z > 0, lambda: PS(z_ref(k, other), k).wait_recv())

        when(n == 0, arrive)

        @pl.loop(0, 3)
        def _(t):
            cols = pl.ds(pl.multiple_of(t * 256, 256), 256)
            qkv[n, cols] = dot_tn(held[0, n // 2, n % 2, :, cols], tokT[...]).astype(bf16)

    def op_head(h):
        attend_head(h, dist, kn, qkv, mixb, lse)

    line = jnp.logical_and(y == 1, x == 1)
    source = jnp.logical_and(line, z == 3)

    def T(peer, n):
        return remote(tail, peer, ts.at[n], tr.at[0])

    def leave(t):
        return pltpu.make_async_copy(held.at[t], result.at[t], out_sem.at[t])

    def op_other(e):
        def tail_z():
            def go():
                when(z < 3, lambda: T(down, 0).wait_recv())
                when(z > 0, lambda: T(down, 0).start())
                T(yp, 1).start()

            when(line, go)

        def tail_x():
            def go():
                when(y == 0, lambda: T(yp, 1).wait_recv())
                T(xp, 2).start()

            when(x == 1, go)

        def out():
            t = e - 2

            def others():
                @pl.loop(0, 3)
                def _(s):
                    n = (t - 1) * 3 + s

                    def theirs():
                        S(c1_ref(t, s, other), n).wait_recv()
                        S(b2_ref(t, s, x, other), 9 + n).wait_recv()

                    when(t != z, theirs)
                    when(t == z, lambda: S(b1_ref(s, 1 - y, other), 45 + s).wait_recv())
                    S(c2_ref(t, s, 1 - x, other), 18 + n).wait_recv()
                    S(b2_ref(t, s, 1 - x, other), 27 + n).wait_recv()
                    S(c3_ref(t, s, 1 - y, other), 36 + n).wait_recv()

            when(t > 0, others)
            leave(t).start()

        def prepare():
            tokT[...] = tokens[...].astype(f32).T.astype(bf16)
            fill_distance(dist, seg_col, seg_row)

        when(e == 0, tail_z)
        when(e == 1, tail_x)
        when(jnp.logical_and(e >= 2, e < 6), out)
        when(e == 6, prepare)

    when(source, lambda: tail.__setitem__(Ellipsis, last[...]))
    local.wait()
    run_plan(z, GATHER_PLAN, [op_p0z, op_p0f, op_p0g, op_own, op_ownup, op_b1, op_bx, op_c1, op_b2, op_c2, op_b3,
                              op_c3, op_proj, op_head, op_other, op_cx])

    when(x == 0, lambda: T(xp, 2).wait_recv())
    when(x == 1, lambda: T(xp, 2).wait_send())

    def tail_sent():
        T(yp, 1).wait_send()
        when(z > 0, lambda: T(down, 0).wait_send())

    when(line, tail_sent)

    @pl.loop(0, 8)
    def _(k):
        def gone(odd):
            PF(k, odd).wait_send()
            PG(k, odd).wait_send()
            PS(f_ref(k, odd), 8 + k).wait_send()
            PS(g_ref(k, odd, False), 16 + k).wait_send()

        by_parity(k, gone)
        when(z < 3, lambda: PZ(k).wait_send())
        when(z > 0, lambda: PS(z_ref(k), k).wait_send())

    @pl.loop(0, 9)
    def _(e):
        t, s = split(e)
        C2(t, s, e).wait_send()
        B3(t, s, e).wait_send()
        C3(t, s, e).wait_send()

        def ups():
            C1U(t, s, e).wait_send()
            B2U(t, s, e).wait_send()

        def downs():
            C1D(t, s, e).wait_send()
            B2D(t, s, e).wait_send()

        when(jnp.logical_and(t <= z, z < 3), ups)
        when(jnp.logical_and(t >= z, z > 0), downs)

        def mine():
            B1(s).wait_send()
            S(b1_ref(s, 1 - y), 45 + s).wait_send()

        def theirs():
            S(c1_ref(t, s), e).wait_send()
            S(b2_ref(t, s, x), 9 + e).wait_send()

        when(t == z, mine)
        when(t != z, theirs)
        S(c2_ref(t, s, 1 - x), 18 + e).wait_send()
        S(b2_ref(t, s, 1 - x), 27 + e).wait_send()
        S(c3_ref(t, s, 1 - y), 36 + e).wait_send()

    for t in range(4):
        leave(t).wait()


def gather_attend(blk, last, tokens, seg):
    Q = pltpu.SemaphoreType.DMA
    any_space = pl.BlockSpec(memory_space=pl.ANY)
    counts = [8] * 6 + [24, 24, 3, 3] + [9] * 12 + [48, 48, 3, 1]
    return pl.pallas_call(
        gather_attend_kernel,
        in_specs=[any_space, VM, VM, VM, VM],
        out_specs=[any_space] + [VM] * 5,
        out_shape=[
            jax.ShapeDtypeStruct((4, 2, 2, D, D), bf16), jax.ShapeDtypeStruct((16, D), bf16),
            *attend_shapes(),
        ],
        scratch_shapes=[
            pltpu.VMEM((4, 2, 2, D, D), bf16), pltpu.VMEM((LEN, LEN), f32), pltpu.VMEM((LEN, HEAD), bf16),
            Q, Q((4,)), *[Q((n,)) for n in counts],
        ],
        compiler_params=pltpu.CompilerParams(
            collective_id=1, has_side_effects=True, vmem_limit_bytes=58 << 20
        ),
        name="gather_attend",
    )(blk, last, tokens, seg.reshape(LEN, 1), seg.reshape(1, LEN))


PLANE_ORDER = (1, 3, 2)
BACK_PLAN = (
    (
        14709104, 65761, 422402, 475168, 2192136, 200769, 4334084, 7606533, 7685670, 2639655,
        8589896, 5255296, 8552726, 4399990, 9454628, 9671313, 3241751, 4531537, 3307544, 3543890,
        10582358, 10713620, 10517269, 3692343, 8905304, 10638131, 11634052, 8803380, 3526835, 11587925,
        9745106, 9934485, 10855635, 10987200, 11843009, 12761014, 12895683, 15779782, 15790320,
    ),
    (
        14709104, 65761, 422402, 526112, 1057139, 328707, 4224034, 7672102, 8589863, 2639425,
        3151488, 4358785, 4748871, 9446435, 9671313, 5273367, 3228453, 4487192, 7934770, 4535969,
        5339668, 5667747, 6378080, 14825527, 6457109, 8750131, 5736096, 10670132, 13719605, 9744816,
        9934485, 11776722, 5559123, 12625316, 10928469, 11842983, 12039874, 12895683, 15779782,
    ),
    (
        14709104, 65761, 422402, 526112, 1057139, 262976, 7603490, 1123905, 2572917, 8595474,
        3151488, 7766657, 2311760, 9539620, 1545106, 4749127, 3217445, 1258104, 5325689, 1324705,
        4477562, 4553635, 3684256, 8852962, 3383940, 6510213, 13644934, 6599088, 3519441, 5747410,
        9802853, 12621718, 5816787, 5481892, 12801218, 11904934, 11949492, 12895671, 15779782,
    ),
    (
        14709104, 65761, 422402, 475168, 2192136, 200769, 4334084, 7606533, 2585894, 8595474,
        3151488, 8552784, 4399990, 9454628, 9671313, 4618007, 3228965, 7870545, 5386823, 4732435,
        1352057, 8102778, 3684256, 8852962, 3383940, 6718803, 5518470, 11587687, 13723840, 5685681,
        9721141, 11703957, 12825538, 13882007, 5744036, 10987096, 11847093, 13022916, 15779767,
    ),
)

GATHER_PLAN = (
    (
        131328, 328707, 15075078, 1184016, 1339411, 1470741, 15855639, 2224754, 6324256, 7545379,
        2369011, 2580865, 12697638, 7635650, 7704976, 16118882, 14868960, 9602000, 13738083, 8688502,
        11597412, 6653394, 10658225, 7894995, 16316308, 9823154, 6719188, 14001075, 6785159, 9872488,
        10868404, 11900887, 10016996, 14263990, 14329783, 12114856, 15724517, 15724527,
    ),
    (
        3289392, 5243110, 5308787, 7623170, 1114896, 1209604, 401413, 1253763, 4276231, 7750164,
        8659478, 1516309, 6381808, 15885041, 6579187, 16184820, 2385285, 16217893, 2586662, 12763584,
        6721670, 14803192, 10512263, 8966370, 13738344, 10662033, 13865682, 13939091, 9754019, 14918834,
        9868758, 11851699, 9951397, 11901145, 14345382, 14395318, 12101815, 15724517,
    ),
    (
        3486771, 7754726, 7820628, 7864576, 200706, 296465, 8848658, 1246752, 4392737, 8918084,
        2233925, 1512816, 15761443, 6550368, 6681700, 16148213, 16316263, 2388328, 8515877, 12592934,
        7520961, 6393986, 14742114, 14852321, 13734864, 13804464, 11773076, 13936083, 14005397, 14067350,
        14985141, 10000343, 11065526, 12030425, 10658266, 12096219, 11710949, 15724515,
    ),
    (
        3684150, 5695222, 5805655, 112128, 200706, 1180689, 401413, 467219, 1328966, 1450568,
        1512819, 15958819, 6776419, 6879479, 2434164, 2524404, 12697639, 8746434, 6644883, 14803189,
        13689507, 10940528, 7438545, 9957728, 13805491, 9986433, 13890162, 9724546, 13936823, 15055012,
        9807317, 11833558, 11903191, 14193124, 9623969, 11655856, 11721634, 15724515,
    ),
)


Q_PART = 96
COLS = D // 2


def reduce_back_kernel(wide, down, w, qkv_in, dO, mixb, lse, tokT, gbranch, first, norm_in, seg_col, seg_row,
                       grad_in, flat_out, own, sl, lc3, lc2, lcz, lczx, lb3, lbz, lbzx, lb1, lf, lg, lz, stage,
                       dist, p_all, ds_all, wv, kn, vn, qkv, fchunk, flat, nacc, nx, ny, nz, nc,
                       own_sem, qkv_sem, w_sem, f_sem, g_sem, o_sem, sib_s, sib_r, st_s, st_r,
                       c3s, c3r, b3s, b3r, c2s, c2r, bus, bur, bds, bdr, cus, cur, cds, cdr, b1s, b1r,
                       fs, fr, gs, gr, zs_, zr_, ns, nr, share_s, share_r, aft_s, aft_r):
    i, c, z, y, x = place()
    xp, yp, sib, up, down_peer = partners(i, c, z, y, x)
    base = c * HALF
    mine = pl.ds(pl.multiple_of(base, 16), HALF)
    other = pl.ds(pl.multiple_of((1 - c) * HALF, 16), HALF)
    planes = [wide.at[0], wide.at[1], down]

    def remote(src, dst, peer, s, r):
        return pltpu.make_async_remote_copy(
            src_ref=src, dst_ref=dst, send_sem=s, recv_sem=r, device_id=peer, device_id_type=MESH
        )

    def local_in(t):
        return pltpu.make_async_copy(planes[t - 1].at[:, :, mine], own.at[t], own_sem.at[t])

    def sib_in(t):
        return remote(planes[t - 1].at[:, :, other], sl.at[t], sib, sib_s.at[t], sib_r.at[t])

    for t in PLANE_ORDER:
        local_in(t).start()
    qkv_copy = pltpu.make_async_copy(qkv_in, qkv, qkv_sem)
    qkv_copy.start()
    enter_more(i, c, z, y, x)
    for t in PLANE_ORDER:
        sib_in(t).start()
    nacc[...] = norm_in[...]
    NX = remote(nacc, nx, xp, ns.at[0], nr.at[0])
    NY = remote(nacc, ny, yp, ns.at[1], nr.at[1])
    NZ = remote(nacc, nz, up, ns.at[2], nr.at[2])
    NC = remote(nacc, nc, sib, ns.at[3], nr.at[3])
    line = jnp.logical_and(x == 1, y == 1)
    last_line = jnp.logical_and(line, z == 3)
    when(x == 0, lambda: NX.start())
    fill_distance(dist, seg_col, seg_row)
    qkv_copy.wait()

    def rb(s, k=0, size=B_PART):
        return pl.ds(pl.multiple_of(s * B_PART + k, 16), size)

    def rc(s, k=0, size=C_PART):
        return pl.ds(pl.multiple_of(3 * B_PART + s * C_PART + k, 16), size)

    def add_rows(dst, src, rows):
        @pl.loop(0, rows // 16)
        def _(n):
            k = pl.multiple_of(n * 16, 16)
            a = dst(k)
            a[...] = (a[...].astype(f32) + src(k)[...].astype(f32)).astype(bf16)

    r16 = lambda k: pl.ds(k, 16)
    split = lambda e: (e // 3 + 1, e % 3)

    def C3(t, s, e):
        return remote(own.at[t, 1 - y, :, rc(s)], lc3.at[e], yp, c3s.at[e], c3r.at[e])

    def B3(t, s, e):
        return remote(own.at[t, :, 1 - x, rb(s)], lb3.at[e], xp, b3s.at[e], b3r.at[e])

    def C2(t, s, e):
        return remote(own.at[t, y, 1 - x, rc(s)], lc2.at[e], xp, c2s.at[e], c2r.at[e])

    def BU(t, s, e):
        return remote(own.at[t, :, x, rb(s)], lbz.at[e], up, bus.at[e], bur.at[e])

    def BD(t, s, e, extra=False):
        return remote(own.at[t, :, x, rb(s)], lbzx.at[s] if extra else lbz.at[e], down_peer, bds.at[e], bdr.at[e])

    def CU(t, s, e):
        return remote(own.at[t, y, x, rc(s)], lcz.at[e], up, cus.at[e], cur.at[e])

    def CD(t, s, e, extra=False):
        return remote(own.at[t, y, x, rc(s)], lczx.at[s] if extra else lcz.at[e], down_peer, cds.at[e], cdr.at[e])

    def B1(s):
        return remote(own.at[z, 1 - y, x, rb(s)], lb1.at[s], yp, b1s.at[s], b1r.at[s])

    def op_sum(e):
        t, s = split(e)

        def arrive():
            for k in (1, 2, 3):
                def both(k=k):
                    local_in(k).wait()
                    sib_in(k).wait_recv()

                when(t == k, both)

        when(s == 0, arrive)
        add_rows(lambda k: own.at[t, :, :, rb(s, k, 16)], lambda k: sl.at[t, :, :, rb(s, k, 16)], B_PART)
        add_rows(lambda k: own.at[t, :, :, rc(s, k, 16)], lambda k: sl.at[t, :, :, rc(s, k, 16)], C_PART)
        C3(t, s, e).start()
        B3(t, s, e).start()

    def op_c3(e):
        t, s = split(e)
        C3(t, s, e).wait_recv()
        add_rows(lambda k: own.at[t, y, :, rc(s, k, 16)], lambda k: lc3.at[e, :, r16(k)], C_PART)
        C2(t, s, e).start()

    def op_b3(e):
        t, s = split(e)
        B3(t, s, e).wait_recv()
        add_rows(lambda k: own.at[t, :, x, rb(s, k, 16)], lambda k: lb3.at[e, :, r16(k)], B_PART)

    def op_c2(e):
        t, s = split(e)
        C2(t, s, e).wait_recv()
        add_rows(lambda k: own.at[t, y, x, rc(s, k, 16)], lambda k: lc2.at[e, r16(k)], C_PART)

    def op_bz(e):
        t, s = split(e)
        dst = lambda k: own.at[t, :, x, rb(s, k, 16)]

        def from_below():
            BU(t, s, e).wait_recv()
            add_rows(dst, lambda k: lbz.at[e, :, r16(k)], B_PART)

        when(jnp.logical_and(t >= z, z > 0), from_below)

        def from_above():
            BD(t, s, e).wait_recv()
            add_rows(dst, lambda k: lbz.at[e, :, r16(k)], B_PART)

        when(t < z, lambda: when(z < 3, from_above))

        def from_above_last():
            BD(t, s, e).wait_recv()
            add_rows(dst, lambda k: lbzx.at[s, :, r16(k)], B_PART)

        when(jnp.logical_and(t == z, z < 3), from_above_last)
        when(t > z, lambda: BU(t, s, e).start())
        when(t == z - 1, lambda: BD(t, s, e, True).start())
        when(t < z - 1, lambda: BD(t, s, e).start())
        when(t == z, lambda: B1(s).start())

    def res(rows):
        return dist.at[rows, pl.ds(0, D)]

    def op_cz(e):
        t, s = split(e)
        dst = lambda k: own.at[t, y, x, rc(s, k, 16)]

        def from_below():
            CU(t, s, e).wait_recv()
            add_rows(dst, lambda k: lcz.at[e, r16(k)], C_PART)

        when(jnp.logical_and(t >= z, z > 0), from_below)

        def from_above():
            CD(t, s, e).wait_recv()
            add_rows(dst, lambda k: lcz.at[e, r16(k)], C_PART)

        when(t < z, lambda: when(z < 3, from_above))

        def from_above_last():
            CD(t, s, e).wait_recv()
            add_rows(dst, lambda k: lczx.at[s, r16(k)], C_PART)

        when(jnp.logical_and(t == z, z < 3), from_above_last)
        when(t > z, lambda: CU(t, s, e).start())
        when(t == z - 1, lambda: CD(t, s, e, True).start())
        when(t < z - 1, lambda: CD(t, s, e).start())

    def op_b1(e):
        t, s = split(e)
        B1(s).wait_recv()
        add_rows(lambda k: own.at[z, y, x, rb(s, k, 16)], lambda k: lb1.at[s, r16(k)], B_PART)

    def op_head(h):
        rows = pl.ds(pl.multiple_of(h * HEAD, HEAD), HEAD)
        kn[...] = qkv[1, rows].astype(f32).T.astype(bf16)
        vn[...] = qkv[2, rows].astype(f32).T.astype(bf16)
        m = slope(h)
        for b in range(LEN // QB):
            cols = pl.ds(b * QB, QB)
            q = qkv[0, rows, cols] * bf16(0.125)
            s = dot(kn[...], q) - m * dist[:, cols]
            p = jnp.exp(s - lse[h, :, cols])
            do = dO[rows, cols]
            delta = jnp.sum(do.astype(f32) * mixb[rows, cols].astype(f32), 0, keepdims=True)
            dp = dot(vn[...], do)
            p_all[:, cols] = p.astype(bf16)
            ds_all[:, cols] = (p * (dp - delta)).astype(bf16)
        grad_q = (dot(qkv[1, rows], ds_all[...]) * 0.125).astype(bf16)
        grad_k = (dot_nt(qkv[0, rows], ds_all[...]) * 0.125).astype(bf16)
        grad_v = dot_nt(dO[rows], p_all[...]).astype(bf16)
        qkv[0, rows] = grad_q
        qkv[1, rows] = grad_k
        qkv[2, rows] = grad_v

    def columns(g):
        return pl.ds(pl.multiple_of(g * COLS, 128), COLS)

    def stage_copy(e):
        g, n = e // 4, e % 4
        return remote(
            stage.at[e], sl.at[0, n // 2, n % 2, :, columns(g)], sib, st_s.at[e], st_r.at[e]
        )

    def op_dw(e):
        g, n = e // 4, e % 4
        cols = columns(g)

        def put(half, value):
            if half == 0:
                own[0, n // 2, n % 2, :, cols] = value.astype(bf16)
            else:
                stage[e] = value.astype(bf16)

        def inputs():
            right = qkv[n, pl.ds(pl.multiple_of(g * COLS, 128), COLS)]
            for half, rows in ((0, mine), (1, other)):
                put(half, dot_nt(tokT[rows], right))

        def output():
            right = gbranch[:, cols]
            for half, rows in ((0, mine), (1, other)):
                put(half, dot(mixb[rows], right))

        when(n < 3, inputs)
        when(n == 3, output)
        stage_copy(e).start()

    def rq(k, n=0, size=Q_PART):
        return pl.ds(pl.multiple_of(k * Q_PART + n, 16), size)

    def F0(e, g, k, odd):
        src = own.at[0, :, 1 - x, rq(k), columns(g)] if odd else own.at[0, 1 - y, :, rq(k), columns(g)]
        return remote(src, lf.at[e], xp if odd else yp, fs.at[e], fr.at[e])

    def G0(e, g, k, odd):
        if odd:
            return remote(own.at[0, 1 - y, x, rq(k), columns(g)], lg.at[e], yp, gs.at[e], gr.at[e])
        return remote(own.at[0, y, 1 - x, rq(k), columns(g)], lg.at[e], xp, gs.at[e], gr.at[e])

    def Z0(e, g, k):
        return remote(own.at[0, y, x, rq(k), columns(g)], lz.at[e], down_peer, zs_.at[e], zr_.at[e])

    def by_parity(k, fn):
        when(k % 2 == 0, lambda: fn(False))
        when(k % 2 == 1, lambda: fn(True))

    def op_sum0(e):
        g, k = e // 4, e % 4

        def arrive():
            @pl.loop(0, 4)
            def _(n):
                stage_copy(g * 4 + n).wait_recv()

        when(k == 0, arrive)
        add_rows(
            lambda n: own.at[0, :, :, rq(k, n, 16), columns(g)],
            lambda n: sl.at[0, :, :, rq(k, n, 16), columns(g)], Q_PART,
        )
        by_parity(k, lambda odd: F0(e, g, k, odd).start())

    def op_f0(e):
        g, k = e // 4, e % 4

        def turn(odd):
            F0(e, g, k, odd).wait_recv()
            if odd:
                dst = lambda n: own.at[0, :, x, rq(k, n, 16), columns(g)]
            else:
                dst = lambda n: own.at[0, y, :, rq(k, n, 16), columns(g)]
            add_rows(dst, lambda n: lf.at[e, :, r16(n)], Q_PART)
            G0(e, g, k, odd).start()

        by_parity(k, turn)

    def op_g0(e):
        g, k = e // 4, e % 4
        by_parity(k, lambda odd: G0(e, g, k, odd).wait_recv())
        add_rows(lambda n: own.at[0, y, x, rq(k, n, 16), columns(g)], lambda n: lg.at[e, r16(n)], Q_PART)

    def op_z0(e):
        g, k = e // 4, e % 4

        def arrive():
            Z0(e, g, k).wait_recv()
            add_rows(lambda n: own.at[0, y, x, rq(k, n, 16), columns(g)], lambda n: lz.at[e, r16(n)], Q_PART)

        when(z < 3, arrive)
        when(z > 0, lambda: Z0(e, g, k).start())

    def first_in(q):
        return pltpu.make_async_copy(first.at[pl.ds(pl.multiple_of(q * 256, 256), 256)], fchunk, f_sem)

    def grad_out(q):
        return pltpu.make_async_copy(fchunk, grad_in.at[pl.ds(pl.multiple_of(q * 256, 256), 256)], g_sem)

    def weight_in(n):
        target = (p_all.at[pl.ds(0, D), pl.ds(0, D)], ds_all.at[pl.ds(0, D), pl.ds(0, D)], wv)[n]
        return pltpu.make_async_copy(w.at[0, n // 2, n % 2], target, w_sem.at[n])

    def op_gin(q):
        def weights():
            for n in range(3):
                weight_in(n).wait()

        when(q == 0, weights)
        when(q > 0, lambda: grad_out(q - 1).wait())
        first_in(q).start()
        cols = pl.ds(pl.multiple_of(q * 256, 256), 256)
        d = pl.ds(0, D)
        acc = dot(p_all[d, d], qkv[0, :, cols]) + dot(ds_all[d, d], qkv[1, :, cols])
        acc = (acc + dot(wv[...], qkv[2, :, cols])).T
        first_in(q).wait()
        fchunk[...] += acc
        grad_out(q).start()

    def op_other(e):
        def norm_y():
            def go():
                NX.wait_recv()
                nacc[...] += nx[...]
                when(y == 0, lambda: NY.start())

            when(x == 1, go)

        def norm_z():
            def go():
                NY.wait_recv()
                nacc[...] += ny[...]

                def more():
                    NZ.wait_recv()
                    nacc[...] += nz[...]

                when(z > 0, more)
                when(z < 3, lambda: NZ.start())
                when(z == 3, lambda: NC.start())

            when(line, go)

        def load():
            for n in range(3):
                weight_in(n).start()

        when(e == 0, norm_y)
        when(e == 1, norm_z)
        when(e == 2, load)

    run_plan(z, BACK_PLAN, [op_sum, op_c3, op_b3, op_c2, op_bz, op_cz, op_b1, op_head, op_dw, op_sum0, op_f0,
                            op_g0, op_z0, op_gin, op_other])

    half = pl.ds(pl.multiple_of(base, 16), HALF)
    res(half)[...] = own[z, y, x].astype(f32)
    share = remote(res(half), res(half), sib, share_s, share_r)
    share.start()

    @pl.loop(0, 9)
    def _(e):
        t, s = split(e)
        C3(t, s, e).wait_send()
        B3(t, s, e).wait_send()
        C2(t, s, e).wait_send()

        def went_up():
            BU(t, s, e).wait_send()
            CU(t, s, e).wait_send()

        def went_down():
            BD(t, s, e).wait_send()
            CD(t, s, e).wait_send()

        when(t > z, went_up)
        when(t < z, went_down)
        when(t == z, lambda: B1(s).wait_send())

    @pl.loop(0, 8)
    def _(e):
        g, k = e // 4, e % 4
        stage_copy(e).wait_send()

        def gone(odd):
            F0(e, g, k, odd).wait_send()
            G0(e, g, k, odd).wait_send()

        by_parity(k, gone)
        when(z > 0, lambda: Z0(e, g, k).wait_send())

    for t in (1, 2, 3):
        sib_in(t).wait_send()
    when(x == 0, lambda: NX.wait_send())
    when(jnp.logical_and(x == 1, y == 0), lambda: NY.wait_send())
    when(jnp.logical_and(line, z < 3), lambda: NZ.wait_send())

    def norm_last():
        NC.wait_recv()
        NC.wait_send()
        nacc[...] += nc[...]

    when(last_line, norm_last)
    grad_out(3).wait()
    share.wait_send()
    oth = pl.ds(pl.multiple_of((1 - c) * HALF, 16), HALF)
    remote(res(oth), res(oth), sib, share_s, share_r).wait_recv()

    spread = jnp.logical_or(z == 1, z == 2)
    for n in range(6):
        cols = pl.ds(n * 128, 128)

        def plain():
            flat[pl.ds(n, D, stride=6)] = dist[pl.ds(0, D), cols]

        def swapped():
            for j in range(4):
                flat[pl.ds(j * 6 + n, D // 4, stride=24)] = dist[pl.ds(j * (D // 4), D // 4), cols]

        when(jnp.logical_not(spread), plain)
        when(spread, swapped)
        when(i == 15, lambda: flat.__setitem__((pl.ds(6 * D + n, 4, stride=6), slice(None)), nacc[:, cols]))

    head_rows, after = pl.ds(0, 24), pl.ds(6 * D, 24)
    give = remote(flat.at[head_rows], flat.at[after], (c, i - 1), aft_s, aft_r)
    when(i > 0, lambda: give.start())
    when(i < 15, lambda: give.wait_recv())
    leave = pltpu.make_async_copy(flat, flat_out, o_sem)
    leave.start()
    when(i > 0, lambda: give.wait_send())
    leave.wait()


def enter_more(i, c, z, y, x):
    barrier = pltpu.get_barrier_semaphore()
    xp, yp, sib, up, down = partners(i, c, z, y, x)

    def signal(peer):
        pl.semaphore_signal(barrier, inc=1, device_id=peer, device_id_type=MESH)

    for peer in (xp, yp, sib):
        signal(peer)
    when(z > 0, lambda: signal(down))
    when(z < 3, lambda: signal(up))
    when(jnp.logical_and(x == 0, i > 0), lambda: signal((c, i - 1)))
    when(jnp.logical_and(x == 1, i < 15), lambda: signal((c, i + 1)))
    more = 1 - jnp.where(i == 0, 1, 0) - jnp.where(i == 15, 1, 0)
    pl.semaphore_wait(barrier, 3 + jnp.minimum(z, 1) + jnp.minimum(3 - z, 1) + more)


def reduce_back(wide, down, w, qkv, dO, mixb, lse, tokT, gbranch, first, norms, seg):
    Q = pltpu.SemaphoreType.DMA
    V = lambda *s: pltpu.VMEM(s, bf16)
    F = lambda *s: pltpu.VMEM(s, f32)
    A = pl.BlockSpec(memory_space=pl.ANY)
    return pl.pallas_call(
        reduce_back_kernel,
        in_specs=[A, A, A, A, VM, VM, VM, VM, VM, A, VM, VM, VM],
        out_specs=[A, A],
        out_shape=[jax.ShapeDtypeStruct((LEN, D), f32), jax.ShapeDtypeStruct((6 * D + 24, 128), f32)],
        scratch_shapes=[
            V(4, 2, 2, HALF, D), V(4, 2, 2, HALF, D), V(9, 2, C_PART, D), V(9, C_PART, D), V(9, C_PART, D),
            V(3, C_PART, D), V(9, 2, B_PART, D), V(9, 2, B_PART, D), V(3, 2, B_PART, D), V(3, B_PART, D),
            V(8, 2, Q_PART, COLS), V(8, Q_PART, COLS), V(8, Q_PART, COLS), V(8, HALF, COLS),
            F(LEN, LEN), V(LEN, LEN), V(LEN, LEN), V(D, D), V(LEN, HEAD), V(LEN, HEAD), V(3, D, LEN),
            F(256, D), F(6 * D + 24, 128), F(4, D), F(4, D), F(4, D), F(4, D), F(4, D),
            Q((4,)), Q, Q((3,)), Q, Q, Q, Q((4,)), Q((4,)), Q((8,)), Q((8,)),
            *[Q((9,))] * 14, Q((3,)), Q((3,)), *[Q((8,))] * 6, Q((4,)), Q((4,)), Q, Q, Q, Q,
        ],
        compiler_params=pltpu.CompilerParams(
            collective_id=2, has_side_effects=True, vmem_limit_bytes=62 << 20
        ),
        name="reduce_back",
    )(wide, down, w, qkv, dO, mixb, lse, tokT, gbranch, first, norms, seg.reshape(LEN, 1), seg.reshape(1, LEN))

SQUARE = D * D
TAIL = 4 * D


def from_wide(blocks):
    return blocks.reshape(4, 4, D // 4, D).transpose(0, 2, 1, 3).reshape(D, FF)


def to_wide(value):
    return value.reshape(4, D // 4, 4, D).transpose(0, 2, 1, 3).reshape(2, 2, D, D)


def swap_wide(block, index):
    swapped = block.reshape(D // 4, 4, D).transpose(1, 0, 2).reshape(D, D)
    wide = jnp.logical_and(index >= 4, index < 12)
    return jnp.where(wide, swapped, block)


def gather_and_attend(master, tokens, segments):
    count = lax.axis_size("zero")
    index = lax.axis_index("zero")
    size = 16 * SQUARE // count
    weights = master.astype(bf16)
    last = weights[-TAIL:]
    before = lax.ppermute(last, "zero", [(k, k + 1) for k in range(count - 1)])
    joined = jnp.concatenate([before, weights])
    block = lax.dynamic_slice(joined, (TAIL - TAIL // count * index,), (size,))
    if count == 16:
        padded = jnp.pad(last.reshape(4, D), ((0, 12), (0, 0)))
        block = swap_wide(block.reshape(D, D), index)
        blocks, tail, *attended = gather_attend(block, padded, tokens, segments)
        norms = tail[:4].astype(f32)
    else:
        natural = lax.all_gather(block.reshape(-1, D), "zero", axis=0, tiled=True)
        parts = natural.reshape(4, 4 * D, D)
        wide = [to_wide(parts[k].reshape(D, FF)) for k in (1, 2)]
        blocks = jnp.stack([parts[0].reshape(2, 2, D, D), *wide, parts[3].reshape(2, 2, D, D)])
        norms = lax.psum(jnp.where(index == count - 1, last.astype(f32), 0.0), "zero").reshape(4, D)
        attended = attend(tokens, blocks, segments)
    return blocks, norms, *attended


def back_and_scatter(blocks, segments, tokT, qkv, mixed, log_sum, grad_mixed, first_grad, branch_grad, norm_grads,
                     down_grad, wide_grad):
    count = lax.axis_size("zero")
    index = lax.axis_index("zero")
    if count == 16:
        input_grad, joined = reduce_back(
            wide_grad, down_grad, blocks, qkv, grad_mixed, mixed, log_sum, tokT, branch_grad, first_grad,
            norm_grads, segments,
        )
        joined = joined.reshape(-1)
    else:
        square, input_grad = attend_back(
            blocks, segments, tokT, qkv, mixed, log_sum, grad_mixed, first_grad, branch_grad
        )
        natural = [from_wide(wide_grad[k]).reshape(4 * D, D) for k in (0, 1)]
        natural = jnp.concatenate([square.reshape(4 * D, D), *natural, down_grad.reshape(4 * D, D)])
        block = lax.psum_scatter(natural, "zero", scatter_dimension=0, tiled=True)
        block = lax.psum(block.astype(f32), "dp")
        tail = lax.psum(norm_grads, ("dp", "zero"))
        flat = block.reshape(-1)
        after = lax.ppermute(flat[:TAIL], "zero", [(k + 1, k) for k in range(count - 1)])
        joined = jnp.concatenate([flat, jnp.where(index == count - 1, tail.reshape(-1), after)])
    shard = 16 * SQUARE // count + TAIL // count
    return input_grad, lax.dynamic_slice(joined, (TAIL // count * index,), (shard,))


def local(tokens, segments, cotangent, master, moment_one, moment_two):
    blocks, norms, tokT, qkv, mixed, log_sum = gather_and_attend(master, tokens, segments)
    output, first_grad, grad_mixed, branch_grad, norm_grads, down_grad, wide_grad = feed(
        tokens, cotangent, mixed, blocks, norms
    )
    input_grad, grad_shard = back_and_scatter(
        blocks, segments, tokT, qkv, mixed, log_sum, grad_mixed, first_grad, branch_grad, norm_grads,
        down_grad.reshape(2, 2, D, D), wide_grad.reshape(2, 2, 2, D, D),
    )
    grad_shard = grad_shard / (lax.axis_size("zero") * lax.axis_size("dp"))
    first = beta_one * moment_one + (1.0 - beta_one) * grad_shard
    second = beta_two * moment_two + (1.0 - beta_two) * grad_shard * grad_shard
    update = first / correct_one / (jnp.sqrt(second / correct_two) + adam_eps)
    master_new = master - learn_rate * (update + weight_decay * master)
    return (
        output,
        input_grad,
        grad_shard,
        first,
        second,
        master_new,
        master_new.astype(jnp.bfloat16),
    )


def solution(mesh):
    return jax.shard_map(
        local,
        mesh=mesh,
        in_specs=(
            P(("dp", "zero"), None),
            P(("dp", "zero")),
            P(("dp", "zero"), None),
            P("zero"),
            P("zero"),
            P("zero"),
        ),
        out_specs=(
            P(("dp", "zero"), None),
            P(("dp", "zero"), None),
            P("zero"),
            P("zero"),
            P("zero"),
            P("zero"),
            P("zero"),
        ),
        check_vma=False,
    )
```

```python
import functools

import jax
import jax.numpy as jnp
from jax import lax
from jax.sharding import PartitionSpec as P
import jax.experimental.pallas as pl
import jax.experimental.pallas.tpu as pltpu

D = 768
HEADS = 12
HEAD = 64
FF = 3072
LEN = 1024


learn_rate = 0.02
beta_one = 0.9
beta_two = 0.999
adam_eps = 1e-08
weight_decay = 0.01
correct_one = 1.0 - 0.9**10
correct_two = 1.0 - 0.999**10
norm_eps = 1e-06
inv_root_two = 0.7071067811865476
inv_root_tau = 0.3989422804014327


bf16=jnp.bfloat16; f32=jnp.float32
FAR=1e33
VM=pl.BlockSpec(memory_space=pltpu.VMEM)

def dot(a,b): return lax.dot_general(a,b,(((1,),(0,)),((),())),preferred_element_type=f32)
def dot_tn(a,b): return lax.dot_general(a,b,(((0,),(0,)),((),())),preferred_element_type=f32)
def dot_nt(a,b): return lax.dot_general(a,b,(((1,),(1,)),((),())),preferred_element_type=f32)

def slope(h):
    return jnp.exp2(-8.0/HEADS*(jnp.full((1,1),h,jnp.int32).astype(f32)+1.0))

def fill_distance(dist,seg_col,seg_row):
    @pl.loop(0,LEN//128)
    def _(k):
        r=pl.ds(pl.multiple_of(k*128,128),128)
        kk=(lax.broadcasted_iota(jnp.int32,(128,LEN),0)+k*128)
        qq=lax.broadcasted_iota(jnp.int32,(128,LEN),1)
        d=jnp.abs(kk-qq).astype(f32)
        dist[r]=jnp.where(seg_col[r]==seg_row[...],d,FAR)

QB=256
def project_all(w,tokT,qkv):
    @pl.loop(0,3)
    def _(n):
        @pl.loop(0,3)
        def _(t):
            c=pl.ds(pl.multiple_of(t*256,256),256)
            qkv[n,c]=dot_tn(w[0,n//2,n%2,:,c],tokT[...]).astype(bf16)

def attend_head(h,dist,qkv,mixb,lse):
    rows=pl.ds(pl.multiple_of(h*HEAD,HEAD),HEAD)
    keys=qkv[1,rows].astype(f32).T.astype(bf16)
    s=dot(keys,qkv[0,rows]*bf16(0.125))-slope(h)*dist[...]
    top=jnp.max(s,0,keepdims=True)
    e=jnp.exp(s-top)
    total=jnp.sum(e,0,keepdims=True)
    mixb[rows]=(dot(qkv[2,rows],e.astype(bf16))/total).astype(bf16)
    lse[h]=top+jnp.log(total)

def attend_kernel(tokens,w,seg_col,seg_row,tokT,qkv,mixb,lse,dist):
    tokT[...]=tokens[...].astype(f32).T.astype(bf16)
    fill_distance(dist,seg_col,seg_row)
    project_all(w,tokT,qkv)
    @pl.loop(0,HEADS)
    def _(h):
        attend_head(h,dist,qkv,mixb,lse)

def attend_shapes():
    S=jax.ShapeDtypeStruct
    return [S((D,LEN),bf16),S((3,D,LEN),bf16),S((D,LEN),bf16),S((HEADS,1,LEN),f32)]

def attend(tokens,w,seg):
    return pl.pallas_call(attend_kernel,grid=(1,),
        in_specs=[VM,pl.BlockSpec((1,2,2,D,D),lambda i:(0,0,0,0,0)),VM,VM],out_specs=[VM]*4,
        out_shape=attend_shapes(),
        scratch_shapes=[pltpu.VMEM((LEN,LEN),f32)],
        compiler_params=pltpu.CompilerParams(vmem_limit_bytes=58<<20),name="attend")(tokens,w,seg.reshape(LEN,1),seg.reshape(1,LEN))

def attend_back_kernel(w,seg_col,seg_row,tokT,qkv,mixb,lse,dO,first,gbranch,g0,grad_in,dist,kn,vn,p_all,ds_all,dqT,dkT,dvT):
    fill_distance(dist,seg_col,seg_row)
    @pl.loop(0,HEADS)
    def _(h):
        rows=pl.ds(pl.multiple_of(h*HEAD,HEAD),HEAD)
        kn[...]=qkv[1,rows].astype(f32).T.astype(bf16)
        vn[...]=qkv[2,rows].astype(f32).T.astype(bf16)
        m=slope(h)
        for b in range(LEN//QB):
            cols=pl.ds(b*QB,QB)
            q=qkv[0,rows,cols]*bf16(0.125)
            s=dot(kn[...],q)-m*dist[:,cols]
            p=jnp.exp(s-lse[h,:,cols])
            do=dO[rows,cols]
            delta=jnp.sum(do.astype(f32)*mixb[rows,cols].astype(f32),0,keepdims=True)
            dp=dot(vn[...],do)
            p_all[:,cols]=p.astype(bf16)
            ds=(p*(dp-delta)).astype(bf16)
            ds_all[:,cols]=ds
            dqT[rows,cols]=(dot(qkv[1,rows],ds)*0.125).astype(bf16)
        dvT[rows]=dot_nt(dO[rows],p_all[...]).astype(bf16)
        dkT[rows]=(dot_nt(qkv[0,rows],ds_all[...])*0.125).astype(bf16)
    g0[1,1]=dot(mixb[...],gbranch[...]).astype(bf16)
    for n,g in enumerate((dqT,dkT,dvT)):
        g0[n//2,n%2]=dot_nt(tokT[...],g[...]).astype(bf16)
    @pl.loop(0,4)
    def _(t):
        c=pl.ds(pl.multiple_of(t*256,256),256)
        acc=dot(w[0,0,0],dqT[:,c])+dot(w[0,0,1],dkT[:,c])+dot(w[0,1,0],dvT[:,c])
        grad_in[c]=first[c]+acc.T

def attend_back(w,seg,tokT,qkv,mixb,lse,dO,first,gbranch):
    B=lambda: pltpu.VMEM((D,LEN),bf16)
    return pl.pallas_call(attend_back_kernel,grid=(1,),
        in_specs=[pl.BlockSpec((1,2,2,D,D),lambda i:(0,0,0,0,0))]+[VM]*9,out_specs=[VM]*2,
        out_shape=[jax.ShapeDtypeStruct((2,2,D,D),bf16),jax.ShapeDtypeStruct((LEN,D),f32)],
        scratch_shapes=[pltpu.VMEM((LEN,LEN),f32),pltpu.VMEM((LEN,HEAD),bf16),pltpu.VMEM((LEN,HEAD),bf16),pltpu.VMEM((LEN,LEN),bf16),pltpu.VMEM((LEN,LEN),bf16),B(),B(),B()],
        compiler_params=pltpu.CompilerParams(vmem_limit_bytes=60<<20),name="attend_back")(w,seg.reshape(LEN,1),seg.reshape(1,LEN),tokT,qkv,mixb,lse,dO,first,gbranch)

TB=256
def feed_kernel(tokens,cot,mixb,wo,w1,w2,w3,norms,output,first,dO,gbranch,ng,gdown,gwide,inner,wide,gffn,fa,fb,acc,hid):
    step=pl.program_id(0)
    gain1=norms[0:1]; shift1=norms[1:2]; gain2=norms[2:3]; shift2=norms[3:4]
    def stats(v):
        c=v-jnp.mean(v,-1,keepdims=True)
        r=lax.rsqrt(jnp.mean(c*c,-1,keepdims=True)+norm_eps)
        return c*r,r
    def back(e,n,r):
        return r*(e-jnp.mean(e,-1,keepdims=True)-n*jnp.mean(e*n,-1,keepdims=True))
    W=lambda p,j: (w1,w2)[p-1][0,:,j].reshape(D,D)
    WD=lambda j: w3[0,j].reshape(D,D)
    WO=lambda: wo[0,0].reshape(D,D)
    @pl.when(step==0)
    def _(): ng[...]=jnp.zeros_like(ng)
    @pl.when(step<LEN//TB)
    def _():
        rows=pl.ds(pl.multiple_of(step*TB,TB),TB)
        branch=dot_tn(mixb[...],WO())
        n1,r1=stats(tokens[...].astype(f32)+branch)
        l1=n1*gain1+shift1
        inner[rows]=l1.astype(bf16)
        acc[...]=l1
        @pl.loop(0,4,unroll=2)
        def _(j):
            inn=inner[rows]
            ga=dot(inn,W(1,j)); up=dot(inn,W(2,j))
            cum=0.5*(1.0+lax.erf(ga*inv_root_two))
            gel=ga*cum
            fb[j]=gel
            fa[j]=up*(cum+ga*(jnp.exp(-0.5*ga*ga)*inv_root_tau))
            h=(gel*up).astype(bf16)
            hid[j,rows]=h
            acc[...]+=dot(h,WD(j))
        n2,r2=stats(acc[...])
        output[...]=(n2*gain2+shift2).astype(bf16)
        c=cot[...].astype(f32)
        ng[2:3]+=jnp.sum(c*n2,0,keepdims=True)
        ng[3:4]+=jnp.sum(c,0,keepdims=True)
        mid=back(c*gain2,n2,r2)
        gffn[rows]=mid.astype(bf16)
        acc[...]=mid
        @pl.loop(0,4,unroll=2)
        def _(j):
            gh=dot_nt(gffn[rows],WD(j))
            a=(gh*fa[j]).astype(bf16); b=(gh*fb[j]).astype(bf16)
            wide[j,rows]=a; wide[4+j,rows]=b
            acc[...]+=dot_nt(a,W(1,j))+dot_nt(b,W(2,j))
        gl=acc[...]
        ng[0:1]+=jnp.sum(gl*n1,0,keepdims=True)
        ng[1:2]+=jnp.sum(gl,0,keepdims=True)
        gfirst=back(gl*gain1,n1,r1)
        first[...]=gfirst
        gb=gfirst.astype(bf16)
        gbranch[...]=gb
        dO[...]=dot_nt(WO(),gb).astype(bf16)
    def put(g,v):
        g[...]=v.astype(bf16).reshape(g.shape)
    base=LEN//TB
    @pl.when(jnp.logical_and(step>=base,step<base+4))
    def _(): put(gdown,dot_tn(hid[step-base],gffn[...]))
    @pl.when(jnp.logical_and(step>=base+4,step<base+12))
    def _(): put(gwide,dot_tn(inner[...],wide[step-base-4]))

def feed(tokens,cot,mixb,w,norms):
    n=LEN//TB
    last=n-1
    row=lambda i:(jnp.minimum(i,last),0)
    col=lambda i:(0,jnp.minimum(i,last))
    one=pl.Buffered(1)
    S=jax.ShapeDtypeStruct
    V=lambda s,d=bf16: pltpu.VMEM(s,d)
    clip=lambda v,a,b: jnp.minimum(jnp.maximum(v,a),b)
    return pl.pallas_call(feed_kernel,grid=(n+12,),
        in_specs=[pl.BlockSpec((TB,D),row),pl.BlockSpec((TB,D),row),pl.BlockSpec((D,TB),col),
            pl.BlockSpec((1,1,4,D//4,D),lambda i:(0,3,0,0,0),pipeline_mode=one),*[pl.BlockSpec((1,4,4,D//4,D),lambda i,p=p:(p,0,0,0,0),pipeline_mode=one) for p in (1,2,3)],pl.BlockSpec((4,D),lambda i:(0,0))],
        out_specs=[pl.BlockSpec((TB,D),row),pl.BlockSpec((TB,D),row),pl.BlockSpec((D,TB),col),pl.BlockSpec((TB,D),row),
            pl.BlockSpec((4,D),lambda i:(0,0)),
            pl.BlockSpec((1,D,D),lambda i:(clip(i-n,0,3),0,0)),
            pl.BlockSpec((1,4,1,D//4,D),lambda i:(clip((i-n-4)//4,0,1),0,clip(i-n-4,0,7)%4,0,0))],
        out_shape=[S((LEN,D),bf16),S((LEN,D),f32),S((D,LEN),bf16),S((LEN,D),bf16),S((4,D),f32),S((4,D,D),bf16),S((2,4,4,D//4,D),bf16)],
        scratch_shapes=[V((LEN,D)),V((8,LEN,D)),V((LEN,D)),V((4,TB,D),f32),V((4,TB,D),f32),V((TB,D),f32),V((4,LEN,D))],
        compiler_params=pltpu.CompilerParams(vmem_limit_bytes=62<<20),name="feed")(tokens,cot,mixb,*[w.reshape(4,4,4,D//4,D)]*4,norms)

MESH = pl.DeviceIdType.MESH
ALL = slice(None)
HALF = D // 2
B_PART, C_PART = 48, 80
P_PART = 48


def place():
    i = lax.axis_index("zero")
    c = lax.axis_index("dp")
    return i, c, i // 4, (i // 2) % 2, i % 2


def partners(i, c, z, y, x):
    return (c, i + 1 - 2 * x), (c, i + 2 - 4 * y), (1 - c, i), (c, i + 4), (c, i - 4)


def when(cond, fn):
    @pl.when(cond)
    def _():
        fn()


def enter(i, c, z, y, x):
    barrier = pltpu.get_barrier_semaphore()
    xp, yp, sib, up, down = partners(i, c, z, y, x)

    def signal(peer):
        pl.semaphore_signal(barrier, inc=1, device_id=peer, device_id_type=MESH)

    for peer in (xp, yp, sib):
        signal(peer)
    when(z > 0, lambda: signal(down))
    when(z < 3, lambda: signal(up))
    pl.semaphore_wait(barrier, 3 + jnp.minimum(z, 1) + jnp.minimum(3 - z, 1))


def pick(z, values):
    out = jnp.int32(values[3])
    for k in (2, 1, 0):
        out = jnp.where(z == k, jnp.int32(values[k]), out)
    return out


def run_plan(z, words, ops):
    count = len(words[0])
    held = [pick(z, [words[k][n] for k in range(4)]) for n in range(count)]

    @pl.loop(0, count)
    def _(n):
        word = held[0]
        for k in range(1, count):
            word = jnp.where(n == k, held[k], word)

        @pl.loop(0, 3)
        def _(m):
            code = jnp.where(m == 0, word, jnp.where(m == 1, word // 256, word // 65536)) % 256
            kind, e = code // 16, code % 16
            branch(kind, e, 0, ops)


def branch(kind, e, low, ops):
    if len(ops) == 1:
        ops[0](e)
        return
    half = len(ops) // 2

    def lower():
        branch(kind, e, low, ops[:half])

    def upper():
        branch(kind, e, low + half, ops[half:])

    lax.cond(kind < low + half, lower, upper)


def gather_attend_kernel(blk, last, tokens, seg_col, seg_row, result, tail, tokT, qkv, mixb, lse,
                         held, dist, own_sem, out_sem, pzs, pzr, pfs, pfr, pgs, pgr, p_s, p_r,
                         b1s, b1r, c1u, c1d, c1r, b2u, b2d, b2r, c2s, c2r, b3s, b3r, c3s, c3r, ss, sr, ts, tr):
    i, c, z, y, x = place()
    xp, yp, sib, up, down = partners(i, c, z, y, x)
    half = c * HALF
    other = (1 - c) * HALF
    local = pltpu.make_async_copy(blk, held.at[z, y, x], own_sem)
    local.start()
    enter(i, c, z, y, x)

    def remote(ref, peer, s, r):
        return pltpu.make_async_remote_copy(
            src_ref=ref, dst_ref=ref, send_sem=s, recv_sem=r, device_id=peer, device_id_type=MESH
        )

    def by_parity(k, fn):
        when(k % 2 == 0, lambda: fn(False))
        when(k % 2 == 1, lambda: fn(True))

    def rp(k, base):
        return pl.ds(pl.multiple_of(base + k * P_PART, 16), P_PART)

    def z_ref(k, base=half):
        return held.at[0, y, x, rp(k, base)]

    def f_ref(k, odd, base=half):
        if odd:
            return held.at[0, 1 - y, x, rp(k, base)]
        return held.at[0, y, 1 - x, rp(k, base)]

    def g_ref(k, odd, mine, base=half):
        if odd:
            return held.at[0, ALL, x if mine else 1 - x, rp(k, base)]
        return held.at[0, y if mine else 1 - y, ALL, rp(k, base)]

    def PZ(k):
        return remote(z_ref(k), up, pzs.at[k], pzr.at[k])

    def PF(k, odd):
        return remote(z_ref(k), yp if odd else xp, pfs.at[k], pfr.at[k])

    def PG(k, odd):
        return remote(g_ref(k, odd, True), xp if odd else yp, pgs.at[k], pgr.at[k])

    def PS(ref, n):
        return remote(ref, sib, p_s.at[n], p_r.at[n])

    def op_p0z(k):
        def arrive():
            PZ(k).wait_recv()
            PS(z_ref(k), k).start()

        when(z > 0, arrive)
        when(z < 3, lambda: PZ(k).start())
        by_parity(k, lambda odd: PF(k, odd).start())

    def op_p0f(k):
        def turn(odd):
            PF(k, odd).wait_recv()
            PG(k, odd).start()
            PS(f_ref(k, odd), 8 + k).start()

        by_parity(k, turn)

    def op_p0g(k):
        def turn(odd):
            PG(k, odd).wait_recv()
            PS(g_ref(k, odd, False), 16 + k).start()

        by_parity(k, turn)

    split = lambda e: (e // 3 + 1, e % 3)

    def rb(s, base):
        return pl.ds(pl.multiple_of(base + s * B_PART, 16), B_PART)

    def rc(s, base):
        return pl.ds(pl.multiple_of(base + 3 * B_PART + s * C_PART, 16), C_PART)

    def b1_ref(s, yy, base=half):
        return held.at[z, yy, x, rb(s, base)]

    def b2_ref(t, s, xx, base=half):
        return held.at[t, ALL, xx, rb(s, base)]

    def c1_ref(t, s, base=half):
        return held.at[t, y, x, rc(s, base)]

    def c2_ref(t, s, xx, base=half):
        return held.at[t, y, xx, rc(s, base)]

    def c3_ref(t, s, yy, base=half):
        return held.at[t, yy, ALL, rc(s, base)]

    B1 = lambda s: remote(b1_ref(s, y), yp, b1s.at[s], b1r.at[s])
    C1U = lambda t, s, e: remote(c1_ref(t, s), up, c1u.at[e], c1r.at[e])
    C1D = lambda t, s, e: remote(c1_ref(t, s), down, c1d.at[e], c1r.at[e])
    B2U = lambda t, s, e: remote(b2_ref(t, s, x), up, b2u.at[e], b2r.at[e])
    B2D = lambda t, s, e: remote(b2_ref(t, s, x), down, b2d.at[e], b2r.at[e])
    C2 = lambda t, s, e: remote(c2_ref(t, s, x), xp, c2s.at[e], c2r.at[e])
    B3 = lambda t, s, e: remote(b2_ref(t, s, x), xp, b3s.at[e], b3r.at[e])
    C3 = lambda t, s, e: remote(c3_ref(t, s, y), yp, c3s.at[e], c3r.at[e])
    S = lambda ref, n: remote(ref, sib, ss.at[n], sr.at[n])

    def op_own(e):
        t, s = split(e)
        B1(s).start()
        C1D(t, s, e).start()

    def op_ownup(e):
        t, s = split(e)

        def go():
            C1U(t, s, e).start()
            B2U(t, s, e).start()

        when(z < 3, go)

    def op_b1(e):
        t, s = split(e)
        B1(s).wait_recv()
        B2D(t, s, e).start()
        S(b1_ref(s, 1 - y), 45 + s).start()

    def op_cx(e):
        t, s = split(e)
        C2(t, s, e).start()

    def op_bx(e):
        t, s = split(e)
        B3(t, s, e).start()

    def op_c1(e):
        t, s = split(e)
        C1U(t, s, e).wait_recv()
        when(jnp.logical_and(t < z, z < 3), lambda: C1U(t, s, e).start())
        when(jnp.logical_and(t > z, z > 0), lambda: C1D(t, s, e).start())
        S(c1_ref(t, s), e).start()

    def op_b2(e):
        t, s = split(e)
        B2U(t, s, e).wait_recv()
        when(jnp.logical_and(t < z, z < 3), lambda: B2U(t, s, e).start())
        when(jnp.logical_and(t > z, z > 0), lambda: B2D(t, s, e).start())
        S(b2_ref(t, s, x), 9 + e).start()

    def op_c2(e):
        t, s = split(e)
        C2(t, s, e).wait_recv()
        C3(t, s, e).start()
        S(c2_ref(t, s, 1 - x), 18 + e).start()

    def op_b3(e):
        t, s = split(e)
        B3(t, s, e).wait_recv()
        S(b2_ref(t, s, 1 - x), 27 + e).start()

    def op_c3(e):
        t, s = split(e)
        C3(t, s, e).wait_recv()
        S(c3_ref(t, s, 1 - y), 36 + e).start()

    def op_proj(n):
        def arrive():
            @pl.loop(0, 8)
            def _(k):
                def got(odd):
                    PS(f_ref(k, odd, other), 8 + k).wait_recv()
                    PS(g_ref(k, odd, False, other), 16 + k).wait_recv()

                by_parity(k, got)
                when(z > 0, lambda: PS(z_ref(k, other), k).wait_recv())

        when(n == 0, arrive)

        @pl.loop(0, 3)
        def _(t):
            cols = pl.ds(pl.multiple_of(t * 256, 256), 256)
            qkv[n, cols] = dot_tn(held[0, n // 2, n % 2, :, cols], tokT[...]).astype(bf16)

    def op_head(h):
        attend_head(h, dist, qkv, mixb, lse)

    line = jnp.logical_and(y == 1, x == 1)
    source = jnp.logical_and(line, z == 3)

    def T(peer, n):
        return remote(tail, peer, ts.at[n], tr.at[0])

    def leave(t):
        return pltpu.make_async_copy(held.at[t], result.at[t], out_sem.at[t])

    def op_other(e):
        def tail_z():
            def go():
                when(z < 3, lambda: T(down, 0).wait_recv())
                when(z > 0, lambda: T(down, 0).start())
                T(yp, 1).start()

            when(line, go)

        def tail_x():
            def go():
                when(y == 0, lambda: T(yp, 1).wait_recv())
                T(xp, 2).start()

            when(x == 1, go)

        def out():
            t = e - 2

            def others():
                @pl.loop(0, 3)
                def _(s):
                    n = (t - 1) * 3 + s

                    def theirs():
                        S(c1_ref(t, s, other), n).wait_recv()
                        S(b2_ref(t, s, x, other), 9 + n).wait_recv()

                    when(t != z, theirs)
                    when(t == z, lambda: S(b1_ref(s, 1 - y, other), 45 + s).wait_recv())
                    S(c2_ref(t, s, 1 - x, other), 18 + n).wait_recv()
                    S(b2_ref(t, s, 1 - x, other), 27 + n).wait_recv()
                    S(c3_ref(t, s, 1 - y, other), 36 + n).wait_recv()

            when(t > 0, others)
            leave(t).start()

        def prepare():
            tokT[...] = tokens[...].astype(f32).T.astype(bf16)
            fill_distance(dist, seg_col, seg_row)

        when(e == 0, tail_z)
        when(e == 1, tail_x)
        when(jnp.logical_and(e >= 2, e < 6), out)
        when(e == 6, prepare)

    when(source, lambda: tail.__setitem__(Ellipsis, last[...]))
    local.wait()
    run_plan(z, GATHER_PLAN, [op_p0z, op_p0f, op_p0g, op_own, op_ownup, op_b1, op_bx, op_c1, op_b2, op_c2, op_b3,
                              op_c3, op_proj, op_head, op_other, op_cx])

    when(x == 0, lambda: T(xp, 2).wait_recv())
    when(x == 1, lambda: T(xp, 2).wait_send())

    def tail_sent():
        T(yp, 1).wait_send()
        when(z > 0, lambda: T(down, 0).wait_send())

    when(line, tail_sent)

    @pl.loop(0, 8)
    def _(k):
        def gone(odd):
            PF(k, odd).wait_send()
            PG(k, odd).wait_send()
            PS(f_ref(k, odd), 8 + k).wait_send()
            PS(g_ref(k, odd, False), 16 + k).wait_send()

        by_parity(k, gone)
        when(z < 3, lambda: PZ(k).wait_send())
        when(z > 0, lambda: PS(z_ref(k), k).wait_send())

    @pl.loop(0, 9)
    def _(e):
        t, s = split(e)
        C2(t, s, e).wait_send()
        B3(t, s, e).wait_send()
        C3(t, s, e).wait_send()

        def ups():
            C1U(t, s, e).wait_send()
            B2U(t, s, e).wait_send()

        def downs():
            C1D(t, s, e).wait_send()
            B2D(t, s, e).wait_send()

        when(jnp.logical_and(t <= z, z < 3), ups)
        when(jnp.logical_and(t >= z, z > 0), downs)

        def mine():
            B1(s).wait_send()
            S(b1_ref(s, 1 - y), 45 + s).wait_send()

        def theirs():
            S(c1_ref(t, s), e).wait_send()
            S(b2_ref(t, s, x), 9 + e).wait_send()

        when(t == z, mine)
        when(t != z, theirs)
        S(c2_ref(t, s, 1 - x), 18 + e).wait_send()
        S(b2_ref(t, s, 1 - x), 27 + e).wait_send()
        S(c3_ref(t, s, 1 - y), 36 + e).wait_send()

    for t in range(4):
        leave(t).wait()


def gather_attend(blk, last, tokens, seg):
    Q = pltpu.SemaphoreType.DMA
    any_space = pl.BlockSpec(memory_space=pl.ANY)
    counts = [8] * 6 + [24, 24, 3, 3] + [9] * 12 + [48, 48, 3, 1]
    return pl.pallas_call(
        gather_attend_kernel,
        in_specs=[any_space, VM, VM, VM, VM],
        out_specs=[any_space] + [VM] * 5,
        out_shape=[
            jax.ShapeDtypeStruct((4, 2, 2, D, D), bf16), jax.ShapeDtypeStruct((16, D), bf16),
            *attend_shapes(),
        ],
        scratch_shapes=[
            pltpu.VMEM((4, 2, 2, D, D), bf16), pltpu.VMEM((LEN, LEN), f32),
            Q, Q((4,)), *[Q((n,)) for n in counts],
        ],
        compiler_params=pltpu.CompilerParams(
            collective_id=1, has_side_effects=True, vmem_limit_bytes=58 << 20
        ),
        name="gather_attend",
    )(blk, last, tokens, seg.reshape(LEN, 1), seg.reshape(1, LEN))


PLANE_ORDER = (3, 1, 2)
BACK_PLAN = (
    (
        7374723, 460401, 29192, 131366, 2556931, 4593157, 2650951, 4724512, 2192448, 7684376,
        8397602, 2392705, 4329744, 9605520, 4428581, 7750980, 5650230, 7803479, 5779512, 7869264,
        10572081, 10713364, 3308053, 10657843, 8082258, 5518644, 8708693, 11568773, 11776689, 9802960,
        13735830, 10855634, 10928339, 11919527, 12760257, 14792630, 12960963, 15714246, 15724527,
    ),
    (
        7374723, 460401, 57352, 7471617, 328707, 2565654, 2627443, 2103412, 4671009, 8487029,
        2232450, 4727843, 9605520, 7737747, 3543589, 3635008, 1261880, 7881538, 1351984, 7947588,
        5723811, 8007957, 5265568, 10629938, 14831995, 11568516, 11699889, 5460659, 9802848, 6395798,
        5518434, 10801205, 12604837, 10987217, 11911873, 11981492, 13878199, 14796228, 15714246,
    ),
    (
        7374723, 460401, 57352, 7471617, 328707, 1451814, 1517683, 2170996, 8418584, 2261633,
        4212259, 9539600, 2397074, 1130823, 4748837, 1193538, 3700535, 3176467, 10571897, 1328035,
        3228794, 4563025, 8066354, 5722710, 11776177, 8708770, 8815960, 9752754, 9934485, 13746624,
        13812674, 3384740, 10987060, 11850549, 11974084, 6535109, 13002084, 14767047, 15684948,
    ),
    (
        7374723, 460401, 29192, 131366, 2556694, 7537924, 7612439, 2168864, 7684416, 8392738,
        2327169, 3556162, 2363766, 2462096, 9638546, 4474694, 7812933, 3688467, 7884848, 5320980,
        10556793, 8016434, 8102816, 8708770, 6719109, 11649200, 9802945, 11704214, 12825538, 13658215,
        5678500, 13719639, 11904934, 12960948, 13022930, 3393463, 5518419, 13849909, 15720928,
    ),
)

GATHER_PLAN = (
    (
        131328, 328707, 15075078, 1184016, 15757331, 7410964, 1513201, 2224754, 6324256, 7545379,
        2396403, 2449793, 6455846, 16020625, 12697639, 9601986, 10548597, 11645027, 9687266, 13760118,
        6594948, 6653394, 10671026, 14940023, 13939604, 16283797, 10716885, 8902246, 11834983, 6850775,
        10805464, 10869173, 14801636, 14399127, 10987160, 12101815, 15724517, 15724527,
    ),
    (
        3207664, 15086129, 5279744, 5308787, 156000, 7639378, 266243, 10487157, 8586928, 4196113,
        10568257, 1315446, 1475761, 2196755, 1406752, 16127779, 16053239, 7926517, 6579192, 2253413,
        6719013, 8857380, 2528871, 12763584, 9672584, 13689448, 13743764, 12046997, 13947794, 13998304,
        14070691, 11851684, 14263768, 14988706, 14395098, 11708385, 12101859, 15724517,
    ),
    (
        16119027, 3486771, 9655270, 5535331, 9721188, 30565, 7902465, 242434, 296611, 8889349,
        504838, 4460867, 10848325, 1208336, 14988564, 1277974, 2168177, 16183319, 16316401, 6776416,
        6390120, 7479331, 2237938, 2581122, 2527268, 12763584, 14848406, 9953488, 10015152, 10532562,
        10933459, 11002325, 14145201, 14202792, 9623969, 14345656, 11721634, 15724515,
    ),
    (
        16316406, 3684150, 9852646, 6772582, 6854488, 11927704, 173569, 12035843, 11011332, 462854,
        4670994, 15054920, 7541777, 1381142, 2105731, 15931252, 2319348, 2253956, 16086309, 8726308,
        2528101, 12763584, 10715360, 15757460, 6353265, 13677538, 10781153, 9818465, 13824626, 13870516,
        9462402, 14988756, 14079377, 14135456, 9623713, 14342577, 11721634, 15724515,
    ),
)


Q_PART = 96
COLS = D // 2


def reduce_back_kernel(wide, down, w, qkv_in, dO, mixb, lse, tokT, gbranch, first, norm_in, seg_col, seg_row,
                       grad_in, flat_out, own, sl, lc3, lc2, lcz, lczx, lb3, lbz, lbzx, lb1, lf, lg, lz, stage,
                       dist, p_all, ds_all, wv, qkv, fchunk, flat, nacc, nx, ny, nz, nc,
                       own_sem, qkv_sem, w_sem, f_sem, g_sem, o_sem, sib_s, sib_r, st_s, st_r,
                       c3s, c3r, b3s, b3r, c2s, c2r, bus, bur, bds, bdr, cus, cur, cds, cdr, b1s, b1r,
                       fs, fr, gs, gr, zs_, zr_, ns, nr, share_s, share_r, aft_s, aft_r):
    i, c, z, y, x = place()
    xp, yp, sib, up, down_peer = partners(i, c, z, y, x)
    base = c * HALF
    mine = pl.ds(pl.multiple_of(base, 16), HALF)
    other = pl.ds(pl.multiple_of((1 - c) * HALF, 16), HALF)
    planes = [wide.at[0], wide.at[1], down]

    def remote(src, dst, peer, s, r):
        return pltpu.make_async_remote_copy(
            src_ref=src, dst_ref=dst, send_sem=s, recv_sem=r, device_id=peer, device_id_type=MESH
        )

    def local_in(t):
        return pltpu.make_async_copy(planes[t - 1].at[:, :, mine], own.at[t], own_sem.at[t])

    def sib_in(t):
        return remote(planes[t - 1].at[:, :, other], sl.at[t], sib, sib_s.at[t], sib_r.at[t])

    for t in PLANE_ORDER:
        local_in(t).start()
    qkv_copy = pltpu.make_async_copy(qkv_in, qkv, qkv_sem)
    qkv_copy.start()
    enter_more(i, c, z, y, x)
    for t in PLANE_ORDER:
        sib_in(t).start()
    nacc[...] = norm_in[...]
    NX = remote(nacc, nx, xp, ns.at[0], nr.at[0])
    NY = remote(nacc, ny, yp, ns.at[1], nr.at[1])
    NZ = remote(nacc, nz, up, ns.at[2], nr.at[2])
    NC = remote(nacc, nc, sib, ns.at[3], nr.at[3])
    line = jnp.logical_and(x == 1, y == 1)
    last_line = jnp.logical_and(line, z == 3)
    when(x == 0, lambda: NX.start())
    fill_distance(dist, seg_col, seg_row)
    qkv_copy.wait()

    def rb(s, k=0, size=B_PART):
        return pl.ds(pl.multiple_of(s * B_PART + k, 16), size)

    def rc(s, k=0, size=C_PART):
        return pl.ds(pl.multiple_of(3 * B_PART + s * C_PART + k, 16), size)

    def add_rows(dst, src, rows):
        @pl.loop(0, rows // 16)
        def _(n):
            k = pl.multiple_of(n * 16, 16)
            a = dst(k)
            a[...] = a[...] + src(k)[...]

    r16 = lambda k: pl.ds(k, 16)
    split = lambda e: (e // 3 + 1, e % 3)

    def C3(t, s, e):
        return remote(own.at[t, 1 - y, :, rc(s)], lc3.at[e], yp, c3s.at[e], c3r.at[e])

    def B3(t, s, e):
        return remote(own.at[t, :, 1 - x, rb(s)], lb3.at[e], xp, b3s.at[e], b3r.at[e])

    def C2(t, s, e):
        return remote(own.at[t, y, 1 - x, rc(s)], lc2.at[e], xp, c2s.at[e], c2r.at[e])

    def BU(t, s, e):
        return remote(own.at[t, :, x, rb(s)], lbz.at[e], up, bus.at[e], bur.at[e])

    def BD(t, s, e, extra=False):
        return remote(own.at[t, :, x, rb(s)], lbzx.at[s] if extra else lbz.at[e], down_peer, bds.at[e], bdr.at[e])

    def CU(t, s, e):
        return remote(own.at[t, y, x, rc(s)], lcz.at[e], up, cus.at[e], cur.at[e])

    def CD(t, s, e, extra=False):
        return remote(own.at[t, y, x, rc(s)], lczx.at[s] if extra else lcz.at[e], down_peer, cds.at[e], cdr.at[e])

    def B1(s):
        return remote(own.at[z, 1 - y, x, rb(s)], lb1.at[s], yp, b1s.at[s], b1r.at[s])

    def op_sum(e):
        t, s = split(e)

        def arrive():
            for k in (1, 2, 3):
                def both(k=k):
                    local_in(k).wait()
                    sib_in(k).wait_recv()

                when(t == k, both)

        when(s == 0, arrive)
        add_rows(lambda k: own.at[t, :, :, rb(s, k, 16)], lambda k: sl.at[t, :, :, rb(s, k, 16)], B_PART)
        add_rows(lambda k: own.at[t, :, :, rc(s, k, 16)], lambda k: sl.at[t, :, :, rc(s, k, 16)], C_PART)
        C3(t, s, e).start()
        B3(t, s, e).start()

    def op_c3(e):
        t, s = split(e)
        C3(t, s, e).wait_recv()
        add_rows(lambda k: own.at[t, y, :, rc(s, k, 16)], lambda k: lc3.at[e, :, r16(k)], C_PART)
        C2(t, s, e).start()

    def op_b3(e):
        t, s = split(e)
        B3(t, s, e).wait_recv()
        add_rows(lambda k: own.at[t, :, x, rb(s, k, 16)], lambda k: lb3.at[e, :, r16(k)], B_PART)

    def op_c2(e):
        t, s = split(e)
        C2(t, s, e).wait_recv()
        add_rows(lambda k: own.at[t, y, x, rc(s, k, 16)], lambda k: lc2.at[e, r16(k)], C_PART)

    def op_bz(e):
        t, s = split(e)
        dst = lambda k: own.at[t, :, x, rb(s, k, 16)]

        def from_below():
            BU(t, s, e).wait_recv()
            add_rows(dst, lambda k: lbz.at[e, :, r16(k)], B_PART)

        when(jnp.logical_and(t >= z, z > 0), from_below)

        def from_above():
            BD(t, s, e).wait_recv()
            add_rows(dst, lambda k: lbz.at[e, :, r16(k)], B_PART)

        when(t < z, lambda: when(z < 3, from_above))

        def from_above_last():
            BD(t, s, e).wait_recv()
            add_rows(dst, lambda k: lbzx.at[s, :, r16(k)], B_PART)

        when(jnp.logical_and(t == z, z < 3), from_above_last)
        when(t > z, lambda: BU(t, s, e).start())
        when(t == z - 1, lambda: BD(t, s, e, True).start())
        when(t < z - 1, lambda: BD(t, s, e).start())
        when(t == z, lambda: B1(s).start())

    def res(rows):
        return dist.at[rows, pl.ds(0, D)]

    def op_cz(e):
        t, s = split(e)
        dst = lambda k: own.at[t, y, x, rc(s, k, 16)]

        def from_below():
            CU(t, s, e).wait_recv()
            add_rows(dst, lambda k: lcz.at[e, r16(k)], C_PART)

        when(jnp.logical_and(t >= z, z > 0), from_below)

        def from_above():
            CD(t, s, e).wait_recv()
            add_rows(dst, lambda k: lcz.at[e, r16(k)], C_PART)

        when(t < z, lambda: when(z < 3, from_above))

        def from_above_last():
            CD(t, s, e).wait_recv()
            add_rows(dst, lambda k: lczx.at[s, r16(k)], C_PART)

        when(jnp.logical_and(t == z, z < 3), from_above_last)
        when(t > z, lambda: CU(t, s, e).start())
        when(t == z - 1, lambda: CD(t, s, e, True).start())
        when(t < z - 1, lambda: CD(t, s, e).start())

    def op_b1(e):
        t, s = split(e)
        B1(s).wait_recv()
        add_rows(lambda k: own.at[z, y, x, rb(s, k, 16)], lambda k: lb1.at[s, r16(k)], B_PART)

    def op_head(h):
        rows = pl.ds(pl.multiple_of(h * HEAD, HEAD), HEAD)
        keys = qkv[1, rows].astype(f32).T.astype(bf16)
        values = qkv[2, rows].astype(f32).T.astype(bf16)
        m = slope(h)
        grad_q = []
        for b in range(LEN // QB):
            cols = pl.ds(b * QB, QB)
            do = dO[rows, cols]
            s = dot(keys, qkv[0, rows, cols] * bf16(0.125)) - m * dist[:, cols]
            dp = dot(values, do)
            delta = jnp.sum(do.astype(f32) * mixb[rows, cols].astype(f32), 0, keepdims=True)
            p = jnp.exp(s - lse[h, :, cols])
            p_all[:, cols] = p.astype(bf16)
            ds = (p * (dp - delta)).astype(bf16)
            ds_all[:, cols] = ds
            grad_q.append((dot(qkv[1, rows], ds) * 0.125).astype(bf16))
        grad_k = (dot_nt(qkv[0, rows], ds_all[...]) * 0.125).astype(bf16)
        grad_v = dot_nt(dO[rows], p_all[...]).astype(bf16)
        for b in range(LEN // QB):
            qkv[0, rows, pl.ds(b * QB, QB)] = grad_q[b]
        qkv[1, rows] = grad_k
        qkv[2, rows] = grad_v

    def columns(g):
        return pl.ds(pl.multiple_of(g * COLS, 128), COLS)

    def stage_copy(e):
        g, n = e // 4, e % 4
        return remote(
            stage.at[e], sl.at[0, n // 2, n % 2, :, columns(g)], sib, st_s.at[e], st_r.at[e]
        )

    def op_dw(e):
        g, n = e // 4, e % 4
        cols = columns(g)

        def put(half, value):
            if half == 0:
                own[0, n // 2, n % 2, :, cols] = value.astype(bf16)
            else:
                stage[e] = value.astype(bf16)

        def inputs():
            right = qkv[n, pl.ds(pl.multiple_of(g * COLS, 128), COLS)]
            for half, rows in ((0, mine), (1, other)):
                put(half, dot_nt(tokT[rows], right))

        def output():
            right = gbranch[:, cols]
            for half, rows in ((0, mine), (1, other)):
                put(half, dot(mixb[rows], right))

        when(n < 3, inputs)
        when(n == 3, output)
        stage_copy(e).start()

    def rq(k, n=0, size=Q_PART):
        return pl.ds(pl.multiple_of(k * Q_PART + n, 16), size)

    def F0(e, g, k, odd):
        src = own.at[0, :, 1 - x, rq(k), columns(g)] if odd else own.at[0, 1 - y, :, rq(k), columns(g)]
        return remote(src, lf.at[e], xp if odd else yp, fs.at[e], fr.at[e])

    def G0(e, g, k, odd):
        if odd:
            return remote(own.at[0, 1 - y, x, rq(k), columns(g)], lg.at[e], yp, gs.at[e], gr.at[e])
        return remote(own.at[0, y, 1 - x, rq(k), columns(g)], lg.at[e], xp, gs.at[e], gr.at[e])

    def Z0(e, g, k):
        return remote(own.at[0, y, x, rq(k), columns(g)], lz.at[e], down_peer, zs_.at[e], zr_.at[e])

    def by_parity(k, fn):
        when(k % 2 == 0, lambda: fn(False))
        when(k % 2 == 1, lambda: fn(True))

    def op_sum0(e):
        g, k = e // 4, e % 4

        def arrive():
            @pl.loop(0, 4)
            def _(n):
                stage_copy(g * 4 + n).wait_recv()

        when(k == 0, arrive)
        add_rows(
            lambda n: own.at[0, :, :, rq(k, n, 16), columns(g)],
            lambda n: sl.at[0, :, :, rq(k, n, 16), columns(g)], Q_PART,
        )
        by_parity(k, lambda odd: F0(e, g, k, odd).start())

    def op_f0(e):
        g, k = e // 4, e % 4

        def turn(odd):
            F0(e, g, k, odd).wait_recv()
            if odd:
                dst = lambda n: own.at[0, :, x, rq(k, n, 16), columns(g)]
            else:
                dst = lambda n: own.at[0, y, :, rq(k, n, 16), columns(g)]
            add_rows(dst, lambda n: lf.at[e, :, r16(n)], Q_PART)
            G0(e, g, k, odd).start()

        by_parity(k, turn)

    def op_g0(e):
        g, k = e // 4, e % 4
        by_parity(k, lambda odd: G0(e, g, k, odd).wait_recv())
        add_rows(lambda n: own.at[0, y, x, rq(k, n, 16), columns(g)], lambda n: lg.at[e, r16(n)], Q_PART)

    def op_z0(e):
        g, k = e // 4, e % 4

        def arrive():
            Z0(e, g, k).wait_recv()
            add_rows(lambda n: own.at[0, y, x, rq(k, n, 16), columns(g)], lambda n: lz.at[e, r16(n)], Q_PART)

        when(z < 3, arrive)
        when(z > 0, lambda: Z0(e, g, k).start())

    def first_in(q):
        return pltpu.make_async_copy(first.at[pl.ds(pl.multiple_of(q * 256, 256), 256)], fchunk, f_sem)

    def grad_out(q):
        return pltpu.make_async_copy(fchunk, grad_in.at[pl.ds(pl.multiple_of(q * 256, 256), 256)], g_sem)

    def weight_in(n):
        target = (p_all.at[pl.ds(0, D), pl.ds(0, D)], ds_all.at[pl.ds(0, D), pl.ds(0, D)], wv)[n]
        return pltpu.make_async_copy(w.at[0, n // 2, n % 2], target, w_sem.at[n])

    def op_gin(q):
        def weights():
            for n in range(3):
                weight_in(n).wait()

        when(q == 0, weights)
        when(q > 0, lambda: grad_out(q - 1).wait())
        first_in(q).start()
        cols = pl.ds(pl.multiple_of(q * 256, 256), 256)
        d = pl.ds(0, D)
        acc = dot(p_all[d, d], qkv[0, :, cols]) + dot(ds_all[d, d], qkv[1, :, cols])
        acc = (acc + dot(wv[...], qkv[2, :, cols])).T
        first_in(q).wait()
        fchunk[...] += acc
        grad_out(q).start()

    def op_other(e):
        def norm_y():
            def go():
                NX.wait_recv()
                nacc[...] += nx[...]
                when(y == 0, lambda: NY.start())

            when(x == 1, go)

        def norm_z():
            def go():
                NY.wait_recv()
                nacc[...] += ny[...]

                def more():
                    NZ.wait_recv()
                    nacc[...] += nz[...]

                when(z > 0, more)
                when(z < 3, lambda: NZ.start())
                when(z == 3, lambda: NC.start())

            when(line, go)

        def load():
            for n in range(3):
                weight_in(n).start()

        when(e == 0, norm_y)
        when(e == 1, norm_z)
        when(e == 2, load)

    run_plan(z, BACK_PLAN, [op_sum, op_c3, op_b3, op_c2, op_bz, op_cz, op_b1, op_head, op_dw, op_sum0, op_f0,
                            op_g0, op_z0, op_gin, op_other])

    half = pl.ds(pl.multiple_of(base, 16), HALF)
    res(half)[...] = own[z, y, x].astype(f32)
    share = remote(res(half), res(half), sib, share_s, share_r)
    share.start()

    @pl.loop(0, 9)
    def _(e):
        t, s = split(e)
        C3(t, s, e).wait_send()
        B3(t, s, e).wait_send()
        C2(t, s, e).wait_send()

        def went_up():
            BU(t, s, e).wait_send()
            CU(t, s, e).wait_send()

        def went_down():
            BD(t, s, e).wait_send()
            CD(t, s, e).wait_send()

        when(t > z, went_up)
        when(t < z, went_down)
        when(t == z, lambda: B1(s).wait_send())

    @pl.loop(0, 8)
    def _(e):
        g, k = e // 4, e % 4
        stage_copy(e).wait_send()

        def gone(odd):
            F0(e, g, k, odd).wait_send()
            G0(e, g, k, odd).wait_send()

        by_parity(k, gone)
        when(z > 0, lambda: Z0(e, g, k).wait_send())

    for t in (1, 2, 3):
        sib_in(t).wait_send()
    when(x == 0, lambda: NX.wait_send())
    when(jnp.logical_and(x == 1, y == 0), lambda: NY.wait_send())
    when(jnp.logical_and(line, z < 3), lambda: NZ.wait_send())

    def norm_last():
        NC.wait_recv()
        NC.wait_send()
        nacc[...] += nc[...]

    when(last_line, norm_last)
    grad_out(3).wait()
    share.wait_send()
    oth = pl.ds(pl.multiple_of((1 - c) * HALF, 16), HALF)
    remote(res(oth), res(oth), sib, share_s, share_r).wait_recv()

    spread = jnp.logical_or(z == 1, z == 2)
    for n in range(6):
        cols = pl.ds(n * 128, 128)

        def plain():
            flat[pl.ds(n, D, stride=6)] = dist[pl.ds(0, D), cols]

        def swapped():
            for j in range(4):
                flat[pl.ds(j * 6 + n, D // 4, stride=24)] = dist[pl.ds(j * (D // 4), D // 4), cols]

        when(jnp.logical_not(spread), plain)
        when(spread, swapped)
        when(i == 15, lambda: flat.__setitem__((pl.ds(6 * D + n, 4, stride=6), slice(None)), nacc[:, cols]))

    head_rows, after = pl.ds(0, 24), pl.ds(6 * D, 24)
    give = remote(flat.at[head_rows], flat.at[after], (c, i - 1), aft_s, aft_r)
    when(i > 0, lambda: give.start())
    when(i < 15, lambda: give.wait_recv())
    leave = pltpu.make_async_copy(flat, flat_out, o_sem)
    leave.start()
    when(i > 0, lambda: give.wait_send())
    leave.wait()


def enter_more(i, c, z, y, x):
    barrier = pltpu.get_barrier_semaphore()
    xp, yp, sib, up, down = partners(i, c, z, y, x)

    def signal(peer):
        pl.semaphore_signal(barrier, inc=1, device_id=peer, device_id_type=MESH)

    for peer in (xp, yp, sib):
        signal(peer)
    when(z > 0, lambda: signal(down))
    when(z < 3, lambda: signal(up))
    when(jnp.logical_and(x == 0, i > 0), lambda: signal((c, i - 1)))
    when(jnp.logical_and(x == 1, i < 15), lambda: signal((c, i + 1)))
    more = 1 - jnp.where(i == 0, 1, 0) - jnp.where(i == 15, 1, 0)
    pl.semaphore_wait(barrier, 3 + jnp.minimum(z, 1) + jnp.minimum(3 - z, 1) + more)


def reduce_back(wide, down, w, qkv, dO, mixb, lse, tokT, gbranch, first, norms, seg):
    Q = pltpu.SemaphoreType.DMA
    V = lambda *s: pltpu.VMEM(s, bf16)
    F = lambda *s: pltpu.VMEM(s, f32)
    A = pl.BlockSpec(memory_space=pl.ANY)
    return pl.pallas_call(
        reduce_back_kernel,
        in_specs=[A, A, A, A, VM, VM, VM, VM, VM, A, VM, VM, VM],
        out_specs=[A, A],
        out_shape=[jax.ShapeDtypeStruct((LEN, D), f32), jax.ShapeDtypeStruct((6 * D + 24, 128), f32)],
        scratch_shapes=[
            V(4, 2, 2, HALF, D), V(4, 2, 2, HALF, D), V(9, 2, C_PART, D), V(9, C_PART, D), V(9, C_PART, D),
            V(3, C_PART, D), V(9, 2, B_PART, D), V(9, 2, B_PART, D), V(3, 2, B_PART, D), V(3, B_PART, D),
            V(8, 2, Q_PART, COLS), V(8, Q_PART, COLS), V(8, Q_PART, COLS), V(8, HALF, COLS),
            F(LEN, LEN), V(LEN, LEN), V(LEN, LEN), V(D, D), V(3, D, LEN),
            F(256, D), F(6 * D + 24, 128), F(4, D), F(4, D), F(4, D), F(4, D), F(4, D),
            Q((4,)), Q, Q((3,)), Q, Q, Q, Q((4,)), Q((4,)), Q((8,)), Q((8,)),
            *[Q((9,))] * 14, Q((3,)), Q((3,)), *[Q((8,))] * 6, Q((4,)), Q((4,)), Q, Q, Q, Q,
        ],
        compiler_params=pltpu.CompilerParams(
            collective_id=2, has_side_effects=True, vmem_limit_bytes=62 << 20
        ),
        name="reduce_back",
    )(wide, down, w, qkv, dO, mixb, lse, tokT, gbranch, first, norms, seg.reshape(LEN, 1), seg.reshape(1, LEN))

SQUARE = D * D
TAIL = 4 * D


def from_wide(blocks):
    return blocks.reshape(4, 4, D // 4, D).transpose(0, 2, 1, 3).reshape(D, FF)


def to_wide(value):
    return value.reshape(4, D // 4, 4, D).transpose(0, 2, 1, 3).reshape(2, 2, D, D)


def swap_wide(block, index):
    swapped = block.reshape(D // 4, 4, D).transpose(1, 0, 2).reshape(D, D)
    wide = jnp.logical_and(index >= 4, index < 12)
    return jnp.where(wide, swapped, block)


def gather_and_attend(master, tokens, segments):
    count = lax.axis_size("zero")
    index = lax.axis_index("zero")
    size = 16 * SQUARE // count
    weights = master.astype(bf16)
    last = weights[-TAIL:]
    before = lax.ppermute(last, "zero", [(k, k + 1) for k in range(count - 1)])
    joined = jnp.concatenate([before, weights])
    block = lax.dynamic_slice(joined, (TAIL - TAIL // count * index,), (size,))
    if count == 16:
        padded = jnp.pad(last.reshape(4, D), ((0, 12), (0, 0)))
        block = swap_wide(block.reshape(D, D), index)
        blocks, tail, *attended = gather_attend(block, padded, tokens, segments)
        norms = tail[:4].astype(f32)
    else:
        natural = lax.all_gather(block.reshape(-1, D), "zero", axis=0, tiled=True)
        parts = natural.reshape(4, 4 * D, D)
        wide = [to_wide(parts[k].reshape(D, FF)) for k in (1, 2)]
        blocks = jnp.stack([parts[0].reshape(2, 2, D, D), *wide, parts[3].reshape(2, 2, D, D)])
        norms = lax.psum(jnp.where(index == count - 1, last.astype(f32), 0.0), "zero").reshape(4, D)
        attended = attend(tokens, blocks, segments)
    return blocks, norms, *attended


def back_and_scatter(blocks, segments, tokT, qkv, mixed, log_sum, grad_mixed, first_grad, branch_grad, norm_grads,
                     down_grad, wide_grad):
    count = lax.axis_size("zero")
    index = lax.axis_index("zero")
    if count == 16:
        input_grad, joined = reduce_back(
            wide_grad, down_grad, blocks, qkv, grad_mixed, mixed, log_sum, tokT, branch_grad, first_grad,
            norm_grads, segments,
        )
        joined = joined.reshape(-1)
    else:
        square, input_grad = attend_back(
            blocks, segments, tokT, qkv, mixed, log_sum, grad_mixed, first_grad, branch_grad
        )
        natural = [from_wide(wide_grad[k]).reshape(4 * D, D) for k in (0, 1)]
        natural = jnp.concatenate([square.reshape(4 * D, D), *natural, down_grad.reshape(4 * D, D)])
        block = lax.psum_scatter(natural, "zero", scatter_dimension=0, tiled=True)
        block = lax.psum(block.astype(f32), "dp")
        tail = lax.psum(norm_grads, ("dp", "zero"))
        flat = block.reshape(-1)
        after = lax.ppermute(flat[:TAIL], "zero", [(k + 1, k) for k in range(count - 1)])
        joined = jnp.concatenate([flat, jnp.where(index == count - 1, tail.reshape(-1), after)])
    shard = 16 * SQUARE // count + TAIL // count
    return input_grad, lax.dynamic_slice(joined, (TAIL // count * index,), (shard,))


def local(tokens, segments, cotangent, master, moment_one, moment_two):
    blocks, norms, tokT, qkv, mixed, log_sum = gather_and_attend(master, tokens, segments)
    output, first_grad, grad_mixed, branch_grad, norm_grads, down_grad, wide_grad = feed(
        tokens, cotangent, mixed, blocks, norms
    )
    input_grad, grad_shard = back_and_scatter(
        blocks, segments, tokT, qkv, mixed, log_sum, grad_mixed, first_grad, branch_grad, norm_grads,
        down_grad.reshape(2, 2, D, D), wide_grad.reshape(2, 2, 2, D, D),
    )
    grad_shard = grad_shard / (lax.axis_size("zero") * lax.axis_size("dp"))
    first = beta_one * moment_one + (1.0 - beta_one) * grad_shard
    second = beta_two * moment_two + (1.0 - beta_two) * grad_shard * grad_shard
    update = first / correct_one / (jnp.sqrt(second / correct_two) + adam_eps)
    master_new = master - learn_rate * (update + weight_decay * master)
    return (
        output,
        input_grad,
        grad_shard,
        first,
        second,
        master_new,
        master_new.astype(jnp.bfloat16),
    )


def solution(mesh):
    return jax.shard_map(
        local,
        mesh=mesh,
        in_specs=(
            P(("dp", "zero"), None),
            P(("dp", "zero")),
            P(("dp", "zero"), None),
            P("zero"),
            P("zero"),
            P("zero"),
        ),
        out_specs=(
            P(("dp", "zero"), None),
            P(("dp", "zero"), None),
            P("zero"),
            P("zero"),
            P("zero"),
            P("zero"),
            P("zero"),
        ),
        check_vma=False,
    )
```

```python
import functools

import jax
import jax.numpy as jnp
from jax import lax
from jax.sharding import PartitionSpec as P
import jax.experimental.pallas as pl
import jax.experimental.pallas.tpu as pltpu

D = 768
HEADS = 12
HEAD = 64
FF = 3072
LEN = 1024


learn_rate = 0.02
beta_one = 0.9
beta_two = 0.999
adam_eps = 1e-08
weight_decay = 0.01
correct_one = 1.0 - 0.9**10
correct_two = 1.0 - 0.999**10
norm_eps = 1e-06
inv_root_two = 0.7071067811865476
inv_root_tau = 0.3989422804014327


bf16=jnp.bfloat16; f32=jnp.float32
FAR=1e33
VM=pl.BlockSpec(memory_space=pltpu.VMEM)

def dot(a,b): return lax.dot_general(a,b,(((1,),(0,)),((),())),preferred_element_type=f32)
def dot_tn(a,b): return lax.dot_general(a,b,(((0,),(0,)),((),())),preferred_element_type=f32)
def dot_nt(a,b): return lax.dot_general(a,b,(((1,),(1,)),((),())),preferred_element_type=f32)

def slope(h):
    return jnp.exp2(-8.0/HEADS*(jnp.full((1,1),h,jnp.int32).astype(f32)+1.0))

def fill_distance(dist,seg_col,seg_row):
    @pl.loop(0,LEN//128)
    def _(k):
        r=pl.ds(pl.multiple_of(k*128,128),128)
        kk=(lax.broadcasted_iota(jnp.int32,(128,LEN),0)+k*128)
        qq=lax.broadcasted_iota(jnp.int32,(128,LEN),1)
        d=jnp.abs(kk-qq).astype(f32)
        dist[r]=jnp.where(seg_col[r]==seg_row[...],d,FAR)

QB=256
def project_all(w,tokT,qkv):
    @pl.loop(0,3)
    def _(n):
        @pl.loop(0,3)
        def _(t):
            c=pl.ds(pl.multiple_of(t*256,256),256)
            qkv[n,c]=dot_tn(w[0,n//2,n%2,:,c],tokT[...]).astype(bf16)

def attend_head(h,dist,qkv,mixb,probs):
    rows=pl.ds(pl.multiple_of(h*HEAD,HEAD),HEAD)
    keys=qkv[1,rows].astype(f32).T.astype(bf16)
    s=dot(keys,qkv[0,rows]*bf16(0.125))-slope(h)*dist[...]
    e=jnp.exp(s-jnp.max(s,0,keepdims=True))
    p=(e*(1.0/jnp.sum(e,0,keepdims=True))).astype(bf16)
    probs[...]=p
    mixb[rows]=dot(qkv[2,rows],p).astype(bf16)

def attend_back_head(h,qkv,dO,mixb,probs,ds_all):
    rows=pl.ds(pl.multiple_of(h*HEAD,HEAD),HEAD)
    values=qkv[2,rows].astype(f32).T.astype(bf16)
    grad_q=[]
    for b in range(LEN//QB):
        cols=pl.ds(b*QB,QB)
        do=dO[rows,cols]
        dp=dot(values,do)
        delta=jnp.sum(do.astype(f32)*mixb[rows,cols].astype(f32),0,keepdims=True)
        ds=(probs[:,cols].astype(f32)*(dp-delta)).astype(bf16)
        ds_all[:,cols]=ds
        grad_q.append((dot(qkv[1,rows],ds)*0.125).astype(bf16))
    grad_k=(dot_nt(qkv[0,rows],ds_all[...])*0.125).astype(bf16)
    grad_v=dot_nt(dO[rows],probs[...]).astype(bf16)
    for b in range(LEN//QB):
        qkv[0,rows,pl.ds(b*QB,QB)]=grad_q[b]
    qkv[1,rows]=grad_k
    qkv[2,rows]=grad_v

def attend_kernel(tokens,w,seg_col,seg_row,tokT,qkv,mixb,probs_out,dist,probs,sem):
    tokT[...]=tokens[...].astype(f32).T.astype(bf16)
    fill_distance(dist,seg_col,seg_row)
    project_all(w,tokT,qkv)
    @pl.loop(0,HEADS)
    def _(h):
        attend_head(h,dist,qkv,mixb,probs)
        move=pltpu.make_async_copy(probs,probs_out.at[h],sem)
        move.start()
        move.wait()

def attend_shapes():
    S=jax.ShapeDtypeStruct
    return [S((D,LEN),bf16),S((3,D,LEN),bf16),S((D,LEN),bf16),S((HEADS,LEN,LEN),bf16)]

ANY=pl.BlockSpec(memory_space=pl.ANY)

def attend(tokens,w,seg):
    return pl.pallas_call(attend_kernel,grid=(1,),
        in_specs=[VM,pl.BlockSpec((1,2,2,D,D),lambda i:(0,0,0,0,0)),VM,VM],out_specs=[VM]*3+[ANY],
        out_shape=attend_shapes(),
        scratch_shapes=[pltpu.VMEM((LEN,LEN),f32),pltpu.VMEM((LEN,LEN),bf16),pltpu.SemaphoreType.DMA],
        compiler_params=pltpu.CompilerParams(vmem_limit_bytes=58<<20),name="attend")(tokens,w,seg.reshape(LEN,1),seg.reshape(1,LEN))

def attend_back_kernel(w,tokT,qkv_in,mixb,probs_in,dO,first,gbranch,g0,grad_in,qkv,probs,ds_all,sem,qkv_sem):
    take=pltpu.make_async_copy(qkv_in,qkv,qkv_sem)
    take.start()
    take.wait()
    @pl.loop(0,HEADS)
    def _(h):
        move=pltpu.make_async_copy(probs_in.at[h],probs,sem)
        move.start()
        move.wait()
        attend_back_head(h,qkv,dO,mixb,probs,ds_all)
    g0[1,1]=dot(mixb[...],gbranch[...]).astype(bf16)
    for n in range(3):
        g0[n//2,n%2]=dot_nt(tokT[...],qkv[n]).astype(bf16)
    @pl.loop(0,4)
    def _(t):
        c=pl.ds(pl.multiple_of(t*256,256),256)
        acc=dot(w[0,0,0],qkv[0,:,c])+dot(w[0,0,1],qkv[1,:,c])+dot(w[0,1,0],qkv[2,:,c])
        grad_in[c]=first[c]+acc.T

def attend_back(w,tokT,qkv,mixb,probs,dO,first,gbranch):
    return pl.pallas_call(attend_back_kernel,grid=(1,),
        in_specs=[pl.BlockSpec((1,2,2,D,D),lambda i:(0,0,0,0,0)),VM,ANY,VM,ANY,VM,VM,VM],out_specs=[VM]*2,
        out_shape=[jax.ShapeDtypeStruct((2,2,D,D),bf16),jax.ShapeDtypeStruct((LEN,D),f32)],
        scratch_shapes=[pltpu.VMEM((3,D,LEN),bf16),pltpu.VMEM((LEN,LEN),bf16),pltpu.VMEM((LEN,LEN),bf16),pltpu.SemaphoreType.DMA,pltpu.SemaphoreType.DMA],
        compiler_params=pltpu.CompilerParams(vmem_limit_bytes=60<<20),name="attend_back")(w,tokT,qkv,mixb,probs,dO,first,gbranch)

TB=256
def feed_kernel(tokens,cot,mixb,w,norms,output,first,dO,gbranch,ng,gdown,gwide,inner,wide,gffn,fa,fb,acc,hid,wo,w1,w2,w3,w_sem,wo_sem):
    step=pl.program_id(0)
    gain1=norms[0:1]; shift1=norms[1:2]; gain2=norms[2:3]; shift2=norms[3:4]
    def stats(v):
        c=v-jnp.mean(v,-1,keepdims=True)
        r=lax.rsqrt(jnp.mean(c*c,-1,keepdims=True)+norm_eps)
        return c*r,r
    def back(e,n,r):
        return r*(e-jnp.mean(e,-1,keepdims=True)-n*jnp.mean(e*n,-1,keepdims=True))
    W=lambda p,j: (w1,w2)[p-1][j].reshape(D,D)
    WD=lambda j: w3[j].reshape(D,D)
    WO=lambda: wo[...].reshape(D,D)
    def load(p,j):
        source=w.at[p,j] if p==3 else w.at[p,:,j]
        return pltpu.make_async_copy(source,(w1,w2,w3)[p-1].at[j],w_sem.at[p-1,j])
    load_out=pltpu.make_async_copy(w.at[0,3],wo,wo_sem)
    @pl.when(step==0)
    def _():
        load_out.start()
        for j in range(4):
            for p in (1,2,3): load(p,j).start()
        ng[...]=jnp.zeros_like(ng)
        load_out.wait()
    @pl.when(step<LEN//TB)
    def _():
        rows=pl.ds(pl.multiple_of(step*TB,TB),TB)
        branch=dot_tn(mixb[...],WO())
        n1,r1=stats(tokens[...].astype(f32)+branch)
        l1=n1*gain1+shift1
        inner[rows]=l1.astype(bf16)
        acc[...]=l1
        @pl.loop(0,4,unroll=2)
        def _(j):
            @pl.when(step==0)
            def _():
                for p in (1,2,3): load(p,j).wait()
            inn=inner[rows]
            ga=dot(inn,W(1,j)); up=dot(inn,W(2,j))
            cum=0.5*(1.0+lax.erf(ga*inv_root_two))
            gel=ga*cum
            fb[j]=gel
            fa[j]=up*(cum+ga*(jnp.exp(-0.5*ga*ga)*inv_root_tau))
            h=(gel*up).astype(bf16)
            hid[j,rows]=h
            acc[...]+=dot(h,WD(j))
        n2,r2=stats(acc[...])
        output[...]=(n2*gain2+shift2).astype(bf16)
        c=cot[...].astype(f32)
        ng[2:3]+=jnp.sum(c*n2,0,keepdims=True)
        ng[3:4]+=jnp.sum(c,0,keepdims=True)
        mid=back(c*gain2,n2,r2)
        gffn[rows]=mid.astype(bf16)
        acc[...]=mid
        @pl.loop(0,4,unroll=2)
        def _(j):
            gh=dot_nt(gffn[rows],WD(j))
            a=(gh*fa[j]).astype(bf16); b=(gh*fb[j]).astype(bf16)
            wide[j,rows]=a; wide[4+j,rows]=b
            acc[...]+=dot_nt(a,W(1,j))+dot_nt(b,W(2,j))
        gl=acc[...]
        ng[0:1]+=jnp.sum(gl*n1,0,keepdims=True)
        ng[1:2]+=jnp.sum(gl,0,keepdims=True)
        gfirst=back(gl*gain1,n1,r1)
        first[...]=gfirst
        gb=gfirst.astype(bf16)
        gbranch[...]=gb
        dO[...]=dot_nt(WO(),gb).astype(bf16)
    def put(g,v):
        g[...]=v.astype(bf16).reshape(g.shape)
    base=LEN//TB
    @pl.when(jnp.logical_and(step>=base,step<base+4))
    def _(): put(gdown,dot_tn(hid[step-base],gffn[...]))
    @pl.when(jnp.logical_and(step>=base+4,step<base+12))
    def _(): put(gwide,dot_tn(inner[...],wide[step-base-4]))

def feed(tokens,cot,mixb,w,norms):
    n=LEN//TB
    last=n-1
    row=lambda i:(jnp.minimum(i,last),0)
    col=lambda i:(0,jnp.minimum(i,last))
    S=jax.ShapeDtypeStruct
    V=lambda s,d=bf16: pltpu.VMEM(s,d)
    clip=lambda v,a,b: jnp.minimum(jnp.maximum(v,a),b)
    return pl.pallas_call(feed_kernel,grid=(n+12,),
        in_specs=[pl.BlockSpec((TB,D),row),pl.BlockSpec((TB,D),row),pl.BlockSpec((D,TB),col),
            pl.BlockSpec(memory_space=pl.ANY),pl.BlockSpec((4,D),lambda i:(0,0))],
        out_specs=[pl.BlockSpec((TB,D),row),pl.BlockSpec((TB,D),row),pl.BlockSpec((D,TB),col),pl.BlockSpec((TB,D),row),
            pl.BlockSpec((4,D),lambda i:(0,0)),
            pl.BlockSpec((1,D,D),lambda i:(clip(i-n,0,3),0,0)),
            pl.BlockSpec((1,4,1,D//4,D),lambda i:(clip((i-n-4)//4,0,1),0,clip(i-n-4,0,7)%4,0,0))],
        out_shape=[S((LEN,D),bf16),S((LEN,D),f32),S((D,LEN),bf16),S((LEN,D),bf16),S((4,D),f32),S((4,D,D),bf16),S((2,4,4,D//4,D),bf16)],
        scratch_shapes=[V((LEN,D)),V((8,LEN,D)),V((LEN,D)),V((4,TB,D),f32),V((4,TB,D),f32),V((TB,D),f32),V((4,LEN,D)),V((4,D//4,D)),*[V((4,4,D//4,D))]*3,pltpu.SemaphoreType.DMA((3,4)),pltpu.SemaphoreType.DMA],
        compiler_params=pltpu.CompilerParams(vmem_limit_bytes=62<<20),name="feed")(tokens,cot,mixb,w.reshape(4,4,4,D//4,D),norms)

MESH = pl.DeviceIdType.MESH
ALL = slice(None)
HALF = D // 2
B_PART, C_PART = 48, 80
P_PART = 48


def place():
    i = lax.axis_index("zero")
    c = lax.axis_index("dp")
    return i, c, i // 4, (i // 2) % 2, i % 2


def partners(i, c, z, y, x):
    return (c, i + 1 - 2 * x), (c, i + 2 - 4 * y), (1 - c, i), (c, i + 4), (c, i - 4)


def when(cond, fn):
    @pl.when(cond)
    def _():
        fn()


def enter(i, c, z, y, x):
    barrier = pltpu.get_barrier_semaphore()
    xp, yp, sib, up, down = partners(i, c, z, y, x)

    def signal(peer):
        pl.semaphore_signal(barrier, inc=1, device_id=peer, device_id_type=MESH)

    for peer in (xp, yp, sib):
        signal(peer)
    when(z > 0, lambda: signal(down))
    when(z < 3, lambda: signal(up))
    pl.semaphore_wait(barrier, 3 + jnp.minimum(z, 1) + jnp.minimum(3 - z, 1))


def pick(z, values):
    out = jnp.int32(values[3])
    for k in (2, 1, 0):
        out = jnp.where(z == k, jnp.int32(values[k]), out)
    return out


def run_plan(z, words, ops):
    count = len(words[0])
    held = [pick(z, [words[k][n] for k in range(4)]) for n in range(count)]

    @pl.loop(0, count)
    def _(n):
        word = held[0]
        for k in range(1, count):
            word = jnp.where(n == k, held[k], word)

        @pl.loop(0, 3)
        def _(m):
            code = jnp.where(m == 0, word, jnp.where(m == 1, word // 256, word // 65536)) % 256
            kind, e = code // 16, code % 16
            branch(kind, e, 0, ops)


def branch(kind, e, low, ops):
    if len(ops) == 1:
        ops[0](e)
        return
    half = len(ops) // 2

    def lower():
        branch(kind, e, low, ops[:half])

    def upper():
        branch(kind, e, low + half, ops[half:])

    lax.cond(kind < low + half, lower, upper)


def gather_attend_kernel(blk, last, tokens, seg_col, seg_row, result, norms, tokT_out, qkv_out, mixb, probs_out,
                         held, dist, tail, tokT, qkv, probs, own_sem, out_sem, t_sem, q_sem, p_sem, pzs, pzr, pfs, pfr, pgs, pgr, p_s, p_r,
                         b1s, b1r, c1u, c1d, c1r, b2u, b2d, b2r, c2s, c2r, b3s, b3r, c3s, c3r, ss, sr, ts, tr):
    i, c, z, y, x = place()
    xp, yp, sib, up, down = partners(i, c, z, y, x)
    half = c * HALF
    other = (1 - c) * HALF
    local = pltpu.make_async_copy(blk, held.at[z, y, x], own_sem)
    local.start()
    enter(i, c, z, y, x)

    def remote(ref, peer, s, r):
        return pltpu.make_async_remote_copy(
            src_ref=ref, dst_ref=ref, send_sem=s, recv_sem=r, device_id=peer, device_id_type=MESH
        )

    def by_parity(k, fn):
        when(k % 2 == 0, lambda: fn(False))
        when(k % 2 == 1, lambda: fn(True))

    def rp(k, base):
        return pl.ds(pl.multiple_of(base + k * P_PART, 16), P_PART)

    def z_ref(k, base=half):
        return held.at[0, y, x, rp(k, base)]

    def f_ref(k, odd, base=half):
        if odd:
            return held.at[0, 1 - y, x, rp(k, base)]
        return held.at[0, y, 1 - x, rp(k, base)]

    def g_ref(k, odd, mine, base=half):
        if odd:
            return held.at[0, ALL, x if mine else 1 - x, rp(k, base)]
        return held.at[0, y if mine else 1 - y, ALL, rp(k, base)]

    def PZ(k):
        return remote(z_ref(k), up, pzs.at[k], pzr.at[k])

    def PF(k, odd):
        return remote(z_ref(k), yp if odd else xp, pfs.at[k], pfr.at[k])

    def PG(k, odd):
        return remote(g_ref(k, odd, True), xp if odd else yp, pgs.at[k], pgr.at[k])

    def PS(ref, n):
        return remote(ref, sib, p_s.at[n], p_r.at[n])

    def op_p0z(k):
        def arrive():
            PZ(k).wait_recv()
            PS(z_ref(k), k).start()

        when(z > 0, arrive)
        when(z < 3, lambda: PZ(k).start())
        by_parity(k, lambda odd: PF(k, odd).start())

    def op_p0f(k):
        def turn(odd):
            PF(k, odd).wait_recv()
            PG(k, odd).start()
            PS(f_ref(k, odd), 8 + k).start()

        by_parity(k, turn)

    def op_p0g(k):
        def turn(odd):
            PG(k, odd).wait_recv()
            PS(g_ref(k, odd, False), 16 + k).start()

        by_parity(k, turn)

    split = lambda e: (e // 3 + 1, e % 3)

    def rb(s, base):
        return pl.ds(pl.multiple_of(base + s * B_PART, 16), B_PART)

    def rc(s, base):
        return pl.ds(pl.multiple_of(base + 3 * B_PART + s * C_PART, 16), C_PART)

    def b1_ref(s, yy, base=half):
        return held.at[z, yy, x, rb(s, base)]

    def b2_ref(t, s, xx, base=half):
        return held.at[t, ALL, xx, rb(s, base)]

    def c1_ref(t, s, base=half):
        return held.at[t, y, x, rc(s, base)]

    def c2_ref(t, s, xx, base=half):
        return held.at[t, y, xx, rc(s, base)]

    def c3_ref(t, s, yy, base=half):
        return held.at[t, yy, ALL, rc(s, base)]

    B1 = lambda s: remote(b1_ref(s, y), yp, b1s.at[s], b1r.at[s])
    C1U = lambda t, s, e: remote(c1_ref(t, s), up, c1u.at[e], c1r.at[e])
    C1D = lambda t, s, e: remote(c1_ref(t, s), down, c1d.at[e], c1r.at[e])
    B2U = lambda t, s, e: remote(b2_ref(t, s, x), up, b2u.at[e], b2r.at[e])
    B2D = lambda t, s, e: remote(b2_ref(t, s, x), down, b2d.at[e], b2r.at[e])
    C2 = lambda t, s, e: remote(c2_ref(t, s, x), xp, c2s.at[e], c2r.at[e])
    B3 = lambda t, s, e: remote(b2_ref(t, s, x), xp, b3s.at[e], b3r.at[e])
    C3 = lambda t, s, e: remote(c3_ref(t, s, y), yp, c3s.at[e], c3r.at[e])
    S = lambda ref, n: remote(ref, sib, ss.at[n], sr.at[n])

    def op_own(e):
        t, s = split(e)
        B1(s).start()
        C1D(t, s, e).start()

    def op_ownup(e):
        t, s = split(e)

        def go():
            C1U(t, s, e).start()
            B2U(t, s, e).start()

        when(z < 3, go)

    def op_b1(e):
        t, s = split(e)
        B1(s).wait_recv()
        B2D(t, s, e).start()
        S(b1_ref(s, 1 - y), 45 + s).start()

    def op_cx(e):
        t, s = split(e)
        C2(t, s, e).start()

    def op_bx(e):
        t, s = split(e)
        B3(t, s, e).start()

    def op_c1(e):
        t, s = split(e)
        C1U(t, s, e).wait_recv()
        when(jnp.logical_and(t < z, z < 3), lambda: C1U(t, s, e).start())
        when(jnp.logical_and(t > z, z > 0), lambda: C1D(t, s, e).start())
        S(c1_ref(t, s), e).start()

    def op_b2(e):
        t, s = split(e)
        B2U(t, s, e).wait_recv()
        when(jnp.logical_and(t < z, z < 3), lambda: B2U(t, s, e).start())
        when(jnp.logical_and(t > z, z > 0), lambda: B2D(t, s, e).start())
        S(b2_ref(t, s, x), 9 + e).start()

    def op_c2(e):
        t, s = split(e)
        C2(t, s, e).wait_recv()
        C3(t, s, e).start()
        S(c2_ref(t, s, 1 - x), 18 + e).start()

    def op_b3(e):
        t, s = split(e)
        B3(t, s, e).wait_recv()
        S(b2_ref(t, s, 1 - x), 27 + e).start()

    def op_c3(e):
        t, s = split(e)
        C3(t, s, e).wait_recv()
        S(c3_ref(t, s, 1 - y), 36 + e).start()

    def qkv_leaves(n):
        return pltpu.make_async_copy(qkv.at[n], qkv_out.at[n], q_sem.at[n])

    tokT_leaves = pltpu.make_async_copy(tokT, tokT_out, t_sem)

    def probs_leave(h):
        return pltpu.make_async_copy(probs.at[h % 2], probs_out.at[h], p_sem.at[h % 2])

    def op_proj(n):
        def arrive():
            @pl.loop(0, 8)
            def _(k):
                def got(odd):
                    PS(f_ref(k, odd, other), 8 + k).wait_recv()
                    PS(g_ref(k, odd, False, other), 16 + k).wait_recv()

                by_parity(k, got)
                when(z > 0, lambda: PS(z_ref(k, other), k).wait_recv())

        when(n == 0, arrive)

        @pl.loop(0, 3)
        def _(t):
            cols = pl.ds(pl.multiple_of(t * 256, 256), 256)
            qkv[n, cols] = dot_tn(held[0, n // 2, n % 2, :, cols], tokT[...]).astype(bf16)

        qkv_leaves(n).start()

    def op_head(h):
        when(h >= 2, lambda: probs_leave(h - 2).wait())
        attend_head(h, dist, qkv, mixb, probs.at[h % 2])
        probs_leave(h).start()

    line = jnp.logical_and(y == 1, x == 1)
    source = jnp.logical_and(line, z == 3)

    def T(peer, n):
        return remote(tail, peer, ts.at[n], tr.at[0])

    def leave(t):
        return pltpu.make_async_copy(held.at[t], result.at[t], out_sem.at[t])

    def op_other(e):
        def tail_z():
            def go():
                when(z < 3, lambda: T(down, 0).wait_recv())
                when(z > 0, lambda: T(down, 0).start())
                T(yp, 1).start()

            when(line, go)

        def tail_x():
            def go():
                when(y == 0, lambda: T(yp, 1).wait_recv())
                T(xp, 2).start()

            when(x == 1, go)

        def out():
            t = e - 2

            def others():
                @pl.loop(0, 3)
                def _(s):
                    n = (t - 1) * 3 + s

                    def theirs():
                        S(c1_ref(t, s, other), n).wait_recv()
                        S(b2_ref(t, s, x, other), 9 + n).wait_recv()

                    when(t != z, theirs)
                    when(t == z, lambda: S(b1_ref(s, 1 - y, other), 45 + s).wait_recv())
                    S(c2_ref(t, s, 1 - x, other), 18 + n).wait_recv()
                    S(b2_ref(t, s, 1 - x, other), 27 + n).wait_recv()
                    S(c3_ref(t, s, 1 - y, other), 36 + n).wait_recv()

            when(t > 0, others)
            leave(t).start()

        def prepare():
            tokT[...] = tokens[...].astype(f32).T.astype(bf16)
            tokT_leaves.start()
            fill_distance(dist, seg_col, seg_row)

        when(e == 0, tail_z)
        when(e == 1, tail_x)
        when(jnp.logical_and(e >= 2, e < 6), out)
        when(e == 6, prepare)

    when(source, lambda: tail.__setitem__(Ellipsis, last[...]))
    local.wait()
    run_plan(z, GATHER_PLAN, [op_p0z, op_p0f, op_p0g, op_own, op_ownup, op_b1, op_bx, op_c1, op_b2, op_c2, op_b3,
                              op_c3, op_proj, op_head, op_other, op_cx])

    when(x == 0, lambda: T(xp, 2).wait_recv())
    when(x == 1, lambda: T(xp, 2).wait_send())

    def tail_sent():
        T(yp, 1).wait_send()
        when(z > 0, lambda: T(down, 0).wait_send())

    when(line, tail_sent)

    @pl.loop(0, 8)
    def _(k):
        def gone(odd):
            PF(k, odd).wait_send()
            PG(k, odd).wait_send()
            PS(f_ref(k, odd), 8 + k).wait_send()
            PS(g_ref(k, odd, False), 16 + k).wait_send()

        by_parity(k, gone)
        when(z < 3, lambda: PZ(k).wait_send())
        when(z > 0, lambda: PS(z_ref(k), k).wait_send())

    @pl.loop(0, 9)
    def _(e):
        t, s = split(e)
        C2(t, s, e).wait_send()
        B3(t, s, e).wait_send()
        C3(t, s, e).wait_send()

        def ups():
            C1U(t, s, e).wait_send()
            B2U(t, s, e).wait_send()

        def downs():
            C1D(t, s, e).wait_send()
            B2D(t, s, e).wait_send()

        when(jnp.logical_and(t <= z, z < 3), ups)
        when(jnp.logical_and(t >= z, z > 0), downs)

        def mine():
            B1(s).wait_send()
            S(b1_ref(s, 1 - y), 45 + s).wait_send()

        def theirs():
            S(c1_ref(t, s), e).wait_send()
            S(b2_ref(t, s, x), 9 + e).wait_send()

        when(t == z, mine)
        when(t != z, theirs)
        S(c2_ref(t, s, 1 - x), 18 + e).wait_send()
        S(b2_ref(t, s, 1 - x), 27 + e).wait_send()
        S(c3_ref(t, s, 1 - y), 36 + e).wait_send()

    norms[...] = tail[pl.ds(0, 4)].astype(f32)
    tokT_leaves.wait()
    for n in range(3):
        qkv_leaves(n).wait()
    for h in (HEADS - 2, HEADS - 1):
        probs_leave(h).wait()
    for t in range(4):
        leave(t).wait()


def gather_attend(blk, last, tokens, seg):
    Q = pltpu.SemaphoreType.DMA
    any_space = pl.BlockSpec(memory_space=pl.ANY)
    counts = [8] * 6 + [24, 24, 3, 3] + [9] * 12 + [48, 48, 3, 1]
    return pl.pallas_call(
        gather_attend_kernel,
        in_specs=[any_space, VM, VM, VM, VM],
        out_specs=[any_space, VM, any_space, any_space, VM, any_space],
        out_shape=[
            jax.ShapeDtypeStruct((4, 2, 2, D, D), bf16), jax.ShapeDtypeStruct((4, D), f32),
            *attend_shapes(),
        ],
        scratch_shapes=[
            pltpu.VMEM((4, 2, 2, D, D), bf16), pltpu.VMEM((LEN, LEN), f32), pltpu.VMEM((16, D), bf16),
            pltpu.VMEM((D, LEN), bf16), pltpu.VMEM((3, D, LEN), bf16), pltpu.VMEM((2, LEN, LEN), bf16),
            Q, Q((4,)), Q, Q((3,)), Q((2,)), *[Q((n,)) for n in counts],
        ],
        compiler_params=pltpu.CompilerParams(
            collective_id=1, has_side_effects=True, vmem_limit_bytes=58 << 20
        ),
        name="gather_attend",
    )(blk, last, tokens, seg.reshape(LEN, 1), seg.reshape(1, LEN))


PLANE_ORDER = (1, 2, 3)
BACK_PLAN = (
    (
        7374723, 131328, 263025, 14681376, 4198406, 4261665, 1122930, 7553544, 7619363, 4461092,
        7685413, 8393510, 5255297, 4592770, 3221366, 1413201, 9605601, 2659143, 3307336, 7870034,
        3429171, 7935828, 8017205, 8067233, 14853024, 10630788, 8815958, 11622199, 3723443, 13742168,
        13882034, 9868692, 12632471, 12756388, 10987203, 12891317, 12957622, 15714246, 15724527,
    ),
    (
        7374723, 131328, 254065, 328736, 7475206, 2230049, 7541000, 1209379, 2454820, 1278016,
        4400705, 8537217, 9467458, 9573521, 4532115, 1406760, 14776390, 4684054, 10557306, 14842696,
        10688644, 8815968, 5255265, 5321058, 9868692, 5386903, 5452704, 3494964, 10630741, 3684182,
        10835920, 13743025, 10797400, 12628135, 11708114, 12825794, 13875125, 12960950, 15714246,
    ),
    (
        7374723, 131328, 263025, 14681376, 7475206, 2230049, 7541000, 7611200, 4334657, 8418578,
        2458241, 1257510, 2573174, 1347984, 7836562, 2634052, 7869776, 1459506, 4600697, 14766497,
        8016407, 8079156, 1591459, 14836533, 8757380, 13645446, 9713570, 9868600, 11645079, 5488996,
        6665138, 10801600, 12829349, 13784404, 11839398, 12867253, 11978195, 5752503, 15714136,
    ),
    (
        7374723, 131328, 263025, 14681376, 4198406, 4261665, 533106, 7553553, 7619363, 4461092,
        7685413, 8552832, 5255206, 9442323, 9578385, 2651795, 3241749, 3307601, 5452626, 3438870,
        8001364, 10714017, 10519778, 3507845, 14787126, 9802837, 9879985, 11580311, 3654592, 11707600,
        10867138, 10998438, 11912372, 11933893, 12047302, 4671175, 5650504, 6842214, 15685719,
    ),
)

GATHER_PLAN = (
    (
        131328, 328707, 15075078, 1184016, 15757331, 7410964, 1513201, 2224754, 6324256, 7545379,
        2396403, 2449793, 6455846, 16020625, 12697639, 9601986, 10548597, 11645027, 9687266, 13760118,
        6594948, 10651090, 14922341, 13891447, 16283796, 9819315, 13985414, 8902307, 11822998, 8970455,
        14182564, 14988709, 11966425, 10019290, 12035803, 12101799, 15724517, 15724527,
    ),
    (
        3207664, 15086129, 5279744, 5308787, 156000, 7639378, 266243, 10487157, 8586928, 4196113,
        10568257, 1315446, 1475761, 2196755, 1406752, 16127779, 16053239, 7926517, 6579192, 2253413,
        6719013, 8857380, 2528871, 12763584, 9672584, 13689448, 13743764, 9622165, 14734263, 11785368,
        14079395, 14136484, 10672293, 14279861, 14801574, 14922407, 12101851, 15724517,
    ),
    (
        16119027, 3486771, 9655270, 5535331, 9721188, 30565, 7902465, 242434, 296611, 8889349,
        504838, 4460867, 10848325, 1208336, 14988564, 1277974, 2168177, 16183319, 16316401, 6776416,
        6390120, 7479331, 2237938, 2581122, 2527268, 12763584, 14848406, 9953488, 10015152, 11968722,
        10933459, 14004705, 11064999, 10606519, 14258904, 10675640, 11721690, 15724515,
    ),
    (
        16316406, 3684150, 9852646, 6772582, 6854488, 11927704, 173569, 12035843, 11011332, 462854,
        4670994, 15054920, 7541777, 1381142, 2105731, 15931252, 2319348, 2253956, 16086309, 8726308,
        2528101, 12763584, 10715360, 15757460, 6353265, 13677538, 10781153, 9818465, 13824626, 6455973,
        9491380, 11899348, 10540516, 10596566, 9623767, 10672561, 11721690, 15724515,
    ),
)


Q_PART = 96
COLS = D // 2


def reduce_back_kernel(wide, down, w, qkv_in, dO_in, mixb_in, probs_in, tokT_in, gbranch_in, first, norm_in,
                       grad_in, flat_out, own, sl, lc3, lc2, lcz, lczx, lb3, lbz, lbzx, lb1, lf, lg, lz, stage,
                       dO, mixb, tokT, gbranch, theirs, probs, ds_all, wv, qkv, fchunk, flat, nacc, nx, ny, nz, nc,
                       own_sem, in_sem, p_sem, w_sem, f_sem, g_sem, o_sem, sib_s, sib_r, st_s, st_r,
                       c3s, c3r, b3s, b3r, c2s, c2r, bus, bur, bds, bdr, cus, cur, cds, cdr, b1s, b1r,
                       fs, fr, gs, gr, zs_, zr_, ns, nr, share_s, share_r, aft_s, aft_r):
    i, c, z, y, x = place()
    xp, yp, sib, up, down_peer = partners(i, c, z, y, x)
    base = c * HALF
    mine = pl.ds(pl.multiple_of(base, 16), HALF)
    other = pl.ds(pl.multiple_of((1 - c) * HALF, 16), HALF)
    planes = [wide.at[0], wide.at[1], down]

    def remote(src, dst, peer, s, r):
        return pltpu.make_async_remote_copy(
            src_ref=src, dst_ref=dst, send_sem=s, recv_sem=r, device_id=peer, device_id_type=MESH
        )

    def local_in(t):
        return pltpu.make_async_copy(planes[t - 1].at[:, :, mine], own.at[t], own_sem.at[t])

    def sib_in(t, s, n):
        k = 2 * ((t - 1) * 3 + s) + n
        start, size = (s * B_PART, B_PART) if n == 0 else (3 * B_PART + s * C_PART, C_PART)
        there = pl.ds(pl.multiple_of((1 - c) * HALF + start, 16), size)
        return remote(planes[t - 1].at[:, :, there], sl.at[t, :, :, pl.ds(start, size)], sib, sib_s.at[k], sib_r.at[k])

    for t in PLANE_ORDER:
        local_in(t).start()
    take = [
        pltpu.make_async_copy(a, b, in_sem.at[n])
        for n, (a, b) in enumerate(
            ((qkv_in, qkv), (dO_in, dO), (mixb_in, mixb), (gbranch_in, gbranch), (tokT_in, tokT))
        )
    ]
    for n in range(3):
        take[n].start()

    def probs_come(h):
        return pltpu.make_async_copy(probs_in.at[h], probs.at[h % 2], p_sem.at[h % 2])

    probs_come(0).start()
    for n in (3, 4):
        take[n].start()
    enter_more(i, c, z, y, x)
    for t in PLANE_ORDER:
        for s in range(3):
            for n in range(2):
                sib_in(t, s, n).start()
    nacc[...] = norm_in[...]
    NX = remote(nacc, nx, xp, ns.at[0], nr.at[0])
    NY = remote(nacc, ny, yp, ns.at[1], nr.at[1])
    NZ = remote(nacc, nz, up, ns.at[2], nr.at[2])
    NC = remote(nacc, nc, sib, ns.at[3], nr.at[3])
    line = jnp.logical_and(x == 1, y == 1)
    last_line = jnp.logical_and(line, z == 3)
    when(x == 0, lambda: NX.start())
    for move in take:
        move.wait()

    def rb(s, k=0, size=B_PART):
        return pl.ds(pl.multiple_of(s * B_PART + k, 16), size)

    def rc(s, k=0, size=C_PART):
        return pl.ds(pl.multiple_of(3 * B_PART + s * C_PART + k, 16), size)

    def add_rows(dst, src, rows):
        @pl.loop(0, rows // 16)
        def _(n):
            k = pl.multiple_of(n * 16, 16)
            a = dst(k)
            a[...] = a[...] + src(k)[...]

    r16 = lambda k: pl.ds(k, 16)
    split = lambda e: (e // 3 + 1, e % 3)

    def C3(t, s, e):
        return remote(own.at[t, 1 - y, :, rc(s)], lc3.at[e], yp, c3s.at[e], c3r.at[e])

    def B3(t, s, e):
        return remote(own.at[t, :, 1 - x, rb(s)], lb3.at[e], xp, b3s.at[e], b3r.at[e])

    def C2(t, s, e):
        return remote(own.at[t, y, 1 - x, rc(s)], lc2.at[e], xp, c2s.at[e], c2r.at[e])

    def BU(t, s, e):
        return remote(own.at[t, :, x, rb(s)], lbz.at[e], up, bus.at[e], bur.at[e])

    def BD(t, s, e, extra=False):
        return remote(own.at[t, :, x, rb(s)], lbzx.at[s] if extra else lbz.at[e], down_peer, bds.at[e], bdr.at[e])

    def CU(t, s, e):
        return remote(own.at[t, y, x, rc(s)], lcz.at[e], up, cus.at[e], cur.at[e])

    def CD(t, s, e, extra=False):
        return remote(own.at[t, y, x, rc(s)], lczx.at[s] if extra else lcz.at[e], down_peer, cds.at[e], cdr.at[e])

    def B1(s):
        return remote(own.at[z, 1 - y, x, rb(s)], lb1.at[s], yp, b1s.at[s], b1r.at[s])

    def op_sum(e):
        t, s = split(e)

        for k in (1, 2, 3):
            when(jnp.logical_and(t == k, s == 0), lambda k=k: local_in(k).wait())
            for m in range(3):
                def arrive(k=k, m=m):
                    for n in range(2):
                        sib_in(k, m, n).wait_recv()

                when(e == (k - 1) * 3 + m, arrive)
        add_rows(lambda k: own.at[t, :, :, rb(s, k, 16)], lambda k: sl.at[t, :, :, rb(s, k, 16)], B_PART)
        add_rows(lambda k: own.at[t, :, :, rc(s, k, 16)], lambda k: sl.at[t, :, :, rc(s, k, 16)], C_PART)
        C3(t, s, e).start()
        B3(t, s, e).start()

    def op_c3(e):
        t, s = split(e)
        C3(t, s, e).wait_recv()
        add_rows(lambda k: own.at[t, y, :, rc(s, k, 16)], lambda k: lc3.at[e, :, r16(k)], C_PART)
        C2(t, s, e).start()

    def op_b3(e):
        t, s = split(e)
        B3(t, s, e).wait_recv()
        add_rows(lambda k: own.at[t, :, x, rb(s, k, 16)], lambda k: lb3.at[e, :, r16(k)], B_PART)

    def op_c2(e):
        t, s = split(e)
        C2(t, s, e).wait_recv()
        add_rows(lambda k: own.at[t, y, x, rc(s, k, 16)], lambda k: lc2.at[e, r16(k)], C_PART)

    def op_bz(e):
        t, s = split(e)
        dst = lambda k: own.at[t, :, x, rb(s, k, 16)]

        def from_below():
            BU(t, s, e).wait_recv()
            add_rows(dst, lambda k: lbz.at[e, :, r16(k)], B_PART)

        when(jnp.logical_and(t >= z, z > 0), from_below)

        def from_above():
            BD(t, s, e).wait_recv()
            add_rows(dst, lambda k: lbz.at[e, :, r16(k)], B_PART)

        when(t < z, lambda: when(z < 3, from_above))

        def from_above_last():
            BD(t, s, e).wait_recv()
            add_rows(dst, lambda k: lbzx.at[s, :, r16(k)], B_PART)

        when(jnp.logical_and(t == z, z < 3), from_above_last)
        when(t > z, lambda: BU(t, s, e).start())
        when(t == z - 1, lambda: BD(t, s, e, True).start())
        when(t < z - 1, lambda: BD(t, s, e).start())
        when(t == z, lambda: B1(s).start())

    def op_cz(e):
        t, s = split(e)
        dst = lambda k: own.at[t, y, x, rc(s, k, 16)]

        def from_below():
            CU(t, s, e).wait_recv()
            add_rows(dst, lambda k: lcz.at[e, r16(k)], C_PART)

        when(jnp.logical_and(t >= z, z > 0), from_below)

        def from_above():
            CD(t, s, e).wait_recv()
            add_rows(dst, lambda k: lcz.at[e, r16(k)], C_PART)

        when(t < z, lambda: when(z < 3, from_above))

        def from_above_last():
            CD(t, s, e).wait_recv()
            add_rows(dst, lambda k: lczx.at[s, r16(k)], C_PART)

        when(jnp.logical_and(t == z, z < 3), from_above_last)
        when(t > z, lambda: CU(t, s, e).start())
        when(t == z - 1, lambda: CD(t, s, e, True).start())
        when(t < z - 1, lambda: CD(t, s, e).start())

    def op_b1(e):
        t, s = split(e)
        B1(s).wait_recv()
        add_rows(lambda k: own.at[z, y, x, rb(s, k, 16)], lambda k: lb1.at[s, r16(k)], B_PART)

    def op_head(h):
        probs_come(h).wait()
        when(h < HEADS - 1, lambda: probs_come(h + 1).start())
        attend_back_head(h, qkv, dO, mixb, probs.at[h % 2], ds_all)

    def columns(g):
        return pl.ds(pl.multiple_of(g * COLS, 128), COLS)

    def stage_copy(e):
        g, n = e // 4, e % 4
        return remote(
            stage.at[e], sl.at[0, n // 2, n % 2, :, columns(g)], sib, st_s.at[e], st_r.at[e]
        )

    def op_dw(e):
        g, n = e // 4, e % 4
        cols = columns(g)

        def put(half, value):
            if half == 0:
                own[0, n // 2, n % 2, :, cols] = value.astype(bf16)
            else:
                stage[e] = value.astype(bf16)

        def inputs():
            right = qkv[n, pl.ds(pl.multiple_of(g * COLS, 128), COLS)]
            for half, rows in ((0, mine), (1, other)):
                put(half, dot_nt(tokT[rows], right))

        def output():
            right = gbranch[:, cols]
            for half, rows in ((0, mine), (1, other)):
                put(half, dot(mixb[rows], right))

        when(n < 3, inputs)
        when(n == 3, output)
        stage_copy(e).start()

    def rq(k, n=0, size=Q_PART):
        return pl.ds(pl.multiple_of(k * Q_PART + n, 16), size)

    def F0(e, g, k, odd):
        src = own.at[0, :, 1 - x, rq(k), columns(g)] if odd else own.at[0, 1 - y, :, rq(k), columns(g)]
        return remote(src, lf.at[e], xp if odd else yp, fs.at[e], fr.at[e])

    def G0(e, g, k, odd):
        if odd:
            return remote(own.at[0, 1 - y, x, rq(k), columns(g)], lg.at[e], yp, gs.at[e], gr.at[e])
        return remote(own.at[0, y, 1 - x, rq(k), columns(g)], lg.at[e], xp, gs.at[e], gr.at[e])

    def Z0(e, g, k):
        return remote(own.at[0, y, x, rq(k), columns(g)], lz.at[e], down_peer, zs_.at[e], zr_.at[e])

    def by_parity(k, fn):
        when(k % 2 == 0, lambda: fn(False))
        when(k % 2 == 1, lambda: fn(True))

    def op_sum0(e):
        g, k = e // 4, e % 4

        def arrive():
            @pl.loop(0, 4)
            def _(n):
                stage_copy(g * 4 + n).wait_recv()

        when(k == 0, arrive)
        add_rows(
            lambda n: own.at[0, :, :, rq(k, n, 16), columns(g)],
            lambda n: sl.at[0, :, :, rq(k, n, 16), columns(g)], Q_PART,
        )
        by_parity(k, lambda odd: F0(e, g, k, odd).start())

    def op_f0(e):
        g, k = e // 4, e % 4

        def turn(odd):
            F0(e, g, k, odd).wait_recv()
            if odd:
                dst = lambda n: own.at[0, :, x, rq(k, n, 16), columns(g)]
            else:
                dst = lambda n: own.at[0, y, :, rq(k, n, 16), columns(g)]
            add_rows(dst, lambda n: lf.at[e, :, r16(n)], Q_PART)
            G0(e, g, k, odd).start()

        by_parity(k, turn)

    def op_g0(e):
        g, k = e // 4, e % 4
        by_parity(k, lambda odd: G0(e, g, k, odd).wait_recv())
        add_rows(lambda n: own.at[0, y, x, rq(k, n, 16), columns(g)], lambda n: lg.at[e, r16(n)], Q_PART)

    def op_z0(e):
        g, k = e // 4, e % 4

        def arrive():
            Z0(e, g, k).wait_recv()
            add_rows(lambda n: own.at[0, y, x, rq(k, n, 16), columns(g)], lambda n: lz.at[e, r16(n)], Q_PART)

        when(z < 3, arrive)
        when(z > 0, lambda: Z0(e, g, k).start())

    def first_in(q):
        return pltpu.make_async_copy(first.at[pl.ds(pl.multiple_of(q * 256, 256), 256)], fchunk, f_sem)

    def grad_out(q):
        return pltpu.make_async_copy(fchunk, grad_in.at[pl.ds(pl.multiple_of(q * 256, 256), 256)], g_sem)

    def weight_in(n):
        target = (probs.at[0, pl.ds(0, D), pl.ds(0, D)], ds_all.at[pl.ds(0, D), pl.ds(0, D)], wv)[n]
        return pltpu.make_async_copy(w.at[0, n // 2, n % 2], target, w_sem.at[n])

    def op_gin(q):
        def weights():
            for n in range(3):
                weight_in(n).wait()

        when(q == 0, weights)
        when(q > 0, lambda: grad_out(q - 1).wait())
        first_in(q).start()
        cols = pl.ds(pl.multiple_of(q * 256, 256), 256)
        d = pl.ds(0, D)
        acc = dot(probs[0, d, d], qkv[0, :, cols]) + dot(ds_all[d, d], qkv[1, :, cols])
        acc = (acc + dot(wv[...], qkv[2, :, cols])).T
        first_in(q).wait()
        fchunk[...] += acc
        grad_out(q).start()

    def op_other(e):
        def norm_y():
            def go():
                NX.wait_recv()
                nacc[...] += nx[...]
                when(y == 0, lambda: NY.start())

            when(x == 1, go)

        def norm_z():
            def go():
                NY.wait_recv()
                nacc[...] += ny[...]

                def more():
                    NZ.wait_recv()
                    nacc[...] += nz[...]

                when(z > 0, more)
                when(z < 3, lambda: NZ.start())
                when(z == 3, lambda: NC.start())

            when(line, go)

        def load():
            for n in range(3):
                weight_in(n).start()

        when(e == 0, norm_y)
        when(e == 1, norm_z)
        when(e == 2, load)

    run_plan(z, BACK_PLAN, [op_sum, op_c3, op_b3, op_c2, op_bz, op_cz, op_b1, op_head, op_dw, op_sum0, op_f0,
                            op_g0, op_z0, op_gin, op_other])

    spread = jnp.logical_or(z == 1, z == 2)

    def flatten(half, get):
        def plain():
            for n in range(6):
                flat[pl.ds(half * (6 * HALF) + n, HALF, stride=6)] = get(pl.ds(0, HALF), pl.ds(n * 128, 128)).astype(f32)

        def swapped():
            for n in range(6):
                for j in range(2):
                    value = get(pl.ds(j * (D // 4), D // 4), pl.ds(n * 128, 128)).astype(f32)
                    flat[pl.ds(half * 12 + j * 6 + n, D // 4, stride=24)] = value

        when(jnp.logical_not(spread), plain)
        when(spread, swapped)

    share = remote(own.at[z, y, x], theirs, sib, share_s, share_r)
    share.start()
    flatten(c, lambda rows, cols: own[z, y, x, rows, cols])

    @pl.loop(0, 9)
    def _(e):
        t, s = split(e)
        C3(t, s, e).wait_send()
        B3(t, s, e).wait_send()
        C2(t, s, e).wait_send()

        def went_up():
            BU(t, s, e).wait_send()
            CU(t, s, e).wait_send()

        def went_down():
            BD(t, s, e).wait_send()
            CD(t, s, e).wait_send()

        when(t > z, went_up)
        when(t < z, went_down)
        when(t == z, lambda: B1(s).wait_send())

    @pl.loop(0, 8)
    def _(e):
        g, k = e // 4, e % 4
        stage_copy(e).wait_send()

        def gone(odd):
            F0(e, g, k, odd).wait_send()
            G0(e, g, k, odd).wait_send()

        by_parity(k, gone)
        when(z > 0, lambda: Z0(e, g, k).wait_send())

    for t in (1, 2, 3):
        for s in range(3):
            for n in range(2):
                sib_in(t, s, n).wait_send()
    when(x == 0, lambda: NX.wait_send())
    when(jnp.logical_and(x == 1, y == 0), lambda: NY.wait_send())
    when(jnp.logical_and(line, z < 3), lambda: NZ.wait_send())

    def norm_last():
        NC.wait_recv()
        NC.wait_send()
        nacc[...] += nc[...]

    when(last_line, norm_last)
    grad_out(3).wait()
    share.wait_recv()
    flatten(1 - c, lambda rows, cols: theirs[rows, cols])
    share.wait_send()
    body, head_rows, after = pl.ds(0, 6 * D), pl.ds(0, 24), pl.ds(6 * D, 24)
    leave = pltpu.make_async_copy(flat.at[body], flat_out.at[body], o_sem.at[0])
    leave.start()

    def ending():
        for n in range(6):
            flat[pl.ds(6 * D + n, 4, stride=6)] = nacc[:, pl.ds(n * 128, 128)]

    when(i == 15, ending)
    give = remote(flat.at[head_rows], flat.at[after], (c, i - 1), aft_s, aft_r)
    when(i > 0, lambda: give.start())
    when(i < 15, lambda: give.wait_recv())
    leave_after = pltpu.make_async_copy(flat.at[after], flat_out.at[after], o_sem.at[1])
    leave_after.start()
    when(i > 0, lambda: give.wait_send())
    leave.wait()
    leave_after.wait()


def enter_more(i, c, z, y, x):
    barrier = pltpu.get_barrier_semaphore()
    xp, yp, sib, up, down = partners(i, c, z, y, x)

    def signal(peer):
        pl.semaphore_signal(barrier, inc=1, device_id=peer, device_id_type=MESH)

    for peer in (xp, yp, sib):
        signal(peer)
    when(z > 0, lambda: signal(down))
    when(z < 3, lambda: signal(up))
    when(jnp.logical_and(x == 0, i > 0), lambda: signal((c, i - 1)))
    when(jnp.logical_and(x == 1, i < 15), lambda: signal((c, i + 1)))
    more = 1 - jnp.where(i == 0, 1, 0) - jnp.where(i == 15, 1, 0)
    pl.semaphore_wait(barrier, 3 + jnp.minimum(z, 1) + jnp.minimum(3 - z, 1) + more)


def reduce_back(wide, down, w, qkv, dO, mixb, probs, tokT, gbranch, first, norms):
    Q = pltpu.SemaphoreType.DMA
    V = lambda *s: pltpu.VMEM(s, bf16)
    F = lambda *s: pltpu.VMEM(s, f32)
    A = pl.BlockSpec(memory_space=pl.ANY)
    return pl.pallas_call(
        reduce_back_kernel,
        in_specs=[A] * 10 + [VM],
        out_specs=[A, A],
        out_shape=[jax.ShapeDtypeStruct((LEN, D), f32), jax.ShapeDtypeStruct((6 * D + 24, 128), f32)],
        scratch_shapes=[
            V(4, 2, 2, HALF, D), V(4, 2, 2, HALF, D), V(9, 2, C_PART, D), V(9, C_PART, D), V(9, C_PART, D),
            V(3, C_PART, D), V(9, 2, B_PART, D), V(9, 2, B_PART, D), V(3, 2, B_PART, D), V(3, B_PART, D),
            V(8, 2, Q_PART, COLS), V(8, Q_PART, COLS), V(8, Q_PART, COLS), V(8, HALF, COLS),
            V(D, LEN), V(D, LEN), V(D, LEN), V(LEN, D), V(HALF, D), V(2, LEN, LEN), V(LEN, LEN), V(D, D), V(3, D, LEN),
            F(256, D), F(6 * D + 24, 128), F(4, D), F(4, D), F(4, D), F(4, D), F(4, D),
            Q((4,)), Q((5,)), Q((2,)), Q((3,)), Q, Q, Q((2,)), Q((18,)), Q((18,)), Q((8,)), Q((8,)),
            *[Q((9,))] * 14, Q((3,)), Q((3,)), *[Q((8,))] * 6, Q((4,)), Q((4,)), Q, Q, Q, Q,
        ],
        compiler_params=pltpu.CompilerParams(
            collective_id=2, has_side_effects=True, vmem_limit_bytes=62 << 20
        ),
        name="reduce_back",
    )(wide, down, w, qkv, dO, mixb, probs, tokT, gbranch, first, norms)

SQUARE = D * D
TAIL = 4 * D


def from_wide(blocks):
    return blocks.reshape(4, 4, D // 4, D).transpose(0, 2, 1, 3).reshape(D, FF)


def to_wide(value):
    return value.reshape(4, D // 4, 4, D).transpose(0, 2, 1, 3).reshape(2, 2, D, D)


def swap_wide(block, index):
    swapped = block.reshape(D // 4, 4, D).transpose(1, 0, 2).reshape(D, D)
    wide = jnp.logical_and(index >= 4, index < 12)
    return jnp.where(wide, swapped, block)


def gather_and_attend(master, tokens, segments):
    count = lax.axis_size("zero")
    index = lax.axis_index("zero")
    size = 16 * SQUARE // count
    weights = master.astype(bf16)
    last = weights[-TAIL:]
    before = lax.ppermute(last, "zero", [(k, k + 1) for k in range(count - 1)])
    joined = jnp.concatenate([before, weights])
    block = lax.dynamic_slice(joined, (TAIL - TAIL // count * index,), (size,))
    if count == 16:
        padded = jnp.pad(last.reshape(4, D), ((0, 12), (0, 0)))
        block = swap_wide(block.reshape(D, D), index)
        blocks, norms, *attended = gather_attend(block, padded, tokens, segments)
    else:
        natural = lax.all_gather(block.reshape(-1, D), "zero", axis=0, tiled=True)
        parts = natural.reshape(4, 4 * D, D)
        wide = [to_wide(parts[k].reshape(D, FF)) for k in (1, 2)]
        blocks = jnp.stack([parts[0].reshape(2, 2, D, D), *wide, parts[3].reshape(2, 2, D, D)])
        norms = lax.psum(jnp.where(index == count - 1, last.astype(f32), 0.0), "zero").reshape(4, D)
        attended = attend(tokens, blocks, segments)
    return blocks, norms, *attended


def back_and_scatter(blocks, tokT, qkv, mixed, probs, grad_mixed, first_grad, branch_grad, norm_grads,
                     down_grad, wide_grad):
    count = lax.axis_size("zero")
    index = lax.axis_index("zero")
    if count == 16:
        input_grad, joined = reduce_back(
            wide_grad, down_grad, blocks, qkv, grad_mixed, mixed, probs, tokT, branch_grad, first_grad,
            norm_grads,
        )
        joined = joined.reshape(-1)
    else:
        square, input_grad = attend_back(
            blocks, tokT, qkv, mixed, probs, grad_mixed, first_grad, branch_grad
        )
        natural = [from_wide(wide_grad[k]).reshape(4 * D, D) for k in (0, 1)]
        natural = jnp.concatenate([square.reshape(4 * D, D), *natural, down_grad.reshape(4 * D, D)])
        block = lax.psum_scatter(natural, "zero", scatter_dimension=0, tiled=True)
        block = lax.psum(block.astype(f32), "dp")
        tail = lax.psum(norm_grads, ("dp", "zero"))
        flat = block.reshape(-1)
        after = lax.ppermute(flat[:TAIL], "zero", [(k + 1, k) for k in range(count - 1)])
        joined = jnp.concatenate([flat, jnp.where(index == count - 1, tail.reshape(-1), after)])
    shard = 16 * SQUARE // count + TAIL // count
    return input_grad, lax.dynamic_slice(joined, (TAIL // count * index,), (shard,))


def local(tokens, segments, cotangent, master, moment_one, moment_two):
    blocks, norms, tokT, qkv, mixed, probs = gather_and_attend(master, tokens, segments)
    output, first_grad, grad_mixed, branch_grad, norm_grads, down_grad, wide_grad = feed(
        tokens, cotangent, mixed, blocks, norms
    )
    input_grad, grad_shard = back_and_scatter(
        blocks, tokT, qkv, mixed, probs, grad_mixed, first_grad, branch_grad, norm_grads,
        down_grad.reshape(2, 2, D, D), wide_grad.reshape(2, 2, 2, D, D),
    )
    grad_shard = grad_shard / (lax.axis_size("zero") * lax.axis_size("dp"))
    first = beta_one * moment_one + (1.0 - beta_one) * grad_shard
    second = beta_two * moment_two + (1.0 - beta_two) * grad_shard * grad_shard
    update = first / correct_one / (jnp.sqrt(second / correct_two) + adam_eps)
    master_new = master - learn_rate * (update + weight_decay * master)
    return (
        output,
        input_grad,
        grad_shard,
        first,
        second,
        master_new,
        master_new.astype(jnp.bfloat16),
    )


def solution(mesh):
    return jax.shard_map(
        local,
        mesh=mesh,
        in_specs=(
            P(("dp", "zero"), None),
            P(("dp", "zero")),
            P(("dp", "zero"), None),
            P("zero"),
            P("zero"),
            P("zero"),
        ),
        out_specs=(
            P(("dp", "zero"), None),
            P(("dp", "zero"), None),
            P("zero"),
            P("zero"),
            P("zero"),
            P("zero"),
            P("zero"),
        ),
        check_vma=False,
    )
```

```python
import functools

import jax
import jax.numpy as jnp
from jax import lax
from jax.sharding import PartitionSpec as P
import jax.experimental.pallas as pl
import jax.experimental.pallas.tpu as pltpu

D = 768
HEADS = 12
HEAD = 64
FF = 3072
LEN = 1024


learn_rate = 0.02
beta_one = 0.9
beta_two = 0.999
adam_eps = 1e-08
weight_decay = 0.01
correct_one = 1.0 - 0.9**10
correct_two = 1.0 - 0.999**10
norm_eps = 1e-06
inv_root_two = 0.7071067811865476
inv_root_tau = 0.3989422804014327


bf16=jnp.bfloat16; f32=jnp.float32
FAR=1e33
VM=pl.BlockSpec(memory_space=pltpu.VMEM)

def dot(a,b): return lax.dot_general(a,b,(((1,),(0,)),((),())),preferred_element_type=f32)
def dot_tn(a,b): return lax.dot_general(a,b,(((0,),(0,)),((),())),preferred_element_type=f32)
def dot_nt(a,b): return lax.dot_general(a,b,(((1,),(1,)),((),())),preferred_element_type=f32)

def slope(h):
    return jnp.exp2(-8.0/HEADS*(jnp.full((1,1),h,jnp.int32).astype(f32)+1.0))

def fill_distance(dist,seg_row,column):
    column[...]=jnp.broadcast_to(seg_row[...].astype(f32),(8,LEN)).T
    @pl.loop(0,LEN//128)
    def _(k):
        r=pl.ds(pl.multiple_of(k*128,128),128)
        kk=(lax.broadcasted_iota(jnp.int32,(128,LEN),0)+k*128)
        qq=lax.broadcasted_iota(jnp.int32,(128,LEN),1)
        d=jnp.abs(kk-qq).astype(f32)
        dist[r]=jnp.where(column[r,0:1]==seg_row[...].astype(f32),d,FAR)

QB=256
def project_all(w,tokT,qkv):
    @pl.loop(0,3)
    def _(n):
        @pl.loop(0,3)
        def _(t):
            c=pl.ds(pl.multiple_of(t*256,256),256)
            qkv[n,c]=dot_tn(w[0,n//2,n%2,:,c],tokT[...]).astype(bf16)

def attend_head(h,dist,qkv,mixb,probs):
    rows=pl.ds(pl.multiple_of(h*HEAD,HEAD),HEAD)
    keys=qkv[1,rows].astype(f32).T.astype(bf16)
    s=dot(keys,qkv[0,rows]*bf16(0.125))-slope(h)*dist[...]
    e=jnp.exp(s-jnp.max(s,0,keepdims=True))
    p=(e*(1.0/jnp.sum(e,0,keepdims=True))).astype(bf16)
    probs[...]=p
    mixb[rows]=dot(qkv[2,rows],p).astype(bf16)

def attend_back_head(h,qkv,dO,mixb,probs,ds_all):
    rows=pl.ds(pl.multiple_of(h*HEAD,HEAD),HEAD)
    values=qkv[2,rows].astype(f32).T.astype(bf16)
    grad_q=[]
    for b in range(LEN//QB):
        cols=pl.ds(b*QB,QB)
        do=dO[rows,cols]
        dp=dot(values,do)
        delta=jnp.sum(do.astype(f32)*mixb[rows,cols].astype(f32),0,keepdims=True)
        ds=(probs[:,cols].astype(f32)*(dp-delta)).astype(bf16)
        ds_all[:,cols]=ds
        grad_q.append((dot(qkv[1,rows],ds)*0.125).astype(bf16))
    grad_k=(dot_nt(qkv[0,rows],ds_all[...])*0.125).astype(bf16)
    grad_v=dot_nt(dO[rows],probs[...]).astype(bf16)
    for b in range(LEN//QB):
        qkv[0,rows,pl.ds(b*QB,QB)]=grad_q[b]
    qkv[1,rows]=grad_k
    qkv[2,rows]=grad_v

def attend_kernel(tokens,w,seg_row,tokT,qkv,mixb,probs_out,dist,column,probs,sem):
    tokT[...]=tokens[...].astype(f32).T.astype(bf16)
    fill_distance(dist,seg_row,column)
    project_all(w,tokT,qkv)
    @pl.loop(0,HEADS)
    def _(h):
        attend_head(h,dist,qkv,mixb,probs)
        move=pltpu.make_async_copy(probs,probs_out.at[h],sem)
        move.start()
        move.wait()

def attend_shapes():
    S=jax.ShapeDtypeStruct
    return [S((D,LEN),bf16),S((3,D,LEN),bf16),S((D,LEN),bf16),S((HEADS,LEN,LEN),bf16)]

ANY=pl.BlockSpec(memory_space=pl.ANY)

def attend(tokens,w,seg):
    return pl.pallas_call(attend_kernel,grid=(1,),
        in_specs=[VM,pl.BlockSpec((1,2,2,D,D),lambda i:(0,0,0,0,0)),VM],out_specs=[VM]*3+[ANY],
        out_shape=attend_shapes(),
        scratch_shapes=[pltpu.VMEM((LEN,LEN),f32),pltpu.VMEM((LEN,8),f32),pltpu.VMEM((LEN,LEN),bf16),pltpu.SemaphoreType.DMA],
        compiler_params=pltpu.CompilerParams(vmem_limit_bytes=58<<20),name="attend")(tokens,w,seg.reshape(1,LEN))

def attend_back_kernel(w,tokT,qkv_in,mixb,probs_in,dO,first,gbranch,g0,grad_in,qkv,probs,ds_all,sem,qkv_sem):
    take=pltpu.make_async_copy(qkv_in,qkv,qkv_sem)
    take.start()
    take.wait()
    @pl.loop(0,HEADS)
    def _(h):
        move=pltpu.make_async_copy(probs_in.at[h],probs,sem)
        move.start()
        move.wait()
        attend_back_head(h,qkv,dO,mixb,probs,ds_all)
    g0[1,1]=dot(mixb[...],gbranch[...]).astype(bf16)
    for n in range(3):
        g0[n//2,n%2]=dot_nt(tokT[...],qkv[n]).astype(bf16)
    @pl.loop(0,4)
    def _(t):
        c=pl.ds(pl.multiple_of(t*256,256),256)
        acc=dot(w[0,0,0],qkv[0,:,c])+dot(w[0,0,1],qkv[1,:,c])+dot(w[0,1,0],qkv[2,:,c])
        grad_in[c]=first[c]+acc.T

def attend_back(w,tokT,qkv,mixb,probs,dO,first,gbranch):
    return pl.pallas_call(attend_back_kernel,grid=(1,),
        in_specs=[pl.BlockSpec((1,2,2,D,D),lambda i:(0,0,0,0,0)),VM,ANY,VM,ANY,VM,VM,VM],out_specs=[VM]*2,
        out_shape=[jax.ShapeDtypeStruct((2,2,D,D),bf16),jax.ShapeDtypeStruct((LEN,D),f32)],
        scratch_shapes=[pltpu.VMEM((3,D,LEN),bf16),pltpu.VMEM((LEN,LEN),bf16),pltpu.VMEM((LEN,LEN),bf16),pltpu.SemaphoreType.DMA,pltpu.SemaphoreType.DMA],
        compiler_params=pltpu.CompilerParams(vmem_limit_bytes=60<<20),name="attend_back")(w,tokT,qkv,mixb,probs,dO,first,gbranch)

TB=256
def feed_kernel(tokens,cot,mixb,w,norms,output,first,dO,gbranch,ng,gdown,gwide,inner,wide,gffn,fa,fb,acc,hid,wo,w1,w2,w3,w_sem,wo_sem):
    step=pl.program_id(0)
    gain1=norms[0:1]; shift1=norms[1:2]; gain2=norms[2:3]; shift2=norms[3:4]
    def stats(v):
        c=v-jnp.mean(v,-1,keepdims=True)
        r=lax.rsqrt(jnp.mean(c*c,-1,keepdims=True)+norm_eps)
        return c*r,r
    def back(e,n,r):
        return r*(e-jnp.mean(e,-1,keepdims=True)-n*jnp.mean(e*n,-1,keepdims=True))
    W=lambda p,j: (w1,w2)[p-1][j].reshape(D,D)
    WD=lambda j: w3[j].reshape(D,D)
    WO=lambda: wo[...].reshape(D,D)
    def load(p,j):
        source=w.at[p,j] if p==3 else w.at[p,:,j]
        return pltpu.make_async_copy(source,(w1,w2,w3)[p-1].at[j],w_sem.at[p-1,j])
    load_out=pltpu.make_async_copy(w.at[0,3],wo,wo_sem)
    @pl.when(step==0)
    def _():
        load_out.start()
        for j in range(4):
            for p in (1,2,3): load(p,j).start()
        ng[...]=jnp.zeros_like(ng)
        load_out.wait()
    @pl.when(step<LEN//TB)
    def _():
        rows=pl.ds(pl.multiple_of(step*TB,TB),TB)
        branch=dot_tn(mixb[...],WO())
        n1,r1=stats(tokens[...].astype(f32)+branch)
        l1=n1*gain1+shift1
        inner[rows]=l1.astype(bf16)
        acc[...]=l1
        @pl.loop(0,2)
        def _(n):
            js=(2*n,2*n+1)
            @pl.when(step==0)
            def _():
                for j in js:
                    for p in (1,2,3): load(p,j).wait()
            inn=inner[rows]
            sides=[(dot(inn,W(1,j)),dot(inn,W(2,j))) for j in js]
            total=None
            for j,(ga,up) in zip(js,sides):
                cum=0.5*(1.0+lax.erf(ga*inv_root_two))
                gel=ga*cum
                fb[j]=gel
                fa[j]=up*(cum+ga*(jnp.exp(-0.5*ga*ga)*inv_root_tau))
                h=(gel*up).astype(bf16)
                hid[j,rows]=h
                part=dot(h,WD(j))
                total=part if total is None else total+part
            acc[...]+=total
        n2,r2=stats(acc[...])
        output[...]=(n2*gain2+shift2).astype(bf16)
        c=cot[...].astype(f32)
        ng[2:3]+=jnp.sum(c*n2,0,keepdims=True)
        ng[3:4]+=jnp.sum(c,0,keepdims=True)
        mid=back(c*gain2,n2,r2)
        gffn[rows]=mid.astype(bf16)
        acc[...]=mid
        @pl.loop(0,2)
        def _(n):
            js=(2*n,2*n+1)
            ghs=[dot_nt(gffn[rows],WD(j)) for j in js]
            total=None
            for j,gh in zip(js,ghs):
                a=(gh*fa[j]).astype(bf16); b=(gh*fb[j]).astype(bf16)
                wide[j,rows]=a; wide[4+j,rows]=b
                part=dot_nt(a,W(1,j))+dot_nt(b,W(2,j))
                total=part if total is None else total+part
            acc[...]+=total
        gl=acc[...]
        ng[0:1]+=jnp.sum(gl*n1,0,keepdims=True)
        ng[1:2]+=jnp.sum(gl,0,keepdims=True)
        gfirst=back(gl*gain1,n1,r1)
        first[...]=gfirst
        gb=gfirst.astype(bf16)
        gbranch[...]=gb
        dO[...]=dot_nt(WO(),gb).astype(bf16)
    def put(g,v):
        g[...]=v.astype(bf16).reshape(g.shape)
    base=LEN//TB
    @pl.when(jnp.logical_and(step>=base,step<base+4))
    def _(): put(gdown,dot_tn(hid[step-base],gffn[...]))
    @pl.when(jnp.logical_and(step>=base+4,step<base+12))
    def _(): put(gwide,dot_tn(inner[...],wide[step-base-4]))

def feed(tokens,cot,mixb,w,norms):
    n=LEN//TB
    last=n-1
    row=lambda i:(jnp.minimum(i,last),0)
    col=lambda i:(0,jnp.minimum(i,last))
    S=jax.ShapeDtypeStruct
    V=lambda s,d=bf16: pltpu.VMEM(s,d)
    clip=lambda v,a,b: jnp.minimum(jnp.maximum(v,a),b)
    return pl.pallas_call(feed_kernel,grid=(n+12,),
        in_specs=[pl.BlockSpec((TB,D),row),pl.BlockSpec((TB,D),row),pl.BlockSpec((D,TB),col),
            pl.BlockSpec(memory_space=pl.ANY),pl.BlockSpec((4,D),lambda i:(0,0))],
        out_specs=[pl.BlockSpec((TB,D),row),pl.BlockSpec((TB,D),row),pl.BlockSpec((D,TB),col),pl.BlockSpec((TB,D),row),
            pl.BlockSpec((4,D),lambda i:(0,0)),
            pl.BlockSpec((1,D,D),lambda i:(clip(i-n,0,3),0,0)),
            pl.BlockSpec((1,4,1,D//4,D),lambda i:(clip((i-n-4)//4,0,1),0,clip(i-n-4,0,7)%4,0,0))],
        out_shape=[S((LEN,D),bf16),S((LEN,D),f32),S((D,LEN),bf16),S((LEN,D),bf16),S((4,D),f32),S((4,D,D),bf16),S((2,4,4,D//4,D),bf16)],
        scratch_shapes=[V((LEN,D)),V((8,LEN,D)),V((LEN,D)),V((4,TB,D),f32),V((4,TB,D),f32),V((TB,D),f32),V((4,LEN,D)),V((4,D//4,D)),*[V((4,4,D//4,D))]*3,pltpu.SemaphoreType.DMA((3,4)),pltpu.SemaphoreType.DMA],
        compiler_params=pltpu.CompilerParams(vmem_limit_bytes=62<<20),name="feed")(tokens,cot,mixb,w.reshape(4,4,4,D//4,D),norms)

MESH = pl.DeviceIdType.MESH
ALL = slice(None)
HALF = D // 2
B_PART, C_PART = 48, 80
P_PART = 48


def place():
    i = lax.axis_index("zero")
    c = lax.axis_index("dp")
    return i, c, i // 4, (i // 2) % 2, i % 2


def partners(i, c, z, y, x):
    return (c, i + 1 - 2 * x), (c, i + 2 - 4 * y), (1 - c, i), (c, i + 4), (c, i - 4)


def when(cond, fn):
    @pl.when(cond)
    def _():
        fn()


def enter(i, c, z, y, x):
    barrier = pltpu.get_barrier_semaphore()
    xp, yp, sib, up, down = partners(i, c, z, y, x)

    def signal(peer):
        pl.semaphore_signal(barrier, inc=1, device_id=peer, device_id_type=MESH)

    for peer in (xp, yp, sib):
        signal(peer)
    when(z > 0, lambda: signal(down))
    when(z < 3, lambda: signal(up))
    pl.semaphore_wait(barrier, 3 + jnp.minimum(z, 1) + jnp.minimum(3 - z, 1))


def pick(z, values):
    out = jnp.int32(values[3])
    for k in (2, 1, 0):
        out = jnp.where(z == k, jnp.int32(values[k]), out)
    return out


def run_plan(z, words, ops):
    count = len(words[0])
    held = [pick(z, [words[k][n] for k in range(4)]) for n in range(count)]

    @pl.loop(0, count)
    def _(n):
        word = held[0]
        for k in range(1, count):
            word = jnp.where(n == k, held[k], word)

        @pl.loop(0, 3)
        def _(m):
            code = jnp.where(m == 0, word, jnp.where(m == 1, word // 256, word // 65536)) % 256
            kind, e = code // 16, code % 16
            branch(kind, e, 0, ops)


def branch(kind, e, low, ops):
    if len(ops) == 1:
        ops[0](e)
        return
    half = len(ops) // 2

    def lower():
        branch(kind, e, low, ops[:half])

    def upper():
        branch(kind, e, low + half, ops[half:])

    lax.cond(kind < low + half, lower, upper)


def gather_attend_kernel(blk, last, tokens, seg_row, result, norms, tokT_out, qkv_out, mixb, probs_out,
                         held, dist, column, tail, tokT, qkv, probs, out_sem, t_sem, q_sem, p_sem, pzs, pzr, pfs, pfr, pgs, pgr, p_s, p_r,
                         b1s, b1r, c1u, c1d, c1r, b2u, b2d, b2r, c2s, c2r, b3s, b3r, c3s, c3r, ss, sr, ts, tr):
    i, c, z, y, x = place()
    xp, yp, sib, up, down = partners(i, c, z, y, x)
    half = c * HALF
    other = (1 - c) * HALF
    spread = jnp.logical_or(z == 1, z == 2)

    def plain():
        for n in range(6):
            held[z, y, x, :, pl.ds(n * 128, 128)] = blk[pl.ds(n, D, stride=6)].astype(bf16)

    def swapped():
        for n in range(6):
            for j in range(4):
                value = blk[pl.ds(j * 6 + n, D // 4, stride=24)].astype(bf16)
                held[z, y, x, pl.ds(j * (D // 4), D // 4), pl.ds(n * 128, 128)] = value

    when(jnp.logical_not(spread), plain)
    when(spread, swapped)
    enter(i, c, z, y, x)

    def remote(ref, peer, s, r):
        return pltpu.make_async_remote_copy(
            src_ref=ref, dst_ref=ref, send_sem=s, recv_sem=r, device_id=peer, device_id_type=MESH
        )

    def by_parity(k, fn):
        when(k % 2 == 0, lambda: fn(False))
        when(k % 2 == 1, lambda: fn(True))

    def rp(k, base):
        return pl.ds(pl.multiple_of(base + k * P_PART, 16), P_PART)

    def z_ref(k, base=half):
        return held.at[0, y, x, rp(k, base)]

    def f_ref(k, odd, base=half):
        if odd:
            return held.at[0, 1 - y, x, rp(k, base)]
        return held.at[0, y, 1 - x, rp(k, base)]

    def g_ref(k, odd, mine, base=half):
        if odd:
            return held.at[0, ALL, x if mine else 1 - x, rp(k, base)]
        return held.at[0, y if mine else 1 - y, ALL, rp(k, base)]

    def PZ(k):
        return remote(z_ref(k), up, pzs.at[k], pzr.at[k])

    def PF(k, odd):
        return remote(z_ref(k), yp if odd else xp, pfs.at[k], pfr.at[k])

    def PG(k, odd):
        return remote(g_ref(k, odd, True), xp if odd else yp, pgs.at[k], pgr.at[k])

    def PS(ref, n):
        return remote(ref, sib, p_s.at[n], p_r.at[n])

    def op_p0z(k):
        def arrive():
            PZ(k).wait_recv()
            PS(z_ref(k), k).start()

        when(z > 0, arrive)
        when(z < 3, lambda: PZ(k).start())
        by_parity(k, lambda odd: PF(k, odd).start())

    def op_p0f(k):
        def turn(odd):
            PF(k, odd).wait_recv()
            PG(k, odd).start()
            PS(f_ref(k, odd), 8 + k).start()

        by_parity(k, turn)

    def op_p0g(k):
        def turn(odd):
            PG(k, odd).wait_recv()
            PS(g_ref(k, odd, False), 16 + k).start()

        by_parity(k, turn)

    split = lambda e: (e // 3 + 1, e % 3)

    def rb(s, base):
        return pl.ds(pl.multiple_of(base + s * B_PART, 16), B_PART)

    def rc(s, base):
        return pl.ds(pl.multiple_of(base + 3 * B_PART + s * C_PART, 16), C_PART)

    def b1_ref(s, yy, base=half):
        return held.at[z, yy, x, rb(s, base)]

    def b2_ref(t, s, xx, base=half):
        return held.at[t, ALL, xx, rb(s, base)]

    def c1_ref(t, s, base=half):
        return held.at[t, y, x, rc(s, base)]

    def c2_ref(t, s, xx, base=half):
        return held.at[t, y, xx, rc(s, base)]

    def c3_ref(t, s, yy, base=half):
        return held.at[t, yy, ALL, rc(s, base)]

    B1 = lambda s: remote(b1_ref(s, y), yp, b1s.at[s], b1r.at[s])
    C1U = lambda t, s, e: remote(c1_ref(t, s), up, c1u.at[e], c1r.at[e])
    C1D = lambda t, s, e: remote(c1_ref(t, s), down, c1d.at[e], c1r.at[e])
    B2U = lambda t, s, e: remote(b2_ref(t, s, x), up, b2u.at[e], b2r.at[e])
    B2D = lambda t, s, e: remote(b2_ref(t, s, x), down, b2d.at[e], b2r.at[e])
    C2 = lambda t, s, e: remote(c2_ref(t, s, x), xp, c2s.at[e], c2r.at[e])
    B3 = lambda t, s, e: remote(b2_ref(t, s, x), xp, b3s.at[e], b3r.at[e])
    C3 = lambda t, s, e: remote(c3_ref(t, s, y), yp, c3s.at[e], c3r.at[e])
    S = lambda ref, n: remote(ref, sib, ss.at[n], sr.at[n])

    def op_own(e):
        t, s = split(e)
        B1(s).start()
        C1D(t, s, e).start()

    def op_ownup(e):
        t, s = split(e)

        def go():
            C1U(t, s, e).start()
            B2U(t, s, e).start()

        when(z < 3, go)

    def op_b1(e):
        t, s = split(e)
        B1(s).wait_recv()
        B2D(t, s, e).start()
        S(b1_ref(s, 1 - y), 45 + s).start()

    def op_cx(e):
        t, s = split(e)
        C2(t, s, e).start()

    def op_bx(e):
        t, s = split(e)
        B3(t, s, e).start()

    def op_c1(e):
        t, s = split(e)
        C1U(t, s, e).wait_recv()
        when(jnp.logical_and(t < z, z < 3), lambda: C1U(t, s, e).start())
        when(jnp.logical_and(t > z, z > 0), lambda: C1D(t, s, e).start())
        S(c1_ref(t, s), e).start()

    def op_b2(e):
        t, s = split(e)
        B2U(t, s, e).wait_recv()
        when(jnp.logical_and(t < z, z < 3), lambda: B2U(t, s, e).start())
        when(jnp.logical_and(t > z, z > 0), lambda: B2D(t, s, e).start())
        S(b2_ref(t, s, x), 9 + e).start()

    def op_c2(e):
        t, s = split(e)
        C2(t, s, e).wait_recv()
        C3(t, s, e).start()
        S(c2_ref(t, s, 1 - x), 18 + e).start()

    def op_b3(e):
        t, s = split(e)
        B3(t, s, e).wait_recv()
        S(b2_ref(t, s, 1 - x), 27 + e).start()

    def op_c3(e):
        t, s = split(e)
        C3(t, s, e).wait_recv()
        S(c3_ref(t, s, 1 - y), 36 + e).start()

    def qkv_leaves(n):
        return pltpu.make_async_copy(qkv.at[n], qkv_out.at[n], q_sem.at[n])

    tokT_leaves = pltpu.make_async_copy(tokT, tokT_out, t_sem)

    def probs_leave(h):
        return pltpu.make_async_copy(probs.at[h % 2], probs_out.at[h], p_sem.at[h % 2])

    def op_proj(n):
        def arrive():
            @pl.loop(0, 8)
            def _(k):
                def got(odd):
                    PS(f_ref(k, odd, other), 8 + k).wait_recv()
                    PS(g_ref(k, odd, False, other), 16 + k).wait_recv()

                by_parity(k, got)
                when(z > 0, lambda: PS(z_ref(k, other), k).wait_recv())

        when(n == 0, arrive)

        @pl.loop(0, 3)
        def _(t):
            cols = pl.ds(pl.multiple_of(t * 256, 256), 256)
            qkv[n, cols] = dot_tn(held[0, n // 2, n % 2, :, cols], tokT[...]).astype(bf16)

        qkv_leaves(n).start()

    def op_head(h):
        when(h >= 2, lambda: probs_leave(h - 2).wait())
        attend_head(h, dist, qkv, mixb, probs.at[h % 2])
        probs_leave(h).start()

    line = jnp.logical_and(y == 1, x == 1)
    source = jnp.logical_and(line, z == 3)

    def T(peer, n):
        return remote(tail, peer, ts.at[n], tr.at[0])

    def leave(t):
        return pltpu.make_async_copy(held.at[t], result.at[t], out_sem.at[t])

    def op_other(e):
        def tail_z():
            def go():
                when(z < 3, lambda: T(down, 0).wait_recv())
                when(z > 0, lambda: T(down, 0).start())
                T(yp, 1).start()

            when(line, go)

        def tail_x():
            def go():
                when(y == 0, lambda: T(yp, 1).wait_recv())
                T(xp, 2).start()

            when(x == 1, go)

        def out():
            t = e - 2

            def others():
                @pl.loop(0, 3)
                def _(s):
                    n = (t - 1) * 3 + s

                    def theirs():
                        S(c1_ref(t, s, other), n).wait_recv()
                        S(b2_ref(t, s, x, other), 9 + n).wait_recv()

                    when(t != z, theirs)
                    when(t == z, lambda: S(b1_ref(s, 1 - y, other), 45 + s).wait_recv())
                    S(c2_ref(t, s, 1 - x, other), 18 + n).wait_recv()
                    S(b2_ref(t, s, 1 - x, other), 27 + n).wait_recv()
                    S(c3_ref(t, s, 1 - y, other), 36 + n).wait_recv()

            when(t > 0, others)
            leave(t).start()

        def prepare():
            tokT[...] = tokens[...].astype(f32).T.astype(bf16)
            tokT_leaves.start()
            fill_distance(dist, seg_row, column)

        when(e == 0, tail_z)
        when(e == 1, tail_x)
        when(jnp.logical_and(e >= 2, e < 6), out)
        when(e == 6, prepare)

    def norms_here():
        for n in range(6):
            tail[pl.ds(0, 4), pl.ds(n * 128, 128)] = last[pl.ds(n, 4, stride=6)].astype(bf16)

    tail[...] = jnp.zeros_like(tail)
    when(source, norms_here)
    run_plan(z, GATHER_PLAN, [op_p0z, op_p0f, op_p0g, op_own, op_ownup, op_b1, op_bx, op_c1, op_b2, op_c2, op_b3,
                              op_c3, op_proj, op_head, op_other, op_cx])

    when(x == 0, lambda: T(xp, 2).wait_recv())
    when(x == 1, lambda: T(xp, 2).wait_send())

    def tail_sent():
        T(yp, 1).wait_send()
        when(z > 0, lambda: T(down, 0).wait_send())

    when(line, tail_sent)

    @pl.loop(0, 8)
    def _(k):
        def gone(odd):
            PF(k, odd).wait_send()
            PG(k, odd).wait_send()
            PS(f_ref(k, odd), 8 + k).wait_send()
            PS(g_ref(k, odd, False), 16 + k).wait_send()

        by_parity(k, gone)
        when(z < 3, lambda: PZ(k).wait_send())
        when(z > 0, lambda: PS(z_ref(k), k).wait_send())

    @pl.loop(0, 9)
    def _(e):
        t, s = split(e)
        C2(t, s, e).wait_send()
        B3(t, s, e).wait_send()
        C3(t, s, e).wait_send()

        def ups():
            C1U(t, s, e).wait_send()
            B2U(t, s, e).wait_send()

        def downs():
            C1D(t, s, e).wait_send()
            B2D(t, s, e).wait_send()

        when(jnp.logical_and(t <= z, z < 3), ups)
        when(jnp.logical_and(t >= z, z > 0), downs)

        def mine():
            B1(s).wait_send()
            S(b1_ref(s, 1 - y), 45 + s).wait_send()

        def theirs():
            S(c1_ref(t, s), e).wait_send()
            S(b2_ref(t, s, x), 9 + e).wait_send()

        when(t == z, mine)
        when(t != z, theirs)
        S(c2_ref(t, s, 1 - x), 18 + e).wait_send()
        S(b2_ref(t, s, 1 - x), 27 + e).wait_send()
        S(c3_ref(t, s, 1 - y), 36 + e).wait_send()

    norms[...] = tail[pl.ds(0, 4)].astype(f32)
    tokT_leaves.wait()
    for n in range(3):
        qkv_leaves(n).wait()
    for h in (HEADS - 2, HEADS - 1):
        probs_leave(h).wait()
    for t in range(4):
        leave(t).wait()


def gather_attend(blk, last, tokens, seg):
    Q = pltpu.SemaphoreType.DMA
    any_space = pl.BlockSpec(memory_space=pl.ANY)
    counts = [8] * 6 + [24, 24, 3, 3] + [9] * 12 + [48, 48, 3, 1]
    return pl.pallas_call(
        gather_attend_kernel,
        in_specs=[VM, VM, VM, VM],
        out_specs=[any_space, VM, any_space, any_space, VM, any_space],
        out_shape=[
            jax.ShapeDtypeStruct((4, 2, 2, D, D), bf16), jax.ShapeDtypeStruct((4, D), f32),
            *attend_shapes(),
        ],
        scratch_shapes=[
            pltpu.VMEM((4, 2, 2, D, D), bf16), pltpu.VMEM((LEN, LEN), f32), pltpu.VMEM((LEN, 8), f32),
            pltpu.VMEM((16, D), bf16),
            pltpu.VMEM((D, LEN), bf16), pltpu.VMEM((3, D, LEN), bf16), pltpu.VMEM((2, LEN, LEN), bf16),
            Q((4,)), Q, Q((3,)), Q((2,)), *[Q((n,)) for n in counts],
        ],
        compiler_params=pltpu.CompilerParams(
            collective_id=1, has_side_effects=True, vmem_limit_bytes=58 << 20
        ),
        name="gather_attend",
    )(blk, last, tokens, seg.reshape(1, LEN))


PLANE_ORDER = (1, 2, 3)
BACK_PLAN = (
    (
        7405680, 291331, 460403, 357748, 532515, 2369408, 4407315, 8484483, 2435092, 71206,
        7816773, 8525688, 3359796, 3547527, 9442784, 1067094, 3641624, 168519, 9664833, 7999792,
        5759611, 10585476, 14759989, 10651219, 2232916, 10523856, 9868632, 10768469, 9937841, 13713970,
        5386672, 12628646, 13870546, 5351347, 11908278, 12961475, 12695492, 15714242, 15724527,
    ),
    (
        33648, 225905, 263795, 329588, 8418784, 1472008, 7807782, 1053816, 8524673, 8026435,
        2658325, 4624676, 8095489, 14819351, 8750144, 10523175, 9646152, 13637766, 3490887, 9806228,
        2463286, 3658070, 13801285, 13869731, 5744036, 11644930, 2212148, 11773752, 12629336, 4317618,
        12760149, 3392422, 12866594, 11952146, 1135557, 12010182, 3327841, 6443600, 15683889,
    ),
    (
        7405680, 197121, 7631730, 401425, 7701252, 8458880, 489009, 1081975, 4200056, 8855952,
        9533704, 9580666, 8098594, 14816416, 1541281, 8802437, 9752642, 9840277, 4301362, 9941074,
        11618344, 3614673, 4662179, 12654770, 14722468, 4596928, 10921938, 377523, 12825875, 12891190,
        5683126, 12923971, 3692356, 13051334, 4542741, 13850849, 5530675, 5584229, 15688531,
    ),
    (
        7405680, 225793, 7540738, 422944, 7763204, 8601619, 3154181, 2232951, 8471168, 2379906,
        1131542, 4421667, 9512336, 4277650, 5386873, 10582675, 8062740, 10650850, 3245701, 8868256,
        3446164, 11645603, 9875649, 9917632, 2598096, 12759973, 10998211, 12891302, 1422600, 13022917,
        12050483, 5453511, 4605734, 1626647, 5580853, 13850184, 14759782, 5728104, 15685688,
    ),
)

GATHER_PLAN = (
    (
        196870, 1026, 7406867, 7401746, 1050388, 15787542, 9443093, 2494834, 2303104, 9565557,
        7631858, 2261281, 2127457, 9827248, 8529701, 9630912, 12748737, 16147091, 6788304, 8835793,
        6330034, 16233847, 13924563, 16287189, 6674082, 14129073, 14182019, 6534048, 14247044, 8955874,
        10007656, 14345121, 14399159, 14722211, 12101030, 15050980, 15724513, 15724527,
    ),
    (
        3273200, 3289330, 5243142, 152067, 7704947, 327684, 1050387, 15941969, 4200210, 1143843,
        1318933, 7770134, 8910310, 2565186, 7807525, 2225286, 6694646, 9658773, 16236992, 8616069,
        8966338, 8675986, 14874833, 10596708, 13788564, 6526870, 14013651, 10934230, 14202008, 11755623,
        10855528, 10729184, 14332633, 14987445, 11000759, 14917794, 15055016, 15724513,
    ),
    (
        3535667, 9647348, 7800565, 7733589, 1442806, 1026, 460049, 4556582, 1184646, 16281976,
        5444887, 1110408, 1369703, 9782128, 4478104, 8396839, 6694391, 9859732, 2355748, 2171522,
        15753314, 8503744, 13681249, 14706897, 9556946, 11777426, 13919412, 14002021, 14063459, 14137521,
        14276790, 10936976, 12049370, 10789544, 15048865, 11576739, 14935218, 15724513,
    ),
    (
        16266807, 9976055, 9958998, 419415, 66151, 12059670, 239192, 458769, 1226501, 8721427,
        2166807, 4617510, 1405255, 2418343, 15738736, 2302705, 16085832, 2487141, 2135656, 12697824,
        9552528, 7655888, 13820291, 13890709, 13926514, 6521986, 8508914, 11625620, 14049939, 11917219,
        11821528, 11970656, 9613529, 14867109, 10673060, 11772389, 11706596, 15724515,
    ),
)


Q_PART = 96
COLS = D // 2


def reduce_back_kernel(wide, down, w, qkv_in, dO_in, mixb_in, probs_in, tokT_in, gbranch_in, first, norm_in,
                       grad_in, flat_out, own, sl, lc3, lc2, lcz, lczx, lb3, lbz, lbzx, lb1, lf, lg, lz, stage,
                       dO, mixb, tokT, gbranch, theirs, probs, ds_all, wv, qkv, fchunk, flat, nacc, nx, ny, nz, nc,
                       own_sem, in_sem, p_sem, w_sem, f_sem, g_sem, o_sem, sib_s, sib_r, st_s, st_r,
                       c3s, c3r, b3s, b3r, c2s, c2r, bus, bur, bds, bdr, cus, cur, cds, cdr, b1s, b1r,
                       fs, fr, gs, gr, zs_, zr_, ns, nr, share_s, share_r, aft_s, aft_r):
    i, c, z, y, x = place()
    xp, yp, sib, up, down_peer = partners(i, c, z, y, x)
    base = c * HALF
    mine = pl.ds(pl.multiple_of(base, 16), HALF)
    other = pl.ds(pl.multiple_of((1 - c) * HALF, 16), HALF)
    planes = [wide.at[0], wide.at[1], down]

    def remote(src, dst, peer, s, r):
        return pltpu.make_async_remote_copy(
            src_ref=src, dst_ref=dst, send_sem=s, recv_sem=r, device_id=peer, device_id_type=MESH
        )

    def local_in(t):
        return pltpu.make_async_copy(planes[t - 1].at[:, :, mine], own.at[t], own_sem.at[t])

    def sib_in(t, s, n):
        k = 2 * ((t - 1) * 3 + s) + n
        start, size = (s * B_PART, B_PART) if n == 0 else (3 * B_PART + s * C_PART, C_PART)
        there = pl.ds(pl.multiple_of((1 - c) * HALF + start, 16), size)
        return remote(planes[t - 1].at[:, :, there], sl.at[t, :, :, pl.ds(start, size)], sib, sib_s.at[k], sib_r.at[k])

    for t in PLANE_ORDER:
        local_in(t).start()
    take = [
        pltpu.make_async_copy(a, b, in_sem.at[n])
        for n, (a, b) in enumerate(
            ((qkv_in, qkv), (dO_in, dO), (mixb_in, mixb), (gbranch_in, gbranch), (tokT_in, tokT))
        )
    ]
    for n in range(3):
        take[n].start()

    def probs_come(h):
        return pltpu.make_async_copy(probs_in.at[h], probs.at[h % 2], p_sem.at[h % 2])

    probs_come(0).start()
    for n in (3, 4):
        take[n].start()
    enter_more(i, c, z, y, x)
    for t in PLANE_ORDER:
        for s in range(3):
            for n in range(2):
                sib_in(t, s, n).start()
    nacc[...] = norm_in[...]
    NX = remote(nacc, nx, xp, ns.at[0], nr.at[0])
    NY = remote(nacc, ny, yp, ns.at[1], nr.at[1])
    NZ = remote(nacc, nz, up, ns.at[2], nr.at[2])
    NC = remote(nacc, nc, sib, ns.at[3], nr.at[3])
    line = jnp.logical_and(x == 1, y == 1)
    last_line = jnp.logical_and(line, z == 3)
    when(x == 0, lambda: NX.start())
    for move in take:
        move.wait()

    def rb(s, k=0, size=B_PART):
        return pl.ds(pl.multiple_of(s * B_PART + k, 16), size)

    def rc(s, k=0, size=C_PART):
        return pl.ds(pl.multiple_of(3 * B_PART + s * C_PART + k, 16), size)

    def add_rows(dst, src, rows):
        @pl.loop(0, rows // 16)
        def _(n):
            k = pl.multiple_of(n * 16, 16)
            a = dst(k)
            a[...] = a[...] + src(k)[...]

    r16 = lambda k: pl.ds(k, 16)
    split = lambda e: (e // 3 + 1, e % 3)

    def C3(t, s, e):
        return remote(own.at[t, 1 - y, :, rc(s)], lc3.at[e], yp, c3s.at[e], c3r.at[e])

    def B3(t, s, e):
        return remote(own.at[t, :, 1 - x, rb(s)], lb3.at[e], xp, b3s.at[e], b3r.at[e])

    def C2(t, s, e):
        return remote(own.at[t, y, 1 - x, rc(s)], lc2.at[e], xp, c2s.at[e], c2r.at[e])

    def BU(t, s, e):
        return remote(own.at[t, :, x, rb(s)], lbz.at[e], up, bus.at[e], bur.at[e])

    def BD(t, s, e, extra=False):
        return remote(own.at[t, :, x, rb(s)], lbzx.at[s] if extra else lbz.at[e], down_peer, bds.at[e], bdr.at[e])

    def CU(t, s, e):
        return remote(own.at[t, y, x, rc(s)], lcz.at[e], up, cus.at[e], cur.at[e])

    def CD(t, s, e, extra=False):
        return remote(own.at[t, y, x, rc(s)], lczx.at[s] if extra else lcz.at[e], down_peer, cds.at[e], cdr.at[e])

    def B1(s):
        return remote(own.at[z, 1 - y, x, rb(s)], lb1.at[s], yp, b1s.at[s], b1r.at[s])

    def op_sum(e):
        t, s = split(e)

        for k in (1, 2, 3):
            when(jnp.logical_and(t == k, s == 0), lambda k=k: local_in(k).wait())
            for m in range(3):
                def arrive(k=k, m=m):
                    for n in range(2):
                        sib_in(k, m, n).wait_recv()

                when(e == (k - 1) * 3 + m, arrive)
        add_rows(lambda k: own.at[t, :, :, rb(s, k, 16)], lambda k: sl.at[t, :, :, rb(s, k, 16)], B_PART)
        add_rows(lambda k: own.at[t, :, :, rc(s, k, 16)], lambda k: sl.at[t, :, :, rc(s, k, 16)], C_PART)
        C3(t, s, e).start()
        B3(t, s, e).start()

    def op_c3(e):
        t, s = split(e)
        C3(t, s, e).wait_recv()
        add_rows(lambda k: own.at[t, y, :, rc(s, k, 16)], lambda k: lc3.at[e, :, r16(k)], C_PART)
        C2(t, s, e).start()

    def op_b3(e):
        t, s = split(e)
        B3(t, s, e).wait_recv()
        add_rows(lambda k: own.at[t, :, x, rb(s, k, 16)], lambda k: lb3.at[e, :, r16(k)], B_PART)

    def op_c2(e):
        t, s = split(e)
        C2(t, s, e).wait_recv()
        add_rows(lambda k: own.at[t, y, x, rc(s, k, 16)], lambda k: lc2.at[e, r16(k)], C_PART)

    def op_bz(e):
        t, s = split(e)
        dst = lambda k: own.at[t, :, x, rb(s, k, 16)]

        def from_below():
            BU(t, s, e).wait_recv()
            add_rows(dst, lambda k: lbz.at[e, :, r16(k)], B_PART)

        when(jnp.logical_and(t >= z, z > 0), from_below)

        def from_above():
            BD(t, s, e).wait_recv()
            add_rows(dst, lambda k: lbz.at[e, :, r16(k)], B_PART)

        when(t < z, lambda: when(z < 3, from_above))

        def from_above_last():
            BD(t, s, e).wait_recv()
            add_rows(dst, lambda k: lbzx.at[s, :, r16(k)], B_PART)

        when(jnp.logical_and(t == z, z < 3), from_above_last)
        when(t > z, lambda: BU(t, s, e).start())
        when(t == z - 1, lambda: BD(t, s, e, True).start())
        when(t < z - 1, lambda: BD(t, s, e).start())
        when(t == z, lambda: B1(s).start())

    def op_cz(e):
        t, s = split(e)
        dst = lambda k: own.at[t, y, x, rc(s, k, 16)]

        def from_below():
            CU(t, s, e).wait_recv()
            add_rows(dst, lambda k: lcz.at[e, r16(k)], C_PART)

        when(jnp.logical_and(t >= z, z > 0), from_below)

        def from_above():
            CD(t, s, e).wait_recv()
            add_rows(dst, lambda k: lcz.at[e, r16(k)], C_PART)

        when(t < z, lambda: when(z < 3, from_above))

        def from_above_last():
            CD(t, s, e).wait_recv()
            add_rows(dst, lambda k: lczx.at[s, r16(k)], C_PART)

        when(jnp.logical_and(t == z, z < 3), from_above_last)
        when(t > z, lambda: CU(t, s, e).start())
        when(t == z - 1, lambda: CD(t, s, e, True).start())
        when(t < z - 1, lambda: CD(t, s, e).start())

    def op_b1(e):
        t, s = split(e)
        B1(s).wait_recv()
        add_rows(lambda k: own.at[z, y, x, rb(s, k, 16)], lambda k: lb1.at[s, r16(k)], B_PART)

    def op_head(h):
        probs_come(h).wait()
        when(h < HEADS - 1, lambda: probs_come(h + 1).start())
        attend_back_head(h, qkv, dO, mixb, probs.at[h % 2], ds_all)

    def columns(g):
        return pl.ds(pl.multiple_of(g * COLS, 128), COLS)

    def stage_copy(e):
        g, n = e // 4, e % 4
        return remote(
            stage.at[e], sl.at[0, n // 2, n % 2, :, columns(g)], sib, st_s.at[e], st_r.at[e]
        )

    def op_dw(e):
        g, n = e // 4, e % 4
        cols = columns(g)

        def put(half, value):
            if half == 0:
                own[0, n // 2, n % 2, :, cols] = value.astype(bf16)
            else:
                stage[e] = value.astype(bf16)

        def inputs():
            right = qkv[n, pl.ds(pl.multiple_of(g * COLS, 128), COLS)]
            for half, rows in ((0, mine), (1, other)):
                put(half, dot_nt(tokT[rows], right))

        def output():
            right = gbranch[:, cols]
            for half, rows in ((0, mine), (1, other)):
                put(half, dot(mixb[rows], right))

        when(n < 3, inputs)
        when(n == 3, output)
        stage_copy(e).start()

    def rq(k, n=0, size=Q_PART):
        return pl.ds(pl.multiple_of(k * Q_PART + n, 16), size)

    def F0(e, g, k, odd):
        src = own.at[0, :, 1 - x, rq(k), columns(g)] if odd else own.at[0, 1 - y, :, rq(k), columns(g)]
        return remote(src, lf.at[e], xp if odd else yp, fs.at[e], fr.at[e])

    def G0(e, g, k, odd):
        if odd:
            return remote(own.at[0, 1 - y, x, rq(k), columns(g)], lg.at[e], yp, gs.at[e], gr.at[e])
        return remote(own.at[0, y, 1 - x, rq(k), columns(g)], lg.at[e], xp, gs.at[e], gr.at[e])

    def Z0(e, g, k):
        return remote(own.at[0, y, x, rq(k), columns(g)], lz.at[e], down_peer, zs_.at[e], zr_.at[e])

    def by_parity(k, fn):
        when(k % 2 == 0, lambda: fn(False))
        when(k % 2 == 1, lambda: fn(True))

    def op_sum0(e):
        g, k = e // 4, e % 4

        def arrive():
            @pl.loop(0, 4)
            def _(n):
                stage_copy(g * 4 + n).wait_recv()

        when(k == 0, arrive)
        add_rows(
            lambda n: own.at[0, :, :, rq(k, n, 16), columns(g)],
            lambda n: sl.at[0, :, :, rq(k, n, 16), columns(g)], Q_PART,
        )
        by_parity(k, lambda odd: F0(e, g, k, odd).start())

    def op_f0(e):
        g, k = e // 4, e % 4

        def turn(odd):
            F0(e, g, k, odd).wait_recv()
            if odd:
                dst = lambda n: own.at[0, :, x, rq(k, n, 16), columns(g)]
            else:
                dst = lambda n: own.at[0, y, :, rq(k, n, 16), columns(g)]
            add_rows(dst, lambda n: lf.at[e, :, r16(n)], Q_PART)
            G0(e, g, k, odd).start()

        by_parity(k, turn)

    def op_g0(e):
        g, k = e // 4, e % 4
        by_parity(k, lambda odd: G0(e, g, k, odd).wait_recv())
        add_rows(lambda n: own.at[0, y, x, rq(k, n, 16), columns(g)], lambda n: lg.at[e, r16(n)], Q_PART)

    def op_z0(e):
        g, k = e // 4, e % 4

        def arrive():
            Z0(e, g, k).wait_recv()
            add_rows(lambda n: own.at[0, y, x, rq(k, n, 16), columns(g)], lambda n: lz.at[e, r16(n)], Q_PART)

        when(z < 3, arrive)
        when(z > 0, lambda: Z0(e, g, k).start())

    def first_in(q):
        return pltpu.make_async_copy(first.at[pl.ds(pl.multiple_of(q * 256, 256), 256)], fchunk, f_sem)

    def grad_out(q):
        return pltpu.make_async_copy(fchunk, grad_in.at[pl.ds(pl.multiple_of(q * 256, 256), 256)], g_sem)

    def weight_in(n):
        target = (probs.at[0, pl.ds(0, D), pl.ds(0, D)], ds_all.at[pl.ds(0, D), pl.ds(0, D)], wv)[n]
        return pltpu.make_async_copy(w.at[0, n // 2, n % 2], target, w_sem.at[n])

    def op_gin(q):
        def weights():
            for n in range(3):
                weight_in(n).wait()

        when(q == 0, weights)
        when(q > 0, lambda: grad_out(q - 1).wait())
        first_in(q).start()
        cols = pl.ds(pl.multiple_of(q * 256, 256), 256)
        d = pl.ds(0, D)
        acc = dot(probs[0, d, d], qkv[0, :, cols]) + dot(ds_all[d, d], qkv[1, :, cols])
        acc = (acc + dot(wv[...], qkv[2, :, cols])).T
        first_in(q).wait()
        fchunk[...] += acc
        grad_out(q).start()

    def op_other(e):
        def norm_y():
            def go():
                NX.wait_recv()
                nacc[...] += nx[...]
                when(y == 0, lambda: NY.start())

            when(x == 1, go)

        def norm_z():
            def go():
                NY.wait_recv()
                nacc[...] += ny[...]

                def more():
                    NZ.wait_recv()
                    nacc[...] += nz[...]

                when(z > 0, more)
                when(z < 3, lambda: NZ.start())
                when(z == 3, lambda: NC.start())

            when(line, go)

        def load():
            for n in range(3):
                weight_in(n).start()

        when(e == 0, norm_y)
        when(e == 1, norm_z)
        when(e == 2, load)

    run_plan(z, BACK_PLAN, [op_sum, op_c3, op_b3, op_c2, op_bz, op_cz, op_b1, op_head, op_dw, op_sum0, op_f0,
                            op_g0, op_z0, op_gin, op_other])

    spread = jnp.logical_or(z == 1, z == 2)

    def flatten(half, get):
        def plain():
            for n in range(6):
                flat[pl.ds(half * (6 * HALF) + n, HALF, stride=6)] = get(pl.ds(0, HALF), pl.ds(n * 128, 128)).astype(f32)

        def swapped():
            for n in range(6):
                for j in range(2):
                    value = get(pl.ds(j * (D // 4), D // 4), pl.ds(n * 128, 128)).astype(f32)
                    flat[pl.ds(half * 12 + j * 6 + n, D // 4, stride=24)] = value

        when(jnp.logical_not(spread), plain)
        when(spread, swapped)

    share = remote(own.at[z, y, x], theirs, sib, share_s, share_r)
    share.start()
    flatten(c, lambda rows, cols: own[z, y, x, rows, cols])

    @pl.loop(0, 9)
    def _(e):
        t, s = split(e)
        C3(t, s, e).wait_send()
        B3(t, s, e).wait_send()
        C2(t, s, e).wait_send()

        def went_up():
            BU(t, s, e).wait_send()
            CU(t, s, e).wait_send()

        def went_down():
            BD(t, s, e).wait_send()
            CD(t, s, e).wait_send()

        when(t > z, went_up)
        when(t < z, went_down)
        when(t == z, lambda: B1(s).wait_send())

    @pl.loop(0, 8)
    def _(e):
        g, k = e // 4, e % 4
        stage_copy(e).wait_send()

        def gone(odd):
            F0(e, g, k, odd).wait_send()
            G0(e, g, k, odd).wait_send()

        by_parity(k, gone)
        when(z > 0, lambda: Z0(e, g, k).wait_send())

    for t in (1, 2, 3):
        for s in range(3):
            for n in range(2):
                sib_in(t, s, n).wait_send()
    when(x == 0, lambda: NX.wait_send())
    when(jnp.logical_and(x == 1, y == 0), lambda: NY.wait_send())
    when(jnp.logical_and(line, z < 3), lambda: NZ.wait_send())

    def norm_last():
        NC.wait_recv()
        NC.wait_send()
        nacc[...] += nc[...]

    when(last_line, norm_last)
    grad_out(3).wait()
    share.wait_recv()
    flatten(1 - c, lambda rows, cols: theirs[rows, cols])
    share.wait_send()
    body, head_rows, after = pl.ds(0, 6 * D), pl.ds(0, 24), pl.ds(6 * D, 24)
    leave = pltpu.make_async_copy(flat.at[body], flat_out.at[body], o_sem.at[0])
    leave.start()

    def ending():
        for n in range(6):
            flat[pl.ds(6 * D + n, 4, stride=6)] = nacc[:, pl.ds(n * 128, 128)]

    when(i == 15, ending)
    give = remote(flat.at[head_rows], flat.at[after], (c, i - 1), aft_s, aft_r)
    when(i > 0, lambda: give.start())
    when(i < 15, lambda: give.wait_recv())
    leave_after = pltpu.make_async_copy(flat.at[after], flat_out.at[after], o_sem.at[1])
    leave_after.start()
    when(i > 0, lambda: give.wait_send())
    leave.wait()
    leave_after.wait()


def enter_more(i, c, z, y, x):
    barrier = pltpu.get_barrier_semaphore()
    xp, yp, sib, up, down = partners(i, c, z, y, x)

    def signal(peer):
        pl.semaphore_signal(barrier, inc=1, device_id=peer, device_id_type=MESH)

    for peer in (xp, yp, sib):
        signal(peer)
    when(z > 0, lambda: signal(down))
    when(z < 3, lambda: signal(up))
    when(jnp.logical_and(x == 0, i > 0), lambda: signal((c, i - 1)))
    when(jnp.logical_and(x == 1, i < 15), lambda: signal((c, i + 1)))
    more = 1 - jnp.where(i == 0, 1, 0) - jnp.where(i == 15, 1, 0)
    pl.semaphore_wait(barrier, 3 + jnp.minimum(z, 1) + jnp.minimum(3 - z, 1) + more)


def reduce_back(wide, down, w, qkv, dO, mixb, probs, tokT, gbranch, first, norms):
    Q = pltpu.SemaphoreType.DMA
    V = lambda *s: pltpu.VMEM(s, bf16)
    F = lambda *s: pltpu.VMEM(s, f32)
    A = pl.BlockSpec(memory_space=pl.ANY)
    return pl.pallas_call(
        reduce_back_kernel,
        in_specs=[A] * 10 + [VM],
        out_specs=[A, A],
        out_shape=[jax.ShapeDtypeStruct((LEN, D), f32), jax.ShapeDtypeStruct((6 * D + 24, 128), f32)],
        scratch_shapes=[
            V(4, 2, 2, HALF, D), V(4, 2, 2, HALF, D), V(9, 2, C_PART, D), V(9, C_PART, D), V(9, C_PART, D),
            V(3, C_PART, D), V(9, 2, B_PART, D), V(9, 2, B_PART, D), V(3, 2, B_PART, D), V(3, B_PART, D),
            V(8, 2, Q_PART, COLS), V(8, Q_PART, COLS), V(8, Q_PART, COLS), V(8, HALF, COLS),
            V(D, LEN), V(D, LEN), V(D, LEN), V(LEN, D), V(HALF, D), V(2, LEN, LEN), V(LEN, LEN), V(D, D), V(3, D, LEN),
            F(256, D), F(6 * D + 24, 128), F(4, D), F(4, D), F(4, D), F(4, D), F(4, D),
            Q((4,)), Q((5,)), Q((2,)), Q((3,)), Q, Q, Q((2,)), Q((18,)), Q((18,)), Q((8,)), Q((8,)),
            *[Q((9,))] * 14, Q((3,)), Q((3,)), *[Q((8,))] * 6, Q((4,)), Q((4,)), Q, Q, Q, Q,
        ],
        compiler_params=pltpu.CompilerParams(
            collective_id=2, has_side_effects=True, vmem_limit_bytes=55 << 20
        ),
        name="reduce_back",
    )(wide, down, w, qkv, dO, mixb, probs, tokT, gbranch, first, norms)

SQUARE = D * D
TAIL = 4 * D


def from_wide(blocks):
    return blocks.reshape(4, 4, D // 4, D).transpose(0, 2, 1, 3).reshape(D, FF)


def to_wide(value):
    return value.reshape(4, D // 4, 4, D).transpose(0, 2, 1, 3).reshape(2, 2, D, D)


def gather_and_attend(master, tokens, segments):
    count = lax.axis_size("zero")
    index = lax.axis_index("zero")
    size = 16 * SQUARE // count
    last = master[-TAIL:]
    before = lax.ppermute(last, "zero", [(k, k + 1) for k in range(count - 1)])
    joined = jnp.concatenate([before, master])
    block = lax.dynamic_slice(joined, (TAIL - TAIL // count * index,), (size,))
    if count == 16:
        block, last = block.reshape(6 * D, 128), last.reshape(24, 128)
        blocks, norms, *attended = gather_attend(block, last, tokens, segments)
    else:
        natural = lax.all_gather(block.astype(bf16).reshape(-1, D), "zero", axis=0, tiled=True)
        parts = natural.reshape(4, 4 * D, D)
        wide = [to_wide(parts[k].reshape(D, FF)) for k in (1, 2)]
        blocks = jnp.stack([parts[0].reshape(2, 2, D, D), *wide, parts[3].reshape(2, 2, D, D)])
        last = last.astype(bf16).astype(f32)
        norms = lax.psum(jnp.where(index == count - 1, last, 0.0), "zero").reshape(4, D)
        attended = attend(tokens, blocks, segments)
    return blocks, norms, *attended


def back_and_scatter(blocks, tokT, qkv, mixed, probs, grad_mixed, first_grad, branch_grad, norm_grads,
                     down_grad, wide_grad):
    count = lax.axis_size("zero")
    index = lax.axis_index("zero")
    if count == 16:
        input_grad, joined = reduce_back(
            wide_grad, down_grad, blocks, qkv, grad_mixed, mixed, probs, tokT, branch_grad, first_grad,
            norm_grads,
        )
        joined = joined.reshape(-1)
    else:
        square, input_grad = attend_back(
            blocks, tokT, qkv, mixed, probs, grad_mixed, first_grad, branch_grad
        )
        natural = [from_wide(wide_grad[k]).reshape(4 * D, D) for k in (0, 1)]
        natural = jnp.concatenate([square.reshape(4 * D, D), *natural, down_grad.reshape(4 * D, D)])
        block = lax.psum_scatter(natural, "zero", scatter_dimension=0, tiled=True)
        block = lax.psum(block.astype(f32), "dp")
        tail = lax.psum(norm_grads, ("dp", "zero"))
        flat = block.reshape(-1)
        after = lax.ppermute(flat[:TAIL], "zero", [(k + 1, k) for k in range(count - 1)])
        joined = jnp.concatenate([flat, jnp.where(index == count - 1, tail.reshape(-1), after)])
    shard = 16 * SQUARE // count + TAIL // count
    return input_grad, lax.dynamic_slice(joined, (TAIL // count * index,), (shard,))


def local(tokens, segments, cotangent, master, moment_one, moment_two):
    blocks, norms, tokT, qkv, mixed, probs = gather_and_attend(master, tokens, segments)
    output, first_grad, grad_mixed, branch_grad, norm_grads, down_grad, wide_grad = feed(
        tokens, cotangent, mixed, blocks, norms
    )
    input_grad, grad_shard = back_and_scatter(
        blocks, tokT, qkv, mixed, probs, grad_mixed, first_grad, branch_grad, norm_grads,
        down_grad.reshape(2, 2, D, D), wide_grad.reshape(2, 2, 2, D, D),
    )
    grad_shard = grad_shard / (lax.axis_size("zero") * lax.axis_size("dp"))
    first = beta_one * moment_one + (1.0 - beta_one) * grad_shard
    second = beta_two * moment_two + (1.0 - beta_two) * grad_shard * grad_shard
    update = first / correct_one / (jnp.sqrt(second / correct_two) + adam_eps)
    master_new = master - learn_rate * (update + weight_decay * master)
    return (
        output,
        input_grad,
        grad_shard,
        first,
        second,
        master_new,
        master_new.astype(jnp.bfloat16),
    )


def solution(mesh):
    return jax.shard_map(
        local,
        mesh=mesh,
        in_specs=(
            P(("dp", "zero"), None),
            P(("dp", "zero")),
            P(("dp", "zero"), None),
            P("zero"),
            P("zero"),
            P("zero"),
        ),
        out_specs=(
            P(("dp", "zero"), None),
            P(("dp", "zero"), None),
            P("zero"),
            P("zero"),
            P("zero"),
            P("zero"),
            P("zero"),
        ),
        check_vma=False,
    )
```

```python
import functools

import jax
import jax.numpy as jnp
from jax import lax
from jax.sharding import PartitionSpec as P
import jax.experimental.pallas as pl
import jax.experimental.pallas.tpu as pltpu

D = 768
HEADS = 12
HEAD = 64
FF = 3072
LEN = 1024


learn_rate = 0.02
beta_one = 0.9
beta_two = 0.999
adam_eps = 1e-08
weight_decay = 0.01
correct_one = 1.0 - 0.9**10
correct_two = 1.0 - 0.999**10
norm_eps = 1e-06
inv_root_two = 0.7071067811865476
inv_root_tau = 0.3989422804014327


bf16=jnp.bfloat16; f32=jnp.float32
FAR=1e33
VM=pl.BlockSpec(memory_space=pltpu.VMEM)

def dot(a,b): return lax.dot_general(a,b,(((1,),(0,)),((),())),preferred_element_type=f32)
def dot_tn(a,b): return lax.dot_general(a,b,(((0,),(0,)),((),())),preferred_element_type=f32)
def dot_nt(a,b): return lax.dot_general(a,b,(((1,),(1,)),((),())),preferred_element_type=f32)

def slope(h):
    return jnp.exp2(-8.0/HEADS*(jnp.full((1,1),h,jnp.int32).astype(f32)+1.0))

def fill_distance(dist,seg_row,column):
    column[...]=jnp.broadcast_to(seg_row[...].astype(f32),(8,LEN)).T
    @pl.loop(0,LEN//128)
    def _(k):
        r=pl.ds(pl.multiple_of(k*128,128),128)
        kk=(lax.broadcasted_iota(jnp.int32,(128,LEN),0)+k*128)
        qq=lax.broadcasted_iota(jnp.int32,(128,LEN),1)
        d=jnp.abs(kk-qq).astype(f32)
        dist[r]=jnp.where(column[r,0:1]==seg_row[...].astype(f32),d,FAR)

QB=256
def project_all(w,tokT,qkv):
    @pl.loop(0,3)
    def _(n):
        @pl.loop(0,3)
        def _(t):
            c=pl.ds(pl.multiple_of(t*256,256),256)
            qkv[n,c]=dot_tn(w[0,n//2,n%2,:,c],tokT[...]).astype(bf16)

def attend_head(h,dist,qkv,mixb,probs):
    rows=pl.ds(pl.multiple_of(h*HEAD,HEAD),HEAD)
    keys=qkv[1,rows].astype(f32).T.astype(bf16)
    s=dot(keys,qkv[0,rows]*bf16(0.125))-slope(h)*dist[...]
    e=jnp.exp(s-jnp.max(s,0,keepdims=True))
    p=(e*(1.0/jnp.sum(e,0,keepdims=True))).astype(bf16)
    probs[...]=p
    mixb[rows]=dot(qkv[2,rows],p).astype(bf16)

def attend_back_head(h,qkv,dO,mixb,probs,ds_all):
    rows=pl.ds(pl.multiple_of(h*HEAD,HEAD),HEAD)
    values=qkv[2,rows].astype(f32).T.astype(bf16)
    grad_q=[]
    for b in range(LEN//QB):
        cols=pl.ds(b*QB,QB)
        do=dO[rows,cols]
        dp=dot(values,do)
        delta=jnp.sum(do.astype(f32)*mixb[rows,cols].astype(f32),0,keepdims=True)
        ds=(probs[:,cols].astype(f32)*(dp-delta)).astype(bf16)
        ds_all[:,cols]=ds
        grad_q.append((dot(qkv[1,rows],ds)*0.125).astype(bf16))
    grad_k=(dot_nt(qkv[0,rows],ds_all[...])*0.125).astype(bf16)
    grad_v=dot_nt(dO[rows],probs[...]).astype(bf16)
    for b in range(LEN//QB):
        qkv[0,rows,pl.ds(b*QB,QB)]=grad_q[b]
    qkv[1,rows]=grad_k
    qkv[2,rows]=grad_v

def attend_kernel(tokens,w,seg_row,tokT,qkv,mixb,probs_out,dist,column,probs,sem):
    tokT[...]=tokens[...].astype(f32).T.astype(bf16)
    fill_distance(dist,seg_row,column)
    project_all(w,tokT,qkv)
    @pl.loop(0,HEADS)
    def _(h):
        attend_head(h,dist,qkv,mixb,probs)
        move=pltpu.make_async_copy(probs,probs_out.at[h],sem)
        move.start()
        move.wait()

def attend_shapes():
    S=jax.ShapeDtypeStruct
    return [S((D,LEN),bf16),S((3,D,LEN),bf16),S((D,LEN),bf16),S((HEADS,LEN,LEN),bf16)]

ANY=pl.BlockSpec(memory_space=pl.ANY)

def attend(tokens,w,seg):
    return pl.pallas_call(attend_kernel,grid=(1,),
        in_specs=[VM,pl.BlockSpec((1,2,2,D,D),lambda i:(0,0,0,0,0)),VM],out_specs=[VM]*3+[ANY],
        out_shape=attend_shapes(),
        scratch_shapes=[pltpu.VMEM((LEN,LEN),f32),pltpu.VMEM((LEN,8),f32),pltpu.VMEM((LEN,LEN),bf16),pltpu.SemaphoreType.DMA],
        compiler_params=pltpu.CompilerParams(vmem_limit_bytes=58<<20),name="attend")(tokens,w,seg.reshape(1,LEN))

def attend_back_kernel(w,tokT,qkv_in,mixb,probs_in,dO,first,gbranch,g0,grad_in,qkv,probs,ds_all,sem,qkv_sem):
    take=pltpu.make_async_copy(qkv_in,qkv,qkv_sem)
    take.start()
    take.wait()
    @pl.loop(0,HEADS)
    def _(h):
        move=pltpu.make_async_copy(probs_in.at[h],probs,sem)
        move.start()
        move.wait()
        attend_back_head(h,qkv,dO,mixb,probs,ds_all)
    g0[1,1]=dot(mixb[...],gbranch[...]).astype(bf16)
    for n in range(3):
        g0[n//2,n%2]=dot_nt(tokT[...],qkv[n]).astype(bf16)
    @pl.loop(0,4)
    def _(t):
        c=pl.ds(pl.multiple_of(t*256,256),256)
        acc=dot(w[0,0,0],qkv[0,:,c])+dot(w[0,0,1],qkv[1,:,c])+dot(w[0,1,0],qkv[2,:,c])
        grad_in[c]=first[c]+acc.T

def attend_back(w,tokT,qkv,mixb,probs,dO,first,gbranch):
    return pl.pallas_call(attend_back_kernel,grid=(1,),
        in_specs=[pl.BlockSpec((1,2,2,D,D),lambda i:(0,0,0,0,0)),VM,ANY,VM,ANY,VM,VM,VM],out_specs=[VM]*2,
        out_shape=[jax.ShapeDtypeStruct((2,2,D,D),bf16),jax.ShapeDtypeStruct((LEN,D),f32)],
        scratch_shapes=[pltpu.VMEM((3,D,LEN),bf16),pltpu.VMEM((LEN,LEN),bf16),pltpu.VMEM((LEN,LEN),bf16),pltpu.SemaphoreType.DMA,pltpu.SemaphoreType.DMA],
        compiler_params=pltpu.CompilerParams(vmem_limit_bytes=60<<20),name="attend_back")(w,tokT,qkv,mixb,probs,dO,first,gbranch)

TB=256
def feed_kernel(tokens,cot,mixb,w,norms,output,first,dO,gbranch,ng,gdown,gwide,inner,wide,gffn,fa,fb,acc,hid,wo,w1,w2,w3,w_sem,wo_sem):
    step=pl.program_id(0)
    gain1=norms[0:1]; shift1=norms[1:2]; gain2=norms[2:3]; shift2=norms[3:4]
    def stats(v):
        c=v-jnp.mean(v,-1,keepdims=True)
        r=lax.rsqrt(jnp.mean(c*c,-1,keepdims=True)+norm_eps)
        return c*r,r
    def back(e,n,r):
        return r*(e-jnp.mean(e,-1,keepdims=True)-n*jnp.mean(e*n,-1,keepdims=True))
    W=lambda p,j: (w1,w2)[p-1][j].reshape(D,D)
    WD=lambda j: w3[j].reshape(D,D)
    WO=lambda: wo[...].reshape(D,D)
    def load(p,j):
        source=w.at[p,j] if p==3 else w.at[p,:,j]
        return pltpu.make_async_copy(source,(w1,w2,w3)[p-1].at[j],w_sem.at[p-1,j])
    load_out=pltpu.make_async_copy(w.at[0,3],wo,wo_sem)
    @pl.when(step==0)
    def _():
        load_out.start()
        for j in range(4):
            for p in (1,2,3): load(p,j).start()
        ng[...]=jnp.zeros_like(ng)
        load_out.wait()
    @pl.when(step<LEN//TB)
    def _():
        rows=pl.ds(pl.multiple_of(step*TB,TB),TB)
        branch=dot_tn(mixb[...],WO())
        n1,r1=stats(tokens[...].astype(f32)+branch)
        l1=n1*gain1+shift1
        inner[rows]=l1.astype(bf16)
        acc[...]=l1
        @pl.loop(0,2)
        def _(n):
            js=(2*n,2*n+1)
            @pl.when(step==0)
            def _():
                for j in js:
                    for p in (1,2,3): load(p,j).wait()
            inn=inner[rows]
            sides=[(dot(inn,W(1,j)),dot(inn,W(2,j))) for j in js]
            total=None
            for j,(ga,up) in zip(js,sides):
                cum=0.5*(1.0+lax.erf(ga*inv_root_two))
                gel=ga*cum
                fb[j]=gel
                fa[j]=up*(cum+ga*(jnp.exp(-0.5*ga*ga)*inv_root_tau))
                h=(gel*up).astype(bf16)
                hid[j,rows]=h
                part=dot(h,WD(j))
                total=part if total is None else total+part
            acc[...]+=total
        n2,r2=stats(acc[...])
        output[...]=(n2*gain2+shift2).astype(bf16)
        c=cot[...].astype(f32)
        ng[2:3]+=jnp.sum(c*n2,0,keepdims=True)
        ng[3:4]+=jnp.sum(c,0,keepdims=True)
        mid=back(c*gain2,n2,r2)
        gffn[rows]=mid.astype(bf16)
        acc[...]=mid
        @pl.loop(0,2)
        def _(n):
            js=(2*n,2*n+1)
            ghs=[dot_nt(gffn[rows],WD(j)) for j in js]
            total=None
            for j,gh in zip(js,ghs):
                a=(gh*fa[j]).astype(bf16); b=(gh*fb[j]).astype(bf16)
                wide[j,rows]=a; wide[4+j,rows]=b
                part=dot_nt(a,W(1,j))+dot_nt(b,W(2,j))
                total=part if total is None else total+part
            acc[...]+=total
        gl=acc[...]
        ng[0:1]+=jnp.sum(gl*n1,0,keepdims=True)
        ng[1:2]+=jnp.sum(gl,0,keepdims=True)
        gfirst=back(gl*gain1,n1,r1)
        first[...]=gfirst
        gb=gfirst.astype(bf16)
        gbranch[...]=gb
        dO[...]=dot_nt(WO(),gb).astype(bf16)
    def put(g,v):
        g[...]=v.astype(bf16).reshape(g.shape)
    base=LEN//TB
    @pl.when(jnp.logical_and(step>=base,step<base+4))
    def _(): put(gdown,dot_tn(hid[step-base],gffn[...]))
    @pl.when(jnp.logical_and(step>=base+4,step<base+12))
    def _(): put(gwide,dot_tn(inner[...],wide[step-base-4]))

def feed(tokens,cot,mixb,w,norms):
    n=LEN//TB
    last=n-1
    row=lambda i:(jnp.minimum(i,last),0)
    col=lambda i:(0,jnp.minimum(i,last))
    S=jax.ShapeDtypeStruct
    V=lambda s,d=bf16: pltpu.VMEM(s,d)
    clip=lambda v,a,b: jnp.minimum(jnp.maximum(v,a),b)
    return pl.pallas_call(feed_kernel,grid=(n+12,),
        in_specs=[pl.BlockSpec((TB,D),row),pl.BlockSpec((TB,D),row),pl.BlockSpec((D,TB),col),
            pl.BlockSpec(memory_space=pl.ANY),pl.BlockSpec((4,D),lambda i:(0,0))],
        out_specs=[pl.BlockSpec((TB,D),row),pl.BlockSpec((TB,D),row),pl.BlockSpec((D,TB),col),pl.BlockSpec((TB,D),row),
            pl.BlockSpec((4,D),lambda i:(0,0)),
            pl.BlockSpec((1,D,D),lambda i:(clip(i-n,0,3),0,0)),
            pl.BlockSpec((1,4,1,D//4,D),lambda i:(clip((i-n-4)//4,0,1),0,clip(i-n-4,0,7)%4,0,0))],
        out_shape=[S((LEN,D),bf16),S((LEN,D),f32),S((D,LEN),bf16),S((LEN,D),bf16),S((4,D),f32),S((4,D,D),bf16),S((2,4,4,D//4,D),bf16)],
        scratch_shapes=[V((LEN,D)),V((8,LEN,D)),V((LEN,D)),V((4,TB,D),f32),V((4,TB,D),f32),V((TB,D),f32),V((4,LEN,D)),V((4,D//4,D)),*[V((4,4,D//4,D))]*3,pltpu.SemaphoreType.DMA((3,4)),pltpu.SemaphoreType.DMA],
        compiler_params=pltpu.CompilerParams(vmem_limit_bytes=62<<20),name="feed")(tokens,cot,mixb,w.reshape(4,4,4,D//4,D),norms)

MESH = pl.DeviceIdType.MESH
ALL = slice(None)
HALF = D // 2
B_PART, C_PART = 48, 80
P_PART = 48


def place():
    i = lax.axis_index("zero")
    c = lax.axis_index("dp")
    return i, c, i // 4, (i // 2) % 2, i % 2


def partners(i, c, z, y, x):
    return (c, i + 1 - 2 * x), (c, i + 2 - 4 * y), (1 - c, i), (c, i + 4), (c, i - 4)


def when(cond, fn):
    @pl.when(cond)
    def _():
        fn()


def enter(i, c, z, y, x):
    barrier = pltpu.get_barrier_semaphore()
    xp, yp, sib, up, down = partners(i, c, z, y, x)

    def signal(peer):
        pl.semaphore_signal(barrier, inc=1, device_id=peer, device_id_type=MESH)

    for peer in (xp, yp, sib):
        signal(peer)
    when(z > 0, lambda: signal(down))
    when(z < 3, lambda: signal(up))
    pl.semaphore_wait(barrier, 3 + jnp.minimum(z, 1) + jnp.minimum(3 - z, 1))


def pick(z, values):
    out = jnp.int32(values[3])
    for k in (2, 1, 0):
        out = jnp.where(z == k, jnp.int32(values[k]), out)
    return out


def run_plan(z, words, ops):
    count = len(words[0])
    held = [pick(z, [words[k][n] for k in range(4)]) for n in range(count)]

    @pl.loop(0, count)
    def _(n):
        word = held[0]
        for k in range(1, count):
            word = jnp.where(n == k, held[k], word)

        @pl.loop(0, 3)
        def _(m):
            code = jnp.where(m == 0, word, jnp.where(m == 1, word // 256, word // 65536)) % 256
            kind, e = code // 16, code % 16
            branch(kind, e, 0, ops)


def branch(kind, e, low, ops):
    if len(ops) == 1:
        ops[0](e)
        return
    half = len(ops) // 2

    def lower():
        branch(kind, e, low, ops[:half])

    def upper():
        branch(kind, e, low + half, ops[half:])

    lax.cond(kind < low + half, lower, upper)


def gather_attend_kernel(blk, before, last, tokens_in, seg_row, result, norms, tokT_out, qkv_out, mixb, probs_out,
                         held, dist, column, tokens, tail, tokT, qkv, probs, tok_sem, out_sem, t_sem, q_sem, p_sem, pzs, pzr, pfs, pfr, pgs, pgr, p_s, p_r,
                         b1s, b1r, c1u, c1d, c1r, b2u, b2d, b2r, c2s, c2r, b3s, b3r, c3s, c3r, ss, sr, ts, tr):
    i, c, z, y, x = place()
    xp, yp, sib, up, down = partners(i, c, z, y, x)
    half = c * HALF
    other = (1 - c) * HALF
    tokens_come = pltpu.make_async_copy(tokens_in, tokens, tok_sem)
    tokens_come.start()
    spread = jnp.logical_or(z == 1, z == 2)

    def plain():
        for n in range(6):
            cols = pl.ds(n * 128, 128)
            held[z, y, x, :, cols] = blk[pl.ds(n, D, stride=6)].astype(bf16)
            held[z, y, x, pl.ds(0, 16), cols] = (
                blk[pl.ds(n, 16, stride=6)] + before[pl.ds(n, 16, stride=6)]
            ).astype(bf16)

    def swapped():
        top = lax.broadcasted_iota(jnp.int32, (16, 128), 0) == 0
        for n in range(6):
            cols = pl.ds(n * 128, 128)
            for j in range(4):
                value = blk[pl.ds(j * 6 + n, D // 4, stride=24)].astype(bf16)
                held[z, y, x, pl.ds(j * (D // 4), D // 4), cols] = value
                held[z, y, x, pl.ds(j * (D // 4), 16), cols] = (
                    blk[pl.ds(j * 6 + n, 16, stride=24)] + jnp.where(top, before[pl.ds(j * 6 + n, 1)], 0.0)
                ).astype(bf16)

    when(jnp.logical_not(spread), plain)
    when(spread, swapped)
    enter(i, c, z, y, x)

    def remote(ref, peer, s, r):
        return pltpu.make_async_remote_copy(
            src_ref=ref, dst_ref=ref, send_sem=s, recv_sem=r, device_id=peer, device_id_type=MESH
        )

    def by_parity(k, fn):
        when(k % 2 == 0, lambda: fn(False))
        when(k % 2 == 1, lambda: fn(True))

    def rp(k, base):
        return pl.ds(pl.multiple_of(base + k * P_PART, 16), P_PART)

    def z_ref(k, base=half):
        return held.at[0, y, x, rp(k, base)]

    def f_ref(k, odd, base=half):
        if odd:
            return held.at[0, 1 - y, x, rp(k, base)]
        return held.at[0, y, 1 - x, rp(k, base)]

    def g_ref(k, odd, mine, base=half):
        if odd:
            return held.at[0, ALL, x if mine else 1 - x, rp(k, base)]
        return held.at[0, y if mine else 1 - y, ALL, rp(k, base)]

    def PZ(k):
        return remote(z_ref(k), up, pzs.at[k], pzr.at[k])

    def PF(k, odd):
        return remote(z_ref(k), yp if odd else xp, pfs.at[k], pfr.at[k])

    def PG(k, odd):
        return remote(g_ref(k, odd, True), xp if odd else yp, pgs.at[k], pgr.at[k])

    def PS(ref, n):
        return remote(ref, sib, p_s.at[n], p_r.at[n])

    def op_p0z(k):
        def arrive():
            PZ(k).wait_recv()
            PS(z_ref(k), k).start()

        when(z > 0, arrive)
        when(z < 3, lambda: PZ(k).start())
        by_parity(k, lambda odd: PF(k, odd).start())

    def op_p0f(k):
        def turn(odd):
            PF(k, odd).wait_recv()
            PG(k, odd).start()
            PS(f_ref(k, odd), 8 + k).start()

        by_parity(k, turn)

    def op_p0g(k):
        def turn(odd):
            PG(k, odd).wait_recv()
            PS(g_ref(k, odd, False), 16 + k).start()

        by_parity(k, turn)

    split = lambda e: (e // 3 + 1, e % 3)

    def rb(s, base):
        return pl.ds(pl.multiple_of(base + s * B_PART, 16), B_PART)

    def rc(s, base):
        return pl.ds(pl.multiple_of(base + 3 * B_PART + s * C_PART, 16), C_PART)

    def b1_ref(s, yy, base=half):
        return held.at[z, yy, x, rb(s, base)]

    def b2_ref(t, s, xx, base=half):
        return held.at[t, ALL, xx, rb(s, base)]

    def c1_ref(t, s, base=half):
        return held.at[t, y, x, rc(s, base)]

    def c2_ref(t, s, xx, base=half):
        return held.at[t, y, xx, rc(s, base)]

    def c3_ref(t, s, yy, base=half):
        return held.at[t, yy, ALL, rc(s, base)]

    B1 = lambda s: remote(b1_ref(s, y), yp, b1s.at[s], b1r.at[s])
    C1U = lambda t, s, e: remote(c1_ref(t, s), up, c1u.at[e], c1r.at[e])
    C1D = lambda t, s, e: remote(c1_ref(t, s), down, c1d.at[e], c1r.at[e])
    B2U = lambda t, s, e: remote(b2_ref(t, s, x), up, b2u.at[e], b2r.at[e])
    B2D = lambda t, s, e: remote(b2_ref(t, s, x), down, b2d.at[e], b2r.at[e])
    C2 = lambda t, s, e: remote(c2_ref(t, s, x), xp, c2s.at[e], c2r.at[e])
    B3 = lambda t, s, e: remote(b2_ref(t, s, x), xp, b3s.at[e], b3r.at[e])
    C3 = lambda t, s, e: remote(c3_ref(t, s, y), yp, c3s.at[e], c3r.at[e])
    S = lambda ref, n: remote(ref, sib, ss.at[n], sr.at[n])

    def op_own(e):
        t, s = split(e)
        B1(s).start()
        C1D(t, s, e).start()

    def op_ownup(e):
        t, s = split(e)

        def go():
            C1U(t, s, e).start()
            B2U(t, s, e).start()

        when(z < 3, go)

    def op_b1(e):
        t, s = split(e)
        B1(s).wait_recv()
        B2D(t, s, e).start()
        S(b1_ref(s, 1 - y), 45 + s).start()

    def op_cx(e):
        t, s = split(e)
        C2(t, s, e).start()

    def op_bx(e):
        t, s = split(e)
        B3(t, s, e).start()

    def op_c1(e):
        t, s = split(e)
        C1U(t, s, e).wait_recv()
        when(jnp.logical_and(t < z, z < 3), lambda: C1U(t, s, e).start())
        when(jnp.logical_and(t > z, z > 0), lambda: C1D(t, s, e).start())
        S(c1_ref(t, s), e).start()

    def op_b2(e):
        t, s = split(e)
        B2U(t, s, e).wait_recv()
        when(jnp.logical_and(t < z, z < 3), lambda: B2U(t, s, e).start())
        when(jnp.logical_and(t > z, z > 0), lambda: B2D(t, s, e).start())
        S(b2_ref(t, s, x), 9 + e).start()

    def op_c2(e):
        t, s = split(e)
        C2(t, s, e).wait_recv()
        C3(t, s, e).start()
        S(c2_ref(t, s, 1 - x), 18 + e).start()

    def op_b3(e):
        t, s = split(e)
        B3(t, s, e).wait_recv()
        S(b2_ref(t, s, 1 - x), 27 + e).start()

    def op_c3(e):
        t, s = split(e)
        C3(t, s, e).wait_recv()
        S(c3_ref(t, s, 1 - y), 36 + e).start()

    def qkv_leaves(n):
        return pltpu.make_async_copy(qkv.at[n], qkv_out.at[n], q_sem.at[n])

    tokT_leaves = pltpu.make_async_copy(tokT, tokT_out, t_sem)

    def probs_leave(h):
        return pltpu.make_async_copy(probs.at[h % 2], probs_out.at[h], p_sem.at[h % 2])

    def op_proj(n):
        def arrive():
            @pl.loop(0, 8)
            def _(k):
                def got(odd):
                    PS(f_ref(k, odd, other), 8 + k).wait_recv()
                    PS(g_ref(k, odd, False, other), 16 + k).wait_recv()

                by_parity(k, got)
                when(z > 0, lambda: PS(z_ref(k, other), k).wait_recv())

        when(n == 0, arrive)

        @pl.loop(0, 3)
        def _(t):
            cols = pl.ds(pl.multiple_of(t * 256, 256), 256)
            qkv[n, cols] = dot_tn(held[0, n // 2, n % 2, :, cols], tokT[...]).astype(bf16)

        qkv_leaves(n).start()

    def op_head(h):
        when(h >= 2, lambda: probs_leave(h - 2).wait())
        attend_head(h, dist, qkv, mixb, probs.at[h % 2])
        probs_leave(h).start()

    line = jnp.logical_and(y == 1, x == 1)
    source = jnp.logical_and(line, z == 3)

    def T(peer, n):
        return remote(tail, peer, ts.at[n], tr.at[0])

    def leave(t):
        return pltpu.make_async_copy(held.at[t], result.at[t], out_sem.at[t])

    def op_other(e):
        def tail_z():
            def go():
                when(z < 3, lambda: T(down, 0).wait_recv())
                when(z > 0, lambda: T(down, 0).start())
                T(yp, 1).start()

            when(line, go)

        def tail_x():
            def go():
                when(y == 0, lambda: T(yp, 1).wait_recv())
                T(xp, 2).start()

            when(x == 1, go)

        def out():
            t = e - 2

            def others():
                @pl.loop(0, 3)
                def _(s):
                    n = (t - 1) * 3 + s

                    def theirs():
                        S(c1_ref(t, s, other), n).wait_recv()
                        S(b2_ref(t, s, x, other), 9 + n).wait_recv()

                    when(t != z, theirs)
                    when(t == z, lambda: S(b1_ref(s, 1 - y, other), 45 + s).wait_recv())
                    S(c2_ref(t, s, 1 - x, other), 18 + n).wait_recv()
                    S(b2_ref(t, s, 1 - x, other), 27 + n).wait_recv()
                    S(c3_ref(t, s, 1 - y, other), 36 + n).wait_recv()

            when(t > 0, others)
            leave(t).start()

        def prepare():
            tokens_come.wait()
            tokT[...] = tokens[...].astype(f32).T.astype(bf16)
            tokT_leaves.start()
            fill_distance(dist, seg_row, column)

        when(e == 0, tail_z)
        when(e == 1, tail_x)
        when(jnp.logical_and(e >= 2, e < 6), out)
        when(e == 6, prepare)

    def norms_here():
        for n in range(6):
            tail[pl.ds(0, 4), pl.ds(n * 128, 128)] = last[pl.ds(n, 4, stride=6)].astype(bf16)

    tail[...] = jnp.zeros_like(tail)
    when(source, norms_here)
    run_plan(z, GATHER_PLAN, [op_p0z, op_p0f, op_p0g, op_own, op_ownup, op_b1, op_bx, op_c1, op_b2, op_c2, op_b3,
                              op_c3, op_proj, op_head, op_other, op_cx])

    when(x == 0, lambda: T(xp, 2).wait_recv())
    when(x == 1, lambda: T(xp, 2).wait_send())

    def tail_sent():
        T(yp, 1).wait_send()
        when(z > 0, lambda: T(down, 0).wait_send())

    when(line, tail_sent)

    @pl.loop(0, 8)
    def _(k):
        def gone(odd):
            PF(k, odd).wait_send()
            PG(k, odd).wait_send()
            PS(f_ref(k, odd), 8 + k).wait_send()
            PS(g_ref(k, odd, False), 16 + k).wait_send()

        by_parity(k, gone)
        when(z < 3, lambda: PZ(k).wait_send())
        when(z > 0, lambda: PS(z_ref(k), k).wait_send())

    @pl.loop(0, 9)
    def _(e):
        t, s = split(e)
        C2(t, s, e).wait_send()
        B3(t, s, e).wait_send()
        C3(t, s, e).wait_send()

        def ups():
            C1U(t, s, e).wait_send()
            B2U(t, s, e).wait_send()

        def downs():
            C1D(t, s, e).wait_send()
            B2D(t, s, e).wait_send()

        when(jnp.logical_and(t <= z, z < 3), ups)
        when(jnp.logical_and(t >= z, z > 0), downs)

        def mine():
            B1(s).wait_send()
            S(b1_ref(s, 1 - y), 45 + s).wait_send()

        def theirs():
            S(c1_ref(t, s), e).wait_send()
            S(b2_ref(t, s, x), 9 + e).wait_send()

        when(t == z, mine)
        when(t != z, theirs)
        S(c2_ref(t, s, 1 - x), 18 + e).wait_send()
        S(b2_ref(t, s, 1 - x), 27 + e).wait_send()
        S(c3_ref(t, s, 1 - y), 36 + e).wait_send()

    norms[...] = tail[pl.ds(0, 4)].astype(f32)
    tokT_leaves.wait()
    for n in range(3):
        qkv_leaves(n).wait()
    for h in (HEADS - 2, HEADS - 1):
        probs_leave(h).wait()
    for t in range(4):
        leave(t).wait()


def gather_attend(blk, before, last, tokens, seg):
    Q = pltpu.SemaphoreType.DMA
    any_space = pl.BlockSpec(memory_space=pl.ANY)
    counts = [8] * 6 + [24, 24, 3, 3] + [9] * 12 + [48, 48, 3, 1]
    return pl.pallas_call(
        gather_attend_kernel,
        in_specs=[VM, VM, VM, any_space, VM],
        out_specs=[any_space, VM, any_space, any_space, VM, any_space],
        out_shape=[
            jax.ShapeDtypeStruct((4, 2, 2, D, D), bf16), jax.ShapeDtypeStruct((4, D), f32),
            *attend_shapes(),
        ],
        scratch_shapes=[
            pltpu.VMEM((4, 2, 2, D, D), bf16), pltpu.VMEM((LEN, LEN), f32), pltpu.VMEM((LEN, 8), f32),
            pltpu.VMEM((LEN, D), bf16), pltpu.VMEM((16, D), bf16),
            pltpu.VMEM((D, LEN), bf16), pltpu.VMEM((3, D, LEN), bf16), pltpu.VMEM((2, LEN, LEN), bf16),
            Q, Q((4,)), Q, Q((3,)), Q((2,)), *[Q((n,)) for n in counts],
        ],
        compiler_params=pltpu.CompilerParams(
            collective_id=1, has_side_effects=True, vmem_limit_bytes=58 << 20
        ),
        name="gather_attend",
    )(blk, before, last, tokens, seg.reshape(1, LEN))


PLANE_ORDER = (1, 2, 3)
BACK_PLAN = (
    (
        7405680, 7471873, 7570180, 488454, 2295925, 2573089, 8393537, 2364545, 345894, 8525430,
        4728834, 7807120, 1523782, 4487222, 2237712, 9574545, 7943987, 8860689, 5667415, 4579349,
        3167099, 3252242, 8665314, 8804485, 9655458, 10589234, 9818165, 9852385, 10699442, 11554980,
        13816215, 5354322, 11642306, 11839398, 11981761, 12892096, 11912135, 15713989, 15724527,
    ),
    (
        7405680, 7471873, 422660, 7671924, 526198, 8422163, 8880769, 364579, 3182967, 7874194,
        2376465, 1447731, 2430073, 2587514, 3642338, 4671016, 165025, 8773684, 8794440, 13645336,
        9802784, 4478870, 5644962, 1417379, 13711511, 10821952, 11707602, 11617624, 14790849, 10900672,
        12727635, 10990421, 12891331, 11878977, 6296261, 11978679, 13878864, 6435425, 15684177,
    ),
    (
        65648, 7565937, 7603728, 8585991, 554464, 8851840, 2502785, 1472130, 161680, 7870353,
        3219833, 2627706, 10588737, 9634976, 14819963, 8750112, 13665872, 4232210, 2376354, 13735207,
        9934407, 10703281, 3658310, 10855617, 12628146, 12727828, 10987095, 377779, 1291336, 3720260,
        12957111, 3298851, 11941063, 2475587, 1399009, 13845842, 5452644, 3499363, 15684948,
    ),
    (
        65648, 7471985, 7602803, 328739, 8397173, 4395393, 8615456, 1278480, 409892, 9539652,
        7807525, 4231698, 7947640, 3380017, 1331248, 8102266, 4383392, 8750087, 10637702, 9744775,
        10692245, 9879728, 2594753, 12759602, 10866771, 11736484, 11839427, 14722756, 12956951, 12006664,
        4601031, 13022742, 13718087, 1626708, 5589032, 6698963, 5715681, 3692135, 15689816,
    ),
)

GATHER_PLAN = (
    (
        196870, 1026, 7406867, 7401746, 1050388, 15787542, 9443093, 2494834, 2303104, 9565557,
        7631858, 2261281, 2127457, 9827248, 8529701, 9630912, 12748737, 16147091, 6788304, 8835793,
        6330034, 16233847, 13924563, 16287189, 6674082, 14129073, 14182019, 6534048, 14247044, 8955874,
        10007656, 14345121, 14399159, 14722211, 12101030, 15050980, 15724513, 15724527,
    ),
    (
        3273200, 3289330, 5243142, 152067, 7704947, 327684, 1050387, 15941969, 4200210, 1143843,
        1318933, 7770134, 8910310, 2565186, 7807525, 2225286, 6694646, 9658773, 16236992, 8616069,
        8966338, 8675986, 14874833, 10596708, 13788564, 6526870, 14013651, 10934230, 14202008, 11755623,
        10855528, 10729184, 14332633, 14987445, 11000759, 14917794, 15055016, 15724513,
    ),
    (
        3535667, 9647348, 7800565, 7733589, 1442806, 1026, 460049, 4556582, 1184646, 16281976,
        5444887, 1110408, 1369703, 9782128, 4478104, 8396839, 6694391, 9859732, 2355748, 2171522,
        15753314, 8503744, 13681249, 14706897, 9556946, 11777426, 13919412, 14002021, 14063459, 14137521,
        14276790, 10936976, 12049370, 10789544, 15048865, 11576739, 14935218, 15724513,
    ),
    (
        16266807, 9976055, 9958998, 419415, 66151, 12059670, 239192, 458769, 1226501, 8721427,
        2166807, 4617510, 1405255, 2418343, 15738736, 2302705, 16085832, 2487141, 2135656, 12697824,
        9552528, 7655888, 13820291, 13890709, 13926514, 6521986, 8508914, 11625620, 14049939, 11917219,
        11821528, 11970656, 9613529, 14867109, 10673060, 11772389, 11706596, 15724515,
    ),
)


Q_PART = 96
COLS = D // 2


def reduce_back_kernel(wide, down, w, qkv_in, dO_in, mixb_in, probs_in, tokT_in, gbranch_in, first, norm_in,
                       grad_in, flat_out, own, sl, lc3, lc2, lcz, lczx, lb3, lbz, lbzx, lb1, lf, lg, lz, stage,
                       dO, mixb, tokT, gbranch, theirs, probs, ds_all, wv, qkv, fchunk, flat, nacc, nx, ny, nz, nc,
                       own_sem, in_sem, p_sem, w_sem, f_sem, g_sem, o_sem, sib_s, sib_r, st_s, st_r,
                       c3s, c3r, b3s, b3r, c2s, c2r, bus, bur, bds, bdr, cus, cur, cds, cdr, b1s, b1r,
                       fs, fr, gs, gr, zs_, zr_, ns, nr, share_s, share_r, aft_s, aft_r):
    i, c, z, y, x = place()
    xp, yp, sib, up, down_peer = partners(i, c, z, y, x)
    base = c * HALF
    mine = pl.ds(pl.multiple_of(base, 16), HALF)
    other = pl.ds(pl.multiple_of((1 - c) * HALF, 16), HALF)
    planes = [wide.at[0], wide.at[1], down]

    def remote(src, dst, peer, s, r):
        return pltpu.make_async_remote_copy(
            src_ref=src, dst_ref=dst, send_sem=s, recv_sem=r, device_id=peer, device_id_type=MESH
        )

    def local_in(t):
        return pltpu.make_async_copy(planes[t - 1].at[:, :, mine], own.at[t], own_sem.at[t])

    def sib_in(t, s, n):
        k = 2 * ((t - 1) * 3 + s) + n
        start, size = (s * B_PART, B_PART) if n == 0 else (3 * B_PART + s * C_PART, C_PART)
        there = pl.ds(pl.multiple_of((1 - c) * HALF + start, 16), size)
        return remote(planes[t - 1].at[:, :, there], sl.at[t, :, :, pl.ds(start, size)], sib, sib_s.at[k], sib_r.at[k])

    for t in PLANE_ORDER:
        local_in(t).start()
    take = [
        pltpu.make_async_copy(a, b, in_sem.at[n])
        for n, (a, b) in enumerate(
            ((qkv_in, qkv), (dO_in, dO), (mixb_in, mixb), (gbranch_in, gbranch), (tokT_in, tokT))
        )
    ]
    for n in range(3):
        take[n].start()

    def probs_come(h):
        return pltpu.make_async_copy(probs_in.at[h], probs.at[h % 2], p_sem.at[h % 2])

    probs_come(0).start()
    enter_more(i, c, z, y, x)
    for t in PLANE_ORDER:
        for s in range(3):
            for n in range(2):
                sib_in(t, s, n).start()
    nacc[...] = norm_in[...]
    NX = remote(nacc, nx, xp, ns.at[0], nr.at[0])
    NY = remote(nacc, ny, yp, ns.at[1], nr.at[1])
    NZ = remote(nacc, nz, up, ns.at[2], nr.at[2])
    NC = remote(nacc, nc, sib, ns.at[3], nr.at[3])
    line = jnp.logical_and(x == 1, y == 1)
    last_line = jnp.logical_and(line, z == 3)
    when(x == 0, lambda: NX.start())

    def rb(s, k=0, size=B_PART):
        return pl.ds(pl.multiple_of(s * B_PART + k, 16), size)

    def rc(s, k=0, size=C_PART):
        return pl.ds(pl.multiple_of(3 * B_PART + s * C_PART + k, 16), size)

    def add_rows(dst, src, rows):
        @pl.loop(0, rows // 16)
        def _(n):
            k = pl.multiple_of(n * 16, 16)
            a = dst(k)
            a[...] = a[...] + src(k)[...]

    r16 = lambda k: pl.ds(k, 16)
    split = lambda e: (e // 3 + 1, e % 3)

    def C3(t, s, e):
        return remote(own.at[t, 1 - y, :, rc(s)], lc3.at[e], yp, c3s.at[e], c3r.at[e])

    def B3(t, s, e):
        return remote(own.at[t, :, 1 - x, rb(s)], lb3.at[e], xp, b3s.at[e], b3r.at[e])

    def C2(t, s, e):
        return remote(own.at[t, y, 1 - x, rc(s)], lc2.at[e], xp, c2s.at[e], c2r.at[e])

    def BU(t, s, e):
        return remote(own.at[t, :, x, rb(s)], lbz.at[e], up, bus.at[e], bur.at[e])

    def BD(t, s, e, extra=False):
        return remote(own.at[t, :, x, rb(s)], lbzx.at[s] if extra else lbz.at[e], down_peer, bds.at[e], bdr.at[e])

    def CU(t, s, e):
        return remote(own.at[t, y, x, rc(s)], lcz.at[e], up, cus.at[e], cur.at[e])

    def CD(t, s, e, extra=False):
        return remote(own.at[t, y, x, rc(s)], lczx.at[s] if extra else lcz.at[e], down_peer, cds.at[e], cdr.at[e])

    def B1(s):
        return remote(own.at[z, 1 - y, x, rb(s)], lb1.at[s], yp, b1s.at[s], b1r.at[s])

    def op_sum(e):
        t, s = split(e)

        for k in (1, 2, 3):
            when(jnp.logical_and(t == k, s == 0), lambda k=k: local_in(k).wait())
            for m in range(3):
                def arrive(k=k, m=m):
                    for n in range(2):
                        sib_in(k, m, n).wait_recv()

                when(e == (k - 1) * 3 + m, arrive)
        add_rows(lambda k: own.at[t, :, :, rb(s, k, 16)], lambda k: sl.at[t, :, :, rb(s, k, 16)], B_PART)
        add_rows(lambda k: own.at[t, :, :, rc(s, k, 16)], lambda k: sl.at[t, :, :, rc(s, k, 16)], C_PART)
        C3(t, s, e).start()
        B3(t, s, e).start()

    def op_c3(e):
        t, s = split(e)
        C3(t, s, e).wait_recv()
        add_rows(lambda k: own.at[t, y, :, rc(s, k, 16)], lambda k: lc3.at[e, :, r16(k)], C_PART)
        C2(t, s, e).start()

    def op_b3(e):
        t, s = split(e)
        B3(t, s, e).wait_recv()
        add_rows(lambda k: own.at[t, :, x, rb(s, k, 16)], lambda k: lb3.at[e, :, r16(k)], B_PART)

    def op_c2(e):
        t, s = split(e)
        C2(t, s, e).wait_recv()
        add_rows(lambda k: own.at[t, y, x, rc(s, k, 16)], lambda k: lc2.at[e, r16(k)], C_PART)

    def op_bz(e):
        t, s = split(e)
        dst = lambda k: own.at[t, :, x, rb(s, k, 16)]

        def from_below():
            BU(t, s, e).wait_recv()
            add_rows(dst, lambda k: lbz.at[e, :, r16(k)], B_PART)

        when(jnp.logical_and(t >= z, z > 0), from_below)

        def from_above():
            BD(t, s, e).wait_recv()
            add_rows(dst, lambda k: lbz.at[e, :, r16(k)], B_PART)

        when(t < z, lambda: when(z < 3, from_above))

        def from_above_last():
            BD(t, s, e).wait_recv()
            add_rows(dst, lambda k: lbzx.at[s, :, r16(k)], B_PART)

        when(jnp.logical_and(t == z, z < 3), from_above_last)
        when(t > z, lambda: BU(t, s, e).start())
        when(t == z - 1, lambda: BD(t, s, e, True).start())
        when(t < z - 1, lambda: BD(t, s, e).start())
        when(t == z, lambda: B1(s).start())

    def op_cz(e):
        t, s = split(e)
        dst = lambda k: own.at[t, y, x, rc(s, k, 16)]

        def from_below():
            CU(t, s, e).wait_recv()
            add_rows(dst, lambda k: lcz.at[e, r16(k)], C_PART)

        when(jnp.logical_and(t >= z, z > 0), from_below)

        def from_above():
            CD(t, s, e).wait_recv()
            add_rows(dst, lambda k: lcz.at[e, r16(k)], C_PART)

        when(t < z, lambda: when(z < 3, from_above))

        def from_above_last():
            CD(t, s, e).wait_recv()
            add_rows(dst, lambda k: lczx.at[s, r16(k)], C_PART)

        when(jnp.logical_and(t == z, z < 3), from_above_last)
        when(t > z, lambda: CU(t, s, e).start())
        when(t == z - 1, lambda: CD(t, s, e, True).start())
        when(t < z - 1, lambda: CD(t, s, e).start())

    def op_b1(e):
        t, s = split(e)
        B1(s).wait_recv()
        add_rows(lambda k: own.at[z, y, x, rb(s, k, 16)], lambda k: lb1.at[s, r16(k)], B_PART)

    def op_head(h):
        def operands():
            for n in range(3):
                take[n].wait()
            for n in (3, 4):
                take[n].start()

        def late_operands():
            for n in (3, 4):
                take[n].wait()

        when(h == 0, operands)
        when(h == 2, late_operands)
        probs_come(h).wait()
        when(h < HEADS - 1, lambda: probs_come(h + 1).start())
        attend_back_head(h, qkv, dO, mixb, probs.at[h % 2], ds_all)

    def columns(g):
        return pl.ds(pl.multiple_of(g * COLS, 128), COLS)

    def stage_copy(e):
        g, n = e // 4, e % 4
        return remote(
            stage.at[e], sl.at[0, n // 2, n % 2, :, columns(g)], sib, st_s.at[e], st_r.at[e]
        )

    def op_dw(e):
        g, n = e // 4, e % 4
        cols = columns(g)

        def put(half, value):
            if half == 0:
                own[0, n // 2, n % 2, :, cols] = value.astype(bf16)
            else:
                stage[e] = value.astype(bf16)

        def inputs():
            right = qkv[n, pl.ds(pl.multiple_of(g * COLS, 128), COLS)]
            for half, rows in ((0, mine), (1, other)):
                put(half, dot_nt(tokT[rows], right))

        def output():
            right = gbranch[:, cols]
            for half, rows in ((0, mine), (1, other)):
                put(half, dot(mixb[rows], right))

        when(n < 3, inputs)
        when(n == 3, output)
        stage_copy(e).start()

    def rq(k, n=0, size=Q_PART):
        return pl.ds(pl.multiple_of(k * Q_PART + n, 16), size)

    def F0(e, g, k, odd):
        src = own.at[0, :, 1 - x, rq(k), columns(g)] if odd else own.at[0, 1 - y, :, rq(k), columns(g)]
        return remote(src, lf.at[e], xp if odd else yp, fs.at[e], fr.at[e])

    def G0(e, g, k, odd):
        if odd:
            return remote(own.at[0, 1 - y, x, rq(k), columns(g)], lg.at[e], yp, gs.at[e], gr.at[e])
        return remote(own.at[0, y, 1 - x, rq(k), columns(g)], lg.at[e], xp, gs.at[e], gr.at[e])

    def Z0(e, g, k):
        return remote(own.at[0, y, x, rq(k), columns(g)], lz.at[e], down_peer, zs_.at[e], zr_.at[e])

    def by_parity(k, fn):
        when(k % 2 == 0, lambda: fn(False))
        when(k % 2 == 1, lambda: fn(True))

    def op_sum0(e):
        g, k = e // 4, e % 4

        def arrive():
            @pl.loop(0, 4)
            def _(n):
                stage_copy(g * 4 + n).wait_recv()

        when(k == 0, arrive)
        add_rows(
            lambda n: own.at[0, :, :, rq(k, n, 16), columns(g)],
            lambda n: sl.at[0, :, :, rq(k, n, 16), columns(g)], Q_PART,
        )
        by_parity(k, lambda odd: F0(e, g, k, odd).start())

    def op_f0(e):
        g, k = e // 4, e % 4

        def turn(odd):
            F0(e, g, k, odd).wait_recv()
            if odd:
                dst = lambda n: own.at[0, :, x, rq(k, n, 16), columns(g)]
            else:
                dst = lambda n: own.at[0, y, :, rq(k, n, 16), columns(g)]
            add_rows(dst, lambda n: lf.at[e, :, r16(n)], Q_PART)
            G0(e, g, k, odd).start()

        by_parity(k, turn)

    def op_g0(e):
        g, k = e // 4, e % 4
        by_parity(k, lambda odd: G0(e, g, k, odd).wait_recv())
        add_rows(lambda n: own.at[0, y, x, rq(k, n, 16), columns(g)], lambda n: lg.at[e, r16(n)], Q_PART)

    def op_z0(e):
        g, k = e // 4, e % 4

        def arrive():
            Z0(e, g, k).wait_recv()
            add_rows(lambda n: own.at[0, y, x, rq(k, n, 16), columns(g)], lambda n: lz.at[e, r16(n)], Q_PART)

        when(z < 3, arrive)
        when(z > 0, lambda: Z0(e, g, k).start())

    def first_in(q):
        return pltpu.make_async_copy(first.at[pl.ds(pl.multiple_of(q * 256, 256), 256)], fchunk, f_sem)

    def grad_out(q):
        return pltpu.make_async_copy(fchunk, grad_in.at[pl.ds(pl.multiple_of(q * 256, 256), 256)], g_sem)

    def weight_in(n):
        target = (probs.at[0, pl.ds(0, D), pl.ds(0, D)], ds_all.at[pl.ds(0, D), pl.ds(0, D)], wv)[n]
        return pltpu.make_async_copy(w.at[0, n // 2, n % 2], target, w_sem.at[n])

    def op_gin(q):
        def weights():
            for n in range(3):
                weight_in(n).wait()

        when(q == 0, weights)
        when(q > 0, lambda: grad_out(q - 1).wait())
        first_in(q).start()
        cols = pl.ds(pl.multiple_of(q * 256, 256), 256)
        d = pl.ds(0, D)
        acc = dot(probs[0, d, d], qkv[0, :, cols]) + dot(ds_all[d, d], qkv[1, :, cols])
        acc = (acc + dot(wv[...], qkv[2, :, cols])).T
        first_in(q).wait()
        fchunk[...] += acc
        grad_out(q).start()

    def op_other(e):
        def norm_y():
            def go():
                NX.wait_recv()
                nacc[...] += nx[...]
                when(y == 0, lambda: NY.start())

            when(x == 1, go)

        def norm_z():
            def go():
                NY.wait_recv()
                nacc[...] += ny[...]

                def more():
                    NZ.wait_recv()
                    nacc[...] += nz[...]

                when(z > 0, more)
                when(z < 3, lambda: NZ.start())
                when(z == 3, lambda: NC.start())

            when(line, go)

        def load():
            for n in range(3):
                weight_in(n).start()

        when(e == 0, norm_y)
        when(e == 1, norm_z)
        when(e == 2, load)

    run_plan(z, BACK_PLAN, [op_sum, op_c3, op_b3, op_c2, op_bz, op_cz, op_b1, op_head, op_dw, op_sum0, op_f0,
                            op_g0, op_z0, op_gin, op_other])

    spread = jnp.logical_or(z == 1, z == 2)

    def flatten(half, get):
        def plain():
            for n in range(6):
                flat[pl.ds(half * (6 * HALF) + n, HALF, stride=6)] = get(pl.ds(0, HALF), pl.ds(n * 128, 128)).astype(f32)

        def swapped():
            for n in range(6):
                for j in range(2):
                    value = get(pl.ds(j * (D // 4), D // 4), pl.ds(n * 128, 128)).astype(f32)
                    flat[pl.ds(half * 12 + j * 6 + n, D // 4, stride=24)] = value

        when(jnp.logical_not(spread), plain)
        when(spread, swapped)

    share = remote(own.at[z, y, x], theirs, sib, share_s, share_r)
    share.start()
    flatten(c, lambda rows, cols: own[z, y, x, rows, cols])

    @pl.loop(0, 9)
    def _(e):
        t, s = split(e)
        C3(t, s, e).wait_send()
        B3(t, s, e).wait_send()
        C2(t, s, e).wait_send()

        def went_up():
            BU(t, s, e).wait_send()
            CU(t, s, e).wait_send()

        def went_down():
            BD(t, s, e).wait_send()
            CD(t, s, e).wait_send()

        when(t > z, went_up)
        when(t < z, went_down)
        when(t == z, lambda: B1(s).wait_send())

    @pl.loop(0, 8)
    def _(e):
        g, k = e // 4, e % 4
        stage_copy(e).wait_send()

        def gone(odd):
            F0(e, g, k, odd).wait_send()
            G0(e, g, k, odd).wait_send()

        by_parity(k, gone)
        when(z > 0, lambda: Z0(e, g, k).wait_send())

    for t in (1, 2, 3):
        for s in range(3):
            for n in range(2):
                sib_in(t, s, n).wait_send()
    when(x == 0, lambda: NX.wait_send())
    when(jnp.logical_and(x == 1, y == 0), lambda: NY.wait_send())
    when(jnp.logical_and(line, z < 3), lambda: NZ.wait_send())

    def norm_last():
        NC.wait_recv()
        NC.wait_send()
        nacc[...] += nc[...]

    when(last_line, norm_last)
    grad_out(3).wait()
    share.wait_recv()
    flatten(1 - c, lambda rows, cols: theirs[rows, cols])
    share.wait_send()
    body, head_rows, after = pl.ds(0, 6 * D), pl.ds(0, 24), pl.ds(6 * D, 24)
    leave = pltpu.make_async_copy(flat.at[body], flat_out.at[body], o_sem.at[0])
    leave.start()

    def ending():
        for n in range(6):
            flat[pl.ds(6 * D + n, 4, stride=6)] = nacc[:, pl.ds(n * 128, 128)]

    when(i == 15, ending)
    give = remote(flat.at[head_rows], flat.at[after], (c, i - 1), aft_s, aft_r)
    when(i > 0, lambda: give.start())
    when(i < 15, lambda: give.wait_recv())
    leave_after = pltpu.make_async_copy(flat.at[after], flat_out.at[after], o_sem.at[1])
    leave_after.start()
    when(i > 0, lambda: give.wait_send())
    leave.wait()
    leave_after.wait()


def enter_more(i, c, z, y, x):
    barrier = pltpu.get_barrier_semaphore()
    xp, yp, sib, up, down = partners(i, c, z, y, x)

    def signal(peer):
        pl.semaphore_signal(barrier, inc=1, device_id=peer, device_id_type=MESH)

    for peer in (xp, yp, sib):
        signal(peer)
    when(z > 0, lambda: signal(down))
    when(z < 3, lambda: signal(up))
    when(jnp.logical_and(x == 0, i > 0), lambda: signal((c, i - 1)))
    when(jnp.logical_and(x == 1, i < 15), lambda: signal((c, i + 1)))
    more = 1 - jnp.where(i == 0, 1, 0) - jnp.where(i == 15, 1, 0)
    pl.semaphore_wait(barrier, 3 + jnp.minimum(z, 1) + jnp.minimum(3 - z, 1) + more)


def reduce_back(wide, down, w, qkv, dO, mixb, probs, tokT, gbranch, first, norms):
    Q = pltpu.SemaphoreType.DMA
    V = lambda *s: pltpu.VMEM(s, bf16)
    F = lambda *s: pltpu.VMEM(s, f32)
    A = pl.BlockSpec(memory_space=pl.ANY)
    return pl.pallas_call(
        reduce_back_kernel,
        in_specs=[A] * 10 + [VM],
        out_specs=[A, A],
        out_shape=[jax.ShapeDtypeStruct((LEN, D), f32), jax.ShapeDtypeStruct((6 * D + 24, 128), f32)],
        scratch_shapes=[
            V(4, 2, 2, HALF, D), V(4, 2, 2, HALF, D), V(9, 2, C_PART, D), V(9, C_PART, D), V(9, C_PART, D),
            V(3, C_PART, D), V(9, 2, B_PART, D), V(9, 2, B_PART, D), V(3, 2, B_PART, D), V(3, B_PART, D),
            V(8, 2, Q_PART, COLS), V(8, Q_PART, COLS), V(8, Q_PART, COLS), V(8, HALF, COLS),
            V(D, LEN), V(D, LEN), V(D, LEN), V(LEN, D), V(HALF, D), V(2, LEN, LEN), V(LEN, LEN), V(D, D), V(3, D, LEN),
            F(256, D), F(6 * D + 24, 128), F(4, D), F(4, D), F(4, D), F(4, D), F(4, D),
            Q((4,)), Q((5,)), Q((2,)), Q((3,)), Q, Q, Q((2,)), Q((18,)), Q((18,)), Q((8,)), Q((8,)),
            *[Q((9,))] * 14, Q((3,)), Q((3,)), *[Q((8,))] * 6, Q((4,)), Q((4,)), Q, Q, Q, Q,
        ],
        compiler_params=pltpu.CompilerParams(
            collective_id=2, has_side_effects=True, vmem_limit_bytes=55 << 20
        ),
        name="reduce_back",
    )(wide, down, w, qkv, dO, mixb, probs, tokT, gbranch, first, norms)

SQUARE = D * D
TAIL = 4 * D


def from_wide(blocks):
    return blocks.reshape(4, 4, D // 4, D).transpose(0, 2, 1, 3).reshape(D, FF)


def to_wide(value):
    return value.reshape(4, D // 4, 4, D).transpose(0, 2, 1, 3).reshape(2, 2, D, D)


def gather_and_attend(master, tokens, segments):
    count = lax.axis_size("zero")
    index = lax.axis_index("zero")
    size = 16 * SQUARE // count
    last = master[-TAIL:]
    step = TAIL // count
    zeros = jnp.zeros((TAIL,), f32)
    ending = lax.dynamic_slice(jnp.concatenate([last, zeros]), (TAIL - step * (index + 1),), (TAIL,))
    before = lax.ppermute(ending, "zero", [(k, k + 1) for k in range(count - 1)])
    block = lax.dynamic_slice(jnp.concatenate([zeros, master]), (TAIL - step * index,), (size,))
    if count == 16:
        before = jnp.pad(before.reshape(24, 128), ((0, 72), (0, 0)))
        block, last = block.reshape(6 * D, 128), last.reshape(24, 128)
        blocks, norms, *attended = gather_attend(block, before, last, tokens, segments)
    else:
        block = jnp.concatenate([block[:TAIL] + before, block[TAIL:]])
        natural = lax.all_gather(block.astype(bf16).reshape(-1, D), "zero", axis=0, tiled=True)
        parts = natural.reshape(4, 4 * D, D)
        wide = [to_wide(parts[k].reshape(D, FF)) for k in (1, 2)]
        blocks = jnp.stack([parts[0].reshape(2, 2, D, D), *wide, parts[3].reshape(2, 2, D, D)])
        last = last.astype(bf16).astype(f32)
        norms = lax.psum(jnp.where(index == count - 1, last, 0.0), "zero").reshape(4, D)
        attended = attend(tokens, blocks, segments)
    return blocks, norms, *attended


def back_and_scatter(blocks, tokT, qkv, mixed, probs, grad_mixed, first_grad, branch_grad, norm_grads,
                     down_grad, wide_grad):
    count = lax.axis_size("zero")
    index = lax.axis_index("zero")
    if count == 16:
        input_grad, joined = reduce_back(
            wide_grad, down_grad, blocks, qkv, grad_mixed, mixed, probs, tokT, branch_grad, first_grad,
            norm_grads,
        )
        joined = joined.reshape(-1)
    else:
        square, input_grad = attend_back(
            blocks, tokT, qkv, mixed, probs, grad_mixed, first_grad, branch_grad
        )
        natural = [from_wide(wide_grad[k]).reshape(4 * D, D) for k in (0, 1)]
        natural = jnp.concatenate([square.reshape(4 * D, D), *natural, down_grad.reshape(4 * D, D)])
        block = lax.psum_scatter(natural, "zero", scatter_dimension=0, tiled=True)
        block = lax.psum(block.astype(f32), "dp")
        tail = lax.psum(norm_grads, ("dp", "zero"))
        flat = block.reshape(-1)
        after = lax.ppermute(flat[:TAIL], "zero", [(k + 1, k) for k in range(count - 1)])
        joined = jnp.concatenate([flat, jnp.where(index == count - 1, tail.reshape(-1), after)])
    shard = 16 * SQUARE // count + TAIL // count
    return input_grad, lax.dynamic_slice(joined, (TAIL // count * index,), (shard,))


def local(tokens, segments, cotangent, master, moment_one, moment_two):
    blocks, norms, tokT, qkv, mixed, probs = gather_and_attend(master, tokens, segments)
    output, first_grad, grad_mixed, branch_grad, norm_grads, down_grad, wide_grad = feed(
        tokens, cotangent, mixed, blocks, norms
    )
    input_grad, grad_shard = back_and_scatter(
        blocks, tokT, qkv, mixed, probs, grad_mixed, first_grad, branch_grad, norm_grads,
        down_grad.reshape(2, 2, D, D), wide_grad.reshape(2, 2, 2, D, D),
    )
    grad_shard = grad_shard / (lax.axis_size("zero") * lax.axis_size("dp"))
    first = beta_one * moment_one + (1.0 - beta_one) * grad_shard
    second = beta_two * moment_two + (1.0 - beta_two) * grad_shard * grad_shard
    update = first / correct_one / (jnp.sqrt(second / correct_two) + adam_eps)
    master_new = master - learn_rate * (update + weight_decay * master)
    return (
        output,
        input_grad,
        grad_shard,
        first,
        second,
        master_new,
        master_new.astype(jnp.bfloat16),
    )


def solution(mesh):
    return jax.shard_map(
        local,
        mesh=mesh,
        in_specs=(
            P(("dp", "zero"), None),
            P(("dp", "zero")),
            P(("dp", "zero"), None),
            P("zero"),
            P("zero"),
            P("zero"),
        ),
        out_specs=(
            P(("dp", "zero"), None),
            P(("dp", "zero"), None),
            P("zero"),
            P("zero"),
            P("zero"),
            P("zero"),
            P("zero"),
        ),
        check_vma=False,
    )
```

```python
import functools

import jax
import jax.numpy as jnp
from jax import lax
from jax.sharding import PartitionSpec as P
import jax.experimental.pallas as pl
import jax.experimental.pallas.tpu as pltpu

D = 768
HEADS = 12
HEAD = 64
FF = 3072
LEN = 1024


learn_rate = 0.02
beta_one = 0.9
beta_two = 0.999
adam_eps = 1e-08
weight_decay = 0.01
correct_one = 1.0 - 0.9**10
correct_two = 1.0 - 0.999**10
norm_eps = 1e-06
inv_root_two = 0.7071067811865476
inv_root_tau = 0.3989422804014327


bf16=jnp.bfloat16; f32=jnp.float32
FAR=1e33
VM=pl.BlockSpec(memory_space=pltpu.VMEM)

def dot(a,b): return lax.dot_general(a,b,(((1,),(0,)),((),())),preferred_element_type=f32)
def dot_tn(a,b): return lax.dot_general(a,b,(((0,),(0,)),((),())),preferred_element_type=f32)
def dot_nt(a,b): return lax.dot_general(a,b,(((1,),(1,)),((),())),preferred_element_type=f32)

def slope(h):
    return jnp.exp2(-8.0/HEADS*(jnp.full((1,1),h,jnp.int32).astype(f32)+1.0))

def fill_distance(dist,seg_row,column):
    column[...]=jnp.broadcast_to(seg_row[...].astype(f32),(8,LEN)).T
    @pl.loop(0,LEN//128)
    def _(k):
        r=pl.ds(pl.multiple_of(k*128,128),128)
        kk=(lax.broadcasted_iota(jnp.int32,(128,LEN),0)+k*128)
        qq=lax.broadcasted_iota(jnp.int32,(128,LEN),1)
        d=jnp.abs(kk-qq).astype(f32)
        dist[r]=jnp.where(column[r,0:1]==seg_row[...].astype(f32),d,FAR)

QB=256
def project_all(w,tokT,qkv):
    @pl.loop(0,3)
    def _(n):
        @pl.loop(0,3)
        def _(t):
            c=pl.ds(pl.multiple_of(t*256,256),256)
            qkv[n,c]=dot_tn(w[0,n//2,n%2,:,c],tokT[...]).astype(bf16)

def attend_head(h,dist,qkv,mixb,probs):
    rows=pl.ds(pl.multiple_of(h*HEAD,HEAD),HEAD)
    keys=qkv[1,rows].astype(f32).T.astype(bf16)
    s=dot(keys,qkv[0,rows]*bf16(0.125))-slope(h)*dist[...]
    e=jnp.exp(s-jnp.max(s,0,keepdims=True))
    p=(e*(1.0/jnp.sum(e,0,keepdims=True))).astype(bf16)
    probs[...]=p
    mixb[rows]=dot(qkv[2,rows],p).astype(bf16)

def attend_back_head(h,qkv,dO,mixb,probs,ds_all):
    rows=pl.ds(pl.multiple_of(h*HEAD,HEAD),HEAD)
    values=qkv[2,rows].astype(f32).T.astype(bf16)
    grad_q=[]
    for b in range(LEN//QB):
        cols=pl.ds(b*QB,QB)
        do=dO[rows,cols]
        dp=dot(values,do)
        delta=jnp.sum(do.astype(f32)*mixb[rows,cols].astype(f32),0,keepdims=True)
        ds=(probs[:,cols].astype(f32)*(dp-delta)).astype(bf16)
        ds_all[:,cols]=ds
        grad_q.append((dot(qkv[1,rows],ds)*0.125).astype(bf16))
    grad_k=(dot_nt(qkv[0,rows],ds_all[...])*0.125).astype(bf16)
    grad_v=dot_nt(dO[rows],probs[...]).astype(bf16)
    for b in range(LEN//QB):
        qkv[0,rows,pl.ds(b*QB,QB)]=grad_q[b]
    qkv[1,rows]=grad_k
    qkv[2,rows]=grad_v

def attend_kernel(tokens,w,seg_row,tokT,qkv,mixb,probs_out,dist,column,probs,sem):
    tokT[...]=tokens[...].astype(f32).T.astype(bf16)
    fill_distance(dist,seg_row,column)
    project_all(w,tokT,qkv)
    @pl.loop(0,HEADS)
    def _(h):
        attend_head(h,dist,qkv,mixb,probs)
        move=pltpu.make_async_copy(probs,probs_out.at[h],sem)
        move.start()
        move.wait()

def attend_shapes():
    S=jax.ShapeDtypeStruct
    return [S((D,LEN),bf16),S((3,D,LEN),bf16),S((D,LEN),bf16),S((HEADS,LEN,LEN),bf16)]

ANY=pl.BlockSpec(memory_space=pl.ANY)

def attend(tokens,w,seg):
    return pl.pallas_call(attend_kernel,grid=(1,),
        in_specs=[VM,pl.BlockSpec((1,2,2,D,D),lambda i:(0,0,0,0,0)),VM],out_specs=[VM]*3+[ANY],
        out_shape=attend_shapes(),
        scratch_shapes=[pltpu.VMEM((LEN,LEN),f32),pltpu.VMEM((LEN,8),f32),pltpu.VMEM((LEN,LEN),bf16),pltpu.SemaphoreType.DMA],
        compiler_params=pltpu.CompilerParams(vmem_limit_bytes=58<<20),name="attend")(tokens,w,seg.reshape(1,LEN))

def attend_back_kernel(w,tokT,qkv_in,mixb,probs_in,dO,first,gbranch,g0,grad_in,qkv,probs,ds_all,sem,qkv_sem):
    take=pltpu.make_async_copy(qkv_in,qkv,qkv_sem)
    take.start()
    take.wait()
    @pl.loop(0,HEADS)
    def _(h):
        move=pltpu.make_async_copy(probs_in.at[h],probs,sem)
        move.start()
        move.wait()
        attend_back_head(h,qkv,dO,mixb,probs,ds_all)
    g0[1,1]=dot(mixb[...],gbranch[...]).astype(bf16)
    for n in range(3):
        g0[n//2,n%2]=dot_nt(tokT[...],qkv[n]).astype(bf16)
    @pl.loop(0,4)
    def _(t):
        c=pl.ds(pl.multiple_of(t*256,256),256)
        acc=dot(w[0,0,0],qkv[0,:,c])+dot(w[0,0,1],qkv[1,:,c])+dot(w[0,1,0],qkv[2,:,c])
        grad_in[c]=first[c]+acc.T

def attend_back(w,tokT,qkv,mixb,probs,dO,first,gbranch):
    return pl.pallas_call(attend_back_kernel,grid=(1,),
        in_specs=[pl.BlockSpec((1,2,2,D,D),lambda i:(0,0,0,0,0)),VM,ANY,VM,ANY,VM,VM,VM],out_specs=[VM]*2,
        out_shape=[jax.ShapeDtypeStruct((2,2,D,D),bf16),jax.ShapeDtypeStruct((LEN,D),f32)],
        scratch_shapes=[pltpu.VMEM((3,D,LEN),bf16),pltpu.VMEM((LEN,LEN),bf16),pltpu.VMEM((LEN,LEN),bf16),pltpu.SemaphoreType.DMA,pltpu.SemaphoreType.DMA],
        compiler_params=pltpu.CompilerParams(vmem_limit_bytes=60<<20),name="attend_back")(w,tokT,qkv,mixb,probs,dO,first,gbranch)

TB=256
def feed_kernel(tokens,cot,mixb,w,norms,output,first,dO,gbranch,ng,gdown,gwide,inner,wide,gffn,fa,fb,acc,hid,wo,w1,w2,w3,w_sem,wo_sem):
    step=pl.program_id(0)
    gain1=norms[0:1]; shift1=norms[1:2]; gain2=norms[2:3]; shift2=norms[3:4]
    def stats(v):
        c=v-jnp.mean(v,-1,keepdims=True)
        r=lax.rsqrt(jnp.mean(c*c,-1,keepdims=True)+norm_eps)
        return c*r,r
    def back(e,n,r):
        return r*(e-jnp.mean(e,-1,keepdims=True)-n*jnp.mean(e*n,-1,keepdims=True))
    W=lambda p,j: (w1,w2)[p-1][j].reshape(D,D)
    WD=lambda j: w3[j].reshape(D,D)
    WO=lambda: wo[...].reshape(D,D)
    def load(p,j):
        source=w.at[p,j] if p==3 else w.at[p,:,j]
        return pltpu.make_async_copy(source,(w1,w2,w3)[p-1].at[j],w_sem.at[p-1,j])
    load_out=pltpu.make_async_copy(w.at[0,3],wo,wo_sem)
    @pl.when(step==0)
    def _():
        load_out.start()
        for j in range(4):
            for p in (1,2,3): load(p,j).start()
        ng[...]=jnp.zeros_like(ng)
        load_out.wait()
    @pl.when(step<LEN//TB)
    def _():
        rows=pl.ds(pl.multiple_of(step*TB,TB),TB)
        branch=dot_tn(mixb[...],WO())
        n1,r1=stats(tokens[...].astype(f32)+branch)
        l1=n1*gain1+shift1
        inner[rows]=l1.astype(bf16)
        acc[...]=l1
        @pl.loop(0,2)
        def _(n):
            js=(2*n,2*n+1)
            @pl.when(step==0)
            def _():
                for j in js:
                    for p in (1,2,3): load(p,j).wait()
            inn=inner[rows]
            sides=[(dot(inn,W(1,j)),dot(inn,W(2,j))) for j in js]
            total=None
            for j,(ga,up) in zip(js,sides):
                cum=0.5*(1.0+lax.erf(ga*inv_root_two))
                gel=ga*cum
                fb[j]=gel
                fa[j]=up*(cum+ga*(jnp.exp(-0.5*ga*ga)*inv_root_tau))
                h=(gel*up).astype(bf16)
                hid[j,rows]=h
                part=dot(h,WD(j))
                total=part if total is None else total+part
            acc[...]+=total
        n2,r2=stats(acc[...])
        output[...]=(n2*gain2+shift2).astype(bf16)
        c=cot[...].astype(f32)
        ng[2:3]+=jnp.sum(c*n2,0,keepdims=True)
        ng[3:4]+=jnp.sum(c,0,keepdims=True)
        mid=back(c*gain2,n2,r2)
        gffn[rows]=mid.astype(bf16)
        acc[...]=mid
        @pl.loop(0,2)
        def _(n):
            js=(2*n,2*n+1)
            ghs=[dot_nt(gffn[rows],WD(j)) for j in js]
            total=None
            for j,gh in zip(js,ghs):
                a=(gh*fa[j]).astype(bf16); b=(gh*fb[j]).astype(bf16)
                wide[j,rows]=a; wide[4+j,rows]=b
                part=dot_nt(a,W(1,j))+dot_nt(b,W(2,j))
                total=part if total is None else total+part
            acc[...]+=total
        gl=acc[...]
        ng[0:1]+=jnp.sum(gl*n1,0,keepdims=True)
        ng[1:2]+=jnp.sum(gl,0,keepdims=True)
        gfirst=back(gl*gain1,n1,r1)
        first[...]=gfirst
        gb=gfirst.astype(bf16)
        gbranch[...]=gb
        dO[...]=dot_nt(WO(),gb).astype(bf16)
    def put(g,v):
        g[...]=v.astype(bf16).reshape(g.shape)
    base=LEN//TB
    @pl.when(jnp.logical_and(step>=base,step<base+4))
    def _(): put(gdown,dot_tn(hid[step-base],gffn[...]))
    @pl.when(jnp.logical_and(step>=base+4,step<base+12))
    def _(): put(gwide,dot_tn(inner[...],wide[step-base-4]))

def feed(tokens,cot,mixb,w,norms):
    n=LEN//TB
    last=n-1
    row=lambda i:(jnp.minimum(i,last),0)
    col=lambda i:(0,jnp.minimum(i,last))
    S=jax.ShapeDtypeStruct
    V=lambda s,d=bf16: pltpu.VMEM(s,d)
    clip=lambda v,a,b: jnp.minimum(jnp.maximum(v,a),b)
    return pl.pallas_call(feed_kernel,grid=(n+12,),
        in_specs=[pl.BlockSpec((TB,D),row),pl.BlockSpec((TB,D),row),pl.BlockSpec((D,TB),col),
            pl.BlockSpec(memory_space=pl.ANY),pl.BlockSpec((4,D),lambda i:(0,0))],
        out_specs=[pl.BlockSpec((TB,D),row),pl.BlockSpec((TB,D),row),pl.BlockSpec((D,TB),col),pl.BlockSpec((TB,D),row),
            pl.BlockSpec((8,D),lambda i:(0,0)),
            pl.BlockSpec((1,D,D),lambda i:(clip(i-n,0,3),0,0)),
            pl.BlockSpec((1,4,1,D//4,D),lambda i:(clip((i-n-4)//4,0,1),0,clip(i-n-4,0,7)%4,0,0))],
        out_shape=[S((LEN,D),bf16),S((LEN,D),f32),S((D,LEN),bf16),S((LEN,D),bf16),S((8,D),f32),S((4,D,D),bf16),S((2,4,4,D//4,D),bf16)],
        scratch_shapes=[V((LEN,D)),V((8,LEN,D)),V((LEN,D)),V((4,TB,D),f32),V((4,TB,D),f32),V((TB,D),f32),V((4,LEN,D)),V((4,D//4,D)),*[V((4,4,D//4,D))]*3,pltpu.SemaphoreType.DMA((3,4)),pltpu.SemaphoreType.DMA],
        compiler_params=pltpu.CompilerParams(vmem_limit_bytes=62<<20),name="feed")(tokens,cot,mixb,w.reshape(4,4,4,D//4,D),norms)

MESH = pl.DeviceIdType.MESH
ALL = slice(None)
HALF = D // 2
B_PART, C_PART = 48, 80
P_PART = 48


def place():
    i = lax.axis_index("zero")
    c = lax.axis_index("dp")
    return i, c, i // 4, (i // 2) % 2, i % 2


def partners(i, c, z, y, x):
    return (c, i + 1 - 2 * x), (c, i + 2 - 4 * y), (1 - c, i), (c, i + 4), (c, i - 4)


def when(cond, fn):
    @pl.when(cond)
    def _():
        fn()


def enter(i, c, z, y, x):
    barrier = pltpu.get_barrier_semaphore()
    xp, yp, sib, up, down = partners(i, c, z, y, x)

    def signal(peer):
        pl.semaphore_signal(barrier, inc=1, device_id=peer, device_id_type=MESH)

    for peer in (xp, yp, sib):
        signal(peer)
    when(z > 0, lambda: signal(down))
    when(z < 3, lambda: signal(up))
    pl.semaphore_wait(barrier, 3 + jnp.minimum(z, 1) + jnp.minimum(3 - z, 1))


def pick(z, values):
    out = jnp.int32(values[3])
    for k in (2, 1, 0):
        out = jnp.where(z == k, jnp.int32(values[k]), out)
    return out


def run_plan(z, words, ops):
    count = len(words[0])
    held = [pick(z, [words[k][n] for k in range(4)]) for n in range(count)]

    @pl.loop(0, count)
    def _(n):
        word = held[0]
        for k in range(1, count):
            word = jnp.where(n == k, held[k], word)

        @pl.loop(0, 3)
        def _(m):
            code = jnp.where(m == 0, word, jnp.where(m == 1, word // 256, word // 65536)) % 256
            kind, e = code // 16, code % 16
            branch(kind, e, 0, ops)


def branch(kind, e, low, ops):
    if len(ops) == 1:
        ops[0](e)
        return
    half = len(ops) // 2

    def lower():
        branch(kind, e, low, ops[:half])

    def upper():
        branch(kind, e, low + half, ops[half:])

    lax.cond(kind < low + half, lower, upper)


def gather_attend_kernel(blk, before, last, tokens_in, seg_row, result, norms, tokT_out, qkv_out, mixb, probs_out,
                         held, dist, column, tokens, tail, tokT, qkv, probs, tok_sem, out_sem, t_sem, q_sem, p_sem, pzs, pzr, pfs, pfr, pgs, pgr, p_s, p_r,
                         b1s, b1r, c1u, c1d, c1r, b2u, b2d, b2r, c2s, c2r, b3s, b3r, c3s, c3r, ss, sr, ts, tr):
    i, c, z, y, x = place()
    xp, yp, sib, up, down = partners(i, c, z, y, x)
    half = c * HALF
    other = (1 - c) * HALF
    tokens_come = pltpu.make_async_copy(tokens_in, tokens, tok_sem)
    tokens_come.start()
    spread = jnp.logical_or(z == 1, z == 2)

    def plain():
        for n in range(6):
            cols = pl.ds(n * 128, 128)
            held[z, y, x, :, cols] = blk[pl.ds(n, D, stride=6)].astype(bf16)
            held[z, y, x, pl.ds(0, 16), cols] = (
                blk[pl.ds(n, 16, stride=6)] + before[pl.ds(n, 16, stride=6)]
            ).astype(bf16)

    def swapped():
        top = lax.broadcasted_iota(jnp.int32, (16, 128), 0) == 0
        for n in range(6):
            cols = pl.ds(n * 128, 128)
            for j in range(4):
                value = blk[pl.ds(j * 6 + n, D // 4, stride=24)].astype(bf16)
                held[z, y, x, pl.ds(j * (D // 4), D // 4), cols] = value
                held[z, y, x, pl.ds(j * (D // 4), 16), cols] = (
                    blk[pl.ds(j * 6 + n, 16, stride=24)] + jnp.where(top, before[pl.ds(j * 6 + n, 1)], 0.0)
                ).astype(bf16)

    when(jnp.logical_not(spread), plain)
    when(spread, swapped)
    enter(i, c, z, y, x)

    def remote(ref, peer, s, r):
        return pltpu.make_async_remote_copy(
            src_ref=ref, dst_ref=ref, send_sem=s, recv_sem=r, device_id=peer, device_id_type=MESH
        )

    def by_parity(k, fn):
        when(k % 2 == 0, lambda: fn(False))
        when(k % 2 == 1, lambda: fn(True))

    def rp(k, base):
        return pl.ds(pl.multiple_of(base + k * P_PART, 16), P_PART)

    def z_ref(k, base=half):
        return held.at[0, y, x, rp(k, base)]

    def f_ref(k, odd, base=half):
        if odd:
            return held.at[0, 1 - y, x, rp(k, base)]
        return held.at[0, y, 1 - x, rp(k, base)]

    def g_ref(k, odd, mine, base=half):
        if odd:
            return held.at[0, ALL, x if mine else 1 - x, rp(k, base)]
        return held.at[0, y if mine else 1 - y, ALL, rp(k, base)]

    def PZ(k):
        return remote(z_ref(k), up, pzs.at[k], pzr.at[k])

    def PF(k, odd):
        return remote(z_ref(k), yp if odd else xp, pfs.at[k], pfr.at[k])

    def PG(k, odd):
        return remote(g_ref(k, odd, True), xp if odd else yp, pgs.at[k], pgr.at[k])

    def PS(ref, n):
        return remote(ref, sib, p_s.at[n], p_r.at[n])

    def op_p0z(k):
        def arrive():
            PZ(k).wait_recv()
            PS(z_ref(k), k).start()

        when(z > 0, arrive)
        when(z < 3, lambda: PZ(k).start())
        by_parity(k, lambda odd: PF(k, odd).start())

    def op_p0f(k):
        def turn(odd):
            PF(k, odd).wait_recv()
            PG(k, odd).start()
            PS(f_ref(k, odd), 8 + k).start()

        by_parity(k, turn)

    def op_p0g(k):
        def turn(odd):
            PG(k, odd).wait_recv()
            PS(g_ref(k, odd, False), 16 + k).start()

        by_parity(k, turn)

    split = lambda e: (e // 3 + 1, e % 3)

    def rb(s, base):
        return pl.ds(pl.multiple_of(base + s * B_PART, 16), B_PART)

    def rc(s, base):
        return pl.ds(pl.multiple_of(base + 3 * B_PART + s * C_PART, 16), C_PART)

    def b1_ref(s, yy, base=half):
        return held.at[z, yy, x, rb(s, base)]

    def b2_ref(t, s, xx, base=half):
        return held.at[t, ALL, xx, rb(s, base)]

    def c1_ref(t, s, base=half):
        return held.at[t, y, x, rc(s, base)]

    def c2_ref(t, s, xx, base=half):
        return held.at[t, y, xx, rc(s, base)]

    def c3_ref(t, s, yy, base=half):
        return held.at[t, yy, ALL, rc(s, base)]

    B1 = lambda s: remote(b1_ref(s, y), yp, b1s.at[s], b1r.at[s])
    C1U = lambda t, s, e: remote(c1_ref(t, s), up, c1u.at[e], c1r.at[e])
    C1D = lambda t, s, e: remote(c1_ref(t, s), down, c1d.at[e], c1r.at[e])
    B2U = lambda t, s, e: remote(b2_ref(t, s, x), up, b2u.at[e], b2r.at[e])
    B2D = lambda t, s, e: remote(b2_ref(t, s, x), down, b2d.at[e], b2r.at[e])
    C2 = lambda t, s, e: remote(c2_ref(t, s, x), xp, c2s.at[e], c2r.at[e])
    B3 = lambda t, s, e: remote(b2_ref(t, s, x), xp, b3s.at[e], b3r.at[e])
    C3 = lambda t, s, e: remote(c3_ref(t, s, y), yp, c3s.at[e], c3r.at[e])
    S = lambda ref, n: remote(ref, sib, ss.at[n], sr.at[n])

    def op_own(e):
        t, s = split(e)
        B1(s).start()
        C1D(t, s, e).start()

    def op_ownup(e):
        t, s = split(e)

        def go():
            C1U(t, s, e).start()
            B2U(t, s, e).start()

        when(z < 3, go)

    def op_b1(e):
        t, s = split(e)
        B1(s).wait_recv()
        B2D(t, s, e).start()
        S(b1_ref(s, 1 - y), 45 + s).start()

    def op_cx(e):
        t, s = split(e)
        C2(t, s, e).start()

    def op_bx(e):
        t, s = split(e)
        B3(t, s, e).start()

    def op_c1(e):
        t, s = split(e)
        C1U(t, s, e).wait_recv()
        when(jnp.logical_and(t < z, z < 3), lambda: C1U(t, s, e).start())
        when(jnp.logical_and(t > z, z > 0), lambda: C1D(t, s, e).start())
        S(c1_ref(t, s), e).start()

    def op_b2(e):
        t, s = split(e)
        B2U(t, s, e).wait_recv()
        when(jnp.logical_and(t < z, z < 3), lambda: B2U(t, s, e).start())
        when(jnp.logical_and(t > z, z > 0), lambda: B2D(t, s, e).start())
        S(b2_ref(t, s, x), 9 + e).start()

    def op_c2(e):
        t, s = split(e)
        C2(t, s, e).wait_recv()
        C3(t, s, e).start()
        S(c2_ref(t, s, 1 - x), 18 + e).start()

    def op_b3(e):
        t, s = split(e)
        B3(t, s, e).wait_recv()
        S(b2_ref(t, s, 1 - x), 27 + e).start()

    def op_c3(e):
        t, s = split(e)
        C3(t, s, e).wait_recv()
        S(c3_ref(t, s, 1 - y), 36 + e).start()

    def qkv_leaves(n):
        return pltpu.make_async_copy(qkv.at[n], qkv_out.at[n], q_sem.at[n])

    tokT_leaves = pltpu.make_async_copy(tokT, tokT_out, t_sem)

    def probs_leave(h):
        return pltpu.make_async_copy(probs.at[h % 2], probs_out.at[h], p_sem.at[h % 2])

    def op_proj(n):
        def arrive():
            @pl.loop(0, 8)
            def _(k):
                def got(odd):
                    PS(f_ref(k, odd, other), 8 + k).wait_recv()
                    PS(g_ref(k, odd, False, other), 16 + k).wait_recv()

                by_parity(k, got)
                when(z > 0, lambda: PS(z_ref(k, other), k).wait_recv())

        when(n == 0, arrive)

        @pl.loop(0, 3)
        def _(t):
            cols = pl.ds(pl.multiple_of(t * 256, 256), 256)
            qkv[n, cols] = dot_tn(held[0, n // 2, n % 2, :, cols], tokT[...]).astype(bf16)

        qkv_leaves(n).start()

    def op_head(h):
        when(h >= 2, lambda: probs_leave(h - 2).wait())
        attend_head(h, dist, qkv, mixb, probs.at[h % 2])
        probs_leave(h).start()

    line = jnp.logical_and(y == 1, x == 1)
    source = jnp.logical_and(line, z == 3)

    def T(peer, n):
        return remote(tail, peer, ts.at[n], tr.at[0])

    def leave(t):
        return pltpu.make_async_copy(held.at[t], result.at[t], out_sem.at[t])

    def op_other(e):
        def tail_z():
            def go():
                when(z < 3, lambda: T(down, 0).wait_recv())
                when(z > 0, lambda: T(down, 0).start())
                T(yp, 1).start()

            when(line, go)

        def tail_x():
            def go():
                when(y == 0, lambda: T(yp, 1).wait_recv())
                T(xp, 2).start()

            when(x == 1, go)

        def out():
            t = e - 2

            def others():
                @pl.loop(0, 3)
                def _(s):
                    n = (t - 1) * 3 + s

                    def theirs():
                        S(c1_ref(t, s, other), n).wait_recv()
                        S(b2_ref(t, s, x, other), 9 + n).wait_recv()

                    when(t != z, theirs)
                    when(t == z, lambda: S(b1_ref(s, 1 - y, other), 45 + s).wait_recv())
                    S(c2_ref(t, s, 1 - x, other), 18 + n).wait_recv()
                    S(b2_ref(t, s, 1 - x, other), 27 + n).wait_recv()
                    S(c3_ref(t, s, 1 - y, other), 36 + n).wait_recv()

            when(t > 0, others)
            leave(t).start()

        def prepare():
            tokens_come.wait()
            tokT[...] = tokens[...].astype(f32).T.astype(bf16)
            tokT_leaves.start()
            fill_distance(dist, seg_row, column)

        when(e == 0, tail_z)
        when(e == 1, tail_x)
        when(jnp.logical_and(e >= 2, e < 6), out)
        when(e == 6, prepare)

    def norms_here():
        for n in range(6):
            tail[pl.ds(0, 4), pl.ds(n * 128, 128)] = last[pl.ds(n, 4, stride=6)].astype(bf16)

    tail[...] = jnp.zeros_like(tail)
    when(source, norms_here)
    run_plan(z, GATHER_PLAN, [op_p0z, op_p0f, op_p0g, op_own, op_ownup, op_b1, op_bx, op_c1, op_b2, op_c2, op_b3,
                              op_c3, op_proj, op_head, op_other, op_cx])

    when(x == 0, lambda: T(xp, 2).wait_recv())
    when(x == 1, lambda: T(xp, 2).wait_send())

    def tail_sent():
        T(yp, 1).wait_send()
        when(z > 0, lambda: T(down, 0).wait_send())

    when(line, tail_sent)

    @pl.loop(0, 8)
    def _(k):
        def gone(odd):
            PF(k, odd).wait_send()
            PG(k, odd).wait_send()
            PS(f_ref(k, odd), 8 + k).wait_send()
            PS(g_ref(k, odd, False), 16 + k).wait_send()

        by_parity(k, gone)
        when(z < 3, lambda: PZ(k).wait_send())
        when(z > 0, lambda: PS(z_ref(k), k).wait_send())

    @pl.loop(0, 9)
    def _(e):
        t, s = split(e)
        C2(t, s, e).wait_send()
        B3(t, s, e).wait_send()
        C3(t, s, e).wait_send()

        def ups():
            C1U(t, s, e).wait_send()
            B2U(t, s, e).wait_send()

        def downs():
            C1D(t, s, e).wait_send()
            B2D(t, s, e).wait_send()

        when(jnp.logical_and(t <= z, z < 3), ups)
        when(jnp.logical_and(t >= z, z > 0), downs)

        def mine():
            B1(s).wait_send()
            S(b1_ref(s, 1 - y), 45 + s).wait_send()

        def theirs():
            S(c1_ref(t, s), e).wait_send()
            S(b2_ref(t, s, x), 9 + e).wait_send()

        when(t == z, mine)
        when(t != z, theirs)
        S(c2_ref(t, s, 1 - x), 18 + e).wait_send()
        S(b2_ref(t, s, 1 - x), 27 + e).wait_send()
        S(c3_ref(t, s, 1 - y), 36 + e).wait_send()

    norms[...] = tail[pl.ds(0, 4)].astype(f32)
    tokT_leaves.wait()
    for n in range(3):
        qkv_leaves(n).wait()
    for h in (HEADS - 2, HEADS - 1):
        probs_leave(h).wait()
    for t in range(4):
        leave(t).wait()


def gather_attend(blk, before, last, tokens, seg):
    Q = pltpu.SemaphoreType.DMA
    any_space = pl.BlockSpec(memory_space=pl.ANY)
    counts = [8] * 6 + [24, 24, 3, 3] + [9] * 12 + [48, 48, 3, 1]
    return pl.pallas_call(
        gather_attend_kernel,
        in_specs=[VM, VM, VM, any_space, VM],
        out_specs=[any_space, VM, any_space, any_space, VM, any_space],
        out_shape=[
            jax.ShapeDtypeStruct((4, 2, 2, D, D), bf16), jax.ShapeDtypeStruct((4, D), f32),
            *attend_shapes(),
        ],
        scratch_shapes=[
            pltpu.VMEM((4, 2, 2, D, D), bf16), pltpu.VMEM((LEN, LEN), f32), pltpu.VMEM((LEN, 8), f32),
            pltpu.VMEM((LEN, D), bf16), pltpu.VMEM((16, D), bf16),
            pltpu.VMEM((D, LEN), bf16), pltpu.VMEM((3, D, LEN), bf16), pltpu.VMEM((2, LEN, LEN), bf16),
            Q, Q((4,)), Q, Q((3,)), Q((2,)), *[Q((n,)) for n in counts],
        ],
        compiler_params=pltpu.CompilerParams(
            collective_id=1, has_side_effects=True, vmem_limit_bytes=58 << 20
        ),
        name="gather_attend",
    )(blk, before, last, tokens, seg.reshape(1, LEN))


PLANE_ORDER = (1, 2, 3)
BACK_PLAN = (
    (
        7405680, 7471873, 7570180, 488454, 2295925, 2573089, 8393537, 2364545, 345894, 8525430,
        4728834, 7807120, 1523782, 4487222, 2237712, 9574545, 7943987, 8860689, 5667415, 4579349,
        3167099, 3252242, 8665314, 8804485, 9655458, 10589234, 9818165, 9852385, 10699442, 11554980,
        13816215, 5354322, 11642306, 11839398, 11981761, 12892096, 11912135, 15713989, 15724527,
    ),
    (
        7405680, 7471873, 422660, 7671924, 526198, 8422163, 8880769, 364579, 3182967, 7874194,
        2376465, 1447731, 2430073, 2587514, 3642338, 4671016, 165025, 8773684, 8794440, 13645336,
        9802784, 4478870, 5644962, 1417379, 13711511, 10821952, 11707602, 11617624, 14790849, 10900672,
        12727635, 10990421, 12891331, 11878977, 6296261, 11978679, 13878864, 6435425, 15684177,
    ),
    (
        65648, 7565937, 7603728, 8585991, 554464, 8851840, 2502785, 1472130, 161680, 7870353,
        3219833, 2627706, 10588737, 9634976, 14819963, 8750112, 13665872, 4232210, 2376354, 13735207,
        9934407, 10703281, 3658310, 10855617, 12628146, 12727828, 10987095, 377779, 1291336, 3720260,
        12957111, 3298851, 11941063, 2475587, 1399009, 13845842, 5452644, 3499363, 15684948,
    ),
    (
        65648, 7471985, 7602803, 328739, 8397173, 4395393, 8615456, 1278480, 409892, 9539652,
        7807525, 4231698, 7947640, 3380017, 1331248, 8102266, 4383392, 8750087, 10637702, 9744775,
        10692245, 9879728, 2594753, 12759602, 10866771, 11736484, 11839427, 14722756, 12956951, 12006664,
        4601031, 13022742, 13718087, 1626708, 5589032, 6698963, 5715681, 3692135, 15689816,
    ),
)

GATHER_PLAN = (
    (
        196870, 1026, 7406867, 7401746, 1050388, 15787542, 9443093, 2494834, 2303104, 9565557,
        7631858, 2261281, 2127457, 9827248, 8529701, 9630912, 12748737, 16147091, 6788304, 8835793,
        6330034, 16233847, 13924563, 16287189, 6674082, 14129073, 14182019, 6534048, 14247044, 8955874,
        10007656, 14345121, 14399159, 14722211, 12101030, 15050980, 15724513, 15724527,
    ),
    (
        3273200, 3289330, 5243142, 152067, 7704947, 327684, 1050387, 15941969, 4200210, 1143843,
        1318933, 7770134, 8910310, 2565186, 7807525, 2225286, 6694646, 9658773, 16236992, 8616069,
        8966338, 8675986, 14874833, 10596708, 13788564, 6526870, 14013651, 10934230, 14202008, 11755623,
        10855528, 10729184, 14332633, 14987445, 11000759, 14917794, 15055016, 15724513,
    ),
    (
        3535667, 9647348, 7800565, 7733589, 1442806, 1026, 460049, 4556582, 1184646, 16281976,
        5444887, 1110408, 1369703, 9782128, 4478104, 8396839, 6694391, 9859732, 2355748, 2171522,
        15753314, 8503744, 13681249, 14706897, 9556946, 11777426, 13919412, 14002021, 14063459, 14137521,
        14276790, 10936976, 12049370, 10789544, 15048865, 11576739, 14935218, 15724513,
    ),
    (
        16266807, 9976055, 9958998, 419415, 66151, 12059670, 239192, 458769, 1226501, 8721427,
        2166807, 4617510, 1405255, 2418343, 15738736, 2302705, 16085832, 2487141, 2135656, 12697824,
        9552528, 7655888, 13820291, 13890709, 13926514, 6521986, 8508914, 11625620, 14049939, 11917219,
        11821528, 11970656, 9613529, 14867109, 10673060, 11772389, 11706596, 15724515,
    ),
)


Q_PART = 96
COLS = D // 2


def reduce_back_kernel(wide, down, w, qkv_in, dO_in, mixb_in, probs_in, tokT_in, gbranch_in, first, norm_in,
                       grad_in, flat_out, own, sl, lc3, lc2, lcz, lczx, lb3, lbz, lbzx, lb1, lf, lg, lz, stage,
                       dO, mixb, tokT, gbranch, theirs, probs, ds_all, wv, qkv, fchunk, flat, nacc, nx, ny, nz, nc,
                       own_sem, in_sem, p_sem, w_sem, f_sem, g_sem, o_sem, sib_s, sib_r, st_s, st_r,
                       c3s, c3r, b3s, b3r, c2s, c2r, bus, bur, bds, bdr, cus, cur, cds, cdr, b1s, b1r,
                       fs, fr, gs, gr, zs_, zr_, ns, nr, share_s, share_r, aft_s, aft_r):
    i, c, z, y, x = place()
    xp, yp, sib, up, down_peer = partners(i, c, z, y, x)
    base = c * HALF
    mine = pl.ds(pl.multiple_of(base, 16), HALF)
    other = pl.ds(pl.multiple_of((1 - c) * HALF, 16), HALF)
    planes = [wide.at[0], wide.at[1], down]

    def remote(src, dst, peer, s, r):
        return pltpu.make_async_remote_copy(
            src_ref=src, dst_ref=dst, send_sem=s, recv_sem=r, device_id=peer, device_id_type=MESH
        )

    def local_in(t):
        return pltpu.make_async_copy(planes[t - 1].at[:, :, mine], own.at[t], own_sem.at[t])

    def sib_in(t, s, n):
        k = 2 * ((t - 1) * 3 + s) + n
        start, size = (s * B_PART, B_PART) if n == 0 else (3 * B_PART + s * C_PART, C_PART)
        there = pl.ds(pl.multiple_of((1 - c) * HALF + start, 16), size)
        return remote(planes[t - 1].at[:, :, there], sl.at[t, :, :, pl.ds(start, size)], sib, sib_s.at[k], sib_r.at[k])

    for t in PLANE_ORDER:
        local_in(t).start()
    take = [
        pltpu.make_async_copy(a, b, in_sem.at[n])
        for n, (a, b) in enumerate(
            ((qkv_in, qkv), (dO_in, dO), (mixb_in, mixb), (gbranch_in, gbranch), (tokT_in, tokT))
        )
    ]
    for n in range(3):
        take[n].start()

    def probs_come(h):
        return pltpu.make_async_copy(probs_in.at[h], probs.at[h % 2], p_sem.at[h % 2])

    probs_come(0).start()
    enter_more(i, c, z, y, x)
    for t in PLANE_ORDER:
        for s in range(3):
            for n in range(2):
                sib_in(t, s, n).start()
    nacc[...] = norm_in[...]
    NX = remote(nacc, nx, xp, ns.at[0], nr.at[0])
    NY = remote(nacc, ny, yp, ns.at[1], nr.at[1])
    NZ = remote(nacc, nz, up, ns.at[2], nr.at[2])
    NC = remote(nacc, nc, sib, ns.at[3], nr.at[3])
    line = jnp.logical_and(x == 1, y == 1)
    last_line = jnp.logical_and(line, z == 3)
    when(x == 0, lambda: NX.start())

    def rb(s, k=0, size=B_PART):
        return pl.ds(pl.multiple_of(s * B_PART + k, 16), size)

    def rc(s, k=0, size=C_PART):
        return pl.ds(pl.multiple_of(3 * B_PART + s * C_PART + k, 16), size)

    def add_rows(dst, src, rows):
        @pl.loop(0, rows // 16)
        def _(n):
            k = pl.multiple_of(n * 16, 16)
            a = dst(k)
            a[...] = a[...] + src(k)[...]

    r16 = lambda k: pl.ds(k, 16)
    split = lambda e: (e // 3 + 1, e % 3)

    def C3(t, s, e):
        return remote(own.at[t, 1 - y, :, rc(s)], lc3.at[e], yp, c3s.at[e], c3r.at[e])

    def B3(t, s, e):
        return remote(own.at[t, :, 1 - x, rb(s)], lb3.at[e], xp, b3s.at[e], b3r.at[e])

    def C2(t, s, e):
        return remote(own.at[t, y, 1 - x, rc(s)], lc2.at[e], xp, c2s.at[e], c2r.at[e])

    def BU(t, s, e):
        return remote(own.at[t, :, x, rb(s)], lbz.at[e], up, bus.at[e], bur.at[e])

    def BD(t, s, e, extra=False):
        return remote(own.at[t, :, x, rb(s)], lbzx.at[s] if extra else lbz.at[e], down_peer, bds.at[e], bdr.at[e])

    def CU(t, s, e):
        return remote(own.at[t, y, x, rc(s)], lcz.at[e], up, cus.at[e], cur.at[e])

    def CD(t, s, e, extra=False):
        return remote(own.at[t, y, x, rc(s)], lczx.at[s] if extra else lcz.at[e], down_peer, cds.at[e], cdr.at[e])

    def B1(s):
        return remote(own.at[z, 1 - y, x, rb(s)], lb1.at[s], yp, b1s.at[s], b1r.at[s])

    def op_sum(e):
        t, s = split(e)

        for k in (1, 2, 3):
            when(jnp.logical_and(t == k, s == 0), lambda k=k: local_in(k).wait())
            for m in range(3):
                def arrive(k=k, m=m):
                    for n in range(2):
                        sib_in(k, m, n).wait_recv()

                when(e == (k - 1) * 3 + m, arrive)
        add_rows(lambda k: own.at[t, :, :, rb(s, k, 16)], lambda k: sl.at[t, :, :, rb(s, k, 16)], B_PART)
        add_rows(lambda k: own.at[t, :, :, rc(s, k, 16)], lambda k: sl.at[t, :, :, rc(s, k, 16)], C_PART)
        C3(t, s, e).start()
        B3(t, s, e).start()

    def op_c3(e):
        t, s = split(e)
        C3(t, s, e).wait_recv()
        add_rows(lambda k: own.at[t, y, :, rc(s, k, 16)], lambda k: lc3.at[e, :, r16(k)], C_PART)
        C2(t, s, e).start()

    def op_b3(e):
        t, s = split(e)
        B3(t, s, e).wait_recv()
        add_rows(lambda k: own.at[t, :, x, rb(s, k, 16)], lambda k: lb3.at[e, :, r16(k)], B_PART)

    def op_c2(e):
        t, s = split(e)
        C2(t, s, e).wait_recv()
        add_rows(lambda k: own.at[t, y, x, rc(s, k, 16)], lambda k: lc2.at[e, r16(k)], C_PART)

    def op_bz(e):
        t, s = split(e)
        dst = lambda k: own.at[t, :, x, rb(s, k, 16)]

        def from_below():
            BU(t, s, e).wait_recv()
            add_rows(dst, lambda k: lbz.at[e, :, r16(k)], B_PART)

        when(jnp.logical_and(t >= z, z > 0), from_below)

        def from_above():
            BD(t, s, e).wait_recv()
            add_rows(dst, lambda k: lbz.at[e, :, r16(k)], B_PART)

        when(t < z, lambda: when(z < 3, from_above))

        def from_above_last():
            BD(t, s, e).wait_recv()
            add_rows(dst, lambda k: lbzx.at[s, :, r16(k)], B_PART)

        when(jnp.logical_and(t == z, z < 3), from_above_last)
        when(t > z, lambda: BU(t, s, e).start())
        when(t == z - 1, lambda: BD(t, s, e, True).start())
        when(t < z - 1, lambda: BD(t, s, e).start())
        when(t == z, lambda: B1(s).start())

    def op_cz(e):
        t, s = split(e)
        dst = lambda k: own.at[t, y, x, rc(s, k, 16)]

        def from_below():
            CU(t, s, e).wait_recv()
            add_rows(dst, lambda k: lcz.at[e, r16(k)], C_PART)

        when(jnp.logical_and(t >= z, z > 0), from_below)

        def from_above():
            CD(t, s, e).wait_recv()
            add_rows(dst, lambda k: lcz.at[e, r16(k)], C_PART)

        when(t < z, lambda: when(z < 3, from_above))

        def from_above_last():
            CD(t, s, e).wait_recv()
            add_rows(dst, lambda k: lczx.at[s, r16(k)], C_PART)

        when(jnp.logical_and(t == z, z < 3), from_above_last)
        when(t > z, lambda: CU(t, s, e).start())
        when(t == z - 1, lambda: CD(t, s, e, True).start())
        when(t < z - 1, lambda: CD(t, s, e).start())

    def op_b1(e):
        t, s = split(e)
        B1(s).wait_recv()
        add_rows(lambda k: own.at[z, y, x, rb(s, k, 16)], lambda k: lb1.at[s, r16(k)], B_PART)

    def op_head(h):
        def operands():
            for n in range(3):
                take[n].wait()
            for n in (3, 4):
                take[n].start()

        def late_operands():
            for n in (3, 4):
                take[n].wait()

        when(h == 0, operands)
        when(h == 2, late_operands)
        probs_come(h).wait()
        when(h < HEADS - 1, lambda: probs_come(h + 1).start())
        attend_back_head(h, qkv, dO, mixb, probs.at[h % 2], ds_all)

    def columns(g):
        return pl.ds(pl.multiple_of(g * COLS, 128), COLS)

    def stage_copy(e):
        g, n = e // 4, e % 4
        return remote(
            stage.at[e], sl.at[0, n // 2, n % 2, :, columns(g)], sib, st_s.at[e], st_r.at[e]
        )

    def op_dw(e):
        g, n = e // 4, e % 4
        cols = columns(g)

        def put(half, value):
            if half == 0:
                own[0, n // 2, n % 2, :, cols] = value.astype(bf16)
            else:
                stage[e] = value.astype(bf16)

        def inputs():
            right = qkv[n, pl.ds(pl.multiple_of(g * COLS, 128), COLS)]
            for half, rows in ((0, mine), (1, other)):
                put(half, dot_nt(tokT[rows], right))

        def output():
            right = gbranch[:, cols]
            for half, rows in ((0, mine), (1, other)):
                put(half, dot(mixb[rows], right))

        when(n < 3, inputs)
        when(n == 3, output)
        stage_copy(e).start()

    def rq(k, n=0, size=Q_PART):
        return pl.ds(pl.multiple_of(k * Q_PART + n, 16), size)

    def F0(e, g, k, odd):
        src = own.at[0, :, 1 - x, rq(k), columns(g)] if odd else own.at[0, 1 - y, :, rq(k), columns(g)]
        return remote(src, lf.at[e], xp if odd else yp, fs.at[e], fr.at[e])

    def G0(e, g, k, odd):
        if odd:
            return remote(own.at[0, 1 - y, x, rq(k), columns(g)], lg.at[e], yp, gs.at[e], gr.at[e])
        return remote(own.at[0, y, 1 - x, rq(k), columns(g)], lg.at[e], xp, gs.at[e], gr.at[e])

    def Z0(e, g, k):
        return remote(own.at[0, y, x, rq(k), columns(g)], lz.at[e], down_peer, zs_.at[e], zr_.at[e])

    def by_parity(k, fn):
        when(k % 2 == 0, lambda: fn(False))
        when(k % 2 == 1, lambda: fn(True))

    def op_sum0(e):
        g, k = e // 4, e % 4

        def arrive():
            @pl.loop(0, 4)
            def _(n):
                stage_copy(g * 4 + n).wait_recv()

        when(k == 0, arrive)
        add_rows(
            lambda n: own.at[0, :, :, rq(k, n, 16), columns(g)],
            lambda n: sl.at[0, :, :, rq(k, n, 16), columns(g)], Q_PART,
        )
        by_parity(k, lambda odd: F0(e, g, k, odd).start())

    def op_f0(e):
        g, k = e // 4, e % 4

        def turn(odd):
            F0(e, g, k, odd).wait_recv()
            if odd:
                dst = lambda n: own.at[0, :, x, rq(k, n, 16), columns(g)]
            else:
                dst = lambda n: own.at[0, y, :, rq(k, n, 16), columns(g)]
            add_rows(dst, lambda n: lf.at[e, :, r16(n)], Q_PART)
            G0(e, g, k, odd).start()

        by_parity(k, turn)

    def op_g0(e):
        g, k = e // 4, e % 4
        by_parity(k, lambda odd: G0(e, g, k, odd).wait_recv())
        add_rows(lambda n: own.at[0, y, x, rq(k, n, 16), columns(g)], lambda n: lg.at[e, r16(n)], Q_PART)

    def op_z0(e):
        g, k = e // 4, e % 4

        def arrive():
            Z0(e, g, k).wait_recv()
            add_rows(lambda n: own.at[0, y, x, rq(k, n, 16), columns(g)], lambda n: lz.at[e, r16(n)], Q_PART)

        when(z < 3, arrive)
        when(z > 0, lambda: Z0(e, g, k).start())

    def first_in(q):
        return pltpu.make_async_copy(first.at[pl.ds(pl.multiple_of(q * 256, 256), 256)], fchunk, f_sem)

    def grad_out(q):
        return pltpu.make_async_copy(fchunk, grad_in.at[pl.ds(pl.multiple_of(q * 256, 256), 256)], g_sem)

    def weight_in(n):
        target = (probs.at[0, pl.ds(0, D), pl.ds(0, D)], ds_all.at[pl.ds(0, D), pl.ds(0, D)], wv)[n]
        return pltpu.make_async_copy(w.at[0, n // 2, n % 2], target, w_sem.at[n])

    def op_gin(q):
        def weights():
            for n in range(3):
                weight_in(n).wait()

        when(q == 0, weights)
        when(q > 0, lambda: grad_out(q - 1).wait())
        first_in(q).start()
        cols = pl.ds(pl.multiple_of(q * 256, 256), 256)
        d = pl.ds(0, D)
        acc = dot(probs[0, d, d], qkv[0, :, cols]) + dot(ds_all[d, d], qkv[1, :, cols])
        acc = (acc + dot(wv[...], qkv[2, :, cols])).T
        first_in(q).wait()
        fchunk[...] += acc
        grad_out(q).start()

    def op_other(e):
        def norm_y():
            def go():
                NX.wait_recv()
                nacc[...] += nx[...]
                when(y == 0, lambda: NY.start())

            when(x == 1, go)

        def norm_z():
            def go():
                NY.wait_recv()
                nacc[...] += ny[...]

                def more():
                    NZ.wait_recv()
                    nacc[...] += nz[...]

                when(z > 0, more)
                when(z < 3, lambda: NZ.start())
                when(z == 3, lambda: NC.start())

            when(line, go)

        def load():
            for n in range(3):
                weight_in(n).start()

        when(e == 0, norm_y)
        when(e == 1, norm_z)
        when(e == 2, load)

    run_plan(z, BACK_PLAN, [op_sum, op_c3, op_b3, op_c2, op_bz, op_cz, op_b1, op_head, op_dw, op_sum0, op_f0,
                            op_g0, op_z0, op_gin, op_other])

    spread = jnp.logical_or(z == 1, z == 2)

    def flatten(half, get):
        def plain():
            for n in range(6):
                flat[pl.ds(half * (6 * HALF) + n, HALF, stride=6)] = get(pl.ds(0, HALF), pl.ds(n * 128, 128)).astype(f32)

        def swapped():
            for n in range(6):
                for j in range(2):
                    value = get(pl.ds(j * (D // 4), D // 4), pl.ds(n * 128, 128)).astype(f32)
                    flat[pl.ds(half * 12 + j * 6 + n, D // 4, stride=24)] = value

        when(jnp.logical_not(spread), plain)
        when(spread, swapped)

    share = remote(own.at[z, y, x], theirs, sib, share_s, share_r)
    share.start()
    flatten(c, lambda rows, cols: own[z, y, x, rows, cols])

    @pl.loop(0, 9)
    def _(e):
        t, s = split(e)
        C3(t, s, e).wait_send()
        B3(t, s, e).wait_send()
        C2(t, s, e).wait_send()

        def went_up():
            BU(t, s, e).wait_send()
            CU(t, s, e).wait_send()

        def went_down():
            BD(t, s, e).wait_send()
            CD(t, s, e).wait_send()

        when(t > z, went_up)
        when(t < z, went_down)
        when(t == z, lambda: B1(s).wait_send())

    @pl.loop(0, 8)
    def _(e):
        g, k = e // 4, e % 4
        stage_copy(e).wait_send()

        def gone(odd):
            F0(e, g, k, odd).wait_send()
            G0(e, g, k, odd).wait_send()

        by_parity(k, gone)
        when(z > 0, lambda: Z0(e, g, k).wait_send())

    for t in (1, 2, 3):
        for s in range(3):
            for n in range(2):
                sib_in(t, s, n).wait_send()
    when(x == 0, lambda: NX.wait_send())
    when(jnp.logical_and(x == 1, y == 0), lambda: NY.wait_send())
    when(jnp.logical_and(line, z < 3), lambda: NZ.wait_send())

    def norm_last():
        NC.wait_recv()
        NC.wait_send()
        nacc[...] += nc[...]

    when(last_line, norm_last)
    grad_out(3).wait()
    share.wait_recv()
    flatten(1 - c, lambda rows, cols: theirs[rows, cols])
    share.wait_send()
    body, head_rows, after = pl.ds(0, 6 * D), pl.ds(0, 24), pl.ds(6 * D, 24)
    leave = pltpu.make_async_copy(flat.at[body], flat_out.at[body], o_sem.at[0])
    leave.start()

    def ending():
        for n in range(6):
            flat[pl.ds(6 * D + n, 8, stride=6)] = nacc[:, pl.ds(n * 128, 128)]

    when(i == 15, ending)
    give = remote(flat.at[head_rows], flat.at[after], (c, i - 1), aft_s, aft_r)
    when(i > 0, lambda: give.start())
    when(i < 15, lambda: give.wait_recv())
    leave_after = pltpu.make_async_copy(flat.at[after], flat_out.at[after], o_sem.at[1])
    leave_after.start()
    when(i > 0, lambda: give.wait_send())
    leave.wait()
    leave_after.wait()


def enter_more(i, c, z, y, x):
    barrier = pltpu.get_barrier_semaphore()
    xp, yp, sib, up, down = partners(i, c, z, y, x)

    def signal(peer):
        pl.semaphore_signal(barrier, inc=1, device_id=peer, device_id_type=MESH)

    for peer in (xp, yp, sib):
        signal(peer)
    when(z > 0, lambda: signal(down))
    when(z < 3, lambda: signal(up))
    when(jnp.logical_and(x == 0, i > 0), lambda: signal((c, i - 1)))
    when(jnp.logical_and(x == 1, i < 15), lambda: signal((c, i + 1)))
    more = 1 - jnp.where(i == 0, 1, 0) - jnp.where(i == 15, 1, 0)
    pl.semaphore_wait(barrier, 3 + jnp.minimum(z, 1) + jnp.minimum(3 - z, 1) + more)


def reduce_back(wide, down, w, qkv, dO, mixb, probs, tokT, gbranch, first, norms):
    Q = pltpu.SemaphoreType.DMA
    V = lambda *s: pltpu.VMEM(s, bf16)
    F = lambda *s: pltpu.VMEM(s, f32)
    A = pl.BlockSpec(memory_space=pl.ANY)
    return pl.pallas_call(
        reduce_back_kernel,
        in_specs=[A] * 10 + [VM],
        out_specs=[A, A],
        out_shape=[jax.ShapeDtypeStruct((LEN, D), f32), jax.ShapeDtypeStruct((6 * D + 24, 128), f32)],
        scratch_shapes=[
            V(4, 2, 2, HALF, D), V(4, 2, 2, HALF, D), V(9, 2, C_PART, D), V(9, C_PART, D), V(9, C_PART, D),
            V(3, C_PART, D), V(9, 2, B_PART, D), V(9, 2, B_PART, D), V(3, 2, B_PART, D), V(3, B_PART, D),
            V(8, 2, Q_PART, COLS), V(8, Q_PART, COLS), V(8, Q_PART, COLS), V(8, HALF, COLS),
            V(D, LEN), V(D, LEN), V(D, LEN), V(LEN, D), V(HALF, D), V(2, LEN, LEN), V(LEN, LEN), V(D, D), V(3, D, LEN),
            F(256, D), F(6 * D + 64, 128), F(8, D), F(8, D), F(8, D), F(8, D), F(8, D),
            Q((4,)), Q((5,)), Q((2,)), Q((3,)), Q, Q, Q((2,)), Q((18,)), Q((18,)), Q((8,)), Q((8,)),
            *[Q((9,))] * 14, Q((3,)), Q((3,)), *[Q((8,))] * 6, Q((4,)), Q((4,)), Q, Q, Q, Q,
        ],
        compiler_params=pltpu.CompilerParams(
            collective_id=2, has_side_effects=True, vmem_limit_bytes=55 << 20
        ),
        name="reduce_back",
    )(wide, down, w, qkv, dO, mixb, probs, tokT, gbranch, first, norms)

SQUARE = D * D
TAIL = 4 * D


def from_wide(blocks):
    return blocks.reshape(4, 4, D // 4, D).transpose(0, 2, 1, 3).reshape(D, FF)


def to_wide(value):
    return value.reshape(4, D // 4, 4, D).transpose(0, 2, 1, 3).reshape(2, 2, D, D)


def gather_and_attend(master, tokens, segments):
    count = lax.axis_size("zero")
    index = lax.axis_index("zero")
    size = 16 * SQUARE // count
    last = master[-TAIL:]
    step = TAIL // count
    zeros = jnp.zeros((TAIL,), f32)
    ending = lax.dynamic_slice(jnp.concatenate([last, zeros]), (TAIL - step * (index + 1),), (TAIL,))
    before = lax.ppermute(ending, "zero", [(k, k + 1) for k in range(count - 1)])
    block = lax.dynamic_slice(jnp.concatenate([zeros, master]), (TAIL - step * index,), (size,))
    if count == 16:
        before = jnp.pad(before.reshape(24, 128), ((0, 104), (0, 0)))
        block, last = block.reshape(6 * D, 128), jnp.pad(last.reshape(24, 128), ((0, 40), (0, 0)))
        blocks, norms, *attended = gather_attend(block, before, last, tokens, segments)
    else:
        block = jnp.concatenate([block[:TAIL] + before, block[TAIL:]])
        natural = lax.all_gather(block.astype(bf16).reshape(-1, D), "zero", axis=0, tiled=True)
        parts = natural.reshape(4, 4 * D, D)
        wide = [to_wide(parts[k].reshape(D, FF)) for k in (1, 2)]
        blocks = jnp.stack([parts[0].reshape(2, 2, D, D), *wide, parts[3].reshape(2, 2, D, D)])
        last = last.astype(bf16).astype(f32)
        norms = lax.psum(jnp.where(index == count - 1, last, 0.0), "zero").reshape(4, D)
        attended = attend(tokens, blocks, segments)
    return blocks, norms, *attended


def back_and_scatter(blocks, tokT, qkv, mixed, probs, grad_mixed, first_grad, branch_grad, norm_grads,
                     down_grad, wide_grad):
    count = lax.axis_size("zero")
    index = lax.axis_index("zero")
    if count == 16:
        input_grad, joined = reduce_back(
            wide_grad, down_grad, blocks, qkv, grad_mixed, mixed, probs, tokT, branch_grad, first_grad,
            norm_grads,
        )
        joined = joined.reshape(-1)
    else:
        square, input_grad = attend_back(
            blocks, tokT, qkv, mixed, probs, grad_mixed, first_grad, branch_grad
        )
        natural = [from_wide(wide_grad[k]).reshape(4 * D, D) for k in (0, 1)]
        natural = jnp.concatenate([square.reshape(4 * D, D), *natural, down_grad.reshape(4 * D, D)])
        block = lax.psum_scatter(natural, "zero", scatter_dimension=0, tiled=True)
        block = lax.psum(block.astype(f32), "dp")
        tail = lax.psum(norm_grads[:4], ("dp", "zero"))
        flat = block.reshape(-1)
        after = lax.ppermute(flat[:TAIL], "zero", [(k + 1, k) for k in range(count - 1)])
        joined = jnp.concatenate([flat, jnp.where(index == count - 1, tail.reshape(-1), after)])
    shard = 16 * SQUARE // count + TAIL // count
    return input_grad, lax.dynamic_slice(joined, (TAIL // count * index,), (shard,))


def local(tokens, segments, cotangent, master, moment_one, moment_two):
    blocks, norms, tokT, qkv, mixed, probs = gather_and_attend(master, tokens, segments)
    output, first_grad, grad_mixed, branch_grad, norm_grads, down_grad, wide_grad = feed(
        tokens, cotangent, mixed, blocks, norms
    )
    input_grad, grad_shard = back_and_scatter(
        blocks, tokT, qkv, mixed, probs, grad_mixed, first_grad, branch_grad, norm_grads,
        down_grad.reshape(2, 2, D, D), wide_grad.reshape(2, 2, 2, D, D),
    )
    grad_shard = grad_shard / (lax.axis_size("zero") * lax.axis_size("dp"))
    first = beta_one * moment_one + (1.0 - beta_one) * grad_shard
    second = beta_two * moment_two + (1.0 - beta_two) * grad_shard * grad_shard
    update = first / correct_one / (jnp.sqrt(second / correct_two) + adam_eps)
    master_new = master - learn_rate * (update + weight_decay * master)
    return (
        output,
        input_grad,
        grad_shard,
        first,
        second,
        master_new,
        master_new.astype(jnp.bfloat16),
    )


def solution(mesh):
    return jax.shard_map(
        local,
        mesh=mesh,
        in_specs=(
            P(("dp", "zero"), None),
            P(("dp", "zero")),
            P(("dp", "zero"), None),
            P("zero"),
            P("zero"),
            P("zero"),
        ),
        out_specs=(
            P(("dp", "zero"), None),
            P(("dp", "zero"), None),
            P("zero"),
            P("zero"),
            P("zero"),
            P("zero"),
            P("zero"),
        ),
        check_vma=False,
    )
```

```python
import functools

import jax
import jax.numpy as jnp
from jax import lax
from jax.sharding import PartitionSpec as P
import jax.experimental.pallas as pl
import jax.experimental.pallas.tpu as pltpu

D = 768
HEADS = 12
HEAD = 64
FF = 3072
LEN = 1024


learn_rate = 0.02
beta_one = 0.9
beta_two = 0.999
adam_eps = 1e-08
weight_decay = 0.01
correct_one = 1.0 - 0.9**10
correct_two = 1.0 - 0.999**10
norm_eps = 1e-06
inv_root_two = 0.7071067811865476
inv_root_tau = 0.3989422804014327


bf16=jnp.bfloat16; f32=jnp.float32
FAR=1e33
VM=pl.BlockSpec(memory_space=pltpu.VMEM)

def dot(a,b): return lax.dot_general(a,b,(((1,),(0,)),((),())),preferred_element_type=f32)
def dot_tn(a,b): return lax.dot_general(a,b,(((0,),(0,)),((),())),preferred_element_type=f32)
def dot_nt(a,b): return lax.dot_general(a,b,(((1,),(1,)),((),())),preferred_element_type=f32)

def slope(h):
    return jnp.exp2(-8.0/HEADS*(jnp.full((1,1),h,jnp.int32).astype(f32)+1.0))

def fill_distance(dist,seg_row,column):
    column[...]=jnp.broadcast_to(seg_row[...].astype(f32),(8,LEN)).T
    @pl.loop(0,LEN//128)
    def _(k):
        r=pl.ds(pl.multiple_of(k*128,128),128)
        kk=(lax.broadcasted_iota(jnp.int32,(128,LEN),0)+k*128)
        qq=lax.broadcasted_iota(jnp.int32,(128,LEN),1)
        d=jnp.abs(kk-qq).astype(f32)
        dist[r]=jnp.where(column[r,0:1]==seg_row[...].astype(f32),d,FAR)

QB=256
def project_all(w,tokT,qkv):
    @pl.loop(0,3)
    def _(n):
        @pl.loop(0,3)
        def _(t):
            c=pl.ds(pl.multiple_of(t*256,256),256)
            qkv[n,c]=dot_tn(w[0,n//2,n%2,:,c],tokT[...]).astype(bf16)

def attend_head(h,dist,qkv,mixb,probs):
    rows=pl.ds(pl.multiple_of(h*HEAD,HEAD),HEAD)
    keys=qkv[1,rows].astype(f32).T.astype(bf16)
    s=dot(keys,qkv[0,rows]*bf16(0.125))-slope(h)*dist[...]
    e=jnp.exp(s-jnp.max(s,0,keepdims=True))
    p=(e*(1.0/jnp.sum(e,0,keepdims=True))).astype(bf16)
    probs[...]=p
    mixb[rows]=dot(qkv[2,rows],p).astype(bf16)

def attend_back_head(h,qkv,dO,mixb,probs,ds_all):
    rows=pl.ds(pl.multiple_of(h*HEAD,HEAD),HEAD)
    values=qkv[2,rows].astype(f32).T.astype(bf16)
    grad_q=[]
    for b in range(LEN//QB):
        cols=pl.ds(b*QB,QB)
        do=dO[rows,cols]
        dp=dot(values,do)
        delta=jnp.sum(do.astype(f32)*mixb[rows,cols].astype(f32),0,keepdims=True)
        ds=(probs[:,cols].astype(f32)*(dp-delta)).astype(bf16)
        ds_all[:,cols]=ds
        grad_q.append((dot(qkv[1,rows],ds)*0.125).astype(bf16))
    grad_k=(dot_nt(qkv[0,rows],ds_all[...])*0.125).astype(bf16)
    grad_v=dot_nt(dO[rows],probs[...]).astype(bf16)
    for b in range(LEN//QB):
        qkv[0,rows,pl.ds(b*QB,QB)]=grad_q[b]
    qkv[1,rows]=grad_k
    qkv[2,rows]=grad_v

def attend_kernel(tokens,w,seg_row,tokT,qkv,mixb,probs_out,dist,column,probs,sem):
    tokT[...]=tokens[...].astype(f32).T.astype(bf16)
    fill_distance(dist,seg_row,column)
    project_all(w,tokT,qkv)
    @pl.loop(0,HEADS)
    def _(h):
        attend_head(h,dist,qkv,mixb,probs)
        move=pltpu.make_async_copy(probs,probs_out.at[h],sem)
        move.start()
        move.wait()

def attend_shapes():
    S=jax.ShapeDtypeStruct
    return [S((D,LEN),bf16),S((3,D,LEN),bf16),S((D,LEN),bf16),S((HEADS,LEN,LEN),bf16)]

ANY=pl.BlockSpec(memory_space=pl.ANY)

def attend(tokens,w,seg):
    return pl.pallas_call(attend_kernel,grid=(1,),
        in_specs=[VM,pl.BlockSpec((1,2,2,D,D),lambda i:(0,0,0,0,0)),VM],out_specs=[VM]*3+[ANY],
        out_shape=attend_shapes(),
        scratch_shapes=[pltpu.VMEM((LEN,LEN),f32),pltpu.VMEM((LEN,8),f32),pltpu.VMEM((LEN,LEN),bf16),pltpu.SemaphoreType.DMA],
        compiler_params=pltpu.CompilerParams(vmem_limit_bytes=58<<20),name="attend")(tokens,w,seg.reshape(1,LEN))

def attend_back_kernel(w,tokT,qkv_in,mixb,probs_in,dO,first,gbranch,g0,grad_in,qkv,probs,ds_all,sem,qkv_sem):
    take=pltpu.make_async_copy(qkv_in,qkv,qkv_sem)
    take.start()
    take.wait()
    @pl.loop(0,HEADS)
    def _(h):
        move=pltpu.make_async_copy(probs_in.at[h],probs,sem)
        move.start()
        move.wait()
        attend_back_head(h,qkv,dO,mixb,probs,ds_all)
    g0[1,1]=dot(mixb[...],gbranch[...]).astype(bf16)
    for n in range(3):
        g0[n//2,n%2]=dot_nt(tokT[...],qkv[n]).astype(bf16)
    @pl.loop(0,4)
    def _(t):
        c=pl.ds(pl.multiple_of(t*256,256),256)
        acc=dot(w[0,0,0],qkv[0,:,c])+dot(w[0,0,1],qkv[1,:,c])+dot(w[0,1,0],qkv[2,:,c])
        grad_in[c]=first[c]+acc.T

def attend_back(w,tokT,qkv,mixb,probs,dO,first,gbranch):
    return pl.pallas_call(attend_back_kernel,grid=(1,),
        in_specs=[pl.BlockSpec((1,2,2,D,D),lambda i:(0,0,0,0,0)),VM,ANY,VM,ANY,VM,VM,VM],out_specs=[VM]*2,
        out_shape=[jax.ShapeDtypeStruct((2,2,D,D),bf16),jax.ShapeDtypeStruct((LEN,D),f32)],
        scratch_shapes=[pltpu.VMEM((3,D,LEN),bf16),pltpu.VMEM((LEN,LEN),bf16),pltpu.VMEM((LEN,LEN),bf16),pltpu.SemaphoreType.DMA,pltpu.SemaphoreType.DMA],
        compiler_params=pltpu.CompilerParams(vmem_limit_bytes=60<<20),name="attend_back")(w,tokT,qkv,mixb,probs,dO,first,gbranch)

TB=256
def feed_kernel(tokens,cot,mixb,w,norms,output,first,dO,gbranch,ng,gdown,gwide,inner,wide,gffn,fa,fb,acc,hid,wo,w1,w2,w3,w_sem,wo_sem):
    step=pl.program_id(0)
    gain1=norms[0:1]; shift1=norms[1:2]; gain2=norms[2:3]; shift2=norms[3:4]
    def stats(v):
        c=v-jnp.mean(v,-1,keepdims=True)
        r=lax.rsqrt(jnp.mean(c*c,-1,keepdims=True)+norm_eps)
        return c*r,r
    def back(e,n,r):
        return r*(e-jnp.mean(e,-1,keepdims=True)-n*jnp.mean(e*n,-1,keepdims=True))
    W=lambda p,j: (w1,w2)[p-1][j].reshape(D,D)
    WD=lambda j: w3[j].reshape(D,D)
    WO=lambda: wo[...].reshape(D,D)
    def load(p,j):
        source=w.at[p,j] if p==3 else w.at[p,:,j]
        return pltpu.make_async_copy(source,(w1,w2,w3)[p-1].at[j],w_sem.at[p-1,j])
    load_out=pltpu.make_async_copy(w.at[0,3],wo,wo_sem)
    @pl.when(step==0)
    def _():
        load_out.start()
        for j in range(4):
            for p in (1,2,3): load(p,j).start()
        ng[...]=jnp.zeros_like(ng)
        load_out.wait()
    @pl.when(step<LEN//TB)
    def _():
        rows=pl.ds(pl.multiple_of(step*TB,TB),TB)
        branch=dot_tn(mixb[...],WO())
        n1,r1=stats(tokens[...].astype(f32)+branch)
        l1=n1*gain1+shift1
        inner[rows]=l1.astype(bf16)
        acc[...]=l1
        @pl.loop(0,2)
        def _(n):
            js=(2*n,2*n+1)
            @pl.when(step==0)
            def _():
                for j in js:
                    for p in (1,2,3): load(p,j).wait()
            inn=inner[rows]
            sides=[(dot(inn,W(1,j)),dot(inn,W(2,j))) for j in js]
            total=None
            for j,(ga,up) in zip(js,sides):
                cum=0.5*(1.0+lax.erf(ga*inv_root_two))
                gel=ga*cum
                fb[j]=gel
                fa[j]=up*(cum+ga*(jnp.exp(-0.5*ga*ga)*inv_root_tau))
                h=(gel*up).astype(bf16)
                hid[j,rows]=h
                part=dot(h,WD(j))
                total=part if total is None else total+part
            acc[...]+=total
        n2,r2=stats(acc[...])
        output[...]=(n2*gain2+shift2).astype(bf16)
        c=cot[...].astype(f32)
        ng[2:3]+=jnp.sum(c*n2,0,keepdims=True)
        ng[3:4]+=jnp.sum(c,0,keepdims=True)
        mid=back(c*gain2,n2,r2)
        gffn[rows]=mid.astype(bf16)
        acc[...]=mid
        @pl.loop(0,2)
        def _(n):
            js=(2*n,2*n+1)
            ghs=[dot_nt(gffn[rows],WD(j)) for j in js]
            total=None
            for j,gh in zip(js,ghs):
                a=(gh*fa[j]).astype(bf16); b=(gh*fb[j]).astype(bf16)
                wide[j,rows]=a; wide[4+j,rows]=b
                part=dot_nt(a,W(1,j))+dot_nt(b,W(2,j))
                total=part if total is None else total+part
            acc[...]+=total
        gl=acc[...]
        ng[0:1]+=jnp.sum(gl*n1,0,keepdims=True)
        ng[1:2]+=jnp.sum(gl,0,keepdims=True)
        gfirst=back(gl*gain1,n1,r1)
        first[...]=gfirst
        gb=gfirst.astype(bf16)
        gbranch[...]=gb
        dO[...]=dot_nt(WO(),gb).astype(bf16)
    def put(g,v):
        g[...]=v.astype(bf16).reshape(g.shape)
    base=LEN//TB
    @pl.when(jnp.logical_and(step>=base,step<base+4))
    def _(): put(gdown,dot_tn(hid[step-base],gffn[...]))
    @pl.when(jnp.logical_and(step>=base+4,step<base+12))
    def _(): put(gwide,dot_tn(inner[...],wide[step-base-4]))

def feed(tokens,cot,mixb,w,norms):
    n=LEN//TB
    last=n-1
    row=lambda i:(jnp.minimum(i,last),0)
    col=lambda i:(0,jnp.minimum(i,last))
    S=jax.ShapeDtypeStruct
    V=lambda s,d=bf16: pltpu.VMEM(s,d)
    clip=lambda v,a,b: jnp.minimum(jnp.maximum(v,a),b)
    return pl.pallas_call(feed_kernel,grid=(n+12,),
        in_specs=[pl.BlockSpec((TB,D),row),pl.BlockSpec((TB,D),row),pl.BlockSpec((D,TB),col),
            pl.BlockSpec(memory_space=pl.ANY),pl.BlockSpec((4,D),lambda i:(0,0))],
        out_specs=[pl.BlockSpec((TB,D),row),pl.BlockSpec((TB,D),row),pl.BlockSpec((D,TB),col),pl.BlockSpec((TB,D),row),
            pl.BlockSpec((8,D),lambda i:(0,0)),
            pl.BlockSpec((1,D,D),lambda i:(clip(i-n,0,3),0,0)),
            pl.BlockSpec((1,4,1,D//4,D),lambda i:(clip((i-n-4)//4,0,1),0,clip(i-n-4,0,7)%4,0,0))],
        out_shape=[S((LEN,D),bf16),S((LEN,D),f32),S((D,LEN),bf16),S((LEN,D),bf16),S((8,D),f32),S((4,D,D),bf16),S((2,4,4,D//4,D),bf16)],
        scratch_shapes=[V((LEN,D)),V((8,LEN,D)),V((LEN,D)),V((4,TB,D),f32),V((4,TB,D),f32),V((TB,D),f32),V((4,LEN,D)),V((4,D//4,D)),*[V((4,4,D//4,D))]*3,pltpu.SemaphoreType.DMA((3,4)),pltpu.SemaphoreType.DMA],
        compiler_params=pltpu.CompilerParams(vmem_limit_bytes=62<<20),name="feed")(tokens,cot,mixb,w.reshape(4,4,4,D//4,D),norms)

MESH = pl.DeviceIdType.MESH
ALL = slice(None)
HALF = D // 2
B_PART, C_PART = 48, 80
P_PART = 48


def place():
    i = lax.axis_index("zero")
    c = lax.axis_index("dp")
    return i, c, i // 4, (i // 2) % 2, i % 2


def partners(i, c, z, y, x):
    return (c, i + 1 - 2 * x), (c, i + 2 - 4 * y), (1 - c, i), (c, i + 4), (c, i - 4)


def when(cond, fn):
    @pl.when(cond)
    def _():
        fn()


def enter(i, c, z, y, x):
    barrier = pltpu.get_barrier_semaphore()
    xp, yp, sib, up, down = partners(i, c, z, y, x)

    def signal(peer):
        pl.semaphore_signal(barrier, inc=1, device_id=peer, device_id_type=MESH)

    for peer in (xp, yp, sib):
        signal(peer)
    when(z > 0, lambda: signal(down))
    when(z < 3, lambda: signal(up))
    pl.semaphore_wait(barrier, 3 + jnp.minimum(z, 1) + jnp.minimum(3 - z, 1))


def pick(z, values):
    out = jnp.int32(values[3])
    for k in (2, 1, 0):
        out = jnp.where(z == k, jnp.int32(values[k]), out)
    return out


def run_plan(z, words, ops):
    count = len(words[0])
    held = [pick(z, [words[k][n] for k in range(4)]) for n in range(count)]

    @pl.loop(0, count)
    def _(n):
        word = held[0]
        for k in range(1, count):
            word = jnp.where(n == k, held[k], word)

        @pl.loop(0, 3)
        def _(m):
            code = jnp.where(m == 0, word, jnp.where(m == 1, word // 256, word // 65536)) % 256
            kind, e = code // 16, code % 16
            branch(kind, e, 0, ops)


def branch(kind, e, low, ops):
    if len(ops) == 1:
        ops[0](e)
        return
    half = len(ops) // 2

    def lower():
        branch(kind, e, low, ops[:half])

    def upper():
        branch(kind, e, low + half, ops[half:])

    lax.cond(kind < low + half, lower, upper)


def gather_attend_kernel(blk, before, last, tokens_in, seg_row, result, norms, tokT_out, qkv_out, mixb, probs_out,
                         held, dist, column, tokens, tail, tokT, qkv, probs, tok_sem, out_sem, t_sem, q_sem, p_sem, pzs, pzr, pfs, pfr, pgs, pgr, p_s, p_r,
                         b1s, b1r, c1u, c1d, c1r, b2u, b2d, b2r, c2s, c2r, b3s, b3r, c3s, c3r, ss, sr, ts, tr):
    i, c, z, y, x = place()
    xp, yp, sib, up, down = partners(i, c, z, y, x)
    half = c * HALF
    other = (1 - c) * HALF
    tokens_come = pltpu.make_async_copy(tokens_in, tokens, tok_sem)
    tokens_come.start()
    spread = jnp.logical_or(z == 1, z == 2)

    def plain():
        for n in range(6):
            cols = pl.ds(n * 128, 128)
            held[z, y, x, :, cols] = blk[pl.ds(n, D, stride=6)].astype(bf16)
            held[z, y, x, pl.ds(0, 16), cols] = (
                blk[pl.ds(n, 16, stride=6)] + before[pl.ds(n, 16, stride=6)]
            ).astype(bf16)

    def swapped():
        top = lax.broadcasted_iota(jnp.int32, (16, 128), 0) == 0
        for n in range(6):
            cols = pl.ds(n * 128, 128)
            for j in range(4):
                value = blk[pl.ds(j * 6 + n, D // 4, stride=24)].astype(bf16)
                held[z, y, x, pl.ds(j * (D // 4), D // 4), cols] = value
                held[z, y, x, pl.ds(j * (D // 4), 16), cols] = (
                    blk[pl.ds(j * 6 + n, 16, stride=24)] + jnp.where(top, before[pl.ds(j * 6 + n, 1)], 0.0)
                ).astype(bf16)

    when(jnp.logical_not(spread), plain)
    when(spread, swapped)
    enter(i, c, z, y, x)

    def remote(ref, peer, s, r):
        return pltpu.make_async_remote_copy(
            src_ref=ref, dst_ref=ref, send_sem=s, recv_sem=r, device_id=peer, device_id_type=MESH
        )

    def by_parity(k, fn):
        when(k % 2 == 0, lambda: fn(False))
        when(k % 2 == 1, lambda: fn(True))

    def rp(k, base):
        return pl.ds(pl.multiple_of(base + k * P_PART, 16), P_PART)

    def z_ref(k, base=half):
        return held.at[0, y, x, rp(k, base)]

    def f_ref(k, odd, base=half):
        if odd:
            return held.at[0, 1 - y, x, rp(k, base)]
        return held.at[0, y, 1 - x, rp(k, base)]

    def g_ref(k, odd, mine, base=half):
        if odd:
            return held.at[0, ALL, x if mine else 1 - x, rp(k, base)]
        return held.at[0, y if mine else 1 - y, ALL, rp(k, base)]

    def PZ(k):
        return remote(z_ref(k), up, pzs.at[k], pzr.at[k])

    def PF(k, odd):
        return remote(z_ref(k), yp if odd else xp, pfs.at[k], pfr.at[k])

    def PG(k, odd):
        return remote(g_ref(k, odd, True), xp if odd else yp, pgs.at[k], pgr.at[k])

    def PS(ref, n):
        return remote(ref, sib, p_s.at[n], p_r.at[n])

    def op_p0z(k):
        def arrive():
            PZ(k).wait_recv()
            PS(z_ref(k), k).start()

        when(z > 0, arrive)
        when(z < 3, lambda: PZ(k).start())
        by_parity(k, lambda odd: PF(k, odd).start())

    def op_p0f(k):
        def turn(odd):
            PF(k, odd).wait_recv()
            PG(k, odd).start()
            PS(f_ref(k, odd), 8 + k).start()

        by_parity(k, turn)

    def op_p0g(k):
        def turn(odd):
            PG(k, odd).wait_recv()
            PS(g_ref(k, odd, False), 16 + k).start()

        by_parity(k, turn)

    split = lambda e: (e // 3 + 1, e % 3)

    def rb(s, base):
        return pl.ds(pl.multiple_of(base + s * B_PART, 16), B_PART)

    def rc(s, base):
        return pl.ds(pl.multiple_of(base + 3 * B_PART + s * C_PART, 16), C_PART)

    def b1_ref(s, yy, base=half):
        return held.at[z, yy, x, rb(s, base)]

    def b2_ref(t, s, xx, base=half):
        return held.at[t, ALL, xx, rb(s, base)]

    def c1_ref(t, s, base=half):
        return held.at[t, y, x, rc(s, base)]

    def c2_ref(t, s, xx, base=half):
        return held.at[t, y, xx, rc(s, base)]

    def c3_ref(t, s, yy, base=half):
        return held.at[t, yy, ALL, rc(s, base)]

    B1 = lambda s: remote(b1_ref(s, y), yp, b1s.at[s], b1r.at[s])
    C1U = lambda t, s, e: remote(c1_ref(t, s), up, c1u.at[e], c1r.at[e])
    C1D = lambda t, s, e: remote(c1_ref(t, s), down, c1d.at[e], c1r.at[e])
    B2U = lambda t, s, e: remote(b2_ref(t, s, x), up, b2u.at[e], b2r.at[e])
    B2D = lambda t, s, e: remote(b2_ref(t, s, x), down, b2d.at[e], b2r.at[e])
    C2 = lambda t, s, e: remote(c2_ref(t, s, x), xp, c2s.at[e], c2r.at[e])
    B3 = lambda t, s, e: remote(b2_ref(t, s, x), xp, b3s.at[e], b3r.at[e])
    C3 = lambda t, s, e: remote(c3_ref(t, s, y), yp, c3s.at[e], c3r.at[e])
    S = lambda ref, n: remote(ref, sib, ss.at[n], sr.at[n])

    def op_own(e):
        t, s = split(e)
        B1(s).start()
        C1D(t, s, e).start()

    def op_ownup(e):
        t, s = split(e)

        def go():
            C1U(t, s, e).start()
            B2U(t, s, e).start()

        when(z < 3, go)

    def op_b1(e):
        t, s = split(e)
        B1(s).wait_recv()
        B2D(t, s, e).start()
        S(b1_ref(s, 1 - y), 45 + s).start()

    def op_cx(e):
        t, s = split(e)
        C2(t, s, e).start()

    def op_bx(e):
        t, s = split(e)
        B3(t, s, e).start()

    def op_c1(e):
        t, s = split(e)
        C1U(t, s, e).wait_recv()
        when(jnp.logical_and(t < z, z < 3), lambda: C1U(t, s, e).start())
        when(jnp.logical_and(t > z, z > 0), lambda: C1D(t, s, e).start())
        S(c1_ref(t, s), e).start()

    def op_b2(e):
        t, s = split(e)
        B2U(t, s, e).wait_recv()
        when(jnp.logical_and(t < z, z < 3), lambda: B2U(t, s, e).start())
        when(jnp.logical_and(t > z, z > 0), lambda: B2D(t, s, e).start())
        S(b2_ref(t, s, x), 9 + e).start()

    def op_c2(e):
        t, s = split(e)
        C2(t, s, e).wait_recv()
        C3(t, s, e).start()
        S(c2_ref(t, s, 1 - x), 18 + e).start()

    def op_b3(e):
        t, s = split(e)
        B3(t, s, e).wait_recv()
        S(b2_ref(t, s, 1 - x), 27 + e).start()

    def op_c3(e):
        t, s = split(e)
        C3(t, s, e).wait_recv()
        S(c3_ref(t, s, 1 - y), 36 + e).start()

    def qkv_leaves(n):
        return pltpu.make_async_copy(qkv.at[n], qkv_out.at[n], q_sem.at[n])

    tokT_leaves = pltpu.make_async_copy(tokT, tokT_out, t_sem)

    def probs_leave(h):
        return pltpu.make_async_copy(probs.at[h % 2], probs_out.at[h], p_sem.at[h % 2])

    def op_proj(n):
        def arrive():
            @pl.loop(0, 8)
            def _(k):
                def got(odd):
                    PS(f_ref(k, odd, other), 8 + k).wait_recv()
                    PS(g_ref(k, odd, False, other), 16 + k).wait_recv()

                by_parity(k, got)
                when(z > 0, lambda: PS(z_ref(k, other), k).wait_recv())

        when(n == 0, arrive)

        @pl.loop(0, 3)
        def _(t):
            cols = pl.ds(pl.multiple_of(t * 256, 256), 256)
            qkv[n, cols] = dot_tn(held[0, n // 2, n % 2, :, cols], tokT[...]).astype(bf16)

        qkv_leaves(n).start()

    def op_head(h):
        when(h >= 2, lambda: probs_leave(h - 2).wait())
        attend_head(h, dist, qkv, mixb, probs.at[h % 2])
        probs_leave(h).start()

    line = jnp.logical_and(y == 1, x == 1)
    source = jnp.logical_and(line, z == 3)

    def T(peer, n):
        return remote(tail, peer, ts.at[n], tr.at[0])

    def leave(t):
        return pltpu.make_async_copy(held.at[t], result.at[t], out_sem.at[t])

    def op_other(e):
        def tail_z():
            def go():
                when(z < 3, lambda: T(down, 0).wait_recv())
                when(z > 0, lambda: T(down, 0).start())
                T(yp, 1).start()

            when(line, go)

        def tail_x():
            def go():
                when(y == 0, lambda: T(yp, 1).wait_recv())
                T(xp, 2).start()

            when(x == 1, go)

        def out():
            t = e - 2

            def others():
                @pl.loop(0, 3)
                def _(s):
                    n = (t - 1) * 3 + s

                    def theirs():
                        S(c1_ref(t, s, other), n).wait_recv()
                        S(b2_ref(t, s, x, other), 9 + n).wait_recv()

                    when(t != z, theirs)
                    when(t == z, lambda: S(b1_ref(s, 1 - y, other), 45 + s).wait_recv())
                    S(c2_ref(t, s, 1 - x, other), 18 + n).wait_recv()
                    S(b2_ref(t, s, 1 - x, other), 27 + n).wait_recv()
                    S(c3_ref(t, s, 1 - y, other), 36 + n).wait_recv()

            when(t > 0, others)
            leave(t).start()

        def prepare():
            tokens_come.wait()
            tokT[...] = tokens[...].astype(f32).T.astype(bf16)
            tokT_leaves.start()
            fill_distance(dist, seg_row, column)

        when(e == 0, tail_z)
        when(e == 1, tail_x)
        when(jnp.logical_and(e >= 2, e < 6), out)
        when(e == 6, prepare)

    def norms_here():
        for n in range(6):
            tail[pl.ds(0, 4), pl.ds(n * 128, 128)] = last[pl.ds(n, 4, stride=6)].astype(bf16)

    tail[...] = jnp.zeros_like(tail)
    when(source, norms_here)
    run_plan(z, GATHER_PLAN, [op_p0z, op_p0f, op_p0g, op_own, op_ownup, op_b1, op_bx, op_c1, op_b2, op_c2, op_b3,
                              op_c3, op_proj, op_head, op_other, op_cx])

    when(x == 0, lambda: T(xp, 2).wait_recv())
    when(x == 1, lambda: T(xp, 2).wait_send())

    def tail_sent():
        T(yp, 1).wait_send()
        when(z > 0, lambda: T(down, 0).wait_send())

    when(line, tail_sent)

    @pl.loop(0, 8)
    def _(k):
        def gone(odd):
            PF(k, odd).wait_send()
            PG(k, odd).wait_send()
            PS(f_ref(k, odd), 8 + k).wait_send()
            PS(g_ref(k, odd, False), 16 + k).wait_send()

        by_parity(k, gone)
        when(z < 3, lambda: PZ(k).wait_send())
        when(z > 0, lambda: PS(z_ref(k), k).wait_send())

    @pl.loop(0, 9)
    def _(e):
        t, s = split(e)
        C2(t, s, e).wait_send()
        B3(t, s, e).wait_send()
        C3(t, s, e).wait_send()

        def ups():
            C1U(t, s, e).wait_send()
            B2U(t, s, e).wait_send()

        def downs():
            C1D(t, s, e).wait_send()
            B2D(t, s, e).wait_send()

        when(jnp.logical_and(t <= z, z < 3), ups)
        when(jnp.logical_and(t >= z, z > 0), downs)

        def mine():
            B1(s).wait_send()
            S(b1_ref(s, 1 - y), 45 + s).wait_send()

        def theirs():
            S(c1_ref(t, s), e).wait_send()
            S(b2_ref(t, s, x), 9 + e).wait_send()

        when(t == z, mine)
        when(t != z, theirs)
        S(c2_ref(t, s, 1 - x), 18 + e).wait_send()
        S(b2_ref(t, s, 1 - x), 27 + e).wait_send()
        S(c3_ref(t, s, 1 - y), 36 + e).wait_send()

    norms[...] = tail[pl.ds(0, 4)].astype(f32)
    tokT_leaves.wait()
    for n in range(3):
        qkv_leaves(n).wait()
    for h in (HEADS - 2, HEADS - 1):
        probs_leave(h).wait()
    for t in range(4):
        leave(t).wait()


def gather_attend(blk, before, last, tokens, seg):
    Q = pltpu.SemaphoreType.DMA
    any_space = pl.BlockSpec(memory_space=pl.ANY)
    counts = [8] * 6 + [24, 24, 3, 3] + [9] * 12 + [48, 48, 3, 1]
    return pl.pallas_call(
        gather_attend_kernel,
        in_specs=[VM, VM, VM, any_space, VM],
        out_specs=[any_space, VM, any_space, any_space, VM, any_space],
        out_shape=[
            jax.ShapeDtypeStruct((4, 2, 2, D, D), bf16), jax.ShapeDtypeStruct((4, D), f32),
            *attend_shapes(),
        ],
        scratch_shapes=[
            pltpu.VMEM((4, 2, 2, D, D), bf16), pltpu.VMEM((LEN, LEN), f32), pltpu.VMEM((LEN, 8), f32),
            pltpu.VMEM((LEN, D), bf16), pltpu.VMEM((16, D), bf16),
            pltpu.VMEM((D, LEN), bf16), pltpu.VMEM((3, D, LEN), bf16), pltpu.VMEM((2, LEN, LEN), bf16),
            Q, Q((4,)), Q, Q((3,)), Q((2,)), *[Q((n,)) for n in counts],
        ],
        compiler_params=pltpu.CompilerParams(
            collective_id=1, has_side_effects=True, vmem_limit_bytes=58 << 20
        ),
        name="gather_attend",
    )(blk, before, last, tokens, seg.reshape(1, LEN))


PLANE_ORDER = (1, 2, 3)
BACK_PLAN = (
    (
        7405680, 7471873, 7570180, 488454, 2295925, 2573089, 8393537, 2364545, 345894, 8525430,
        4728834, 7807120, 1523782, 4487222, 2237712, 9574545, 7943987, 8860689, 5667415, 4579349,
        3167099, 3252242, 8665314, 8804485, 9655458, 10589234, 9818165, 9852385, 10699442, 11554980,
        13816215, 5354322, 11642306, 11839398, 11981761, 12892096, 11912135, 15713989, 15724527,
    ),
    (
        7405680, 7471873, 422660, 7671924, 526198, 8422163, 8880769, 364579, 3182967, 7874194,
        2376465, 1447731, 2430073, 2587514, 3642338, 4671016, 165025, 8773684, 8794440, 13645336,
        9802784, 4478870, 5644962, 1417379, 13711511, 10821952, 11707602, 11617624, 14790849, 10900672,
        12727635, 10990421, 12891331, 11878977, 6296261, 11978679, 13878864, 6435425, 15684177,
    ),
    (
        65648, 7565937, 7603728, 8585991, 554464, 8851840, 2502785, 1472130, 161680, 7870353,
        3219833, 2627706, 10588737, 9634976, 14819963, 8750112, 13665872, 4232210, 2376354, 13735207,
        9934407, 10703281, 3658310, 10855617, 12628146, 12727828, 10987095, 377779, 1291336, 3720260,
        12957111, 3298851, 11941063, 2475587, 1399009, 13845842, 5452644, 3499363, 15684948,
    ),
    (
        65648, 7471985, 7602803, 328739, 8397173, 4395393, 8615456, 1278480, 409892, 9539652,
        7807525, 4231698, 7947640, 3380017, 1331248, 8102266, 4383392, 8750087, 10637702, 9744775,
        10692245, 9879728, 2594753, 12759602, 10866771, 11736484, 11839427, 14722756, 12956951, 12006664,
        4601031, 13022742, 13718087, 1626708, 5589032, 6698963, 5715681, 3692135, 15689816,
    ),
)

GATHER_PLAN = (
    (
        196870, 1026, 7406867, 7401746, 1050388, 15787542, 9443093, 2494834, 2303104, 9565557,
        7631858, 2261281, 2127457, 9827248, 8529701, 9630912, 12748737, 16147091, 6788304, 8835793,
        6330034, 16233847, 13924563, 16287189, 6674082, 14129073, 14182019, 6534048, 14247044, 8955874,
        10007656, 14345121, 14399159, 14722211, 12101030, 15050980, 15724513, 15724527,
    ),
    (
        3273200, 3289330, 5243142, 152067, 7704947, 327684, 1050387, 15941969, 4200210, 1143843,
        1318933, 7770134, 8910310, 2565186, 7807525, 2225286, 6694646, 9658773, 16236992, 8616069,
        8966338, 8675986, 14874833, 10596708, 13788564, 6526870, 14013651, 10934230, 14202008, 11755623,
        10855528, 10729184, 14332633, 14987445, 11000759, 14917794, 15055016, 15724513,
    ),
    (
        3535667, 9647348, 7800565, 7733589, 1442806, 1026, 460049, 4556582, 1184646, 16281976,
        5444887, 1110408, 1369703, 9782128, 4478104, 8396839, 6694391, 9859732, 2355748, 2171522,
        15753314, 8503744, 13681249, 14706897, 9556946, 11777426, 13919412, 14002021, 14063459, 14137521,
        14276790, 10936976, 12049370, 10789544, 15048865, 11576739, 14935218, 15724513,
    ),
    (
        16266807, 9976055, 9958998, 419415, 66151, 12059670, 239192, 458769, 1226501, 8721427,
        2166807, 4617510, 1405255, 2418343, 15738736, 2302705, 16085832, 2487141, 2135656, 12697824,
        9552528, 7655888, 13820291, 13890709, 13926514, 6521986, 8508914, 11625620, 14049939, 11917219,
        11821528, 11970656, 9613529, 14867109, 10673060, 11772389, 11706596, 15724515,
    ),
)


Q_PART = 96
COLS = D // 2


def reduce_back_kernel(wide, down, w, qkv_in, dO_in, mixb_in, probs_in, tokT_in, gbranch_in, first, norm_in,
                       grad_in, flat_out, own, sl, lc3, lc2, lcz, lczx, lb3, lbz, lbzx, lb1, lf, lg, lz, stage,
                       dO, mixb, tokT, gbranch, theirs, probs, ds_all, wv, qkv, fchunk, flat, nacc, nx, ny, nz, nc,
                       own_sem, in_sem, p_sem, w_sem, f_sem, g_sem, o_sem, sib_s, sib_r, st_s, st_r,
                       c3s, c3r, b3s, b3r, c2s, c2r, bus, bur, bds, bdr, cus, cur, cds, cdr, b1s, b1r,
                       fs, fr, gs, gr, zs_, zr_, ns, nr, share_s, share_r, aft_s, aft_r):
    i, c, z, y, x = place()
    xp, yp, sib, up, down_peer = partners(i, c, z, y, x)
    base = c * HALF
    mine = pl.ds(pl.multiple_of(base, 16), HALF)
    other = pl.ds(pl.multiple_of((1 - c) * HALF, 16), HALF)
    planes = [wide.at[0], wide.at[1], down]

    def remote(src, dst, peer, s, r):
        return pltpu.make_async_remote_copy(
            src_ref=src, dst_ref=dst, send_sem=s, recv_sem=r, device_id=peer, device_id_type=MESH
        )

    def local_in(t):
        return pltpu.make_async_copy(planes[t - 1].at[:, :, mine], own.at[t], own_sem.at[t])

    def sib_in(t, s, n):
        k = 2 * ((t - 1) * 3 + s) + n
        start, size = (s * B_PART, B_PART) if n == 0 else (3 * B_PART + s * C_PART, C_PART)
        there = pl.ds(pl.multiple_of((1 - c) * HALF + start, 16), size)
        return remote(planes[t - 1].at[:, :, there], sl.at[t, :, :, pl.ds(start, size)], sib, sib_s.at[k], sib_r.at[k])

    for t in PLANE_ORDER:
        local_in(t).start()
    take = [
        pltpu.make_async_copy(a, b, in_sem.at[n])
        for n, (a, b) in enumerate(
            ((qkv_in, qkv), (dO_in, dO), (mixb_in, mixb), (gbranch_in, gbranch), (tokT_in, tokT))
        )
    ]
    for n in range(3):
        take[n].start()

    def probs_come(h):
        return pltpu.make_async_copy(probs_in.at[h], probs.at[h % 2], p_sem.at[h % 2])

    probs_come(0).start()
    enter_more(i, c, z, y, x)
    for t in PLANE_ORDER:
        for s in range(3):
            for n in range(2):
                sib_in(t, s, n).start()
    nacc[...] = norm_in[...]
    NX = remote(nacc, nx, xp, ns.at[0], nr.at[0])
    NY = remote(nacc, ny, yp, ns.at[1], nr.at[1])
    NZ = remote(nacc, nz, up, ns.at[2], nr.at[2])
    NC = remote(nacc, nc, sib, ns.at[3], nr.at[3])
    line = jnp.logical_and(x == 1, y == 1)
    last_line = jnp.logical_and(line, z == 3)
    when(x == 0, lambda: NX.start())

    def rb(s, k=0, size=B_PART):
        return pl.ds(pl.multiple_of(s * B_PART + k, 16), size)

    def rc(s, k=0, size=C_PART):
        return pl.ds(pl.multiple_of(3 * B_PART + s * C_PART + k, 16), size)

    def add_rows(dst, src, rows):
        @pl.loop(0, rows // 16)
        def _(n):
            k = pl.multiple_of(n * 16, 16)
            a = dst(k)
            a[...] = a[...] + src(k)[...]

    r16 = lambda k: pl.ds(k, 16)
    split = lambda e: (e // 3 + 1, e % 3)

    def C3(t, s, e):
        return remote(own.at[t, 1 - y, :, rc(s)], lc3.at[e], yp, c3s.at[e], c3r.at[e])

    def B3(t, s, e):
        return remote(own.at[t, :, 1 - x, rb(s)], lb3.at[e], xp, b3s.at[e], b3r.at[e])

    def C2(t, s, e):
        return remote(own.at[t, y, 1 - x, rc(s)], lc2.at[e], xp, c2s.at[e], c2r.at[e])

    def BU(t, s, e):
        return remote(own.at[t, :, x, rb(s)], lbz.at[e], up, bus.at[e], bur.at[e])

    def BD(t, s, e, extra=False):
        return remote(own.at[t, :, x, rb(s)], lbzx.at[s] if extra else lbz.at[e], down_peer, bds.at[e], bdr.at[e])

    def CU(t, s, e):
        return remote(own.at[t, y, x, rc(s)], lcz.at[e], up, cus.at[e], cur.at[e])

    def CD(t, s, e, extra=False):
        return remote(own.at[t, y, x, rc(s)], lczx.at[s] if extra else lcz.at[e], down_peer, cds.at[e], cdr.at[e])

    def B1(s):
        return remote(own.at[z, 1 - y, x, rb(s)], lb1.at[s], yp, b1s.at[s], b1r.at[s])

    def op_sum(e):
        t, s = split(e)

        for k in (1, 2, 3):
            when(jnp.logical_and(t == k, s == 0), lambda k=k: local_in(k).wait())
            for m in range(3):
                def arrive(k=k, m=m):
                    for n in range(2):
                        sib_in(k, m, n).wait_recv()

                when(e == (k - 1) * 3 + m, arrive)
        add_rows(lambda k: own.at[t, :, :, rb(s, k, 16)], lambda k: sl.at[t, :, :, rb(s, k, 16)], B_PART)
        add_rows(lambda k: own.at[t, :, :, rc(s, k, 16)], lambda k: sl.at[t, :, :, rc(s, k, 16)], C_PART)
        C3(t, s, e).start()
        B3(t, s, e).start()

    def op_c3(e):
        t, s = split(e)
        C3(t, s, e).wait_recv()
        add_rows(lambda k: own.at[t, y, :, rc(s, k, 16)], lambda k: lc3.at[e, :, r16(k)], C_PART)
        C2(t, s, e).start()

    def op_b3(e):
        t, s = split(e)
        B3(t, s, e).wait_recv()
        add_rows(lambda k: own.at[t, :, x, rb(s, k, 16)], lambda k: lb3.at[e, :, r16(k)], B_PART)

    def op_c2(e):
        t, s = split(e)
        C2(t, s, e).wait_recv()
        add_rows(lambda k: own.at[t, y, x, rc(s, k, 16)], lambda k: lc2.at[e, r16(k)], C_PART)

    def op_bz(e):
        t, s = split(e)
        dst = lambda k: own.at[t, :, x, rb(s, k, 16)]

        def from_below():
            BU(t, s, e).wait_recv()
            add_rows(dst, lambda k: lbz.at[e, :, r16(k)], B_PART)

        when(jnp.logical_and(t >= z, z > 0), from_below)

        def from_above():
            BD(t, s, e).wait_recv()
            add_rows(dst, lambda k: lbz.at[e, :, r16(k)], B_PART)

        when(t < z, lambda: when(z < 3, from_above))

        def from_above_last():
            BD(t, s, e).wait_recv()
            add_rows(dst, lambda k: lbzx.at[s, :, r16(k)], B_PART)

        when(jnp.logical_and(t == z, z < 3), from_above_last)
        when(t > z, lambda: BU(t, s, e).start())
        when(t == z - 1, lambda: BD(t, s, e, True).start())
        when(t < z - 1, lambda: BD(t, s, e).start())
        when(t == z, lambda: B1(s).start())

    def op_cz(e):
        t, s = split(e)
        dst = lambda k: own.at[t, y, x, rc(s, k, 16)]

        def from_below():
            CU(t, s, e).wait_recv()
            add_rows(dst, lambda k: lcz.at[e, r16(k)], C_PART)

        when(jnp.logical_and(t >= z, z > 0), from_below)

        def from_above():
            CD(t, s, e).wait_recv()
            add_rows(dst, lambda k: lcz.at[e, r16(k)], C_PART)

        when(t < z, lambda: when(z < 3, from_above))

        def from_above_last():
            CD(t, s, e).wait_recv()
            add_rows(dst, lambda k: lczx.at[s, r16(k)], C_PART)

        when(jnp.logical_and(t == z, z < 3), from_above_last)
        when(t > z, lambda: CU(t, s, e).start())
        when(t == z - 1, lambda: CD(t, s, e, True).start())
        when(t < z - 1, lambda: CD(t, s, e).start())

    def op_b1(e):
        t, s = split(e)
        B1(s).wait_recv()
        add_rows(lambda k: own.at[z, y, x, rb(s, k, 16)], lambda k: lb1.at[s, r16(k)], B_PART)

    def op_head(h):
        def operands():
            for n in range(3):
                take[n].wait()
            for n in (3, 4):
                take[n].start()

        def late_operands():
            for n in (3, 4):
                take[n].wait()

        when(h == 0, operands)
        when(h == 2, late_operands)
        probs_come(h).wait()
        when(h < HEADS - 1, lambda: probs_come(h + 1).start())
        attend_back_head(h, qkv, dO, mixb, probs.at[h % 2], ds_all)

    def columns(g):
        return pl.ds(pl.multiple_of(g * COLS, 128), COLS)

    def stage_copy(e):
        g, n = e // 4, e % 4
        return remote(
            stage.at[e], sl.at[0, n // 2, n % 2, :, columns(g)], sib, st_s.at[e], st_r.at[e]
        )

    def op_dw(e):
        g, n = e // 4, e % 4
        cols = columns(g)

        def put(half, value):
            if half == 0:
                own[0, n // 2, n % 2, :, cols] = value.astype(bf16)
            else:
                stage[e] = value.astype(bf16)

        def inputs():
            right = qkv[n, pl.ds(pl.multiple_of(g * COLS, 128), COLS)]
            for half, rows in ((0, mine), (1, other)):
                put(half, dot_nt(tokT[rows], right))

        def output():
            right = gbranch[:, cols]
            for half, rows in ((0, mine), (1, other)):
                put(half, dot(mixb[rows], right))

        when(n < 3, inputs)
        when(n == 3, output)
        stage_copy(e).start()

    def rq(k, n=0, size=Q_PART):
        return pl.ds(pl.multiple_of(k * Q_PART + n, 16), size)

    def F0(e, g, k, odd):
        src = own.at[0, :, 1 - x, rq(k), columns(g)] if odd else own.at[0, 1 - y, :, rq(k), columns(g)]
        return remote(src, lf.at[e], xp if odd else yp, fs.at[e], fr.at[e])

    def G0(e, g, k, odd):
        if odd:
            return remote(own.at[0, 1 - y, x, rq(k), columns(g)], lg.at[e], yp, gs.at[e], gr.at[e])
        return remote(own.at[0, y, 1 - x, rq(k), columns(g)], lg.at[e], xp, gs.at[e], gr.at[e])

    def Z0(e, g, k):
        return remote(own.at[0, y, x, rq(k), columns(g)], lz.at[e], down_peer, zs_.at[e], zr_.at[e])

    def by_parity(k, fn):
        when(k % 2 == 0, lambda: fn(False))
        when(k % 2 == 1, lambda: fn(True))

    def op_sum0(e):
        g, k = e // 4, e % 4

        def arrive():
            @pl.loop(0, 4)
            def _(n):
                stage_copy(g * 4 + n).wait_recv()

        when(k == 0, arrive)
        add_rows(
            lambda n: own.at[0, :, :, rq(k, n, 16), columns(g)],
            lambda n: sl.at[0, :, :, rq(k, n, 16), columns(g)], Q_PART,
        )
        by_parity(k, lambda odd: F0(e, g, k, odd).start())

    def op_f0(e):
        g, k = e // 4, e % 4

        def turn(odd):
            F0(e, g, k, odd).wait_recv()
            if odd:
                dst = lambda n: own.at[0, :, x, rq(k, n, 16), columns(g)]
            else:
                dst = lambda n: own.at[0, y, :, rq(k, n, 16), columns(g)]
            add_rows(dst, lambda n: lf.at[e, :, r16(n)], Q_PART)
            G0(e, g, k, odd).start()

        by_parity(k, turn)

    def op_g0(e):
        g, k = e // 4, e % 4
        by_parity(k, lambda odd: G0(e, g, k, odd).wait_recv())
        add_rows(lambda n: own.at[0, y, x, rq(k, n, 16), columns(g)], lambda n: lg.at[e, r16(n)], Q_PART)

    def op_z0(e):
        g, k = e // 4, e % 4

        def arrive():
            Z0(e, g, k).wait_recv()
            add_rows(lambda n: own.at[0, y, x, rq(k, n, 16), columns(g)], lambda n: lz.at[e, r16(n)], Q_PART)

        when(z < 3, arrive)
        when(z > 0, lambda: Z0(e, g, k).start())

    def first_in(q):
        return pltpu.make_async_copy(first.at[pl.ds(pl.multiple_of(q * 256, 256), 256)], fchunk, f_sem)

    def grad_out(q):
        return pltpu.make_async_copy(fchunk, grad_in.at[pl.ds(pl.multiple_of(q * 256, 256), 256)], g_sem)

    def weight_in(n):
        target = (probs.at[0, pl.ds(0, D), pl.ds(0, D)], ds_all.at[pl.ds(0, D), pl.ds(0, D)], wv)[n]
        return pltpu.make_async_copy(w.at[0, n // 2, n % 2], target, w_sem.at[n])

    def op_gin(q):
        def weights():
            for n in range(3):
                weight_in(n).wait()

        when(q == 0, weights)
        when(q > 0, lambda: grad_out(q - 1).wait())
        first_in(q).start()
        cols = pl.ds(pl.multiple_of(q * 256, 256), 256)
        d = pl.ds(0, D)
        acc = dot(probs[0, d, d], qkv[0, :, cols]) + dot(ds_all[d, d], qkv[1, :, cols])
        acc = (acc + dot(wv[...], qkv[2, :, cols])).T
        first_in(q).wait()
        fchunk[...] += acc
        grad_out(q).start()

    def op_other(e):
        def norm_y():
            def go():
                NX.wait_recv()
                nacc[...] += nx[...]
                when(y == 0, lambda: NY.start())

            when(x == 1, go)

        def norm_z():
            def go():
                NY.wait_recv()
                nacc[...] += ny[...]

                def more():
                    NZ.wait_recv()
                    nacc[...] += nz[...]

                when(z > 0, more)
                when(z < 3, lambda: NZ.start())
                when(z == 3, lambda: NC.start())

            when(line, go)

        def load():
            for n in range(3):
                weight_in(n).start()

        when(e == 0, norm_y)
        when(e == 1, norm_z)
        when(e == 2, load)

    run_plan(z, BACK_PLAN, [op_sum, op_c3, op_b3, op_c2, op_bz, op_cz, op_b1, op_head, op_dw, op_sum0, op_f0,
                            op_g0, op_z0, op_gin, op_other])

    spread = jnp.logical_or(z == 1, z == 2)

    def flatten(half, get):
        def plain():
            for n in range(6):
                flat[pl.ds(half * (6 * HALF) + n, HALF, stride=6)] = get(pl.ds(0, HALF), pl.ds(n * 128, 128)).astype(f32)

        def swapped():
            for n in range(6):
                for j in range(2):
                    value = get(pl.ds(j * (D // 4), D // 4), pl.ds(n * 128, 128)).astype(f32)
                    flat[pl.ds(half * 12 + j * 6 + n, D // 4, stride=24)] = value

        when(jnp.logical_not(spread), plain)
        when(spread, swapped)

    share = remote(own.at[z, y, x], theirs, sib, share_s, share_r)
    share.start()
    flatten(c, lambda rows, cols: own[z, y, x, rows, cols])

    def leave(half, n):
        rows = pl.ds(pl.multiple_of(half * (6 * HALF), 8), 6 * HALF)
        return pltpu.make_async_copy(flat.at[rows], flat_out.at[rows], o_sem.at[n])

    when(jnp.logical_not(spread), lambda: leave(c, 0).start())

    @pl.loop(0, 9)
    def _(e):
        t, s = split(e)
        C3(t, s, e).wait_send()
        B3(t, s, e).wait_send()
        C2(t, s, e).wait_send()

        def went_up():
            BU(t, s, e).wait_send()
            CU(t, s, e).wait_send()

        def went_down():
            BD(t, s, e).wait_send()
            CD(t, s, e).wait_send()

        when(t > z, went_up)
        when(t < z, went_down)
        when(t == z, lambda: B1(s).wait_send())

    @pl.loop(0, 8)
    def _(e):
        g, k = e // 4, e % 4
        stage_copy(e).wait_send()

        def gone(odd):
            F0(e, g, k, odd).wait_send()
            G0(e, g, k, odd).wait_send()

        by_parity(k, gone)
        when(z > 0, lambda: Z0(e, g, k).wait_send())

    for t in (1, 2, 3):
        for s in range(3):
            for n in range(2):
                sib_in(t, s, n).wait_send()
    when(x == 0, lambda: NX.wait_send())
    when(jnp.logical_and(x == 1, y == 0), lambda: NY.wait_send())
    when(jnp.logical_and(line, z < 3), lambda: NZ.wait_send())

    def norm_last():
        NC.wait_recv()
        NC.wait_send()
        nacc[...] += nc[...]

    when(last_line, norm_last)
    grad_out(3).wait()
    share.wait_recv()
    flatten(1 - c, lambda rows, cols: theirs[rows, cols])
    share.wait_send()
    head_rows, after = pl.ds(0, 24), pl.ds(6 * D, 24)
    when(spread, lambda: leave(c, 0).start())
    leave(1 - c, 2).start()

    def ending():
        for n in range(6):
            flat[pl.ds(6 * D + n, 8, stride=6)] = nacc[:, pl.ds(n * 128, 128)]

    when(i == 15, ending)
    give = remote(flat.at[head_rows], flat.at[after], (c, i - 1), aft_s, aft_r)
    when(i > 0, lambda: give.start())
    when(i < 15, lambda: give.wait_recv())
    leave_after = pltpu.make_async_copy(flat.at[after], flat_out.at[after], o_sem.at[1])
    leave_after.start()
    when(i > 0, lambda: give.wait_send())
    leave(c, 0).wait()
    leave(1 - c, 2).wait()
    leave_after.wait()


def enter_more(i, c, z, y, x):
    barrier = pltpu.get_barrier_semaphore()
    xp, yp, sib, up, down = partners(i, c, z, y, x)

    def signal(peer):
        pl.semaphore_signal(barrier, inc=1, device_id=peer, device_id_type=MESH)

    for peer in (xp, yp, sib):
        signal(peer)
    when(z > 0, lambda: signal(down))
    when(z < 3, lambda: signal(up))
    when(jnp.logical_and(x == 0, i > 0), lambda: signal((c, i - 1)))
    when(jnp.logical_and(x == 1, i < 15), lambda: signal((c, i + 1)))
    more = 1 - jnp.where(i == 0, 1, 0) - jnp.where(i == 15, 1, 0)
    pl.semaphore_wait(barrier, 3 + jnp.minimum(z, 1) + jnp.minimum(3 - z, 1) + more)


def reduce_back(wide, down, w, qkv, dO, mixb, probs, tokT, gbranch, first, norms):
    Q = pltpu.SemaphoreType.DMA
    V = lambda *s: pltpu.VMEM(s, bf16)
    F = lambda *s: pltpu.VMEM(s, f32)
    A = pl.BlockSpec(memory_space=pl.ANY)
    return pl.pallas_call(
        reduce_back_kernel,
        in_specs=[A] * 10 + [VM],
        out_specs=[A, A],
        out_shape=[jax.ShapeDtypeStruct((LEN, D), f32), jax.ShapeDtypeStruct((6 * D + 24, 128), f32)],
        scratch_shapes=[
            V(4, 2, 2, HALF, D), V(4, 2, 2, HALF, D), V(9, 2, C_PART, D), V(9, C_PART, D), V(9, C_PART, D),
            V(3, C_PART, D), V(9, 2, B_PART, D), V(9, 2, B_PART, D), V(3, 2, B_PART, D), V(3, B_PART, D),
            V(8, 2, Q_PART, COLS), V(8, Q_PART, COLS), V(8, Q_PART, COLS), V(8, HALF, COLS),
            V(D, LEN), V(D, LEN), V(D, LEN), V(LEN, D), V(HALF, D), V(2, LEN, LEN), V(LEN, LEN), V(D, D), V(3, D, LEN),
            F(256, D), F(6 * D + 64, 128), F(8, D), F(8, D), F(8, D), F(8, D), F(8, D),
            Q((4,)), Q((5,)), Q((2,)), Q((3,)), Q, Q, Q((3,)), Q((18,)), Q((18,)), Q((8,)), Q((8,)),
            *[Q((9,))] * 14, Q((3,)), Q((3,)), *[Q((8,))] * 6, Q((4,)), Q((4,)), Q, Q, Q, Q,
        ],
        compiler_params=pltpu.CompilerParams(
            collective_id=2, has_side_effects=True, vmem_limit_bytes=55 << 20
        ),
        name="reduce_back",
    )(wide, down, w, qkv, dO, mixb, probs, tokT, gbranch, first, norms)

SQUARE = D * D
TAIL = 4 * D


def from_wide(blocks):
    return blocks.reshape(4, 4, D // 4, D).transpose(0, 2, 1, 3).reshape(D, FF)


def to_wide(value):
    return value.reshape(4, D // 4, 4, D).transpose(0, 2, 1, 3).reshape(2, 2, D, D)


def gather_and_attend(master, tokens, segments):
    count = lax.axis_size("zero")
    index = lax.axis_index("zero")
    size = 16 * SQUARE // count
    last = master[-TAIL:]
    step = TAIL // count
    zeros = jnp.zeros((TAIL,), f32)
    ending = lax.dynamic_slice(jnp.concatenate([last, zeros]), (TAIL - step * (index + 1),), (TAIL,))
    before = lax.ppermute(ending, "zero", [(k, k + 1) for k in range(count - 1)])
    block = lax.dynamic_slice(jnp.concatenate([zeros, master]), (TAIL - step * index,), (size,))
    if count == 16:
        before = jnp.pad(before.reshape(24, 128), ((0, 104), (0, 0)))
        block, last = block.reshape(6 * D, 128), jnp.pad(last.reshape(24, 128), ((0, 40), (0, 0)))
        blocks, norms, *attended = gather_attend(block, before, last, tokens, segments)
    else:
        block = jnp.concatenate([block[:TAIL] + before, block[TAIL:]])
        natural = lax.all_gather(block.astype(bf16).reshape(-1, D), "zero", axis=0, tiled=True)
        parts = natural.reshape(4, 4 * D, D)
        wide = [to_wide(parts[k].reshape(D, FF)) for k in (1, 2)]
        blocks = jnp.stack([parts[0].reshape(2, 2, D, D), *wide, parts[3].reshape(2, 2, D, D)])
        last = last.astype(bf16).astype(f32)
        norms = lax.psum(jnp.where(index == count - 1, last, 0.0), "zero").reshape(4, D)
        attended = attend(tokens, blocks, segments)
    return blocks, norms, *attended


def back_and_scatter(blocks, tokT, qkv, mixed, probs, grad_mixed, first_grad, branch_grad, norm_grads,
                     down_grad, wide_grad):
    count = lax.axis_size("zero")
    index = lax.axis_index("zero")
    if count == 16:
        input_grad, joined = reduce_back(
            wide_grad, down_grad, blocks, qkv, grad_mixed, mixed, probs, tokT, branch_grad, first_grad,
            norm_grads,
        )
        joined = joined.reshape(-1)
    else:
        square, input_grad = attend_back(
            blocks, tokT, qkv, mixed, probs, grad_mixed, first_grad, branch_grad
        )
        natural = [from_wide(wide_grad[k]).reshape(4 * D, D) for k in (0, 1)]
        natural = jnp.concatenate([square.reshape(4 * D, D), *natural, down_grad.reshape(4 * D, D)])
        block = lax.psum_scatter(natural, "zero", scatter_dimension=0, tiled=True)
        block = lax.psum(block.astype(f32), "dp")
        tail = lax.psum(norm_grads[:4], ("dp", "zero"))
        flat = block.reshape(-1)
        after = lax.ppermute(flat[:TAIL], "zero", [(k + 1, k) for k in range(count - 1)])
        joined = jnp.concatenate([flat, jnp.where(index == count - 1, tail.reshape(-1), after)])
    shard = 16 * SQUARE // count + TAIL // count
    return input_grad, lax.dynamic_slice(joined, (TAIL // count * index,), (shard,))


def local(tokens, segments, cotangent, master, moment_one, moment_two):
    blocks, norms, tokT, qkv, mixed, probs = gather_and_attend(master, tokens, segments)
    output, first_grad, grad_mixed, branch_grad, norm_grads, down_grad, wide_grad = feed(
        tokens, cotangent, mixed, blocks, norms
    )
    input_grad, grad_shard = back_and_scatter(
        blocks, tokT, qkv, mixed, probs, grad_mixed, first_grad, branch_grad, norm_grads,
        down_grad.reshape(2, 2, D, D), wide_grad.reshape(2, 2, 2, D, D),
    )
    grad_shard = grad_shard / (lax.axis_size("zero") * lax.axis_size("dp"))
    first = beta_one * moment_one + (1.0 - beta_one) * grad_shard
    second = beta_two * moment_two + (1.0 - beta_two) * grad_shard * grad_shard
    update = first / correct_one / (jnp.sqrt(second / correct_two) + adam_eps)
    master_new = master - learn_rate * (update + weight_decay * master)
    return (
        output,
        input_grad,
        grad_shard,
        first,
        second,
        master_new,
        master_new.astype(jnp.bfloat16),
    )


def solution(mesh):
    return jax.shard_map(
        local,
        mesh=mesh,
        in_specs=(
            P(("dp", "zero"), None),
            P(("dp", "zero")),
            P(("dp", "zero"), None),
            P("zero"),
            P("zero"),
            P("zero"),
        ),
        out_specs=(
            P(("dp", "zero"), None),
            P(("dp", "zero"), None),
            P("zero"),
            P("zero"),
            P("zero"),
            P("zero"),
            P("zero"),
        ),
        check_vma=False,
    )
```
